32 devices in a mesh: row: 4 (over z), col: 8 (over y, x, core).
Axes of the slice: x: 2, y: 2, z: 4, core: 2. Of those that a mesh axis runs over, the one named last changes fastest.
Arguments:
- obj: float32 [2, 1024, 2048], P(None, 'row', 'col'), may hold values from -4.2 to 4.2
- probe: float32 [2, 256, 256], replicated, may hold values from -4.2 to 4.2
- amplitudes: bfloat16 [128, 256, 256], P(('row', 'col')), may hold values from 0.049804688 to 4
- positions: int32 [128, 2], replicated, may hold values from 0 to 1792, as said below
Outputs:
- new_object: float32 [2, 1024, 2048], P(None, 'row', 'col')
- new_probe: float32 [2, 256, 256], replicated
The draws below stay inside these ranges and needn't reach their ends.
Inputs may be any that keep to these rules, and one draw needn't show every extreme that they name: `positions`: entry p is the top-left cell (row, column) of pattern p's window of 256 x 256 cells, which lies inside the object. Pattern p is held by device p // 4 in row-major order of (row, col), and its row offset lies in that device's band of 256 object rows. One device holds at most 2 patterns whose window starts in one tile, and exactly 2 for some tile in every draw; at most 8 windows start in one tile, and in every row of tiles exactly 8 start in one tile.
All inputs are finite; a program needn't handle non-finite values.
Results may differ from the reference program's by a relative error of at most 0.0018.
Values may be sent and summed in bfloat16 or wider, within the bound.
No kernel may reach another device: no remote copies, remote signals or barrier semaphores. Data moves between devices by JAX's collectives and lax.ppermute only.
A program may use at most 128 MiB of HBM per device.

```python
import math
import jax
import jax.numpy as jnp
from jax import lax

M = 256
TH = 256
TW = 256
PAT_DEV = 4
ITERS = 2
SEND = 2
CAP = 8
NY = 1024
NX = 2048
PATTERNS = 128
N_ROW = 4
N_COL = 8


def route_tables(key):
    base = jax.random.fold_in(key, 11)
    band_keys = jax.random.split(base, N_ROW)
    busy_count = CAP // SEND

    def one_band(band_key, band):
        keys = jax.random.split(band_key, 6)
        busy_owner = jax.random.randint(keys[0], (), 0, N_COL)
        source_order = jax.random.permutation(keys[1], N_COL)
        is_busy = jnp.zeros((N_COL,), jnp.int32).at[source_order[:busy_count]].set(1)
        others = jax.random.permutation(keys[2], N_COL - 1).astype(jnp.int32)
        others = others + (others >= busy_owner).astype(jnp.int32)
        drawn_count = PAT_DEV - is_busy * SEND
        first = jnp.cumsum(drawn_count) - drawn_count
        local = jnp.arange(PAT_DEV, dtype=jnp.int32)
        to_busy = (is_busy[:, None] == 1) & (local[None, :] < SEND)
        counter = first[:, None] + local[None, :] - is_busy[:, None] * SEND
        owner = jnp.where(to_busy, busy_owner, others[jnp.maximum(counter, 0) % (N_COL - 1)])
        shuffle_keys = jax.random.split(keys[3], N_COL)
        owner = jax.vmap(lambda shuffle_key, values: values[jax.random.permutation(shuffle_key, PAT_DEV)])(shuffle_keys, owner)
        y_limit = jnp.where(band == N_ROW - 1, TH - M + 1, TH)
        y_start = band * TH + jax.random.randint(keys[4], (N_COL, PAT_DEV), 0, y_limit)
        x_limit = jnp.where(owner == N_COL - 1, TW - M + 1, TW)
        x_start = owner * TW + jax.random.randint(keys[5], (N_COL, PAT_DEV), 0, x_limit)
        return (owner, y_start, x_start)
    owners, y_all, x_all = jax.vmap(one_band)(band_keys, jnp.arange(N_ROW, dtype=jnp.int32))
    positions = jnp.stack([y_all.reshape(-1), x_all.reshape(-1)], axis=-1).astype(jnp.int32)
    return positions


def draw_positions(key, part):
    return route_tables(key)


def levels(key, dims, cuts, low, largest):
    gain = 1.0
    for position, shards_of in cuts:
        steps = jax.random.uniform(jax.random.fold_in(jax.random.fold_in(key, 6), position), (shards_of,), jnp.float32, low / len(cuts), largest / len(cuts))
        gain = gain * jnp.repeat(jnp.exp(steps), dims[position] // shards_of).reshape((-1,) + (1,) * (len(dims) - 1 - position))
    return gain


def centred(key, shape, deviation, reach, shards=(), kind=jnp.bfloat16):
    entries = jax.random.normal(key, shape, jnp.float32) * deviation
    if len(shards) > 0:
        entries = levels(key, shape, shards, -0.22, 0.18) * entries
    return jnp.clip(entries, min=-reach, max=reach).astype(kind)


def setup_inputs(seed: int = 0) -> dict:
    streams_of = jax.random.split(jax.random.key(seed), 5)
    obj = centred(streams_of[0], (2, NY, NX), 0.7, 4.2, ((1, 4), (2, 8)), jnp.float32)
    probe = centred(streams_of[1], (2, M, M), 0.7, 4.2, (), jnp.float32)
    amplitudes = jnp.clip(jnp.exp(math.log(4.0) - 4.3859405 * jax.random.uniform(streams_of[2], (PATTERNS, M, M), jnp.float32) ** levels(streams_of[2], (PATTERNS, M, M), ((0, 32),), -0.2, 0.2)), 0.049804688, 4.0).astype(jnp.bfloat16)
    positions = draw_positions(jax.random.fold_in(streams_of[4], 71), 0)
    return {"obj": obj, "probe": probe, "amplitudes": amplitudes, "positions": positions}


amplitude_floor = 0.1
object_regular = 0.5
probe_regular = 1.0

def reference(obj, probe, amplitudes, positions):
    order = probe.shape[1]
    listed = jnp.arange(positions.shape[0], dtype=jnp.int32)
    obj_re, obj_im = (obj[0], obj[1])
    probe_re, probe_im = (probe[0], probe[1])
    for sweep in range(ITERS):
        probe_c = lax.complex(probe_re, probe_im)
        obj_c = lax.complex(obj_re, obj_im)
        power = probe_re * probe_re + probe_im * probe_im

        def visit(carry, index):
            gathered, numer = carry
            spot = positions[index].astype(jnp.int32)
            window = lax.dynamic_slice(obj_c, (spot[0], spot[1]), (order, order))
            exit_wave = probe_c * window
            far = jnp.fft.fft2(exit_wave, norm='ortho')
            factor = amplitudes[index].astype(obj.dtype) / jnp.sqrt(far.real * far.real + far.imag * far.imag + amplitude_floor)
            revised = jnp.fft.ifft2(far * factor, norm='ortho')
            change = revised - exit_wave
            obj_term = jnp.conj(probe_c) * change
            piece = jnp.stack([obj_term.real, obj_term.imag, power])
            start = (jnp.int32(0), spot[0], spot[1])
            block = lax.dynamic_slice(gathered, start, (3, order, order))
            gathered = lax.dynamic_update_slice(gathered, block + piece, start)
            probe_term = jnp.conj(window) * change
            numer = numer + jnp.stack([probe_term.real, probe_term.imag, window.real * window.real + window.imag * window.imag])
            return ((gathered, numer), None)
        start_sums = (jnp.zeros((3,) + obj_re.shape, obj.dtype), jnp.zeros((3, order, order), obj.dtype))
        (gathered, numer), unused = lax.scan(visit, start_sums, listed)
        new_re = obj_re + gathered[0] / (gathered[2] + object_regular)
        new_im = obj_im + gathered[1] / (gathered[2] + object_regular)
        probe_re = probe_re + numer[0] / (numer[2] + probe_regular)
        probe_im = probe_im + numer[1] / (numer[2] + probe_regular)
        obj_re, obj_im = (new_re, new_im)
    return (jnp.stack([obj_re, obj_im]), jnp.stack([probe_re, probe_im]))
```

```python
import functools

import jax
import jax.numpy as jnp
import numpy as np
from jax import lax
from jax.experimental import pallas as pl
from jax.experimental.pallas import tpu as pltpu
from jax.sharding import PartitionSpec as P

ITERS = 2
SEND = 2

amplitude_floor = 0.1
object_regular = 0.5
probe_regular = 1.0

LANES = 128
SUBLANES = 8
CHUNK = 32
VMEM = pl.BlockSpec(memory_space=pltpu.VMEM)
SMEM = pl.BlockSpec(memory_space=pltpu.SMEM)
ANY = pl.BlockSpec(memory_space=pl.ANY)
f32 = jnp.float32
bf16 = jnp.bfloat16


def tables(order):
    half = order // 2
    counter = np.arange(half)
    angles = 2.0 * np.pi * ((counter[:, None] * counter[None, :]) % half) / half
    cos, sin = np.cos(angles), np.sin(angles)
    scale = 1.0 / np.sqrt(order)
    plus = np.block([[cos, sin], [-sin, cos]]) * scale
    minus = np.block([[cos, -sin], [sin, cos]]) * scale

    def halves(matrix):
        high = matrix.astype(jnp.bfloat16)
        low = (matrix - high.astype(np.float64)).astype(jnp.bfloat16)
        return high, low

    plus_high, plus_low = halves(plus)
    minus_high, minus_low = halves(minus)
    along_rows = np.stack(
        [
            np.concatenate([plus_high, plus_high, plus_low], axis=1),
            np.concatenate([minus_high, minus_high, minus_low], axis=1),
        ]
    )
    along_cols = np.stack(
        [
            np.concatenate([minus_high, minus_high, minus_low], axis=0),
            np.concatenate([plus_high, plus_high, plus_low], axis=0),
        ]
    )
    turn = 2.0 * np.pi * counter / order
    twiddle = np.stack([np.cos(turn), -np.sin(turn)]).astype(np.float32)
    twiddle_cols = np.broadcast_to(twiddle[:, None, :], (2, 8, half))
    twiddle_rows = np.broadcast_to(twiddle[:, :, None], (2, half, half))
    sorting = np.zeros((order, order), np.float32)
    sorting[np.arange(half), 2 * np.arange(half)] = 1.0
    sorting[half + np.arange(half), 2 * np.arange(half) + 1] = 1.0
    return (
        jnp.asarray(along_rows),
        jnp.asarray(along_cols),
        jnp.asarray(np.ascontiguousarray(twiddle_cols)),
        jnp.asarray(np.ascontiguousarray(twiddle_rows)),
        jnp.asarray(np.stack([sorting, sorting.T]).astype(jnp.bfloat16)),
    )


def list_patterns(dims, pos_ref, me_ref, ys_ref, xs_ref, slots_ref):
    tile_rows, tile_cols, pat_count, col_count, capacity = dims
    my_row, my_col = me_ref[0], me_ref[1]
    band_count = pat_count * col_count
    first = my_row * band_count

    def visit(index, carry):
        found, source, rank = carry
        y = pos_ref[2 * (first + index)]
        x = pos_ref[2 * (first + index) + 1]
        here = lax.div(x, tile_cols) == my_col
        holder = lax.div(index, pat_count)
        rank = jnp.where(holder == source, rank, 0)

        @pl.when(here & (found < capacity))
        def _():
            ys_ref[found] = y - my_row * tile_rows
            xs_ref[found] = x - my_col * tile_cols
            slots_ref[found] = holder * SEND + jnp.minimum(rank, SEND - 1)

        step = here.astype(jnp.int32)
        return found + step, holder, rank + step

    found, _, _ = lax.fori_loop(0, band_count, visit, (jnp.int32(0), jnp.int32(-1), jnp.int32(0)))
    return jnp.minimum(found, capacity)


def lane_index(rows):
    return lax.broadcasted_iota(jnp.int32, (rows, LANES), 1)


def shifted_left(tiles, shift):
    lane = lane_index(tiles[0].shape[0])
    turn = lax.rem(LANES - shift, LANES)
    rolled = [pltpu.roll(tile, turn, axis=1) for tile in tiles]
    inside = lane < LANES - shift
    return [jnp.where(inside, a, b) for a, b in zip(rolled[:-1], rolled[1:])]


def shifted_right(tiles, shift):
    lane = lane_index(tiles[0].shape[0])
    rolled = [pltpu.roll(tile, shift, axis=1) for tile in tiles]
    outside = lane < shift
    zero = jnp.zeros_like(rolled[0])
    firsts = [zero] + rolled
    seconds = rolled + [zero]
    return [jnp.where(outside, a, b) for a, b in zip(firsts, seconds)]


def row_groups(tile):
    return [tile[k : k + SUBLANES] for k in range(0, tile.shape[0], SUBLANES)]


def shifted_up(tile, shift):
    row = lax.broadcasted_iota(jnp.int32, (SUBLANES, LANES), 0)
    turn = lax.rem(SUBLANES - shift, SUBLANES)
    rolled = [pltpu.roll(group, turn, axis=0) for group in row_groups(tile)]
    inside = row < SUBLANES - shift
    return jnp.concatenate([jnp.where(inside, a, b) for a, b in zip(rolled[:-1], rolled[1:])], axis=0)


def shifted_down(before, tile, shift):
    row = lax.broadcasted_iota(jnp.int32, (SUBLANES, LANES), 0)
    rolled = [before] + [pltpu.roll(group, shift, axis=0) for group in row_groups(tile)]
    outside = row < shift
    return rolled[-1], jnp.concatenate([jnp.where(outside, a, b) for a, b in zip(rolled[:-1], rolled[1:])], axis=0)


class Deposit:
    def __init__(self, add, top, left):
        self.add = add
        self.row = pl.multiple_of(lax.div(top, SUBLANES) * SUBLANES, SUBLANES)
        self.col = pl.multiple_of(lax.div(left, LANES) * LANES, LANES)
        self.down = lax.rem(top, SUBLANES)
        self.right = lax.rem(left, LANES)
        self.carried = None

    def place(self, first, tiles):
        moved = jnp.concatenate(shifted_right(tiles, self.right), axis=1)
        self.add(pl.ds(self.row + first, tiles[0].shape[0]), pl.ds(self.col, moved.shape[1]), moved)

    def put(self, first, tiles):
        if self.carried is None:
            self.carried = [jnp.zeros((SUBLANES, LANES), f32) for _ in tiles]
        pairs = [shifted_down(before, tile, self.down) for before, tile in zip(self.carried, tiles)]
        self.carried = [carried for carried, _ in pairs]
        self.place(first, [tile for _, tile in pairs])

    def finish(self, first):
        row = lax.broadcasted_iota(jnp.int32, (SUBLANES, LANES), 0)
        self.place(first, [jnp.where(row < self.down, tile, 0.0) for tile in self.carried])


def lane_tiles(value):
    return [value[:, k : k + LANES] for k in range(0, value.shape[1], LANES)]


def store_split(ref, rows, cols, value):
    high = value.astype(bf16)
    ref[0, rows, cols] = high
    ref[1, rows, cols] = (value - high.astype(f32)).astype(bf16)


def right_dot(x_ref, table):
    left = jnp.concatenate([x_ref[0], x_ref[1], x_ref[0]], axis=1)
    return jnp.dot(left, table, preferred_element_type=f32)


def left_dot(table, x_ref):
    right = jnp.concatenate([x_ref[0], x_ref[1], x_ref[0]], axis=0)
    return jnp.dot(table, right, preferred_element_type=f32)


def cut_chunk(ext_ref, comp, first, top, left, rows):
    row = pl.multiple_of(lax.div(top, SUBLANES) * SUBLANES, SUBLANES)
    col = pl.multiple_of(lax.div(left, LANES) * LANES, LANES)
    block = ext_ref[comp, pl.ds(row + first, rows + SUBLANES), pl.ds(col, 3 * LANES)]
    tiles = shifted_left(lane_tiles(block), lax.rem(left, LANES))
    return [shifted_up(tile, lax.rem(top, SUBLANES)) for tile in tiles]


def forward(order, ext_ref, probe_ref, consts, y, x, win_ref, power_ref, weight, xa_ref, xb_ref, ya_ref, yb_ref, far_ref):
    rows_table, cols_table, tw_cols, tw_rows = consts
    half = order // 2
    tw_re = jnp.concatenate([tw_cols[0]] * (CHUNK // 8), axis=0)
    tw_im = jnp.concatenate([tw_cols[1]] * (CHUNK // 8), axis=0)
    for first in range(0, order, CHUNK):
        rows = pl.ds(first, CHUNK)
        win_re = cut_chunk(ext_ref, 0, first, y, x, CHUNK)
        win_im = cut_chunk(ext_ref, 1, first, y, x, CHUNK)
        exits = []
        for k in range(2):
            cols = pl.ds(k * half, half)
            win_ref[0, rows, cols] = win_re[k]
            win_ref[1, rows, cols] = win_im[k]
            power_ref[rows, cols] += weight * (win_re[k] * win_re[k] + win_im[k] * win_im[k])
            p_re, p_im = probe_ref[0, rows, cols], probe_ref[1, rows, cols]
            exits.append((p_re * win_re[k] - p_im * win_im[k], p_re * win_im[k] + p_im * win_re[k]))
        (lo_re, lo_im), (hi_re, hi_im) = exits
        store_split(xa_ref, rows, pl.ds(0, half), lo_re + hi_re)
        store_split(xa_ref, rows, pl.ds(half, half), lo_im + hi_im)
        d_re, d_im = lo_re - hi_re, lo_im - hi_im
        store_split(xb_ref, rows, pl.ds(0, half), d_re * tw_re - d_im * tw_im)
        store_split(xb_ref, rows, pl.ds(half, half), d_re * tw_im + d_im * tw_re)
    yield
    ya_ref[...] = right_dot(xa_ref, cols_table[0])
    yb_ref[...] = right_dot(xb_ref, cols_table[0])
    yield
    for first in range(0, half, CHUNK):
        rows = pl.ds(first, CHUNK)
        below = pl.ds(half + first, CHUNK)
        t_re, t_im = tw_rows[0, rows, :], tw_rows[1, rows, :]
        for k, y_ref in enumerate((ya_ref, yb_ref)):
            cols = pl.ds(k * half, half)
            up_re, up_im = y_ref[rows, 0:half], y_ref[rows, half:order]
            dn_re, dn_im = y_ref[below, 0:half], y_ref[below, half:order]
            store_split(xa_ref, rows, cols, up_re + dn_re)
            store_split(xa_ref, below, cols, up_im + dn_im)
            d_re, d_im = up_re - dn_re, up_im - dn_im
            store_split(xb_ref, rows, cols, d_re * t_re - d_im * t_im)
            store_split(xb_ref, below, cols, d_re * t_im + d_im * t_re)
    yield
    far_ref[0] = left_dot(rows_table[0], xa_ref)
    far_ref[1] = left_dot(rows_table[0], xb_ref)
    yield


def backward(order, far_ref, amp_ref, consts, y, x, weight, probe_ref, win_ref, xa_ref, xb_ref, ya_ref, yb_ref, grad_ref, numer_ref):
    rows_table, cols_table, tw_cols, tw_rows = consts
    half = order // 2
    tw_re = jnp.concatenate([tw_cols[0]] * (CHUNK // 8), axis=0)
    tw_im = jnp.concatenate([tw_cols[1]] * (CHUNK // 8), axis=0)
    for k, x_ref in enumerate((xa_ref, xb_ref)):
        for first in range(0, half, CHUNK):
            rows = pl.ds(first, CHUNK)
            below = pl.ds(half + first, CHUNK)
            far_re, far_im = far_ref[k, rows, :], far_ref[k, below, :]
            amp = amp_ref[pl.ds(k * half + first, CHUNK), :].astype(f32)
            factor = amp * lax.rsqrt(far_re * far_re + far_im * far_im + amplitude_floor)
            store_split(x_ref, rows, slice(None), far_re * factor)
            store_split(x_ref, below, slice(None), far_im * factor)
    yield
    ya_ref[...] = left_dot(rows_table[1], xa_ref)
    yb_ref[...] = left_dot(rows_table[1], xb_ref)
    yield
    for first in range(0, half, CHUNK):
        rows = pl.ds(first, CHUNK)
        below = pl.ds(half + first, CHUNK)
        t_re, t_im = tw_rows[0, rows, :], tw_rows[1, rows, :]
        for k, x_ref in enumerate((xa_ref, xb_ref)):
            cols = slice(k * half, (k + 1) * half)
            a_re, a_im = ya_ref[rows, cols], ya_ref[below, cols]
            b_re, b_im = yb_ref[rows, cols], yb_ref[below, cols]
            c_re, c_im = b_re * t_re + b_im * t_im, b_im * t_re - b_re * t_im
            store_split(x_ref, rows, pl.ds(0, half), a_re + c_re)
            store_split(x_ref, rows, pl.ds(half, half), a_im + c_im)
            store_split(x_ref, below, pl.ds(0, half), a_re - c_re)
            store_split(x_ref, below, pl.ds(half, half), a_im - c_im)
    yield
    ya_ref[...] = right_dot(xa_ref, cols_table[1])
    yb_ref[...] = right_dot(xb_ref, cols_table[1])
    yield

    def adder(comp):
        def add(rows, cols, moved):
            grad_ref[comp, rows, cols] += moved

        return add

    deposits = [Deposit(adder(comp), y, x) for comp in range(2)]
    for first in range(0, order, CHUNK):
        rows = pl.ds(first, CHUNK)
        a_re, a_im = ya_ref[rows, 0:half], ya_ref[rows, half:order]
        b_re, b_im = yb_ref[rows, 0:half], yb_ref[rows, half:order]
        c_re, c_im = b_re * tw_re + b_im * tw_im, b_im * tw_re - b_re * tw_im
        waves = [(a_re + c_re, a_im + c_im), (a_re - c_re, a_im - c_im)]
        terms = ([], [])
        for k, (wave_re, wave_im) in enumerate(waves):
            cols = pl.ds(k * half, half)
            wave_re, wave_im = weight * wave_re, weight * wave_im
            p_re, p_im = probe_ref[0, rows, cols], probe_ref[1, rows, cols]
            w_re, w_im = win_ref[0, rows, cols], win_ref[1, rows, cols]
            terms[0].append(p_re * wave_re + p_im * wave_im)
            terms[1].append(p_re * wave_im - p_im * wave_re)
            numer_ref[0, rows, cols] += w_re * wave_re + w_im * wave_im
            numer_ref[1, rows, cols] += w_re * wave_im - w_im * wave_re
        for comp in range(2):
            deposits[comp].put(first, terms[comp])
    for deposit in deposits:
        deposit.finish(order)
    yield


def interleaved(*stages):
    live = list(stages)
    while live:
        still = []
        for stage in live:
            try:
                next(stage)
                still.append(stage)
            except StopIteration:
                pass
        live = still


def outgoing_kernel(dims, pos_ref, me_ref, amp_ref, out_ref, sems):
    tile_rows, tile_cols, pat_count, col_count, capacity = dims
    first = (me_ref[0] * col_count + me_ref[1]) * pat_count
    owners = [lax.div(pos_ref[2 * (first + k) + 1], tile_cols) for k in range(pat_count)]
    copies = []
    for k in range(pat_count):
        rank = sum(((owners[e] == owners[k]).astype(jnp.int32) for e in range(k)), jnp.int32(0))
        slot = owners[k] * SEND + jnp.minimum(rank, SEND - 1)
        copies.append(pltpu.make_async_copy(amp_ref.at[k], out_ref.at[slot], sems.at[k]))
        copies[-1].start()
    for copy in copies:
        copy.wait()


def weights_kernel(dims, span, pos_ref, me_ref, probe_ref, out_ref, sums_ref, power_ref):
    tile_rows, tile_cols, pat_count, col_count, capacity = dims
    order = probe_ref.shape[1]
    top = (me_ref[0] - 1) * tile_rows
    left = (me_ref[1] - 1) * tile_cols
    for first in range(0, sums_ref.shape[0], order):
        sums_ref[pl.ds(first, order), :] = jnp.zeros((order, sums_ref.shape[1]), f32)
    power_ref[...] = probe_ref[0] * probe_ref[0] + probe_ref[1] * probe_ref[1]

    def visit(index, carry):
        y = pos_ref[2 * index] - top
        x = pos_ref[2 * index + 1] - left

        @pl.when((y > 0) & (y < (span + 1) * tile_rows) & (x > 0) & (x < (span + 1) * tile_cols))
        def _():
            def add(rows, cols, moved):
                sums_ref[rows, cols] += moved

            deposit = Deposit(add, y, x)
            for first in range(0, order, CHUNK):
                deposit.put(first, lane_tiles(power_ref[pl.ds(first, CHUNK), :]))
            deposit.finish(order)

        return carry

    lax.fori_loop(0, pos_ref.shape[0] // 2, visit, 0)
    out_ref[...] = sums_ref[tile_rows : (span + 1) * tile_rows, tile_cols : (span + 1) * tile_cols]


def first_half_kernel(dims, pos_ref, me_ref, own_ref, right_ref, below_ref, diag_ref, probe_ref, rows_table, cols_table, tw_cols, tw_rows,
                      far_out, power_out, ext_ref, win_ref, xa_ref, xb_ref, ya_ref, yb_ref, far_ref, ys_ref, xs_ref, slots_ref, sems):
    tile_rows, tile_cols, pat_count, col_count, capacity = dims
    order = probe_ref.shape[1]
    count = list_patterns(dims, pos_ref, me_ref, ys_ref, xs_ref, slots_ref)
    ext_ref[:, 0:tile_rows, 0:tile_cols] = own_ref[...]
    ext_ref[:, 0:tile_rows, tile_cols:] = right_ref[...]
    ext_ref[:, tile_rows:, 0:tile_cols] = below_ref[...]
    ext_ref[:, tile_rows:, tile_cols:] = diag_ref[...]
    power_out[...] = jnp.zeros_like(power_out)
    consts = (rows_table, cols_table, tw_cols, tw_rows)

    def pair(step, carry):
        stages = []
        for k in range(2):
            listed = 2 * step + k
            weight = (listed < count).astype(f32)
            index = jnp.minimum(listed, count - 1)
            stages.append(forward(order, ext_ref, probe_ref, consts, ys_ref[index], xs_ref[index], win_ref.at[k], power_out, weight,
                                  xa_ref.at[k], xb_ref.at[k], ya_ref.at[k], yb_ref.at[k], far_ref.at[listed]))
        interleaved(*stages)
        for k in range(2):
            listed = 2 * step + k
            pltpu.make_async_copy(far_ref.at[listed], far_out.at[listed], sems.at[listed]).start()
        return carry

    pairs = lax.div(count + 1, 2)
    lax.fori_loop(0, pairs, pair, 0)

    def settle(listed, carry):
        pltpu.make_async_copy(far_ref.at[listed], far_out.at[listed], sems.at[listed]).wait()
        return carry

    lax.fori_loop(0, 2 * pairs, settle, 0)


def second_half_kernel(dims, pos_ref, me_ref, own_ref, right_ref, below_ref, diag_ref, probe_ref, far_in, amp_in, rows_table, cols_table, tw_cols, tw_rows, sorting,
                       top_out, bottom_out, numer_out, amp_out,
                       ext_ref, grad_ref, win_ref, xa_ref, xb_ref, ya_ref, yb_ref, far_ref, amp_ref, sorted_ref, ys_ref, xs_ref, slots_ref, far_sems, amp_sems, out_sems):
    tile_rows, tile_cols, pat_count, col_count, capacity = dims
    order = probe_ref.shape[1]
    half = order // 2
    count = list_patterns(dims, pos_ref, me_ref, ys_ref, xs_ref, slots_ref)
    pairs = lax.div(count + 1, 2)

    def copies(listed):
        return (
            pltpu.make_async_copy(far_in.at[listed], far_ref.at[listed], far_sems.at[listed]),
            pltpu.make_async_copy(amp_in.at[slots_ref[jnp.minimum(listed, count - 1)]], amp_ref.at[listed], amp_sems.at[listed]),
        )

    def begin(listed, carry):
        for copy in copies(listed):
            copy.start()
        return carry

    lax.fori_loop(0, 2 * pairs, begin, 0)
    ext_ref[:, 0:tile_rows, 0:tile_cols] = own_ref[...]
    ext_ref[:, 0:tile_rows, tile_cols:] = right_ref[...]
    ext_ref[:, tile_rows:, 0:tile_cols] = below_ref[...]
    ext_ref[:, tile_rows:, tile_cols:] = diag_ref[...]
    grad_ref[...] = jnp.zeros_like(grad_ref)
    numer_out[...] = jnp.zeros_like(numer_out)
    consts = (rows_table, cols_table, tw_cols, tw_rows)

    def pair(step, carry):
        stages = []
        for k in range(2):
            listed = 2 * step + k
            for copy in copies(listed):
                copy.wait()
        for k in range(2):
            listed = 2 * step + k
            weight = (listed < count).astype(f32)
            index = jnp.minimum(listed, count - 1)
            y, x = ys_ref[index], xs_ref[index]
            rows_sorted = jnp.dot(sorting[0], amp_ref[listed], preferred_element_type=f32).astype(bf16)
            sorted_ref[listed] = jnp.dot(rows_sorted, sorting[1], preferred_element_type=f32).astype(bf16)
            for first in range(0, order, CHUNK):
                for comp in range(2):
                    for c, tile in enumerate(cut_chunk(ext_ref, comp, first, y, x, CHUNK)):
                        win_ref[k, comp, pl.ds(first, CHUNK), pl.ds(c * half, half)] = tile
            stages.append(backward(order, far_ref.at[listed], sorted_ref.at[listed], consts, y, x, weight, probe_ref, win_ref.at[k],
                                   xa_ref.at[k], xb_ref.at[k], ya_ref.at[k], yb_ref.at[k], grad_ref, numer_out))
        interleaved(*stages)
        for k in range(2):
            listed = 2 * step + k
            pltpu.make_async_copy(sorted_ref.at[listed], amp_out.at[listed], out_sems.at[listed]).start()
        return carry

    lax.fori_loop(0, pairs, pair, 0)
    top_out[...] = grad_ref[:, 0:tile_rows, :]
    bottom_out[...] = grad_ref[:, tile_rows:, :]

    def settle(listed, carry):
        pltpu.make_async_copy(sorted_ref.at[listed], amp_out.at[listed], out_sems.at[listed]).wait()
        return carry

    lax.fori_loop(0, 2 * pairs, settle, 0)


def whole_kernel(dims, pos_ref, me_ref, own_ref, right_ref, below_ref, diag_ref, sum_left_ref, sum_right_ref, from_left_ref, from_right_ref, weights_ref,
                 probe_ref, amp_in, rows_table, cols_table, tw_cols, tw_rows,
                 current_out, own_out, right_out, below_out, diag_out, numer_out,
                 ext_ref, grad_ref, win_ref, xa_ref, xb_ref, ya_ref, yb_ref, far_ref, amp_ref, ys_ref, xs_ref, slots_ref, amp_sems):
    tile_rows, tile_cols, pat_count, col_count, capacity = dims
    order = probe_ref.shape[1]
    count = list_patterns(dims, pos_ref, me_ref, ys_ref, xs_ref, slots_ref)
    pairs = lax.div(count + 1, 2)

    def fetch(listed):
        return pltpu.make_async_copy(amp_in.at[jnp.minimum(listed, count - 1)], amp_ref.at[listed], amp_sems.at[listed])

    def begin(listed, carry):
        fetch(listed).start()
        return carry

    lax.fori_loop(0, 2 * pairs, begin, 0)
    olds = ((own_ref, right_ref), (below_ref, diag_ref))
    sums = ((sum_left_ref, from_left_ref), (sum_right_ref, from_right_ref))
    for i in range(2):
        for j in range(2):
            for first in range(0, tile_rows, CHUNK):
                rows = pl.ds(first, CHUNK)
                ext_rows = pl.ds(i * tile_rows + first, CHUNK)
                ext_cols = pl.ds(j * tile_cols, tile_cols)
                scale = 1.0 / (weights_ref[ext_rows, ext_cols] + object_regular)
                for comp in range(2):
                    total = sums[j][0][comp, ext_rows, :] + sums[j][1][comp, ext_rows, :]
                    ext_ref[comp, ext_rows, ext_cols] = (object_regular * olds[i][j][comp, rows, :] + total) * scale
    current_out[...] = ext_ref[:, 0:tile_rows, 0:tile_cols]
    grad_ref[...] = jnp.zeros_like(grad_ref)
    numer_out[...] = jnp.zeros_like(numer_out)
    consts = (rows_table, cols_table, tw_cols, tw_rows)

    def pair(step, carry):
        stages = []
        for k in range(2):
            fetch(2 * step + k).wait()
        for k in range(2):
            listed = 2 * step + k
            weight = (listed < count).astype(f32)
            index = jnp.minimum(listed, count - 1)
            y, x = ys_ref[index], xs_ref[index]

            def both(k=k, listed=listed, weight=weight, y=y, x=x):
                yield from forward(order, ext_ref, probe_ref, consts, y, x, win_ref.at[k], numer_out.at[2], weight,
                                   xa_ref.at[k], xb_ref.at[k], ya_ref.at[k], yb_ref.at[k], far_ref.at[k])
                yield from backward(order, far_ref.at[k], amp_ref.at[listed], consts, y, x, weight, probe_ref, win_ref.at[k],
                                    xa_ref.at[k], xb_ref.at[k], ya_ref.at[k], yb_ref.at[k], grad_ref, numer_out)

            stages.append(both())
        interleaved(*stages)
        return carry

    lax.fori_loop(0, pairs, pair, 0)
    own_out[...] = grad_ref[:, 0:tile_rows, 0:tile_cols]
    right_out[...] = grad_ref[:, 0:tile_rows, tile_cols:]
    below_out[...] = grad_ref[:, tile_rows:, 0:tile_cols]
    diag_out[...] = grad_ref[:, tile_rows:, tile_cols:]


def shape(dims, dtype=f32):
    return jax.ShapeDtypeStruct(dims, dtype)


def work_scratch(order):
    return [
        pltpu.VMEM((2, 2, order, order), f32),
        pltpu.VMEM((2, 2, order, order), bf16),
        pltpu.VMEM((2, 2, order, order), bf16),
        pltpu.VMEM((2, order, order), f32),
        pltpu.VMEM((2, order, order), f32),
    ]


def list_scratch(capacity):
    return [pltpu.SMEM((capacity,), jnp.int32)] * 3


def call(kernel, outs, out_specs, in_specs, scratch, flops, limit=48 << 20):
    return pl.pallas_call(
        kernel,
        out_shape=outs,
        out_specs=out_specs,
        in_specs=in_specs,
        scratch_shapes=scratch,
        compiler_params=pltpu.CompilerParams(vmem_limit_bytes=limit),
        cost_estimate=pl.CostEstimate(flops=flops, bytes_accessed=8 << 20, transcendentals=0),
    )


def passed_along(value, axis, steps):
    count = lax.axis_size(axis)
    leading, last = (max(0, -steps), min(count, count - steps))
    return lax.ppermute(value, axis, [(source, source + steps) for source in range(leading, last)])


def passed_both(value, row_steps, col_steps):
    rows, cols = lax.axis_size("row"), lax.axis_size("col")
    pairs = []
    for r in range(rows):
        for c in range(cols):
            if 0 <= r + row_steps < rows and 0 <= c + col_steps < cols:
                pairs.append((r * cols + c, (r + row_steps) * cols + c + col_steps))
    return lax.ppermute(value, ("row", "col"), pairs)


def swapped(value, axis, mask):
    return lax.ppermute(value, axis, [(k, k ^ mask) for k in range(lax.axis_size(axis))])


def summed_over_rows(value):
    parts = [value] + [swapped(value, "row", mask) for mask in range(1, lax.axis_size("row"))]
    while len(parts) > 1:
        parts = [a + b for a, b in zip(parts[::2], parts[1::2])]
    return parts[0]


def probe_update(probe, numer):
    cols = lax.axis_size("col")
    my_col = lax.axis_index("col")
    masks = [1 << k for k in range(cols.bit_length() - 1)]
    share, old = numer, probe
    for mask in masks:
        upper = (my_col & mask) != 0
        half = share.shape[1] // 2
        first, last = share[:, :half], share[:, half:]
        given = jnp.where(upper, first, last)
        share = jnp.where(upper, last, first) + swapped(given, "col", mask)
        old = jnp.where(upper, old[:, half:], old[:, :half])
    share = summed_over_rows(share)
    fresh = (old + share[:2]) / (share[2] + probe_regular)[None]
    for mask in reversed(masks):
        upper = (my_col & mask) != 0
        other = swapped(fresh, "col", mask)
        fresh = jnp.where(upper, jnp.concatenate([other, fresh], axis=1), jnp.concatenate([fresh, other], axis=1))
    return fresh


def local(obj, probe, amplitudes, positions):
    col_count = lax.axis_size("col")
    tile_rows, tile_cols = obj.shape[1], obj.shape[2]
    order = probe.shape[1]
    pat_count = amplitudes.shape[0]
    capacity = 2 * pat_count
    dims = (tile_rows, tile_cols, pat_count, col_count, capacity)
    me = jnp.stack([lax.axis_index("row"), lax.axis_index("col")]).astype(jnp.int32)
    pos = positions.reshape(-1)
    rows_table, cols_table, tw_cols, tw_rows, sorting = tables(order)
    consts = (rows_table, cols_table, tw_cols, tw_rows)
    tile = (2, tile_rows, tile_cols)
    window = (2, order, order)
    wide = (2, 2 * tile_rows, 2 * tile_cols)
    one_pattern = 24 * 2 * order**3

    outgoing = call(
        functools.partial(outgoing_kernel, dims), shape((col_count * SEND, order, order), bf16), ANY, [SMEM, SMEM, ANY],
        [pltpu.SemaphoreType.DMA((pat_count,))], 1 << 20,
    )(pos, me, amplitudes)
    incoming = lax.all_to_all(outgoing, "col", split_axis=0, concat_axis=0, tiled=True)

    right = passed_along(obj, "col", -1)
    below = passed_along(obj, "row", -1)
    diag = passed_both(obj, -1, -1)
    pieces = (obj, right, below, diag)

    def weights(probe_now, span):
        return call(
            functools.partial(weights_kernel, dims, span), shape((span * tile_rows, span * tile_cols)), VMEM, [SMEM, SMEM, VMEM],
            [pltpu.VMEM(((span + 2) * tile_rows, (span + 2) * tile_cols), f32), pltpu.VMEM((order, order), f32)], 8 << 30,
        )(pos, me, probe_now)

    weights_now = weights(probe, 2)

    far, power = call(
        functools.partial(first_half_kernel, dims), (shape((capacity,) + window), shape((order, order))), (ANY, VMEM),
        [SMEM, SMEM] + [VMEM] * 9,
        [pltpu.VMEM(wide, f32)] + work_scratch(order) + [pltpu.VMEM((capacity,) + window, f32)] + list_scratch(capacity)
        + [pltpu.SemaphoreType.DMA((capacity,))],
        capacity * one_pattern // 2,
    )(pos, me, *pieces, probe, *consts)

    top, bottom, numer, sorted_amps = call(
        functools.partial(second_half_kernel, dims),
        (shape((2, tile_rows, 2 * tile_cols)), shape((2, tile_rows, 2 * tile_cols)), shape(window), shape((capacity, order, order), bf16)),
        (VMEM, VMEM, VMEM, ANY),
        [SMEM, SMEM] + [VMEM] * 5 + [ANY, ANY] + [VMEM] * 5,
        [pltpu.VMEM(wide, f32), pltpu.VMEM(wide, f32)] + work_scratch(order)
        + [pltpu.VMEM((capacity,) + window, f32), pltpu.VMEM((capacity, order, order), bf16), pltpu.VMEM((capacity, order, order), bf16)]
        + list_scratch(capacity) + [pltpu.SemaphoreType.DMA((capacity,))] * 3,
        capacity * one_pattern // 2,
    )(pos, me, *pieces, probe, far, incoming, *consts, sorting)

    probe_now = probe_update(probe, jnp.concatenate([numer, power[None]]))
    sums = jnp.concatenate([top + passed_along(bottom, "row", 1), bottom + passed_along(top, "row", -1)], axis=1)
    sum_left, sum_right = sums[:, :, :tile_cols], sums[:, :, tile_cols:]
    from_left = passed_along(sum_right, "col", 1)
    from_right = passed_along(sum_left, "col", -1)

    current, own, to_right, to_below, to_diag, numer = call(
        functools.partial(whole_kernel, dims), (shape(tile),) * 5 + (shape((3, order, order)),), (VMEM,) * 6,
        [SMEM, SMEM] + [VMEM] * 10 + [ANY] + [VMEM] * 4,
        [pltpu.VMEM(wide, f32), pltpu.VMEM(wide, f32)] + work_scratch(order)
        + [pltpu.VMEM((2,) + window, f32), pltpu.VMEM((capacity, order, order), bf16)] + list_scratch(capacity) + [pltpu.SemaphoreType.DMA((capacity,))],
        capacity * one_pattern,
    )(pos, me, *pieces, sum_left, sum_right, from_left, from_right, weights_now, probe_now, sorted_amps, *consts)

    weights_now = weights(probe_now, 1)
    new_probe = probe_update(probe_now, numer)
    total = own + passed_along(to_right, "col", 1) + passed_along(to_below, "row", 1) + passed_both(to_diag, 1, 1)
    new_object = (object_regular * current + total) / (weights_now + object_regular)[None]
    return new_object, new_probe


def solution(mesh):
    placed = (P(None, "row", "col"), P(), P(("row", "col"), None, None), P())
    return jax.shard_map(local, mesh=mesh, in_specs=placed, out_specs=(P(None, "row", "col"), P()), check_vma=False)
```

```python
import functools

import jax
import jax.numpy as jnp
import numpy as np
from jax import lax
from jax.experimental import pallas as pl
from jax.experimental.pallas import tpu as pltpu
from jax.sharding import PartitionSpec as P

ITERS = 2
SEND = 2

amplitude_floor = 0.1
object_regular = 0.5
probe_regular = 1.0

LANES = 128
SUBLANES = 8
LEVELS = 32767.0
CHUNK = 32
VMEM = pl.BlockSpec(memory_space=pltpu.VMEM)
SMEM = pl.BlockSpec(memory_space=pltpu.SMEM)
ANY = pl.BlockSpec(memory_space=pl.ANY)
f32 = jnp.float32
bf16 = jnp.bfloat16


def tables(order):
    half = order // 2
    counter = np.arange(half)
    angles = 2.0 * np.pi * ((counter[:, None] * counter[None, :]) % half) / half
    cos, sin = np.cos(angles), np.sin(angles)
    scale = 1.0 / np.sqrt(order)
    turns = []
    for block in ([[cos, -sin], [sin, cos]], [[cos, sin], [-sin, cos]]):
        matrix = np.block(block) * scale
        high = matrix.astype(jnp.bfloat16)
        turns.append(np.stack([high, (matrix - high.astype(np.float64)).astype(jnp.bfloat16)]))
    turn = 2.0 * np.pi * counter / order
    twiddle = np.stack([np.cos(turn), -np.sin(turn)]).astype(np.float32)
    twiddles = np.concatenate(
        [np.broadcast_to(twiddle[:, :, None], (2, half, half)), np.broadcast_to(twiddle[:, None, :], (2, SUBLANES, half))], axis=1
    )
    sorting = np.zeros((order, order), np.float32)
    sorting[np.arange(half), 2 * np.arange(half)] = 1.0
    sorting[half + np.arange(half), 2 * np.arange(half) + 1] = 1.0
    return (
        jnp.asarray(np.stack(turns)),
        jnp.asarray(np.ascontiguousarray(twiddles)),
        jnp.asarray(np.stack([sorting, sorting.T]).astype(jnp.bfloat16)),
    )


def list_patterns(dims, pos_ref, me_ref, ys_ref, xs_ref, slots_ref):
    tile_rows, tile_cols, pat_count, col_count, capacity = dims
    my_row, my_col = me_ref[0], me_ref[1]
    band_count = pat_count * col_count
    first = my_row * band_count

    def visit(index, carry):
        found, source, rank = carry
        y = pos_ref[2 * (first + index)]
        x = pos_ref[2 * (first + index) + 1]
        here = lax.div(x, tile_cols) == my_col
        holder = lax.div(index, pat_count)
        rank = jnp.where(holder == source, rank, 0)

        @pl.when(here & (found < capacity))
        def _():
            ys_ref[found] = y - my_row * tile_rows
            xs_ref[found] = x - my_col * tile_cols
            slots_ref[found] = holder * SEND + jnp.minimum(rank, SEND - 1)

        step = here.astype(jnp.int32)
        return found + step, holder, rank + step

    found, _, _ = lax.fori_loop(0, band_count, visit, (jnp.int32(0), jnp.int32(-1), jnp.int32(0)))
    return jnp.minimum(found, capacity)


def lane_index(rows):
    return lax.broadcasted_iota(jnp.int32, (rows, LANES), 1)


def shifted_left(tiles, shift):
    lane = lane_index(tiles[0].shape[0])
    turn = lax.rem(LANES - shift, LANES)
    rolled = [pltpu.roll(tile, turn, axis=1) for tile in tiles]
    inside = lane < LANES - shift
    return [jnp.where(inside, a, b) for a, b in zip(rolled[:-1], rolled[1:])]


def shifted_right(tiles, shift):
    lane = lane_index(tiles[0].shape[0])
    rolled = [pltpu.roll(tile, shift, axis=1) for tile in tiles]
    outside = lane < shift
    zero = jnp.zeros_like(rolled[0])
    firsts = [zero] + rolled
    seconds = rolled + [zero]
    return [jnp.where(outside, a, b) for a, b in zip(firsts, seconds)]


def row_groups(tile):
    return [tile[k : k + SUBLANES] for k in range(0, tile.shape[0], SUBLANES)]


def shifted_up(tile, shift):
    row = lax.broadcasted_iota(jnp.int32, (SUBLANES, LANES), 0)
    turn = lax.rem(SUBLANES - shift, SUBLANES)
    rolled = [pltpu.roll(group, turn, axis=0) for group in row_groups(tile)]
    inside = row < SUBLANES - shift
    return jnp.concatenate([jnp.where(inside, a, b) for a, b in zip(rolled[:-1], rolled[1:])], axis=0)


def shifted_down(before, tile, shift):
    row = lax.broadcasted_iota(jnp.int32, (SUBLANES, LANES), 0)
    rolled = [before] + [pltpu.roll(group, shift, axis=0) for group in row_groups(tile)]
    outside = row < shift
    return rolled[-1], jnp.concatenate([jnp.where(outside, a, b) for a, b in zip(rolled[:-1], rolled[1:])], axis=0)


class Deposit:
    def __init__(self, add, top, left):
        self.add = add
        self.row = pl.multiple_of(lax.div(top, SUBLANES) * SUBLANES, SUBLANES)
        self.col = pl.multiple_of(lax.div(left, LANES) * LANES, LANES)
        self.down = lax.rem(top, SUBLANES)
        self.right = lax.rem(left, LANES)
        self.carried = None

    def place(self, first, tiles):
        moved = jnp.concatenate(shifted_right(tiles, self.right), axis=1)
        self.add(pl.ds(self.row + first, tiles[0].shape[0]), pl.ds(self.col, moved.shape[1]), moved)

    def put(self, first, tiles):
        if self.carried is None:
            self.carried = [jnp.zeros((SUBLANES, LANES), f32) for _ in tiles]
        pairs = [shifted_down(before, tile, self.down) for before, tile in zip(self.carried, tiles)]
        self.carried = [carried for carried, _ in pairs]
        self.place(first, [tile for _, tile in pairs])

    def finish(self, first):
        row = lax.broadcasted_iota(jnp.int32, (SUBLANES, LANES), 0)
        self.place(first, [jnp.where(row < self.down, tile, 0.0) for tile in self.carried])


def lane_tiles(value):
    return [value[:, k : k + LANES] for k in range(0, value.shape[1], LANES)]


def store_split(ref, rows, cols, value):
    high = value.astype(bf16)
    ref[0, rows, cols] = high
    ref[1, rows, cols] = (value - high.astype(f32)).astype(bf16)


def right_dot(x_ref, table_ref):
    left = jnp.concatenate([x_ref[0], x_ref[1], x_ref[0]], axis=1)
    right = jnp.concatenate([table_ref[0], table_ref[0], table_ref[1]], axis=0)
    return jnp.dot(left, right, preferred_element_type=f32)


def left_dot(table_ref, x_ref):
    left = jnp.concatenate([table_ref[0], table_ref[0], table_ref[1]], axis=1)
    right = jnp.concatenate([x_ref[0], x_ref[1], x_ref[0]], axis=0)
    return jnp.dot(left, right, preferred_element_type=f32)


def repeated(group, rows):
    return jnp.concatenate([group] * (rows // SUBLANES), axis=0)


def encode(read, out_ref, rows, first, last):
    for col in range(0, out_ref.shape[1], LANES):
        cols = pl.ds(col, LANES)
        largest = jnp.full((SUBLANES, LANES), 1e-30, f32)
        for start in range(0, rows, CHUNK):
            for comp in range(2):
                for group in row_groups(jnp.abs(read(comp, pl.ds(start, CHUNK), cols))):
                    largest = jnp.maximum(largest, group)
        exponent = jnp.ceil(jnp.log2(largest))
        out_ref[last : last + SUBLANES, cols] = exponent.astype(jnp.int32)
        scale = repeated(jnp.exp2(-exponent) * LEVELS, CHUNK)
        for start in range(0, rows, CHUNK):
            codes = []
            for comp in range(2):
                scaled = jnp.clip(read(comp, pl.ds(start, CHUNK), cols) * scale, -LEVELS, LEVELS)
                codes.append(jnp.round(scaled).astype(jnp.int32))
            out_ref[pl.ds(first + start, CHUNK), cols] = (codes[0] << 16) | (codes[1] & 0xFFFF)


def decode(ref, start, last, col):
    cols = pl.ds(col, LANES)
    words = ref[pl.ds(start, CHUNK), cols]
    scale = repeated(jnp.exp2(ref[last : last + SUBLANES, cols].astype(f32)) * (1.0 / LEVELS), CHUNK)
    return (words >> 16).astype(f32) * scale, ((words << 16) >> 16).astype(f32) * scale


def cut_chunk(ext_ref, comp, first, top, left, rows):
    row = pl.multiple_of(lax.div(top, SUBLANES) * SUBLANES, SUBLANES)
    col = pl.multiple_of(lax.div(left, LANES) * LANES, LANES)
    block = ext_ref[comp, pl.ds(row + first, rows + SUBLANES), pl.ds(col, 3 * LANES)]
    tiles = shifted_left(lane_tiles(block), lax.rem(left, LANES))
    return [shifted_up(tile, lax.rem(top, SUBLANES)) for tile in tiles]


def forward(order, ext_ref, probe_ref, consts, y, x, win_ref, power_ref, weight, xa_ref, xb_ref, ya_ref, yb_ref, far_ref):
    turns, twiddles = consts
    half = order // 2
    tw_re = repeated(twiddles[0, half : half + SUBLANES, :], CHUNK)
    tw_im = repeated(twiddles[1, half : half + SUBLANES, :], CHUNK)
    for first in range(0, order, CHUNK):
        rows = pl.ds(first, CHUNK)
        win_re = cut_chunk(ext_ref, 0, first, y, x, CHUNK)
        win_im = cut_chunk(ext_ref, 1, first, y, x, CHUNK)
        exits = []
        for k in range(2):
            cols = pl.ds(k * half, half)
            win_ref[0, rows, cols] = win_re[k]
            win_ref[1, rows, cols] = win_im[k]
            power_ref[rows, cols] += weight * (win_re[k] * win_re[k] + win_im[k] * win_im[k])
            p_re, p_im = probe_ref[0, rows, cols], probe_ref[1, rows, cols]
            exits.append((p_re * win_re[k] - p_im * win_im[k], p_re * win_im[k] + p_im * win_re[k]))
        (lo_re, lo_im), (hi_re, hi_im) = exits
        store_split(xa_ref, rows, pl.ds(0, half), lo_re + hi_re)
        store_split(xa_ref, rows, pl.ds(half, half), lo_im + hi_im)
        d_re, d_im = lo_re - hi_re, lo_im - hi_im
        store_split(xb_ref, rows, pl.ds(0, half), d_re * tw_re - d_im * tw_im)
        store_split(xb_ref, rows, pl.ds(half, half), d_re * tw_im + d_im * tw_re)
    yield
    ya_ref[...] = right_dot(xa_ref, turns.at[0])
    yb_ref[...] = right_dot(xb_ref, turns.at[0])
    yield
    for first in range(0, half, CHUNK):
        rows = pl.ds(first, CHUNK)
        below = pl.ds(half + first, CHUNK)
        t_re, t_im = twiddles[0, rows, :], twiddles[1, rows, :]
        for k, y_ref in enumerate((ya_ref, yb_ref)):
            cols = pl.ds(k * half, half)
            up_re, up_im = y_ref[rows, 0:half], y_ref[rows, half:order]
            dn_re, dn_im = y_ref[below, 0:half], y_ref[below, half:order]
            store_split(xa_ref, rows, cols, up_re + dn_re)
            store_split(xa_ref, below, cols, up_im + dn_im)
            d_re, d_im = up_re - dn_re, up_im - dn_im
            store_split(xb_ref, rows, cols, d_re * t_re - d_im * t_im)
            store_split(xb_ref, below, cols, d_re * t_im + d_im * t_re)
    yield
    far_ref[0] = left_dot(turns.at[1], xa_ref)
    far_ref[1] = left_dot(turns.at[1], xb_ref)
    yield


def backward(order, far_ref, amp_ref, consts, y, x, weight, probe_ref, win_ref, xa_ref, xb_ref, ya_ref, yb_ref, grad_ref, numer_ref):
    turns, twiddles = consts
    half = order // 2
    tw_re = repeated(twiddles[0, half : half + SUBLANES, :], CHUNK)
    tw_im = repeated(twiddles[1, half : half + SUBLANES, :], CHUNK)
    for k, x_ref in enumerate((xa_ref, xb_ref)):
        for first in range(0, half, CHUNK):
            rows = pl.ds(first, CHUNK)
            below = pl.ds(half + first, CHUNK)
            far_re, far_im = far_ref[k, rows, :], far_ref[k, below, :]
            amp = amp_ref[pl.ds(k * half + first, CHUNK), :].astype(f32)
            factor = amp * lax.rsqrt(far_re * far_re + far_im * far_im + amplitude_floor)
            store_split(x_ref, rows, slice(None), far_re * factor)
            store_split(x_ref, below, slice(None), far_im * factor)
    yield
    ya_ref[...] = left_dot(turns.at[0], xa_ref)
    yb_ref[...] = left_dot(turns.at[0], xb_ref)
    yield
    for first in range(0, half, CHUNK):
        rows = pl.ds(first, CHUNK)
        below = pl.ds(half + first, CHUNK)
        t_re, t_im = twiddles[0, rows, :], twiddles[1, rows, :]
        for k, x_ref in enumerate((xa_ref, xb_ref)):
            cols = slice(k * half, (k + 1) * half)
            a_re, a_im = ya_ref[rows, cols], ya_ref[below, cols]
            b_re, b_im = yb_ref[rows, cols], yb_ref[below, cols]
            c_re, c_im = b_re * t_re + b_im * t_im, b_im * t_re - b_re * t_im
            store_split(x_ref, rows, pl.ds(0, half), a_re + c_re)
            store_split(x_ref, rows, pl.ds(half, half), a_im + c_im)
            store_split(x_ref, below, pl.ds(0, half), a_re - c_re)
            store_split(x_ref, below, pl.ds(half, half), a_im - c_im)
    yield
    ya_ref[...] = right_dot(xa_ref, turns.at[1])
    yb_ref[...] = right_dot(xb_ref, turns.at[1])
    yield

    def adder(comp):
        def add(rows, cols, moved):
            grad_ref[comp, rows, cols] += moved

        return add

    deposits = [Deposit(adder(comp), y, x) for comp in range(2)]
    for first in range(0, order, CHUNK):
        rows = pl.ds(first, CHUNK)
        a_re, a_im = ya_ref[rows, 0:half], ya_ref[rows, half:order]
        b_re, b_im = yb_ref[rows, 0:half], yb_ref[rows, half:order]
        c_re, c_im = b_re * tw_re + b_im * tw_im, b_im * tw_re - b_re * tw_im
        waves = [(a_re + c_re, a_im + c_im), (a_re - c_re, a_im - c_im)]
        terms = ([], [])
        for k, (wave_re, wave_im) in enumerate(waves):
            cols = pl.ds(k * half, half)
            wave_re, wave_im = weight * wave_re, weight * wave_im
            p_re, p_im = probe_ref[0, rows, cols], probe_ref[1, rows, cols]
            w_re, w_im = win_ref[0, rows, cols], win_ref[1, rows, cols]
            terms[0].append(p_re * wave_re + p_im * wave_im)
            terms[1].append(p_re * wave_im - p_im * wave_re)
            numer_ref[0, rows, cols] += w_re * wave_re + w_im * wave_im
            numer_ref[1, rows, cols] += w_re * wave_im - w_im * wave_re
        for comp in range(2):
            deposits[comp].put(first, terms[comp])
    for deposit in deposits:
        deposit.finish(order)
    yield


def interleaved(*stages):
    live = list(stages)
    while live:
        still = []
        for stage in live:
            try:
                next(stage)
                still.append(stage)
            except StopIteration:
                pass
        live = still


def outgoing_kernel(dims, pos_ref, me_ref, amp_ref, after_ref, out_ref, sems):
    tile_rows, tile_cols, pat_count, col_count, capacity = dims
    first = (me_ref[0] * col_count + me_ref[1]) * pat_count
    owners = [lax.div(pos_ref[2 * (first + k) + 1], tile_cols) for k in range(pat_count)]
    copies = []
    for k in range(pat_count):
        rank = sum(((owners[e] == owners[k]).astype(jnp.int32) for e in range(k)), jnp.int32(0))
        slot = owners[k] * SEND + jnp.minimum(rank, SEND - 1)
        copies.append(pltpu.make_async_copy(amp_ref.at[k], out_ref.at[slot], sems.at[k]))
        copies[-1].start()
    for copy in copies:
        copy.wait()


def weights_kernel(dims, span, pos_ref, me_ref, probe_ref, out_ref, sums_ref, power_ref):
    tile_rows, tile_cols, pat_count, col_count, capacity = dims
    order = probe_ref.shape[1]
    top = (me_ref[0] - 1) * tile_rows
    left = (me_ref[1] - 1) * tile_cols
    for first in range(0, sums_ref.shape[0], order):
        sums_ref[pl.ds(first, order), :] = jnp.zeros((order, sums_ref.shape[1]), f32)
    power_ref[...] = probe_ref[0] * probe_ref[0] + probe_ref[1] * probe_ref[1]

    def visit(index, carry):
        y = pos_ref[2 * index] - top
        x = pos_ref[2 * index + 1] - left

        @pl.when((y > 0) & (y < (span + 1) * tile_rows) & (x > 0) & (x < (span + 1) * tile_cols))
        def _():
            def add(rows, cols, moved):
                sums_ref[rows, cols] += moved

            deposit = Deposit(add, y, x)
            for first in range(0, order, CHUNK):
                deposit.put(first, lane_tiles(power_ref[pl.ds(first, CHUNK), :]))
            deposit.finish(order)

        return carry

    lax.fori_loop(0, pos_ref.shape[0] // 2, visit, 0)
    out_ref[...] = sums_ref[tile_rows : (span + 1) * tile_rows, tile_cols : (span + 1) * tile_cols]


def encode_kernel(obj_ref, out_ref):
    rows = obj_ref.shape[1]
    encode(lambda comp, at, cols: obj_ref[comp, at, cols], out_ref, rows, 0, rows)


def unfold(dims, ext_ref, own_ref, coded_refs):
    tile_rows, tile_cols = dims[:2]
    ext_ref[:, 0:tile_rows, 0:tile_cols] = own_ref[...]
    for (i, j), ref in zip(((0, 1), (1, 0), (1, 1)), coded_refs):
        for col in range(0, tile_cols, LANES):
            for start in range(0, tile_rows, CHUNK):
                parts = decode(ref, start, tile_rows, col)
                for comp in range(2):
                    ext_ref[comp, pl.ds(i * tile_rows + start, CHUNK), pl.ds(j * tile_cols + col, LANES)] = parts[comp]


def chunked(out_ref, plane, planes, value_ref):
    chunks = out_ref.shape[0]
    rows = value_ref.shape[0] // chunks
    for chunk in range(chunks):
        out_ref[chunk, plane * rows : (plane + 1) * rows, :] = value_ref[chunk * rows : (chunk + 1) * rows, :]


def first_half_kernel(dims, pos_ref, me_ref, own_ref, right_ref, below_ref, diag_ref, probe_ref, turns, twiddles,
                      far_out, power_out, ext_out, win_ref, xa_ref, xb_ref, ya_ref, yb_ref, far_ref, ys_ref, xs_ref, slots_ref, sems):
    tile_rows, tile_cols, pat_count, col_count, capacity = dims
    order = probe_ref.shape[1]
    count = list_patterns(dims, pos_ref, me_ref, ys_ref, xs_ref, slots_ref)
    unfold(dims, ext_out, own_ref, (right_ref, below_ref, diag_ref))
    power_out[...] = jnp.zeros_like(power_out)
    consts = (turns, twiddles)

    def pair(step, carry):
        stages = []
        for k in range(2):
            listed = 2 * step + k
            weight = (listed < count).astype(f32)
            index = jnp.minimum(listed, count - 1)
            stages.append(forward(order, ext_out, probe_ref, consts, ys_ref[index], xs_ref[index], win_ref.at[k], power_out, weight,
                                  xa_ref.at[k], xb_ref.at[k], ya_ref.at[k], yb_ref.at[k], far_ref.at[listed]))
        interleaved(*stages)
        for k in range(2):
            listed = 2 * step + k
            pltpu.make_async_copy(far_ref.at[listed], far_out.at[listed], sems.at[listed]).start()
        return carry

    pairs = lax.div(count + 1, 2)
    lax.fori_loop(0, pairs, pair, 0)

    def settle(listed, carry):
        pltpu.make_async_copy(far_ref.at[listed], far_out.at[listed], sems.at[listed]).wait()
        return carry

    lax.fori_loop(0, 2 * pairs, settle, 0)


def second_half_kernel(dims, pos_ref, me_ref, ext_ref, probe_ref, power_ref, weights_ref, far_in, amp_in, turns, twiddles, sorting,
                       share_out, top_out, bottom_out, numer_out, amp_out,
                       win_ref, xa_ref, xb_ref, ya_ref, yb_ref, numer_ref, far_ref, amp_ref, sorted_ref, ys_ref, xs_ref, slots_ref, far_sems, amp_sems, out_sems):
    tile_rows, tile_cols, pat_count, col_count, capacity = dims
    order = probe_ref.shape[1]
    half = order // 2
    count = list_patterns(dims, pos_ref, me_ref, ys_ref, xs_ref, slots_ref)
    pairs = lax.div(count + 1, 2)

    def copies(listed):
        return (
            pltpu.make_async_copy(far_in.at[listed], far_ref.at[listed], far_sems.at[listed]),
            pltpu.make_async_copy(amp_in.at[slots_ref[jnp.minimum(listed, count - 1)]], amp_ref.at[listed], amp_sems.at[listed]),
        )

    def begin(listed, carry):
        for copy in copies(listed):
            copy.start()
        return carry

    lax.fori_loop(0, 2 * pairs, begin, 0)
    share_out[...] = jnp.zeros_like(share_out)
    numer_ref[...] = jnp.zeros_like(numer_ref)
    consts = (turns, twiddles)

    def pair(step, carry):
        stages = []
        for k in range(2):
            listed = 2 * step + k
            for copy in copies(listed):
                copy.wait()
        for k in range(2):
            listed = 2 * step + k
            weight = (listed < count).astype(f32)
            index = jnp.minimum(listed, count - 1)
            y, x = ys_ref[index], xs_ref[index]
            rows_sorted = jnp.dot(sorting[0], amp_ref[listed], preferred_element_type=f32).astype(bf16)
            sorted_ref[listed] = jnp.dot(rows_sorted, sorting[1], preferred_element_type=f32).astype(bf16)
            for first in range(0, order, CHUNK):
                for comp in range(2):
                    for c, tile in enumerate(cut_chunk(ext_ref, comp, first, y, x, CHUNK)):
                        win_ref[k, comp, pl.ds(first, CHUNK), pl.ds(c * half, half)] = tile
            stages.append(backward(order, far_ref.at[listed], sorted_ref.at[listed], consts, y, x, weight, probe_ref, win_ref.at[k],
                                   xa_ref.at[k], xb_ref.at[k], ya_ref.at[k], yb_ref.at[k], share_out, numer_ref))
        interleaved(*stages)
        for k in range(2):
            listed = 2 * step + k
            pltpu.make_async_copy(sorted_ref.at[listed], amp_out.at[listed], out_sems.at[listed]).start()
        return carry

    lax.fori_loop(0, pairs, pair, 0)
    for first in range(0, 2 * tile_rows, CHUNK):
        rows = pl.ds(first, CHUNK)
        scale = 1.0 / (weights_ref[rows, :] + object_regular)
        for comp in range(2):
            share_out[comp, rows, :] = share_out[comp, rows, :] * scale
    encode(lambda comp, at, cols: share_out[comp, at, cols], top_out, tile_rows, 0, tile_rows)
    encode(lambda comp, at, cols: share_out[comp, pl.ds(tile_rows + at.start, at.size), cols], bottom_out, tile_rows, 0, tile_rows)
    for plane, ref in enumerate((numer_ref.at[0], numer_ref.at[1], power_ref)):
        chunked(numer_out, plane, 3, ref)

    def settle(listed, carry):
        pltpu.make_async_copy(sorted_ref.at[listed], amp_out.at[listed], out_sems.at[listed]).wait()
        return carry

    lax.fori_loop(0, 2 * pairs, settle, 0)


def rows_sum_kernel(dims, share_ref, above_ref, below_ref, sum_out, left_out, right_out):
    tile_rows, tile_cols = dims[:2]
    for i, ref in enumerate((above_ref, below_ref)):
        for col in range(0, 2 * tile_cols, LANES):
            for start in range(0, tile_rows, CHUNK):
                rows, cols = pl.ds(i * tile_rows + start, CHUNK), pl.ds(col, LANES)
                parts = decode(ref, start, tile_rows, col)
                for comp in range(2):
                    sum_out[comp, rows, cols] = share_ref[comp, rows, cols] + parts[comp]
    for j, ref in enumerate((left_out, right_out)):
        for i in range(2):

            def read(comp, at, cols, i=i, j=j):
                return sum_out[comp, pl.ds(i * tile_rows + at.start, at.size), pl.ds(j * tile_cols + cols.start, cols.size)]

            encode(read, ref, tile_rows, i * tile_rows, 2 * tile_rows + i * SUBLANES)


def whole_kernel(dims, pos_ref, me_ref, old_ref, sum_ref, from_left_ref, from_right_ref, weights_ref,
                 probe_ref, amp_in, turns, twiddles,
                 current_out, own_out, right_out, below_out, diag_out, numer_out,
                 ext_ref, grad_ref, win_ref, xa_ref, xb_ref, ya_ref, yb_ref, numer_ref, far_ref, amp_ref, ys_ref, xs_ref, slots_ref, amp_sems):
    tile_rows, tile_cols, pat_count, col_count, capacity = dims
    order = probe_ref.shape[1]
    count = list_patterns(dims, pos_ref, me_ref, ys_ref, xs_ref, slots_ref)
    pairs = lax.div(count + 1, 2)

    def fetch(listed):
        return pltpu.make_async_copy(amp_in.at[jnp.minimum(listed, count - 1)], amp_ref.at[listed], amp_sems.at[listed])

    def begin(listed, carry):
        fetch(listed).start()
        return carry

    lax.fori_loop(0, 2 * pairs, begin, 0)
    for j, ref in enumerate((from_left_ref, from_right_ref)):
        for i in range(2):
            for col in range(0, tile_cols, LANES):
                for start in range(0, tile_rows, CHUNK):
                    rows, cols = pl.ds(i * tile_rows + start, CHUNK), pl.ds(j * tile_cols + col, LANES)
                    parts = decode(ref, i * tile_rows + start, 2 * tile_rows + i * SUBLANES, col)
                    scale = object_regular / (weights_ref[rows, cols] + object_regular)
                    for comp in range(2):
                        ext_ref[comp, rows, cols] = old_ref[comp, rows, cols] * scale + (sum_ref[comp, rows, cols] + parts[comp])
    current_out[...] = ext_ref[:, 0:tile_rows, 0:tile_cols]
    grad_ref[...] = jnp.zeros_like(grad_ref)
    numer_ref[...] = jnp.zeros_like(numer_ref)
    consts = (turns, twiddles)

    def pair(step, carry):
        stages = []
        for k in range(2):
            fetch(2 * step + k).wait()
        for k in range(2):
            listed = 2 * step + k
            weight = (listed < count).astype(f32)
            index = jnp.minimum(listed, count - 1)
            y, x = ys_ref[index], xs_ref[index]

            def both(k=k, listed=listed, weight=weight, y=y, x=x):
                yield from forward(order, ext_ref, probe_ref, consts, y, x, win_ref.at[k], numer_ref.at[2], weight,
                                   xa_ref.at[k], xb_ref.at[k], ya_ref.at[k], yb_ref.at[k], far_ref.at[k])
                yield from backward(order, far_ref.at[k], amp_ref.at[listed], consts, y, x, weight, probe_ref, win_ref.at[k],
                                    xa_ref.at[k], xb_ref.at[k], ya_ref.at[k], yb_ref.at[k], grad_ref, numer_ref)

            stages.append(both())
        interleaved(*stages)
        return carry

    lax.fori_loop(0, pairs, pair, 0)
    own_out[...] = grad_ref[:, 0:tile_rows, 0:tile_cols]
    for (i, j), ref in zip(((0, 1), (1, 0), (1, 1)), (right_out, below_out, diag_out)):

        def read(comp, at, cols, i=i, j=j):
            rows, cols = pl.ds(i * tile_rows + at.start, at.size), pl.ds(j * tile_cols + cols.start, cols.size)
            return grad_ref[comp, rows, cols] / (weights_ref[rows, cols] + object_regular)

        encode(read, ref, tile_rows, 0, tile_rows)
    for plane in range(3):
        chunked(numer_out, plane, 3, numer_ref.at[plane])


def object_kernel(dims, current_ref, own_ref, left_ref, above_ref, diag_ref, before_ref, weights_ref, out_ref):
    tile_rows, tile_cols = dims[:2]
    for col in range(0, tile_cols, LANES):
        for start in range(0, tile_rows, CHUNK):
            rows, cols = pl.ds(start, CHUNK), pl.ds(col, LANES)
            scale = 1.0 / (weights_ref[rows, cols] + object_regular)
            back = (before_ref[rows, cols] + object_regular) * scale
            parts = [decode(ref, start, tile_rows, col) for ref in (left_ref, above_ref, diag_ref)]
            for comp in range(2):
                coded = parts[0][comp] + parts[1][comp] + parts[2][comp]
                old = object_regular * current_ref[comp, rows, cols] + own_ref[comp, rows, cols]
                out_ref[comp, rows, cols] = old * scale + coded * back


def shape(dims, dtype=f32):
    return jax.ShapeDtypeStruct(dims, dtype)


def work_scratch(order):
    return [
        pltpu.VMEM((2, 2, order, order), f32),
        pltpu.VMEM((2, 2, order, order), bf16),
        pltpu.VMEM((2, 2, order, order), bf16),
        pltpu.VMEM((2, order, order), f32),
        pltpu.VMEM((2, order, order), f32),
    ]


def list_scratch(capacity):
    return [pltpu.SMEM((capacity,), jnp.int32)] * 3


def call(kernel, outs, out_specs, in_specs, scratch, flops, limit=48 << 20):
    return pl.pallas_call(
        kernel,
        out_shape=outs,
        out_specs=out_specs,
        in_specs=in_specs,
        scratch_shapes=scratch,
        compiler_params=pltpu.CompilerParams(vmem_limit_bytes=limit),
        cost_estimate=pl.CostEstimate(flops=flops, bytes_accessed=8 << 20, transcendentals=0),
    )


def passed_along(value, axis, steps):
    count = lax.axis_size(axis)
    leading, last = (max(0, -steps), min(count, count - steps))
    return lax.ppermute(value, axis, [(source, source + steps) for source in range(leading, last)])


def passed_both(value, row_steps, col_steps):
    rows, cols = lax.axis_size("row"), lax.axis_size("col")
    pairs = []
    for r in range(rows):
        for c in range(cols):
            if 0 <= r + row_steps < rows and 0 <= c + col_steps < cols:
                pairs.append((r * cols + c, (r + row_steps) * cols + c + col_steps))
    return lax.ppermute(value, ("row", "col"), pairs)


def swapped(value, axis, mask):
    return lax.ppermute(value, axis, [(k, k ^ mask) for k in range(lax.axis_size(axis))])


def summed_over_rows(value):
    parts = [value] + [swapped(value, "row", mask) for mask in range(1, lax.axis_size("row"))]
    while len(parts) > 1:
        parts = [a + b for a, b in zip(parts[::2], parts[1::2])]
    return parts[0]


def probe_update(probe, numer):
    cols, order = lax.axis_size("col"), probe.shape[1]
    rows = order // cols
    parts = lax.all_to_all(numer, "col", split_axis=0, concat_axis=0, tiled=True)
    total = summed_over_rows(jnp.sum(parts, axis=0)).reshape(3, rows, order)
    old = lax.dynamic_slice_in_dim(probe, lax.axis_index("col") * rows, rows, 1)
    fresh = (old + total[:2]) / (total[2] + probe_regular)[None]
    spread = jnp.broadcast_to(fresh.reshape(1, 2 * rows, order), (cols, 2 * rows, order))
    chunks = lax.all_to_all(spread, "col", split_axis=0, concat_axis=0, tiled=True)
    return chunks.reshape(cols, 2, rows, order).transpose(1, 0, 2, 3).reshape(2, order, order)


def local(obj, probe, amplitudes, positions):
    col_count = lax.axis_size("col")
    tile_rows, tile_cols = obj.shape[1], obj.shape[2]
    order = probe.shape[1]
    pat_count = amplitudes.shape[0]
    capacity = 2 * pat_count
    dims = (tile_rows, tile_cols, pat_count, col_count, capacity)
    me = jnp.stack([lax.axis_index("row"), lax.axis_index("col")]).astype(jnp.int32)
    pos = positions.reshape(-1)
    turns, twiddles, sorting = tables(order)
    tile = (2, tile_rows, tile_cols)
    window = (2, order, order)
    wide = (2, 2 * tile_rows, 2 * tile_cols)
    shares = (col_count, 3 * order // col_count, order)
    coded_tile = shape((tile_rows + SUBLANES, tile_cols), jnp.int32)
    coded_row = shape((tile_rows + SUBLANES, 2 * tile_cols), jnp.int32)
    coded_col = shape((2 * (tile_rows + SUBLANES), tile_cols), jnp.int32)
    one_pattern = 24 * 2 * order**3

    coded = call(encode_kernel, coded_tile, VMEM, [VMEM], [], 1 << 26)(obj)
    right = passed_along(coded, "col", -1)
    below = passed_along(coded, "row", -1)
    diag = passed_both(coded, -1, -1)

    outgoing = call(
        functools.partial(outgoing_kernel, dims), shape((col_count * SEND, order, order), bf16), ANY, [SMEM, SMEM, ANY, ANY],
        [pltpu.SemaphoreType.DMA((pat_count,))], 1 << 20,
    )(pos, me, amplitudes, coded)
    incoming = lax.all_to_all(outgoing, "col", split_axis=0, concat_axis=0, tiled=True)

    def weights(probe_now, span):
        return call(
            functools.partial(weights_kernel, dims, span), shape((span * tile_rows, span * tile_cols)), VMEM, [SMEM, SMEM, VMEM],
            [pltpu.VMEM(((span + 2) * tile_rows, (span + 2) * tile_cols), f32), pltpu.VMEM((order, order), f32)], 8 << 30,
        )(pos, me, probe_now)

    weights_old = weights(probe, 2)

    far, power, ext = call(
        functools.partial(first_half_kernel, dims), (shape((capacity,) + window), shape((order, order)), shape(wide)), (ANY, VMEM, VMEM),
        [SMEM, SMEM] + [VMEM] * 7,
        work_scratch(order) + [pltpu.VMEM((capacity,) + window, f32)] + list_scratch(capacity) + [pltpu.SemaphoreType.DMA((capacity,))],
        capacity * one_pattern // 2,
    )(pos, me, obj, right, below, diag, probe, turns, twiddles)

    share, top, bottom, numer, sorted_amps = call(
        functools.partial(second_half_kernel, dims),
        (shape(wide), coded_row, coded_row, shape(shares), shape((capacity, order, order), bf16)),
        (VMEM, VMEM, VMEM, VMEM, ANY),
        [SMEM, SMEM] + [VMEM] * 4 + [ANY, ANY] + [VMEM] * 3,
        work_scratch(order)
        + [pltpu.VMEM(window, f32), pltpu.VMEM((capacity,) + window, f32), pltpu.VMEM((capacity, order, order), bf16), pltpu.VMEM((capacity, order, order), bf16)]
        + list_scratch(capacity) + [pltpu.SemaphoreType.DMA((capacity,))] * 3,
        capacity * one_pattern // 2,
    )(pos, me, ext, probe, power, weights_old, far, incoming, turns, twiddles, sorting)

    from_above = passed_along(bottom, "row", 1)
    from_below = passed_along(top, "row", -1)
    probe_now = probe_update(probe, numer)
    sums, to_left, to_right = call(
        functools.partial(rows_sum_kernel, dims), (shape(wide), coded_col, coded_col), (VMEM,) * 3, [VMEM] * 3, [], 1 << 26,
    )(share, from_above, from_below)
    from_left = passed_along(to_right, "col", 1)
    from_right = passed_along(to_left, "col", -1)

    current, own, to_right, to_below, to_diag, numer = call(
        functools.partial(whole_kernel, dims), (shape(tile), shape(tile), coded_tile, coded_tile, coded_tile, shape(shares)), (VMEM,) * 6,
        [SMEM, SMEM] + [VMEM] * 6 + [ANY] + [VMEM] * 2,
        [pltpu.VMEM(wide, f32), pltpu.VMEM(wide, f32)] + work_scratch(order)
        + [pltpu.VMEM((3, order, order), f32), pltpu.VMEM((2,) + window, f32), pltpu.VMEM((capacity, order, order), bf16)]
        + list_scratch(capacity) + [pltpu.SemaphoreType.DMA((capacity,))],
        capacity * one_pattern,
    )(pos, me, ext, sums, from_left, from_right, weights_old, probe_now, sorted_amps, turns, twiddles)

    from_left = passed_along(to_right, "col", 1)
    from_above = passed_along(to_below, "row", 1)
    from_diag = passed_both(to_diag, 1, 1)
    weights_new = weights(probe_now, 1)
    new_probe = probe_update(probe_now, numer)
    new_object = call(functools.partial(object_kernel, dims), shape(tile), VMEM, [VMEM] * 7, [], 1 << 26)(
        current, own, from_left, from_above, from_diag, weights_old[:tile_rows, :tile_cols], weights_new
    )
    return new_object, new_probe


def solution(mesh):
    placed = (P(None, "row", "col"), P(), P(("row", "col"), None, None), P())
    return jax.shard_map(local, mesh=mesh, in_specs=placed, out_specs=(P(None, "row", "col"), P()), check_vma=False)
```

```python
import functools

import jax
import jax.numpy as jnp
import numpy as np
from jax import lax
from jax.experimental import pallas as pl
from jax.experimental.pallas import tpu as pltpu
from jax.sharding import PartitionSpec as P

ITERS = 2
SEND = 2

amplitude_floor = 0.1
object_regular = 0.5
probe_regular = 1.0

LANES = 128
SUBLANES = 8
LEVELS = 32767.0
CHUNK = 32
VMEM = pl.BlockSpec(memory_space=pltpu.VMEM)
SMEM = pl.BlockSpec(memory_space=pltpu.SMEM)
HBM = pl.BlockSpec(memory_space=pltpu.HBM)
LOAD = object()
f32 = jnp.float32
bf16 = jnp.bfloat16


def tables(order):
    half = order // 2
    counter = np.arange(half)
    angles = 2.0 * np.pi * ((counter[:, None] * counter[None, :]) % half) / half
    cos, sin = np.cos(angles), np.sin(angles)
    scale = 1.0 / np.sqrt(order)
    turns = []
    for block in ([[cos, -sin], [sin, cos]], [[cos, sin], [-sin, cos]]):
        matrix = np.block(block) * scale
        high = matrix.astype(jnp.bfloat16)
        turns.append(np.stack([high, (matrix - high.astype(np.float64)).astype(jnp.bfloat16)]))
    turn = 2.0 * np.pi * counter / order
    twiddle = np.stack([np.cos(turn), -np.sin(turn)]).astype(np.float32)
    twiddles = np.concatenate(
        [np.broadcast_to(twiddle[:, :, None], (2, half, half)), np.broadcast_to(twiddle[:, None, :], (2, SUBLANES, half))], axis=1
    )
    sorting = np.zeros((order, order), np.float32)
    sorting[np.arange(half), 2 * np.arange(half)] = 1.0
    sorting[half + np.arange(half), 2 * np.arange(half) + 1] = 1.0
    return (
        jnp.asarray(np.stack(turns)),
        jnp.asarray(np.ascontiguousarray(twiddles)),
        jnp.asarray(np.stack([sorting, sorting.T]).astype(jnp.bfloat16)),
    )


def list_patterns(dims, pos_ref, me_ref, ys_ref, xs_ref, slots_ref):
    tile_rows, tile_cols, pat_count, col_count, capacity = dims
    my_row, my_col = me_ref[0], me_ref[1]
    band_count = pat_count * col_count
    first = my_row * band_count
    total = pos_ref.shape[0] // 2

    def visit(index, carry):
        found, source, rank = carry
        y = pos_ref[first + index]
        x = pos_ref[total + first + index]
        here = lax.div(x, tile_cols) == my_col
        holder = lax.div(index, pat_count)
        rank = jnp.where(holder == source, rank, 0)

        @pl.when(here & (found < capacity))
        def _():
            ys_ref[found] = y - my_row * tile_rows
            xs_ref[found] = x - my_col * tile_cols
            slots_ref[found] = holder * SEND + jnp.minimum(rank, SEND - 1)

        step = here.astype(jnp.int32)
        return found + step, holder, rank + step

    found, _, _ = lax.fori_loop(0, band_count, visit, (jnp.int32(0), jnp.int32(-1), jnp.int32(0)))
    return jnp.minimum(found, capacity)


def lane_index(rows):
    return lax.broadcasted_iota(jnp.int32, (rows, LANES), 1)


def shifted_left(tiles, shift):
    lane = lane_index(tiles[0].shape[0])
    turn = lax.rem(LANES - shift, LANES)
    rolled = [pltpu.roll(tile, turn, axis=1) for tile in tiles]
    inside = lane < LANES - shift
    return [jnp.where(inside, a, b) for a, b in zip(rolled[:-1], rolled[1:])]


def shifted_right(tiles, shift):
    lane = lane_index(tiles[0].shape[0])
    rolled = [pltpu.roll(tile, shift, axis=1) for tile in tiles]
    outside = lane < shift
    zero = jnp.zeros_like(rolled[0])
    firsts = [zero] + rolled
    seconds = rolled + [zero]
    return [jnp.where(outside, a, b) for a, b in zip(firsts, seconds)]


def row_groups(tile):
    return [tile[k : k + SUBLANES] for k in range(0, tile.shape[0], SUBLANES)]


def shifted_up(tile, shift):
    row = lax.broadcasted_iota(jnp.int32, (SUBLANES, LANES), 0)
    turn = lax.rem(SUBLANES - shift, SUBLANES)
    rolled = [pltpu.roll(group, turn, axis=0) for group in row_groups(tile)]
    inside = row < SUBLANES - shift
    return jnp.concatenate([jnp.where(inside, a, b) for a, b in zip(rolled[:-1], rolled[1:])], axis=0)


def shifted_down(before, tile, shift):
    row = lax.broadcasted_iota(jnp.int32, (SUBLANES, LANES), 0)
    rolled = [before] + [pltpu.roll(group, shift, axis=0) for group in row_groups(tile)]
    outside = row < shift
    return rolled[-1], jnp.concatenate([jnp.where(outside, a, b) for a, b in zip(rolled[:-1], rolled[1:])], axis=0)


class Deposit:
    def __init__(self, add, top, left):
        self.add = add
        self.row = pl.multiple_of(lax.div(top, SUBLANES) * SUBLANES, SUBLANES)
        self.col = pl.multiple_of(lax.div(left, LANES) * LANES, LANES)
        self.down = lax.rem(top, SUBLANES)
        self.right = lax.rem(left, LANES)
        self.carried = None

    def place(self, first, tiles):
        moved = jnp.concatenate(shifted_right(tiles, self.right), axis=1)
        self.add(pl.ds(self.row + first, tiles[0].shape[0]), pl.ds(self.col, moved.shape[1]), moved)

    def put(self, first, tiles):
        if self.carried is None:
            self.carried = [jnp.zeros((SUBLANES, LANES), f32) for _ in tiles]
        pairs = [shifted_down(before, tile, self.down) for before, tile in zip(self.carried, tiles)]
        self.carried = [carried for carried, _ in pairs]
        self.place(first, [tile for _, tile in pairs])

    def finish(self, first):
        row = lax.broadcasted_iota(jnp.int32, (SUBLANES, LANES), 0)
        self.place(first, [jnp.where(row < self.down, tile, 0.0) for tile in self.carried])


def lane_tiles(value):
    return [value[:, k : k + LANES] for k in range(0, value.shape[1], LANES)]


def store_split(ref, rows, cols, value):
    high = value.astype(bf16)
    ref[0, rows, cols] = high
    ref[1, rows, cols] = (value - high.astype(f32)).astype(bf16)


def right_dot(x_ref, table_ref):
    left = jnp.concatenate([x_ref[0], x_ref[1], x_ref[0]], axis=1)
    right = jnp.concatenate([table_ref[0], table_ref[0], table_ref[1]], axis=0)
    return jnp.dot(left, right, preferred_element_type=f32)


def left_dot(table_ref, x_ref):
    left = jnp.concatenate([table_ref[0], table_ref[0], table_ref[1]], axis=1)
    right = jnp.concatenate([x_ref[0], x_ref[1], x_ref[0]], axis=0)
    return jnp.dot(left, right, preferred_element_type=f32)


def repeated(group, rows):
    return jnp.concatenate([group] * (rows // SUBLANES), axis=0)


def encode(read, out_ref, rows, first, last):
    for col in range(0, out_ref.shape[1], LANES):
        cols = pl.ds(col, LANES)
        largest = jnp.full((SUBLANES, LANES), 1e-30, f32)
        for start in range(0, rows, CHUNK):
            for comp in range(2):
                for group in row_groups(jnp.abs(read(comp, pl.ds(start, CHUNK), cols))):
                    largest = jnp.maximum(largest, group)
        exponent = jnp.ceil(jnp.log2(largest))
        out_ref[last : last + SUBLANES, cols] = exponent.astype(jnp.int32)
        scale = repeated(jnp.exp2(-exponent) * LEVELS, CHUNK)
        for start in range(0, rows, CHUNK):
            codes = []
            for comp in range(2):
                scaled = jnp.clip(read(comp, pl.ds(start, CHUNK), cols) * scale, -LEVELS, LEVELS)
                codes.append(jnp.round(scaled).astype(jnp.int32))
            out_ref[pl.ds(first + start, CHUNK), cols] = (codes[0] << 16) | (codes[1] & 0xFFFF)


def decode(ref, start, last, col):
    cols = pl.ds(col, LANES)
    words = ref[pl.ds(start, CHUNK), cols]
    scale = repeated(jnp.exp2(ref[last : last + SUBLANES, cols].astype(f32)) * (1.0 / LEVELS), CHUNK)
    return (words >> 16).astype(f32) * scale, ((words << 16) >> 16).astype(f32) * scale


def largest_exponent(values):
    largest = jnp.full((SUBLANES, LANES), 1e-30, f32)
    for value in values:
        for group in row_groups(jnp.abs(value)):
            largest = jnp.maximum(largest, group)
    return jnp.ceil(jnp.log2(largest))


def fixed(value, exponent):
    scaled = value * repeated(jnp.exp2(-exponent) * LEVELS, value.shape[0])
    return jnp.round(jnp.clip(scaled, -LEVELS, LEVELS)).astype(jnp.int32)


def paired(first, second):
    return (first << 16) | (second & 0xFFFF)


def unpaired(words):
    return words >> 16, (words << 16) >> 16


def scaled_back(codes, exponent):
    return codes.astype(f32) * repeated(jnp.exp2(exponent.astype(f32)) * (1.0 / LEVELS), codes.shape[0])


def sums_rows(rows):
    return rows + rows // 2 + SUBLANES


def encode_sums(out_ref, cols, u_re, u_im, v):
    rows = v.shape[0]
    half = rows // 2
    of_u, of_v = largest_exponent([u_re, u_im]), largest_exponent([v])
    out_ref[0:rows, cols] = paired(fixed(u_re, of_u), fixed(u_im, of_u))
    codes = fixed(v, of_v)
    out_ref[rows : rows + half, cols] = paired(codes[:half], codes[half:])
    out_ref[rows + half : rows + half + SUBLANES, cols] = paired(of_u.astype(jnp.int32), of_v.astype(jnp.int32))


def decode_sums(ref, cols, rows):
    half = rows // 2
    of_u, of_v = unpaired(ref[rows + half : rows + half + SUBLANES, cols])
    u_re, u_im = unpaired(ref[0:rows, cols])
    v = jnp.concatenate(unpaired(ref[rows : rows + half, cols]), axis=0)
    return scaled_back(u_re, of_u), scaled_back(u_im, of_u), scaled_back(v, of_v)


def decode_probe(out_ref, chunks_ref):
    chunks = chunks_ref.shape[0]
    rows = out_ref.shape[1] // chunks
    for chunk in range(chunks):
        for col in range(0, out_ref.shape[2], LANES):
            cols = pl.ds(col, LANES)
            exponent = chunks_ref[chunk, rows : rows + SUBLANES, cols]
            for comp, codes in enumerate(unpaired(chunks_ref[chunk, 0:rows, cols])):
                out_ref[comp, chunk * rows : (chunk + 1) * rows, cols] = scaled_back(codes, exponent)


def cut_chunk(ext_ref, comp, first, top, left, rows):
    row = pl.multiple_of(lax.div(top, SUBLANES) * SUBLANES, SUBLANES)
    col = pl.multiple_of(lax.div(left, LANES) * LANES, LANES)
    block = ext_ref[comp, pl.ds(row + first, rows + SUBLANES), pl.ds(col, 3 * LANES)]
    tiles = shifted_left(lane_tiles(block), lax.rem(left, LANES))
    return [shifted_up(tile, lax.rem(top, SUBLANES)) for tile in tiles]


def forward(order, ext_ref, probe_ref, consts, y, x, win_ref, power_ref, weight, xa_ref, xb_ref, ya_ref, yb_ref, far_ref):
    turns, twiddles = consts
    half = order // 2
    tw_re = repeated(twiddles[0, half : half + SUBLANES, :], CHUNK)
    tw_im = repeated(twiddles[1, half : half + SUBLANES, :], CHUNK)
    for first in range(0, order, CHUNK):
        rows = pl.ds(first, CHUNK)
        win_re = cut_chunk(ext_ref, 0, first, y, x, CHUNK)
        win_im = cut_chunk(ext_ref, 1, first, y, x, CHUNK)
        exits = []
        for k in range(2):
            cols = pl.ds(k * half, half)
            win_ref[0, rows, cols] = win_re[k]
            win_ref[1, rows, cols] = win_im[k]
            power_ref[rows, cols] += weight * (win_re[k] * win_re[k] + win_im[k] * win_im[k])
            p_re, p_im = probe_ref[0, rows, cols], probe_ref[1, rows, cols]
            exits.append((p_re * win_re[k] - p_im * win_im[k], p_re * win_im[k] + p_im * win_re[k]))
        (lo_re, lo_im), (hi_re, hi_im) = exits
        store_split(xa_ref, rows, pl.ds(0, half), lo_re + hi_re)
        store_split(xa_ref, rows, pl.ds(half, half), lo_im + hi_im)
        d_re, d_im = lo_re - hi_re, lo_im - hi_im
        store_split(xb_ref, rows, pl.ds(0, half), d_re * tw_re - d_im * tw_im)
        store_split(xb_ref, rows, pl.ds(half, half), d_re * tw_im + d_im * tw_re)
    yield
    ya_ref[...] = right_dot(xa_ref, turns.at[0])
    yb_ref[...] = right_dot(xb_ref, turns.at[0])
    yield
    for first in range(0, half, CHUNK):
        rows = pl.ds(first, CHUNK)
        below = pl.ds(half + first, CHUNK)
        t_re, t_im = twiddles[0, rows, :], twiddles[1, rows, :]
        for k, y_ref in enumerate((ya_ref, yb_ref)):
            cols = pl.ds(k * half, half)
            up_re, up_im = y_ref[rows, 0:half], y_ref[rows, half:order]
            dn_re, dn_im = y_ref[below, 0:half], y_ref[below, half:order]
            store_split(xa_ref, rows, cols, up_re + dn_re)
            store_split(xa_ref, below, cols, up_im + dn_im)
            d_re, d_im = up_re - dn_re, up_im - dn_im
            store_split(xb_ref, rows, cols, d_re * t_re - d_im * t_im)
            store_split(xb_ref, below, cols, d_re * t_im + d_im * t_re)
    yield
    far_ref[0] = left_dot(turns.at[1], xa_ref)
    far_ref[1] = left_dot(turns.at[1], xb_ref)
    yield


def backward(order, far_ref, amp_ref, consts, y, x, weight, probe_ref, win_ref, xa_ref, xb_ref, ya_ref, yb_ref, grad_ref, numer_ref):
    turns, twiddles = consts
    half = order // 2
    tw_re = repeated(twiddles[0, half : half + SUBLANES, :], CHUNK)
    tw_im = repeated(twiddles[1, half : half + SUBLANES, :], CHUNK)
    for k, x_ref in enumerate((xa_ref, xb_ref)):
        for first in range(0, half, CHUNK):
            rows = pl.ds(first, CHUNK)
            below = pl.ds(half + first, CHUNK)
            far_re, far_im = far_ref[k, rows, :], far_ref[k, below, :]
            amp = amp_ref[pl.ds(k * half + first, CHUNK), :].astype(f32)
            factor = amp * lax.rsqrt(far_re * far_re + far_im * far_im + amplitude_floor)
            store_split(x_ref, rows, slice(None), far_re * factor)
            store_split(x_ref, below, slice(None), far_im * factor)
    yield
    ya_ref[...] = left_dot(turns.at[0], xa_ref)
    yb_ref[...] = left_dot(turns.at[0], xb_ref)
    yield
    for first in range(0, half, CHUNK):
        rows = pl.ds(first, CHUNK)
        below = pl.ds(half + first, CHUNK)
        t_re, t_im = twiddles[0, rows, :], twiddles[1, rows, :]
        for k, x_ref in enumerate((xa_ref, xb_ref)):
            cols = slice(k * half, (k + 1) * half)
            a_re, a_im = ya_ref[rows, cols], ya_ref[below, cols]
            b_re, b_im = yb_ref[rows, cols], yb_ref[below, cols]
            c_re, c_im = b_re * t_re + b_im * t_im, b_im * t_re - b_re * t_im
            store_split(x_ref, rows, pl.ds(0, half), a_re + c_re)
            store_split(x_ref, rows, pl.ds(half, half), a_im + c_im)
            store_split(x_ref, below, pl.ds(0, half), a_re - c_re)
            store_split(x_ref, below, pl.ds(half, half), a_im - c_im)
    yield
    ya_ref[...] = right_dot(xa_ref, turns.at[1])
    yb_ref[...] = right_dot(xb_ref, turns.at[1])
    yield

    def adder(comp):
        def add(rows, cols, moved):
            grad_ref[comp, rows, cols] += moved

        return add

    deposits = [Deposit(adder(comp), y, x) for comp in range(2)]
    for first in range(0, order, CHUNK):
        rows = pl.ds(first, CHUNK)
        a_re, a_im = ya_ref[rows, 0:half], ya_ref[rows, half:order]
        b_re, b_im = yb_ref[rows, 0:half], yb_ref[rows, half:order]
        c_re, c_im = b_re * tw_re + b_im * tw_im, b_im * tw_re - b_re * tw_im
        waves = [(a_re + c_re, a_im + c_im), (a_re - c_re, a_im - c_im)]
        terms = ([], [])
        for k, (wave_re, wave_im) in enumerate(waves):
            cols = pl.ds(k * half, half)
            wave_re, wave_im = weight * wave_re, weight * wave_im
            p_re, p_im = probe_ref[0, rows, cols], probe_ref[1, rows, cols]
            w_re, w_im = win_ref[0, rows, cols], win_ref[1, rows, cols]
            terms[0].append(p_re * wave_re + p_im * wave_im)
            terms[1].append(p_re * wave_im - p_im * wave_re)
            numer_ref[0, rows, cols] += w_re * wave_re + w_im * wave_im
            numer_ref[1, rows, cols] += w_re * wave_im - w_im * wave_re
        for comp in range(2):
            deposits[comp].put(first, terms[comp])
    for deposit in deposits:
        deposit.finish(order)
    yield


def interleaved(*stages):
    live = list(stages)
    while live:
        still = []
        for stage in live:
            try:
                next(stage)
                still.append(stage)
            except StopIteration:
                pass
        live = still


def outgoing_kernel(dims, pos_ref, me_ref, amp_ref, after_ref, out_ref, sems):
    tile_rows, tile_cols, pat_count, col_count, capacity = dims
    first = (me_ref[0] * col_count + me_ref[1]) * pat_count
    total = pos_ref.shape[0] // 2
    owners = [lax.div(pos_ref[total + first + k], tile_cols) for k in range(pat_count)]
    copies = []
    for k in range(pat_count):
        rank = sum(((owners[e] == owners[k]).astype(jnp.int32) for e in range(k)), jnp.int32(0))
        slot = owners[k] * SEND + jnp.minimum(rank, SEND - 1)
        copies.append(pltpu.make_async_copy(amp_ref.at[k], out_ref.at[slot], sems.at[k]))
        copies[-1].start()
    for copy in copies:
        copy.wait()


def weights_kernel(dims, span, pos_ref, me_ref, probe_ref, out_ref, sums_ref, power_ref):
    tile_rows, tile_cols, pat_count, col_count, capacity = dims
    order = probe_ref.shape[1]
    top = (me_ref[0] - 1) * tile_rows
    left = (me_ref[1] - 1) * tile_cols
    total = pos_ref.shape[0] // 2
    for first in range(0, sums_ref.shape[0], order):
        sums_ref[pl.ds(first, order), :] = jnp.zeros((order, sums_ref.shape[1]), f32)
    power_ref[...] = probe_ref[0] * probe_ref[0] + probe_ref[1] * probe_ref[1]

    def visit(index, carry):
        y = pos_ref[index] - top
        x = pos_ref[total + index] - left

        @pl.when((y > 0) & (y < (span + 1) * tile_rows) & (x > 0) & (x < (span + 1) * tile_cols))
        def _():
            def add(rows, cols, moved):
                sums_ref[rows, cols] += moved

            deposit = Deposit(add, y, x)
            for first in range(0, order, CHUNK):
                deposit.put(first, lane_tiles(power_ref[pl.ds(first, CHUNK), :]))
            deposit.finish(order)

        return carry

    lax.fori_loop(0, total, visit, 0)
    out_ref[...] = sums_ref[tile_rows : (span + 1) * tile_rows, tile_cols : (span + 1) * tile_cols]


def encode_kernel(obj_ref, out_ref):
    rows = obj_ref.shape[1]
    encode(lambda comp, at, cols: obj_ref[comp, at, cols], out_ref, rows, 0, rows)


def unfold(dims, ext_ref, own_ref, coded_refs):
    tile_rows, tile_cols = dims[:2]
    ext_ref[:, 0:tile_rows, 0:tile_cols] = own_ref[...]
    for (i, j), ref in zip(((0, 1), (1, 0), (1, 1)), coded_refs):
        for col in range(0, tile_cols, LANES):
            for start in range(0, tile_rows, CHUNK):
                parts = decode(ref, start, tile_rows, col)
                for comp in range(2):
                    ext_ref[comp, pl.ds(i * tile_rows + start, CHUNK), pl.ds(j * tile_cols + col, LANES)] = parts[comp]


def spread_sums(out_ref, u_ref, v_ref):
    chunks = out_ref.shape[0]
    rows = v_ref.shape[0] // chunks
    for chunk in range(chunks):
        at = pl.ds(chunk * rows, rows)
        for col in range(0, v_ref.shape[1], LANES):
            cols = pl.ds(col, LANES)
            encode_sums(out_ref.at[chunk], cols, u_ref[0, at, cols], u_ref[1, at, cols], v_ref[at, cols])


def added(parts):
    while len(parts) > 1:
        parts = [tuple(x + y for x, y in zip(a, b)) for a, b in zip(parts[::2], parts[1::2])]
    return parts[0]


def sums_kernel(rows, parts_ref, out_ref):
    for col in range(0, out_ref.shape[1], LANES):
        cols = pl.ds(col, LANES)
        total = added([decode_sums(parts_ref.at[k], cols, rows) for k in range(parts_ref.shape[0])])
        encode_sums(out_ref, cols, *total)


def update_kernel(rows, me_ref, probe_ref, *refs):
    *parts, out_ref = refs
    first = pl.multiple_of(me_ref[1] * rows, SUBLANES)
    for col in range(0, out_ref.shape[2], LANES):
        cols = pl.ds(col, LANES)
        u_re, u_im, v = added([decode_sums(ref, cols, rows) for ref in parts])
        scale = 1.0 / (v + probe_regular)
        re = (probe_ref[0, pl.ds(first, rows), cols] + u_re) * scale
        im = (probe_ref[1, pl.ds(first, rows), cols] + u_im) * scale
        exponent = largest_exponent([re, im])
        words = paired(fixed(re, exponent), fixed(im, exponent))
        for chunk in range(out_ref.shape[0]):
            out_ref[chunk, 0:rows, cols] = words
            out_ref[chunk, rows : rows + SUBLANES, cols] = exponent.astype(jnp.int32)


def probe_kernel(chunks_ref, out_ref):
    decode_probe(out_ref, chunks_ref)


def first_half_kernel(dims, pos_ref, me_ref, own_ref, right_ref, below_ref, diag_ref, probe_ref, turns, twiddles,
                      far_out, power_out, ext_out, ext_ref, win_ref, xa_ref, xb_ref, ya_ref, yb_ref, far_ref, ys_ref, xs_ref, slots_ref, sems, ext_sem):
    tile_rows, tile_cols, pat_count, col_count, capacity = dims
    order = probe_ref.shape[1]
    count = list_patterns(dims, pos_ref, me_ref, ys_ref, xs_ref, slots_ref)
    unfold(dims, ext_ref, own_ref, (right_ref, below_ref, diag_ref))
    keep = pltpu.make_async_copy(ext_ref, ext_out, ext_sem)
    keep.start()
    power_out[...] = jnp.zeros_like(power_out)
    consts = (turns, twiddles)

    def pair(step, carry):
        stages = []
        for k in range(2):
            listed = 2 * step + k
            weight = (listed < count).astype(f32)
            index = jnp.minimum(listed, count - 1)
            stages.append(forward(order, ext_ref, probe_ref, consts, ys_ref[index], xs_ref[index], win_ref.at[k], power_out, weight,
                                  xa_ref.at[k], xb_ref.at[k], ya_ref.at[k], yb_ref.at[k], far_ref.at[listed]))
        interleaved(*stages)
        for k in range(2):
            listed = 2 * step + k
            pltpu.make_async_copy(far_ref.at[listed], far_out.at[listed], sems.at[listed]).start()
        return carry

    pairs = lax.div(count + 1, 2)
    lax.fori_loop(0, pairs, pair, 0)

    def settle(listed, carry):
        pltpu.make_async_copy(far_ref.at[listed], far_out.at[listed], sems.at[listed]).wait()
        return carry

    lax.fori_loop(0, 2 * pairs, settle, 0)
    keep.wait()


def second_half_kernel(dims, pos_ref, me_ref, ext_ref, probe_ref, power_ref, weights_ref, far_in, amp_in, turns, twiddles, sorting,
                       share_out, top_out, bottom_out, numer_out, amp_out,
                       sum_ref, win_ref, xa_ref, xb_ref, ya_ref, yb_ref, numer_ref, far_ref, amp_ref, sorted_ref, ys_ref, xs_ref, slots_ref, far_sems, amp_sems, out_sems, sum_sem):
    tile_rows, tile_cols, pat_count, col_count, capacity = dims
    order = probe_ref.shape[1]
    half = order // 2
    count = list_patterns(dims, pos_ref, me_ref, ys_ref, xs_ref, slots_ref)
    pairs = lax.div(count + 1, 2)

    def copies(listed):
        return (
            pltpu.make_async_copy(far_in.at[listed], far_ref.at[listed], far_sems.at[listed]),
            pltpu.make_async_copy(amp_in.at[slots_ref[jnp.minimum(listed, count - 1)]], amp_ref.at[listed], amp_sems.at[listed]),
        )

    def begin(listed, carry):
        for copy in copies(listed):
            copy.start()
        return carry

    lax.fori_loop(0, 2 * pairs, begin, 0)
    sum_ref[...] = jnp.zeros_like(sum_ref)
    numer_ref[...] = jnp.zeros_like(numer_ref)
    consts = (turns, twiddles)

    def pair(step, carry):
        stages = []
        for k in range(2):
            listed = 2 * step + k
            for copy in copies(listed):
                copy.wait()
        for k in range(2):
            listed = 2 * step + k
            weight = (listed < count).astype(f32)
            index = jnp.minimum(listed, count - 1)
            y, x = ys_ref[index], xs_ref[index]
            rows_sorted = jnp.dot(sorting[0], amp_ref[listed], preferred_element_type=f32).astype(bf16)
            sorted_ref[listed] = jnp.dot(rows_sorted, sorting[1], preferred_element_type=f32).astype(bf16)
            for first in range(0, order, CHUNK):
                for comp in range(2):
                    for c, tile in enumerate(cut_chunk(ext_ref, comp, first, y, x, CHUNK)):
                        win_ref[k, comp, pl.ds(first, CHUNK), pl.ds(c * half, half)] = tile
            stages.append(backward(order, far_ref.at[listed], sorted_ref.at[listed], consts, y, x, weight, probe_ref, win_ref.at[k],
                                   xa_ref.at[k], xb_ref.at[k], ya_ref.at[k], yb_ref.at[k], sum_ref, numer_ref))
        interleaved(*stages)
        for k in range(2):
            listed = 2 * step + k
            pltpu.make_async_copy(sorted_ref.at[listed], amp_out.at[listed], out_sems.at[listed]).start()
        return carry

    lax.fori_loop(0, pairs, pair, 0)
    for first in range(0, 2 * tile_rows, CHUNK):
        rows = pl.ds(first, CHUNK)
        scale = 1.0 / (weights_ref[rows, :] + object_regular)
        for comp in range(2):
            sum_ref[comp, rows, :] = sum_ref[comp, rows, :] * scale
    keep = pltpu.make_async_copy(sum_ref, share_out, sum_sem)
    keep.start()
    encode(lambda comp, at, cols: sum_ref[comp, at, cols], top_out, tile_rows, 0, tile_rows)
    encode(lambda comp, at, cols: sum_ref[comp, pl.ds(tile_rows + at.start, at.size), cols], bottom_out, tile_rows, 0, tile_rows)
    spread_sums(numer_out, numer_ref, power_ref)

    def settle(listed, carry):
        pltpu.make_async_copy(sorted_ref.at[listed], amp_out.at[listed], out_sems.at[listed]).wait()
        return carry

    lax.fori_loop(0, 2 * pairs, settle, 0)
    keep.wait()


def rows_sum_kernel(dims, share_ref, above_ref, below_ref, after_ref, sum_out, left_out, right_out):
    tile_rows, tile_cols = dims[:2]
    for i, ref in enumerate((above_ref, below_ref)):
        for col in range(0, 2 * tile_cols, LANES):
            for start in range(0, tile_rows, CHUNK):
                rows, cols = pl.ds(i * tile_rows + start, CHUNK), pl.ds(col, LANES)
                parts = decode(ref, start, tile_rows, col)
                for comp in range(2):
                    sum_out[comp, rows, cols] = share_ref[comp, rows, cols] + parts[comp]
    for j, ref in enumerate((left_out, right_out)):
        for i in range(2):

            def read(comp, at, cols, i=i, j=j):
                return sum_out[comp, pl.ds(i * tile_rows + at.start, at.size), pl.ds(j * tile_cols + cols.start, cols.size)]

            encode(read, ref, tile_rows, i * tile_rows, 2 * tile_rows + i * SUBLANES)


def whole_kernel(dims, pos_ref, me_ref, old_ref, sum_ref, from_left_ref, from_right_ref, weights_ref,
                 chunks_ref, amp_in, turns, twiddles,
                 current_out, own_out, right_out, below_out, diag_out, numer_out, probe_ref,
                 ext_ref, grad_ref, win_ref, xa_ref, xb_ref, ya_ref, yb_ref, numer_ref, far_ref, amp_ref, ys_ref, xs_ref, slots_ref, amp_sems, own_sem):
    tile_rows, tile_cols, pat_count, col_count, capacity = dims
    order = probe_ref.shape[1]
    count = list_patterns(dims, pos_ref, me_ref, ys_ref, xs_ref, slots_ref)
    pairs = lax.div(count + 1, 2)
    decode_probe(probe_ref, chunks_ref)

    def fetch(listed):
        return pltpu.make_async_copy(amp_in.at[jnp.minimum(listed, count - 1)], amp_ref.at[listed], amp_sems.at[listed])

    def begin(listed, carry):
        fetch(listed).start()
        return carry

    lax.fori_loop(0, 2 * pairs, begin, 0)
    for j, ref in enumerate((from_left_ref, from_right_ref)):
        for i in range(2):
            for col in range(0, tile_cols, LANES):
                for start in range(0, tile_rows, CHUNK):
                    rows, cols = pl.ds(i * tile_rows + start, CHUNK), pl.ds(j * tile_cols + col, LANES)
                    parts = decode(ref, i * tile_rows + start, 2 * tile_rows + i * SUBLANES, col)
                    scale = object_regular / (weights_ref[rows, cols] + object_regular)
                    for comp in range(2):
                        ext_ref[comp, rows, cols] = old_ref[comp, rows, cols] * scale + (sum_ref[comp, rows, cols] + parts[comp])
    keep = pltpu.make_async_copy(ext_ref.at[:, pl.ds(0, tile_rows), pl.ds(0, tile_cols)], current_out, own_sem)
    keep.start()
    grad_ref[...] = jnp.zeros_like(grad_ref)
    numer_ref[...] = jnp.zeros_like(numer_ref)
    consts = (turns, twiddles)

    def pair(step, carry):
        stages = []
        for k in range(2):
            fetch(2 * step + k).wait()
        for k in range(2):
            listed = 2 * step + k
            weight = (listed < count).astype(f32)
            index = jnp.minimum(listed, count - 1)
            y, x = ys_ref[index], xs_ref[index]

            def both(k=k, listed=listed, weight=weight, y=y, x=x):
                yield from forward(order, ext_ref, probe_ref, consts, y, x, win_ref.at[k], numer_ref.at[2], weight,
                                   xa_ref.at[k], xb_ref.at[k], ya_ref.at[k], yb_ref.at[k], far_ref.at[k])
                yield from backward(order, far_ref.at[k], amp_ref.at[listed], consts, y, x, weight, probe_ref, win_ref.at[k],
                                    xa_ref.at[k], xb_ref.at[k], ya_ref.at[k], yb_ref.at[k], grad_ref, numer_ref)

            stages.append(both())
        interleaved(*stages)
        return carry

    lax.fori_loop(0, pairs, pair, 0)
    own_out[...] = grad_ref[:, 0:tile_rows, 0:tile_cols]
    for (i, j), ref in zip(((0, 1), (1, 0), (1, 1)), (right_out, below_out, diag_out)):

        def read(comp, at, cols, i=i, j=j):
            rows, cols = pl.ds(i * tile_rows + at.start, at.size), pl.ds(j * tile_cols + cols.start, cols.size)
            return grad_ref[comp, rows, cols] / (weights_ref[rows, cols] + object_regular)

        encode(read, ref, tile_rows, 0, tile_rows)
    spread_sums(numer_out, numer_ref, numer_ref.at[2])
    keep.wait()


def object_kernel(dims, current_ref, own_ref, left_ref, above_ref, diag_ref, before_ref, weights_ref, out_ref):
    tile_rows, tile_cols = dims[:2]
    for col in range(0, tile_cols, LANES):
        for start in range(0, tile_rows, CHUNK):
            rows, cols = pl.ds(start, CHUNK), pl.ds(col, LANES)
            scale = 1.0 / (weights_ref[rows, cols] + object_regular)
            back = (before_ref[rows, cols] + object_regular) * scale
            parts = [decode(ref, start, tile_rows, col) for ref in (left_ref, above_ref, diag_ref)]
            for comp in range(2):
                coded = parts[0][comp] + parts[1][comp] + parts[2][comp]
                old = object_regular * current_ref[comp, rows, cols] + own_ref[comp, rows, cols]
                out_ref[comp, rows, cols] = old * scale + coded * back


def shape(dims, dtype=f32):
    return jax.ShapeDtypeStruct(dims, dtype)


def work_scratch(order):
    return [
        pltpu.VMEM((2, 2, order, order), f32),
        pltpu.VMEM((2, 2, order, order), bf16),
        pltpu.VMEM((2, 2, order, order), bf16),
        pltpu.VMEM((2, order, order), f32),
        pltpu.VMEM((2, order, order), f32),
    ]


def list_scratch(capacity):
    return [pltpu.SMEM((capacity,), jnp.int32)] * 3


def call(kernel, outs, out_specs, in_specs, scratch, flops, limit=26 << 20):
    several = isinstance(outs, tuple)
    out_count = len(outs) if several else 1
    in_count = len(in_specs)
    loaded = [k for k, spec in enumerate(in_specs) if spec is LOAD]

    def body(*refs):
        ins, rest = list(refs[:in_count]), refs[in_count:]
        given, kept = rest[: out_count + len(scratch)], rest[out_count + len(scratch) :]
        copies = [pltpu.make_async_copy(ins[k], kept[n], kept[-1].at[n]) for n, k in enumerate(loaded)]
        for copy in copies:
            copy.start()
        for n, k in enumerate(loaded):
            copies[n].wait()
            ins[k] = kept[n]
        kernel(*ins, *given)

    def called(*args):
        own = [pltpu.VMEM(args[k].shape, args[k].dtype) for k in loaded]
        if loaded:
            own.append(pltpu.SemaphoreType.DMA((len(loaded),)))
        return pl.pallas_call(
            body,
            out_shape=outs,
            out_specs=out_specs,
            in_specs=[HBM if spec is LOAD else spec for spec in in_specs],
            scratch_shapes=list(scratch) + own,
            compiler_params=pltpu.CompilerParams(vmem_limit_bytes=limit),
            cost_estimate=pl.CostEstimate(flops=flops, bytes_accessed=8 << 20, transcendentals=0),
        )(*args)

    return called


def passed_along(value, axis, steps):
    count = lax.axis_size(axis)
    leading, last = (max(0, -steps), min(count, count - steps))
    return lax.ppermute(value, axis, [(source, source + steps) for source in range(leading, last)])


def passed_both(value, row_steps, col_steps):
    rows, cols = lax.axis_size("row"), lax.axis_size("col")
    pairs = []
    for r in range(rows):
        for c in range(cols):
            if 0 <= r + row_steps < rows and 0 <= c + col_steps < cols:
                pairs.append((r * cols + c, (r + row_steps) * cols + c + col_steps))
    return lax.ppermute(value, ("row", "col"), pairs)


def swapped(value, axis, mask):
    return lax.ppermute(value, axis, [(k, k ^ mask) for k in range(lax.axis_size(axis))])


def probe_update(me, probe, numer, kind):
    cols, order = lax.axis_size("col"), probe.shape[1]
    rows = order // cols
    parts = lax.all_to_all(numer, "col", split_axis=0, concat_axis=0, tiled=True)
    total = call(functools.partial(sums_kernel, rows), shape((sums_rows(rows), order), jnp.int32), VMEM, [VMEM], [], 1 << 26)(parts)
    totals = [total] + [swapped(total, "row", mask) for mask in range(1, lax.axis_size("row"))]
    fresh = call(
        functools.partial(update_kernel, rows), shape((cols, rows + SUBLANES, order), jnp.int32), VMEM,
        [SMEM, kind] + [VMEM] * len(totals), [], 1 << 26,
    )(me, probe, *totals)
    return fresh, lax.all_to_all(fresh, "col", split_axis=0, concat_axis=0, tiled=True)


def local(obj, probe, amplitudes, positions):
    col_count = lax.axis_size("col")
    tile_rows, tile_cols = obj.shape[1], obj.shape[2]
    order = probe.shape[1]
    pat_count = amplitudes.shape[0]
    capacity = 2 * pat_count
    dims = (tile_rows, tile_cols, pat_count, col_count, capacity)
    me = jnp.stack([lax.axis_index("row"), lax.axis_index("col")]).astype(jnp.int32)
    pos = positions.T.reshape(-1)
    turns, twiddles, sorting = tables(order)
    tile = (2, tile_rows, tile_cols)
    window = (2, order, order)
    wide = (2, 2 * tile_rows, 2 * tile_cols)
    shares = shape((col_count, sums_rows(order // col_count), order), jnp.int32)
    coded_tile = shape((tile_rows + SUBLANES, tile_cols), jnp.int32)
    coded_row = shape((tile_rows + SUBLANES, 2 * tile_cols), jnp.int32)
    coded_col = shape((2 * (tile_rows + SUBLANES), tile_cols), jnp.int32)
    one_pattern = 24 * 2 * order**3

    coded = call(encode_kernel, coded_tile, VMEM, [LOAD], [], 1 << 26)(obj)
    right = passed_along(coded, "col", -1)
    below = passed_along(coded, "row", -1)
    diag = passed_along(right, "row", -1)

    outgoing = call(
        functools.partial(outgoing_kernel, dims), shape((col_count * SEND, order, order), bf16), HBM, [SMEM, SMEM, HBM, HBM],
        [pltpu.SemaphoreType.DMA((pat_count,))], 1 << 20,
    )(pos, me, amplitudes, right)
    incoming = lax.all_to_all(outgoing, "col", split_axis=0, concat_axis=0, tiled=True)

    def weights(probe_now, span, kind):
        return call(
            functools.partial(weights_kernel, dims, span), shape((span * tile_rows, span * tile_cols)), VMEM, [SMEM, SMEM, kind],
            [pltpu.VMEM(((span + 2) * tile_rows, (span + 2) * tile_cols), f32), pltpu.VMEM((order, order), f32)], 8 << 30,
        )(pos, me, probe_now)

    weights_old = weights(probe, 2, LOAD)

    far, power, ext = call(
        functools.partial(first_half_kernel, dims), (shape((capacity,) + window), shape((order, order)), shape(wide)), (HBM, VMEM, HBM),
        [SMEM, SMEM, LOAD] + [VMEM] * 3 + [LOAD] * 3,
        [pltpu.VMEM(wide, f32)] + work_scratch(order) + [pltpu.VMEM((capacity,) + window, f32)] + list_scratch(capacity)
        + [pltpu.SemaphoreType.DMA((capacity,)), pltpu.SemaphoreType.DMA],
        capacity * one_pattern // 2,
    )(pos, me, obj, right, below, diag, probe, turns, twiddles)

    share, top, bottom, numer, sorted_amps = call(
        functools.partial(second_half_kernel, dims),
        (shape(wide), coded_row, coded_row, shares, shape((capacity, order, order), bf16)),
        (HBM, VMEM, VMEM, VMEM, HBM),
        [SMEM, SMEM, LOAD, LOAD, VMEM, LOAD, HBM, HBM] + [LOAD] * 3,
        [pltpu.VMEM(wide, f32)] + work_scratch(order)
        + [pltpu.VMEM(window, f32), pltpu.VMEM((capacity,) + window, f32), pltpu.VMEM((capacity, order, order), bf16), pltpu.VMEM((capacity, order, order), bf16)]
        + list_scratch(capacity) + [pltpu.SemaphoreType.DMA((capacity,))] * 3 + [pltpu.SemaphoreType.DMA],
        capacity * one_pattern // 2,
    )(pos, me, ext, probe, power, weights_old, far, incoming, turns, twiddles, sorting)

    from_above = passed_along(bottom, "row", 1)
    from_below = passed_along(top, "row", -1)
    fresh, chunks = probe_update(me, probe, numer, LOAD)
    sums, to_left, to_right = call(
        functools.partial(rows_sum_kernel, dims), (shape(wide), coded_col, coded_col), (VMEM,) * 3, [LOAD, VMEM, VMEM, HBM], [], 1 << 26,
    )(share, from_above, from_below, fresh)
    from_left = passed_along(to_right, "col", 1)
    from_right = passed_along(to_left, "col", -1)

    current, own, to_right, to_below, to_diag, numer, probe_now = call(
        functools.partial(whole_kernel, dims), (shape(tile), shape(tile), coded_tile, coded_tile, coded_tile, shares, shape(window)), (HBM,) + (VMEM,) * 6,
        [SMEM, SMEM, LOAD] + [VMEM] * 3 + [LOAD, VMEM, HBM, LOAD, LOAD],
        [pltpu.VMEM(wide, f32), pltpu.VMEM(wide, f32)] + work_scratch(order)
        + [pltpu.VMEM((3, order, order), f32), pltpu.VMEM((2,) + window, f32), pltpu.VMEM((capacity, order, order), bf16)]
        + list_scratch(capacity) + [pltpu.SemaphoreType.DMA((capacity,)), pltpu.SemaphoreType.DMA],
        capacity * one_pattern,
    )(pos, me, ext, sums, from_left, from_right, weights_old, chunks, sorted_amps, turns, twiddles)

    from_left = passed_along(to_right, "col", 1)
    from_above = passed_along(to_below, "row", 1)
    from_diag = passed_both(to_diag, 1, 1)
    weights_new = weights(probe_now, 1, VMEM)
    new_object = call(functools.partial(object_kernel, dims), shape(tile), VMEM, [LOAD] + [VMEM] * 4 + [LOAD, VMEM], [], 1 << 26)(
        current, own, from_left, from_above, from_diag, weights_old, weights_new
    )
    _, chunks = probe_update(me, probe_now, numer, VMEM)
    new_probe = call(probe_kernel, shape(window), VMEM, [VMEM], [], 1 << 26)(chunks)
    return new_object, new_probe


def solution(mesh):
    placed = (P(None, "row", "col"), P(), P(("row", "col"), None, None), P())
    return jax.shard_map(local, mesh=mesh, in_specs=placed, out_specs=(P(None, "row", "col"), P()), check_vma=False)
```

```python
import functools

import jax
import jax.numpy as jnp
import numpy as np
from jax import lax
from jax.experimental import pallas as pl
from jax.experimental.pallas import tpu as pltpu
from jax.sharding import PartitionSpec as P

ITERS = 2
SEND = 2

amplitude_floor = 0.1
object_regular = 0.5
probe_regular = 1.0

LANES = 128
SUBLANES = 8
LEVELS = 32767.0
CHUNK = 32
VMEM = pl.BlockSpec(memory_space=pltpu.VMEM)
SMEM = pl.BlockSpec(memory_space=pltpu.SMEM)
HBM = pl.BlockSpec(memory_space=pltpu.HBM)
LOAD = object()
f32 = jnp.float32
bf16 = jnp.bfloat16


def tables(order):
    half = order // 2
    counter = np.arange(half)
    angles = 2.0 * np.pi * ((counter[:, None] * counter[None, :]) % half) / half
    cos, sin = np.cos(angles), np.sin(angles)
    scale = 1.0 / np.sqrt(order)
    turns = []
    for block in ([[cos, -sin], [sin, cos]], [[cos, sin], [-sin, cos]]):
        matrix = np.block(block) * scale
        high = matrix.astype(jnp.bfloat16)
        turns.append(np.stack([high, (matrix - high.astype(np.float64)).astype(jnp.bfloat16)]))
    turn = 2.0 * np.pi * counter / order
    twiddle = np.stack([np.cos(turn), -np.sin(turn)]).astype(np.float32)
    twiddles = np.concatenate(
        [np.broadcast_to(twiddle[:, :, None], (2, half, half)), np.broadcast_to(twiddle[:, None, :], (2, SUBLANES, half))], axis=1
    )
    sorting = np.zeros((order, order), np.float32)
    sorting[np.arange(half), 2 * np.arange(half)] = 1.0
    sorting[half + np.arange(half), 2 * np.arange(half) + 1] = 1.0
    return (
        jnp.asarray(np.stack(turns)),
        jnp.asarray(np.ascontiguousarray(twiddles)),
        jnp.asarray(np.stack([sorting, sorting.T]).astype(jnp.bfloat16)),
    )


def list_patterns(dims, pos_ref, me_ref, ys_ref, xs_ref, holders_ref, ranks_ref):
    tile_rows, tile_cols, pat_count, col_count, capacity = dims
    my_row, my_col = me_ref[0], me_ref[1]
    band_count = pat_count * col_count
    first = my_row * band_count
    total = pos_ref.shape[0] // 2

    def visit(index, carry):
        found, source, rank = carry
        y = pos_ref[first + index]
        x = pos_ref[total + first + index]
        here = lax.div(x, tile_cols) == my_col
        holder = lax.div(index, pat_count)
        rank = jnp.where(holder == source, rank, 0)

        @pl.when(here & (found < capacity))
        def _():
            ys_ref[found] = y - my_row * tile_rows
            xs_ref[found] = x - my_col * tile_cols
            holders_ref[found] = holder
            ranks_ref[found] = rank

        step = here.astype(jnp.int32)
        return found + step, holder, rank + step

    found, _, _ = lax.fori_loop(0, band_count, visit, (jnp.int32(0), jnp.int32(-1), jnp.int32(0)))
    return jnp.minimum(found, capacity)


def lane_index(rows):
    return lax.broadcasted_iota(jnp.int32, (rows, LANES), 1)


def shifted_left(tiles, shift):
    lane = lane_index(tiles[0].shape[0])
    turn = lax.rem(LANES - shift, LANES)
    rolled = [pltpu.roll(tile, turn, axis=1) for tile in tiles]
    inside = lane < LANES - shift
    return [jnp.where(inside, a, b) for a, b in zip(rolled[:-1], rolled[1:])]


def shifted_right(tiles, shift):
    lane = lane_index(tiles[0].shape[0])
    rolled = [pltpu.roll(tile, shift, axis=1) for tile in tiles]
    outside = lane < shift
    zero = jnp.zeros_like(rolled[0])
    firsts = [zero] + rolled
    seconds = rolled + [zero]
    return [jnp.where(outside, a, b) for a, b in zip(firsts, seconds)]


def row_groups(tile):
    return [tile[k : k + SUBLANES] for k in range(0, tile.shape[0], SUBLANES)]


def shifted_up(tile, shift):
    row = lax.broadcasted_iota(jnp.int32, (SUBLANES, LANES), 0)
    turn = lax.rem(SUBLANES - shift, SUBLANES)
    rolled = [pltpu.roll(group, turn, axis=0) for group in row_groups(tile)]
    inside = row < SUBLANES - shift
    return jnp.concatenate([jnp.where(inside, a, b) for a, b in zip(rolled[:-1], rolled[1:])], axis=0)


def shifted_down(before, tile, shift):
    row = lax.broadcasted_iota(jnp.int32, (SUBLANES, LANES), 0)
    rolled = [before] + [pltpu.roll(group, shift, axis=0) for group in row_groups(tile)]
    outside = row < shift
    return rolled[-1], jnp.concatenate([jnp.where(outside, a, b) for a, b in zip(rolled[:-1], rolled[1:])], axis=0)


class Deposit:
    def __init__(self, add, top, left):
        self.add = add
        self.row = pl.multiple_of(lax.div(top, SUBLANES) * SUBLANES, SUBLANES)
        self.col = pl.multiple_of(lax.div(left, LANES) * LANES, LANES)
        self.down = lax.rem(top, SUBLANES)
        self.right = lax.rem(left, LANES)
        self.carried = None

    def place(self, first, tiles):
        moved = jnp.concatenate(shifted_right(tiles, self.right), axis=1)
        self.add(pl.ds(self.row + first, tiles[0].shape[0]), pl.ds(self.col, moved.shape[1]), moved)

    def put(self, first, tiles):
        if self.carried is None:
            self.carried = [jnp.zeros((SUBLANES, LANES), f32) for _ in tiles]
        pairs = [shifted_down(before, tile, self.down) for before, tile in zip(self.carried, tiles)]
        self.carried = [carried for carried, _ in pairs]
        self.place(first, [tile for _, tile in pairs])

    def finish(self, first):
        row = lax.broadcasted_iota(jnp.int32, (SUBLANES, LANES), 0)
        self.place(first, [jnp.where(row < self.down, tile, 0.0) for tile in self.carried])


def lane_tiles(value):
    return [value[:, k : k + LANES] for k in range(0, value.shape[1], LANES)]


def store_split(ref, rows, cols, value):
    high = value.astype(bf16)
    ref[0, rows, cols] = high
    ref[1, rows, cols] = (value - high.astype(f32)).astype(bf16)


def right_dot(x_ref, table_ref):
    left = jnp.concatenate([x_ref[0], x_ref[1], x_ref[0]], axis=1)
    right = jnp.concatenate([table_ref[0], table_ref[0], table_ref[1]], axis=0)
    return jnp.dot(left, right, preferred_element_type=f32)


def left_dot(table_ref, x_ref):
    left = jnp.concatenate([table_ref[0], table_ref[0], table_ref[1]], axis=1)
    right = jnp.concatenate([x_ref[0], x_ref[1], x_ref[0]], axis=0)
    return jnp.dot(left, right, preferred_element_type=f32)


def repeated(group, rows):
    return jnp.concatenate([group] * (rows // SUBLANES), axis=0)


def encode(read, out_ref, rows, first, last):
    for col in range(0, out_ref.shape[1], LANES):
        cols = pl.ds(col, LANES)
        largest = jnp.full((SUBLANES, LANES), 1e-30, f32)
        for start in range(0, rows, CHUNK):
            for comp in range(2):
                for group in row_groups(jnp.abs(read(comp, pl.ds(start, CHUNK), cols))):
                    largest = jnp.maximum(largest, group)
        exponent = jnp.ceil(jnp.log2(largest))
        out_ref[last : last + SUBLANES, cols] = exponent.astype(jnp.int32)
        scale = repeated(jnp.exp2(-exponent) * LEVELS, CHUNK)
        for start in range(0, rows, CHUNK):
            codes = []
            for comp in range(2):
                scaled = jnp.clip(read(comp, pl.ds(start, CHUNK), cols) * scale, -LEVELS, LEVELS)
                codes.append(jnp.round(scaled).astype(jnp.int32))
            out_ref[pl.ds(first + start, CHUNK), cols] = (codes[0] << 16) | (codes[1] & 0xFFFF)


def decode(ref, start, last, col):
    cols = pl.ds(col, LANES)
    words = ref[pl.ds(start, CHUNK), cols]
    scale = repeated(jnp.exp2(ref[last : last + SUBLANES, cols].astype(f32)) * (1.0 / LEVELS), CHUNK)
    return (words >> 16).astype(f32) * scale, ((words << 16) >> 16).astype(f32) * scale


def largest_exponent(values):
    largest = jnp.full((SUBLANES, LANES), 1e-30, f32)
    for value in values:
        for group in row_groups(jnp.abs(value)):
            largest = jnp.maximum(largest, group)
    return jnp.ceil(jnp.log2(largest))


def fixed(value, exponent):
    scaled = value * repeated(jnp.exp2(-exponent) * LEVELS, value.shape[0])
    return jnp.round(jnp.clip(scaled, -LEVELS, LEVELS)).astype(jnp.int32)


def paired(first, second):
    return (first << 16) | (second & 0xFFFF)


def unpaired(words):
    return words >> 16, (words << 16) >> 16


def scaled_back(codes, exponent):
    return codes.astype(f32) * repeated(jnp.exp2(exponent.astype(f32)) * (1.0 / LEVELS), codes.shape[0])


def sums_rows(rows):
    return rows + rows // 2 + SUBLANES


def encode_sums(out_ref, cols, u_re, u_im, v):
    rows = v.shape[0]
    half = rows // 2
    of_u, of_v = largest_exponent([u_re, u_im]), largest_exponent([v])
    out_ref[0:rows, cols] = paired(fixed(u_re, of_u), fixed(u_im, of_u))
    codes = fixed(v, of_v)
    out_ref[rows : rows + half, cols] = paired(codes[:half], codes[half:])
    out_ref[rows + half : rows + half + SUBLANES, cols] = paired(of_u.astype(jnp.int32), of_v.astype(jnp.int32))


def decode_sums(ref, cols, rows):
    half = rows // 2
    of_u, of_v = unpaired(ref[rows + half : rows + half + SUBLANES, cols])
    u_re, u_im = unpaired(ref[0:rows, cols])
    v = jnp.concatenate(unpaired(ref[rows : rows + half, cols]), axis=0)
    return scaled_back(u_re, of_u), scaled_back(u_im, of_u), scaled_back(v, of_v)


def decode_probe(out_ref, chunks_ref):
    chunks = chunks_ref.shape[0]
    rows = out_ref.shape[1] // chunks
    for chunk in range(chunks):
        for col in range(0, out_ref.shape[2], LANES):
            cols = pl.ds(col, LANES)
            exponent = chunks_ref[chunk, rows : rows + SUBLANES, cols]
            for comp, codes in enumerate(unpaired(chunks_ref[chunk, 0:rows, cols])):
                out_ref[comp, chunk * rows : (chunk + 1) * rows, cols] = scaled_back(codes, exponent)


def cut_chunk(ext_ref, comp, first, top, left, rows):
    row = pl.multiple_of(lax.div(top, SUBLANES) * SUBLANES, SUBLANES)
    col = pl.multiple_of(lax.div(left, LANES) * LANES, LANES)
    block = ext_ref[comp, pl.ds(row + first, rows + SUBLANES), pl.ds(col, 3 * LANES)]
    tiles = shifted_left(lane_tiles(block), lax.rem(left, LANES))
    return [shifted_up(tile, lax.rem(top, SUBLANES)) for tile in tiles]


def forward(order, ext_ref, probe_ref, consts, y, x, win_ref, power_ref, weight, xa_ref, xb_ref, ya_ref, yb_ref, far_ref):
    turns, twiddles = consts
    half = order // 2
    tw_re = repeated(twiddles[0, half : half + SUBLANES, :], CHUNK)
    tw_im = repeated(twiddles[1, half : half + SUBLANES, :], CHUNK)
    for first in range(0, order, CHUNK):
        rows = pl.ds(first, CHUNK)
        win_re = cut_chunk(ext_ref, 0, first, y, x, CHUNK)
        win_im = cut_chunk(ext_ref, 1, first, y, x, CHUNK)
        exits = []
        for k in range(2):
            cols = pl.ds(k * half, half)
            win_ref[0, rows, cols] = win_re[k]
            win_ref[1, rows, cols] = win_im[k]
            power_ref[rows, cols] += weight * (win_re[k] * win_re[k] + win_im[k] * win_im[k])
            p_re, p_im = probe_ref[0, rows, cols], probe_ref[1, rows, cols]
            exits.append((p_re * win_re[k] - p_im * win_im[k], p_re * win_im[k] + p_im * win_re[k]))
        (lo_re, lo_im), (hi_re, hi_im) = exits
        store_split(xa_ref, rows, pl.ds(0, half), lo_re + hi_re)
        store_split(xa_ref, rows, pl.ds(half, half), lo_im + hi_im)
        d_re, d_im = lo_re - hi_re, lo_im - hi_im
        store_split(xb_ref, rows, pl.ds(0, half), d_re * tw_re - d_im * tw_im)
        store_split(xb_ref, rows, pl.ds(half, half), d_re * tw_im + d_im * tw_re)
    yield
    ya_ref[...] = right_dot(xa_ref, turns.at[0])
    yb_ref[...] = right_dot(xb_ref, turns.at[0])
    yield
    for first in range(0, half, CHUNK):
        rows = pl.ds(first, CHUNK)
        below = pl.ds(half + first, CHUNK)
        t_re, t_im = twiddles[0, rows, :], twiddles[1, rows, :]
        for k, y_ref in enumerate((ya_ref, yb_ref)):
            cols = pl.ds(k * half, half)
            up_re, up_im = y_ref[rows, 0:half], y_ref[rows, half:order]
            dn_re, dn_im = y_ref[below, 0:half], y_ref[below, half:order]
            store_split(xa_ref, rows, cols, up_re + dn_re)
            store_split(xa_ref, below, cols, up_im + dn_im)
            d_re, d_im = up_re - dn_re, up_im - dn_im
            store_split(xb_ref, rows, cols, d_re * t_re - d_im * t_im)
            store_split(xb_ref, below, cols, d_re * t_im + d_im * t_re)
    yield
    far_ref[0] = left_dot(turns.at[1], xa_ref)
    far_ref[1] = left_dot(turns.at[1], xb_ref)
    yield


def backward(order, far_ref, amp_ref, consts, y, x, weight, probe_ref, win_ref, xa_ref, xb_ref, ya_ref, yb_ref, grad_ref, numer_ref):
    turns, twiddles = consts
    half = order // 2
    tw_re = repeated(twiddles[0, half : half + SUBLANES, :], CHUNK)
    tw_im = repeated(twiddles[1, half : half + SUBLANES, :], CHUNK)
    for k, x_ref in enumerate((xa_ref, xb_ref)):
        for first in range(0, half, CHUNK):
            rows = pl.ds(first, CHUNK)
            below = pl.ds(half + first, CHUNK)
            far_re, far_im = far_ref[k, rows, :], far_ref[k, below, :]
            amp = amp_ref[pl.ds(k * half + first, CHUNK), :].astype(f32)
            factor = amp * lax.rsqrt(far_re * far_re + far_im * far_im + amplitude_floor)
            store_split(x_ref, rows, slice(None), far_re * factor)
            store_split(x_ref, below, slice(None), far_im * factor)
    yield
    ya_ref[...] = left_dot(turns.at[0], xa_ref)
    yb_ref[...] = left_dot(turns.at[0], xb_ref)
    yield
    for first in range(0, half, CHUNK):
        rows = pl.ds(first, CHUNK)
        below = pl.ds(half + first, CHUNK)
        t_re, t_im = twiddles[0, rows, :], twiddles[1, rows, :]
        for k, x_ref in enumerate((xa_ref, xb_ref)):
            cols = slice(k * half, (k + 1) * half)
            a_re, a_im = ya_ref[rows, cols], ya_ref[below, cols]
            b_re, b_im = yb_ref[rows, cols], yb_ref[below, cols]
            c_re, c_im = b_re * t_re + b_im * t_im, b_im * t_re - b_re * t_im
            store_split(x_ref, rows, pl.ds(0, half), a_re + c_re)
            store_split(x_ref, rows, pl.ds(half, half), a_im + c_im)
            store_split(x_ref, below, pl.ds(0, half), a_re - c_re)
            store_split(x_ref, below, pl.ds(half, half), a_im - c_im)
    yield
    ya_ref[...] = right_dot(xa_ref, turns.at[1])
    yb_ref[...] = right_dot(xb_ref, turns.at[1])
    yield

    def adder(comp):
        def add(rows, cols, moved):
            grad_ref[comp, rows, cols] += moved

        return add

    deposits = [Deposit(adder(comp), y, x) for comp in range(2)]
    for first in range(0, order, CHUNK):
        rows = pl.ds(first, CHUNK)
        a_re, a_im = ya_ref[rows, 0:half], ya_ref[rows, half:order]
        b_re, b_im = yb_ref[rows, 0:half], yb_ref[rows, half:order]
        c_re, c_im = b_re * tw_re + b_im * tw_im, b_im * tw_re - b_re * tw_im
        waves = [(a_re + c_re, a_im + c_im), (a_re - c_re, a_im - c_im)]
        terms = ([], [])
        for k, (wave_re, wave_im) in enumerate(waves):
            cols = pl.ds(k * half, half)
            wave_re, wave_im = weight * wave_re, weight * wave_im
            p_re, p_im = probe_ref[0, rows, cols], probe_ref[1, rows, cols]
            w_re, w_im = win_ref[0, rows, cols], win_ref[1, rows, cols]
            terms[0].append(p_re * wave_re + p_im * wave_im)
            terms[1].append(p_re * wave_im - p_im * wave_re)
            numer_ref[0, rows, cols] += w_re * wave_re + w_im * wave_im
            numer_ref[1, rows, cols] += w_re * wave_im - w_im * wave_re
        for comp in range(2):
            deposits[comp].put(first, terms[comp])
    for deposit in deposits:
        deposit.finish(order)
    yield


def interleaved(*stages):
    live = list(stages)
    while live:
        still = []
        for stage in live:
            try:
                next(stage)
                still.append(stage)
            except StopIteration:
                pass
        live = still


def outgoing_kernel(dims, wanted, pos_ref, me_ref, amp_ref, after_ref, out_ref, sems):
    tile_rows, tile_cols, pat_count, col_count, capacity = dims
    first = (me_ref[0] * col_count + me_ref[1]) * pat_count
    total = pos_ref.shape[0] // 2
    owners = [lax.div(pos_ref[total + first + k], tile_cols) for k in range(pat_count)]
    copies = []
    for k in range(pat_count):
        rank = sum(((owners[e] == owners[k]).astype(jnp.int32) for e in range(k)), jnp.int32(0))
        copies.append((rank == wanted, pltpu.make_async_copy(amp_ref.at[k], out_ref.at[owners[k]], sems.at[k])))
    for chosen, copy in copies:
        pl.when(chosen)(copy.start)
    for chosen, copy in copies:
        pl.when(chosen)(copy.wait)


def weights_kernel(dims, span, pos_ref, me_ref, probe_ref, out_ref, sums_ref, power_ref):
    tile_rows, tile_cols, pat_count, col_count, capacity = dims
    order = probe_ref.shape[1]
    top = (me_ref[0] - 1) * tile_rows
    left = (me_ref[1] - 1) * tile_cols
    total = pos_ref.shape[0] // 2
    for first in range(0, sums_ref.shape[0], order):
        sums_ref[pl.ds(first, order), :] = jnp.zeros((order, sums_ref.shape[1]), f32)
    power_ref[...] = probe_ref[0] * probe_ref[0] + probe_ref[1] * probe_ref[1]

    def visit(index, carry):
        y = pos_ref[index] - top
        x = pos_ref[total + index] - left

        @pl.when((y > 0) & (y < (span + 1) * tile_rows) & (x > 0) & (x < (span + 1) * tile_cols))
        def _():
            def add(rows, cols, moved):
                sums_ref[rows, cols] += moved

            deposit = Deposit(add, y, x)
            for first in range(0, order, CHUNK):
                deposit.put(first, lane_tiles(power_ref[pl.ds(first, CHUNK), :]))
            deposit.finish(order)

        return carry

    lax.fori_loop(0, total, visit, 0)
    out_ref[...] = sums_ref[tile_rows : (span + 1) * tile_rows, tile_cols : (span + 1) * tile_cols]


def encode_kernel(obj_ref, out_ref):
    rows = obj_ref.shape[1]
    encode(lambda comp, at, cols: obj_ref[comp, at, cols], out_ref, rows, 0, rows)


def unfold(dims, ext_ref, own_ref, coded_refs):
    tile_rows, tile_cols = dims[:2]
    ext_ref[:, 0:tile_rows, 0:tile_cols] = own_ref[...]
    for (i, j), ref in zip(((0, 1), (1, 0), (1, 1)), coded_refs):
        for col in range(0, tile_cols, LANES):
            for start in range(0, tile_rows, CHUNK):
                parts = decode(ref, start, tile_rows, col)
                for comp in range(2):
                    ext_ref[comp, pl.ds(i * tile_rows + start, CHUNK), pl.ds(j * tile_cols + col, LANES)] = parts[comp]


def spread_sums(out_ref, u_ref, v_ref):
    chunks = out_ref.shape[0]
    rows = v_ref.shape[0] // chunks
    for chunk in range(chunks):
        at = pl.ds(chunk * rows, rows)
        for col in range(0, v_ref.shape[1], LANES):
            cols = pl.ds(col, LANES)
            encode_sums(out_ref.at[chunk], cols, u_ref[0, at, cols], u_ref[1, at, cols], v_ref[at, cols])


def added(parts):
    while len(parts) > 1:
        parts = [tuple(x + y for x, y in zip(a, b)) for a, b in zip(parts[::2], parts[1::2])]
    return parts[0]


def sums_kernel(rows, parts_ref, out_ref):
    for col in range(0, out_ref.shape[1], LANES):
        cols = pl.ds(col, LANES)
        total = added([decode_sums(parts_ref.at[k], cols, rows) for k in range(parts_ref.shape[0])])
        encode_sums(out_ref, cols, *total)


def update_kernel(rows, me_ref, probe_ref, *refs):
    *parts, out_ref = refs
    first = pl.multiple_of(me_ref[1] * rows, SUBLANES)
    for col in range(0, out_ref.shape[2], LANES):
        cols = pl.ds(col, LANES)
        u_re, u_im, v = added([decode_sums(ref, cols, rows) for ref in parts])
        scale = 1.0 / (v + probe_regular)
        re = (probe_ref[0, pl.ds(first, rows), cols] + u_re) * scale
        im = (probe_ref[1, pl.ds(first, rows), cols] + u_im) * scale
        exponent = largest_exponent([re, im])
        words = paired(fixed(re, exponent), fixed(im, exponent))
        for chunk in range(out_ref.shape[0]):
            out_ref[chunk, 0:rows, cols] = words
            out_ref[chunk, rows : rows + SUBLANES, cols] = exponent.astype(jnp.int32)


def probe_kernel(chunks_ref, out_ref):
    decode_probe(out_ref, chunks_ref)


def first_half_kernel(dims, pos_ref, me_ref, own_ref, right_ref, below_ref, diag_ref, probe_ref, turns, twiddles,
                      far_out, power_out, ext_out, ext_ref, win_ref, xa_ref, xb_ref, ya_ref, yb_ref, far_ref, ys_ref, xs_ref, holders_ref, ranks_ref, sems, ext_sem):
    tile_rows, tile_cols, pat_count, col_count, capacity = dims
    order = probe_ref.shape[1]
    count = list_patterns(dims, pos_ref, me_ref, ys_ref, xs_ref, holders_ref, ranks_ref)
    unfold(dims, ext_ref, own_ref, (right_ref, below_ref, diag_ref))
    keep = pltpu.make_async_copy(ext_ref, ext_out, ext_sem)
    keep.start()
    power_out[...] = jnp.zeros_like(power_out)
    consts = (turns, twiddles)

    def pair(step, carry):
        stages = []
        for k in range(2):
            listed = 2 * step + k
            weight = (listed < count).astype(f32)
            index = jnp.minimum(listed, count - 1)
            stages.append(forward(order, ext_ref, probe_ref, consts, ys_ref[index], xs_ref[index], win_ref.at[k], power_out, weight,
                                  xa_ref.at[k], xb_ref.at[k], ya_ref.at[k], yb_ref.at[k], far_ref.at[listed]))
        interleaved(*stages)
        for k in range(2):
            listed = 2 * step + k
            pltpu.make_async_copy(far_ref.at[listed], far_out.at[listed], sems.at[listed]).start()
        return carry

    pairs = lax.div(count + 1, 2)
    lax.fori_loop(0, pairs, pair, 0)

    def settle(listed, carry):
        pltpu.make_async_copy(far_ref.at[listed], far_out.at[listed], sems.at[listed]).wait()
        return carry

    lax.fori_loop(0, 2 * pairs, settle, 0)
    keep.wait()


def second_half_kernel(dims, pos_ref, me_ref, ext_ref, probe_ref, power_ref, weights_ref, far_in, amp_first, amp_second, turns, twiddles, sorting,
                       share_out, top_out, bottom_out, numer_out, amp_out,
                       sum_ref, win_ref, xa_ref, xb_ref, ya_ref, yb_ref, numer_ref, far_ref, amp_ref, sorted_ref, ys_ref, xs_ref, holders_ref, ranks_ref, far_sems, amp_sems, out_sems, sum_sem):
    tile_rows, tile_cols, pat_count, col_count, capacity = dims
    order = probe_ref.shape[1]
    half = order // 2
    amp_ins = (amp_first, amp_second)
    count = list_patterns(dims, pos_ref, me_ref, ys_ref, xs_ref, holders_ref, ranks_ref)
    pairs = lax.div(count + 1, 2)

    def far_copy(listed):
        return pltpu.make_async_copy(far_in.at[listed], far_ref.at[listed], far_sems.at[listed])

    def amp_copy(listed, source):
        return pltpu.make_async_copy(source.at[holders_ref[jnp.minimum(listed, count - 1)]], amp_ref.at[listed], amp_sems.at[listed])

    def begin(listed, carry):
        far_copy(listed).start()
        rank = ranks_ref[jnp.minimum(listed, count - 1)]
        for wanted, source in enumerate(amp_ins):

            @pl.when(rank == wanted)
            def _():
                amp_copy(listed, source).start()

        return carry

    lax.fori_loop(0, 2 * pairs, begin, 0)
    sum_ref[...] = jnp.zeros_like(sum_ref)
    numer_ref[...] = jnp.zeros_like(numer_ref)
    consts = (turns, twiddles)

    def pair(step, carry):
        stages = []
        for k in range(2):
            listed = 2 * step + k
            far_copy(listed).wait()
            amp_copy(listed, amp_ins[0]).wait()
        for k in range(2):
            listed = 2 * step + k
            weight = (listed < count).astype(f32)
            index = jnp.minimum(listed, count - 1)
            y, x = ys_ref[index], xs_ref[index]
            rows_sorted = jnp.dot(sorting[0], amp_ref[listed], preferred_element_type=f32).astype(bf16)
            sorted_ref[listed] = jnp.dot(rows_sorted, sorting[1], preferred_element_type=f32).astype(bf16)
            for first in range(0, order, CHUNK):
                for comp in range(2):
                    for c, tile in enumerate(cut_chunk(ext_ref, comp, first, y, x, CHUNK)):
                        win_ref[k, comp, pl.ds(first, CHUNK), pl.ds(c * half, half)] = tile
            stages.append(backward(order, far_ref.at[listed], sorted_ref.at[listed], consts, y, x, weight, probe_ref, win_ref.at[k],
                                   xa_ref.at[k], xb_ref.at[k], ya_ref.at[k], yb_ref.at[k], sum_ref, numer_ref))
        interleaved(*stages)
        for k in range(2):
            listed = 2 * step + k
            pltpu.make_async_copy(sorted_ref.at[listed], amp_out.at[listed], out_sems.at[listed]).start()
        return carry

    lax.fori_loop(0, pairs, pair, 0)
    for first in range(0, 2 * tile_rows, CHUNK):
        rows = pl.ds(first, CHUNK)
        scale = 1.0 / (weights_ref[rows, :] + object_regular)
        for comp in range(2):
            sum_ref[comp, rows, :] = sum_ref[comp, rows, :] * scale
    keep = pltpu.make_async_copy(sum_ref, share_out, sum_sem)
    keep.start()
    encode(lambda comp, at, cols: sum_ref[comp, at, cols], top_out, tile_rows, 0, tile_rows)
    encode(lambda comp, at, cols: sum_ref[comp, pl.ds(tile_rows + at.start, at.size), cols], bottom_out, tile_rows, 0, tile_rows)
    spread_sums(numer_out, numer_ref, power_ref)

    def settle(listed, carry):
        pltpu.make_async_copy(sorted_ref.at[listed], amp_out.at[listed], out_sems.at[listed]).wait()
        return carry

    lax.fori_loop(0, 2 * pairs, settle, 0)
    keep.wait()


def rows_sum_kernel(dims, share_ref, above_ref, below_ref, after_ref, sum_out, left_out, right_out):
    tile_rows, tile_cols = dims[:2]
    for i, ref in enumerate((above_ref, below_ref)):
        for col in range(0, 2 * tile_cols, LANES):
            for start in range(0, tile_rows, CHUNK):
                rows, cols = pl.ds(i * tile_rows + start, CHUNK), pl.ds(col, LANES)
                parts = decode(ref, start, tile_rows, col)
                for comp in range(2):
                    sum_out[comp, rows, cols] = share_ref[comp, rows, cols] + parts[comp]
    for j, ref in enumerate((left_out, right_out)):
        for i in range(2):

            def read(comp, at, cols, i=i, j=j):
                return sum_out[comp, pl.ds(i * tile_rows + at.start, at.size), pl.ds(j * tile_cols + cols.start, cols.size)]

            encode(read, ref, tile_rows, i * tile_rows, 2 * tile_rows + i * SUBLANES)


def whole_kernel(dims, pos_ref, me_ref, old_ref, sum_ref, from_left_ref, from_right_ref, weights_ref,
                 chunks_ref, amp_in, turns, twiddles,
                 current_out, top_out, bottom_out, numer_out, probe_ref,
                 ext_ref, grad_ref, win_ref, xa_ref, xb_ref, ya_ref, yb_ref, numer_ref, far_ref, amp_ref, ys_ref, xs_ref, holders_ref, ranks_ref, amp_sems, own_sem):
    tile_rows, tile_cols, pat_count, col_count, capacity = dims
    order = probe_ref.shape[1]
    count = list_patterns(dims, pos_ref, me_ref, ys_ref, xs_ref, holders_ref, ranks_ref)
    pairs = lax.div(count + 1, 2)
    decode_probe(probe_ref, chunks_ref)

    def fetch(listed):
        return pltpu.make_async_copy(amp_in.at[jnp.minimum(listed, count - 1)], amp_ref.at[listed], amp_sems.at[listed])

    def begin(listed, carry):
        fetch(listed).start()
        return carry

    lax.fori_loop(0, 2 * pairs, begin, 0)
    for j, ref in enumerate((from_left_ref, from_right_ref)):
        for i in range(2):
            for col in range(0, tile_cols, LANES):
                for start in range(0, tile_rows, CHUNK):
                    rows, cols = pl.ds(i * tile_rows + start, CHUNK), pl.ds(j * tile_cols + col, LANES)
                    parts = decode(ref, i * tile_rows + start, 2 * tile_rows + i * SUBLANES, col)
                    scale = object_regular / (weights_ref[rows, cols] + object_regular)
                    for comp in range(2):
                        ext_ref[comp, rows, cols] = old_ref[comp, rows, cols] * scale + (sum_ref[comp, rows, cols] + parts[comp])
    keep = pltpu.make_async_copy(ext_ref.at[:, pl.ds(0, tile_rows), pl.ds(0, tile_cols)], current_out, own_sem)
    keep.start()
    grad_ref[...] = jnp.zeros_like(grad_ref)
    numer_ref[...] = jnp.zeros_like(numer_ref)
    consts = (turns, twiddles)

    def pair(step, carry):
        stages = []
        for k in range(2):
            fetch(2 * step + k).wait()
        for k in range(2):
            listed = 2 * step + k
            weight = (listed < count).astype(f32)
            index = jnp.minimum(listed, count - 1)
            y, x = ys_ref[index], xs_ref[index]

            def both(k=k, listed=listed, weight=weight, y=y, x=x):
                yield from forward(order, ext_ref, probe_ref, consts, y, x, win_ref.at[k], numer_ref.at[2], weight,
                                   xa_ref.at[k], xb_ref.at[k], ya_ref.at[k], yb_ref.at[k], far_ref.at[k])
                yield from backward(order, far_ref.at[k], amp_ref.at[listed], consts, y, x, weight, probe_ref, win_ref.at[k],
                                    xa_ref.at[k], xb_ref.at[k], ya_ref.at[k], yb_ref.at[k], grad_ref, numer_ref)

            stages.append(both())
        interleaved(*stages)
        return carry

    lax.fori_loop(0, pairs, pair, 0)
    for first in range(0, tile_rows, CHUNK):
        rows = pl.ds(first, CHUNK)
        scale = 1.0 / (weights_ref[rows, :] + object_regular)
        for comp in range(2):
            top_out[comp, rows, :] = grad_ref[comp, rows, :] * scale

    def read(comp, at, cols):
        rows = pl.ds(tile_rows + at.start, at.size)
        return grad_ref[comp, rows, cols] / (weights_ref[rows, cols] + object_regular)

    encode(read, bottom_out, tile_rows, 0, tile_rows)
    spread_sums(numer_out, numer_ref, numer_ref.at[2])
    keep.wait()


def fold_kernel(dims, top_ref, above_ref, own_out, right_out):
    tile_rows, tile_cols = dims[:2]
    for col in range(0, 2 * tile_cols, LANES):
        for start in range(0, tile_rows, CHUNK):
            rows, cols = pl.ds(start, CHUNK), pl.ds(col, LANES)
            parts = decode(above_ref, start, tile_rows, col)
            for comp in range(2):
                if col < tile_cols:
                    own_out[comp, rows, cols] = top_ref[comp, rows, cols] + parts[comp]
                else:
                    top_ref[comp, rows, cols] += parts[comp]
    encode(lambda comp, at, cols: top_ref[comp, at, pl.ds(tile_cols + cols.start, cols.size)], right_out, tile_rows, 0, tile_rows)


def object_kernel(dims, current_ref, own_ref, left_ref, before_ref, weights_ref, out_ref):
    tile_rows, tile_cols = dims[:2]
    for col in range(0, tile_cols, LANES):
        for start in range(0, tile_rows, CHUNK):
            rows, cols = pl.ds(start, CHUNK), pl.ds(col, LANES)
            scale = 1.0 / (weights_ref[rows, cols] + object_regular)
            back = (before_ref[rows, cols] + object_regular) * scale
            parts = decode(left_ref, start, tile_rows, col)
            for comp in range(2):
                old = object_regular * scale * current_ref[comp, rows, cols]
                out_ref[comp, rows, cols] = old + (own_ref[comp, rows, cols] + parts[comp]) * back


def shape(dims, dtype=f32):
    return jax.ShapeDtypeStruct(dims, dtype)


def work_scratch(order):
    return [
        pltpu.VMEM((2, 2, order, order), f32),
        pltpu.VMEM((2, 2, order, order), bf16),
        pltpu.VMEM((2, 2, order, order), bf16),
        pltpu.VMEM((2, order, order), f32),
        pltpu.VMEM((2, order, order), f32),
    ]


def list_scratch(capacity):
    return [pltpu.SMEM((capacity,), jnp.int32)] * 4


def call(kernel, outs, out_specs, in_specs, scratch, flops, limit=48 << 20):
    several = isinstance(outs, tuple)
    out_count = len(outs) if several else 1
    in_count = len(in_specs)
    loaded = [k for k, spec in enumerate(in_specs) if spec is LOAD]

    def body(*refs):
        ins, rest = list(refs[:in_count]), refs[in_count:]
        given, kept = rest[: out_count + len(scratch)], rest[out_count + len(scratch) :]
        copies = [pltpu.make_async_copy(ins[k], kept[n], kept[-1].at[n]) for n, k in enumerate(loaded)]
        for copy in copies:
            copy.start()
        for n, k in enumerate(loaded):
            copies[n].wait()
            ins[k] = kept[n]
        kernel(*ins, *given)

    def called(*args):
        own = [pltpu.VMEM(args[k].shape, args[k].dtype) for k in loaded]
        if loaded:
            own.append(pltpu.SemaphoreType.DMA((len(loaded),)))
        return pl.pallas_call(
            body,
            out_shape=outs,
            out_specs=out_specs,
            in_specs=[HBM if spec is LOAD else spec for spec in in_specs],
            scratch_shapes=list(scratch) + own,
            compiler_params=pltpu.CompilerParams(vmem_limit_bytes=limit),
            cost_estimate=pl.CostEstimate(flops=flops, bytes_accessed=8 << 20, transcendentals=0),
        )(*args)

    return called


def passed_along(value, axis, steps):
    count = lax.axis_size(axis)
    leading, last = (max(0, -steps), min(count, count - steps))
    return lax.ppermute(value, axis, [(source, source + steps) for source in range(leading, last)])


def swapped(value, axis, mask):
    return lax.ppermute(value, axis, [(k, k ^ mask) for k in range(lax.axis_size(axis))])


def probe_update(me, probe, numer, kind):
    cols, order = lax.axis_size("col"), probe.shape[1]
    rows = order // cols
    parts = lax.all_to_all(numer, "col", split_axis=0, concat_axis=0, tiled=True)
    total = call(functools.partial(sums_kernel, rows), shape((sums_rows(rows), order), jnp.int32), VMEM, [VMEM], [], 1 << 26)(parts)
    totals = [total] + [swapped(total, "row", mask) for mask in range(1, lax.axis_size("row"))]
    fresh = call(
        functools.partial(update_kernel, rows), shape((cols, rows + SUBLANES, order), jnp.int32), VMEM,
        [SMEM, kind] + [VMEM] * len(totals), [], 1 << 26,
    )(me, probe, *totals)
    return totals[1], lax.all_to_all(fresh, "col", split_axis=0, concat_axis=0, tiled=True)


def local(obj, probe, amplitudes, positions):
    col_count = lax.axis_size("col")
    tile_rows, tile_cols = obj.shape[1], obj.shape[2]
    order = probe.shape[1]
    pat_count = amplitudes.shape[0]
    capacity = 2 * pat_count
    dims = (tile_rows, tile_cols, pat_count, col_count, capacity)
    me = jnp.stack([lax.axis_index("row"), lax.axis_index("col")]).astype(jnp.int32)
    pos = positions.T.reshape(-1)
    turns, twiddles, sorting = tables(order)
    tile = (2, tile_rows, tile_cols)
    window = (2, order, order)
    wide = (2, 2 * tile_rows, 2 * tile_cols)
    shares = shape((col_count, sums_rows(order // col_count), order), jnp.int32)
    coded_tile = shape((tile_rows + SUBLANES, tile_cols), jnp.int32)
    coded_row = shape((tile_rows + SUBLANES, 2 * tile_cols), jnp.int32)
    coded_col = shape((2 * (tile_rows + SUBLANES), tile_cols), jnp.int32)
    one_pattern = 24 * 2 * order**3

    coded = call(encode_kernel, coded_tile, VMEM, [LOAD], [], 1 << 26)(obj)
    right = passed_along(coded, "col", -1)
    below = passed_along(coded, "row", -1)
    diag = passed_along(right, "row", -1)

    incoming = []
    for wanted, after in enumerate((coded, right)):
        outgoing = call(
            functools.partial(outgoing_kernel, dims, wanted), shape((col_count, order, order), bf16), HBM, [SMEM, SMEM, HBM, HBM],
            [pltpu.SemaphoreType.DMA((pat_count,))], 1 << 20,
        )(pos, me, amplitudes, after)
        incoming.append(lax.all_to_all(outgoing, "col", split_axis=0, concat_axis=0, tiled=True))

    def weights(probe_now, span, kind):
        return call(
            functools.partial(weights_kernel, dims, span), shape((span * tile_rows, span * tile_cols)), VMEM, [SMEM, SMEM, kind],
            [pltpu.VMEM(((span + 2) * tile_rows, (span + 2) * tile_cols), f32), pltpu.VMEM((order, order), f32)], 8 << 30,
        )(pos, me, probe_now)

    weights_old = weights(probe, 2, LOAD)

    far, power, ext = call(
        functools.partial(first_half_kernel, dims), (shape((capacity,) + window), shape((order, order)), shape(wide)), (HBM, VMEM, HBM),
        [SMEM, SMEM, LOAD] + [VMEM] * 3 + [LOAD] * 3,
        [pltpu.VMEM(wide, f32)] + work_scratch(order) + [pltpu.VMEM((capacity,) + window, f32)] + list_scratch(capacity)
        + [pltpu.SemaphoreType.DMA((capacity,)), pltpu.SemaphoreType.DMA],
        capacity * one_pattern // 2,
    )(pos, me, obj, right, below, diag, probe, turns, twiddles)

    share, top, bottom, numer, sorted_amps = call(
        functools.partial(second_half_kernel, dims),
        (shape(wide), coded_row, coded_row, shares, shape((capacity, order, order), bf16)),
        (HBM, VMEM, VMEM, VMEM, HBM),
        [SMEM, SMEM, LOAD, LOAD, VMEM, LOAD, HBM, HBM, HBM] + [LOAD] * 3,
        [pltpu.VMEM(wide, f32)] + work_scratch(order)
        + [pltpu.VMEM(window, f32), pltpu.VMEM((capacity,) + window, f32), pltpu.VMEM((capacity, order, order), bf16), pltpu.VMEM((capacity, order, order), bf16)]
        + list_scratch(capacity) + [pltpu.SemaphoreType.DMA((capacity,))] * 3 + [pltpu.SemaphoreType.DMA],
        capacity * one_pattern // 2,
    )(pos, me, ext, probe, power, weights_old, far, *incoming, turns, twiddles, sorting)

    from_above = passed_along(bottom, "row", 1)
    from_below = passed_along(top, "row", -1)
    begun, chunks = probe_update(me, probe, numer, LOAD)
    sums, to_left, to_right = call(
        functools.partial(rows_sum_kernel, dims), (shape(wide), coded_col, coded_col), (VMEM,) * 3, [LOAD, VMEM, VMEM, HBM], [], 1 << 26,
    )(share, from_above, from_below, begun)
    from_left = passed_along(to_right, "col", 1)
    from_right = passed_along(to_left, "col", -1)

    current, top, bottom, numer, probe_now = call(
        functools.partial(whole_kernel, dims), (shape(tile), shape((2, tile_rows, 2 * tile_cols)), coded_row, shares, shape(window)), (HBM,) + (VMEM,) * 4,
        [SMEM, SMEM, LOAD] + [VMEM] * 3 + [LOAD, VMEM, HBM, LOAD, LOAD],
        [pltpu.VMEM(wide, f32), pltpu.VMEM(wide, f32)] + work_scratch(order)
        + [pltpu.VMEM((3, order, order), f32), pltpu.VMEM((2,) + window, f32), pltpu.VMEM((capacity, order, order), bf16)]
        + list_scratch(capacity) + [pltpu.SemaphoreType.DMA((capacity,)), pltpu.SemaphoreType.DMA],
        capacity * one_pattern,
    )(pos, me, ext, sums, from_left, from_right, weights_old, chunks, sorted_amps, turns, twiddles)

    from_above = passed_along(bottom, "row", 1)
    _, chunks = probe_update(me, probe_now, numer, VMEM)
    own, to_right = call(
        functools.partial(fold_kernel, dims), (shape(tile), coded_tile), (VMEM, VMEM), [LOAD, VMEM], [], 1 << 26,
    )(top, from_above)
    from_left = passed_along(to_right, "col", 1)
    weights_new = weights(probe_now, 1, VMEM)
    new_object = call(functools.partial(object_kernel, dims), shape(tile), VMEM, [LOAD, VMEM, VMEM, LOAD, VMEM], [], 1 << 26)(
        current, own, from_left, weights_old, weights_new
    )
    new_probe = call(probe_kernel, shape(window), VMEM, [VMEM], [], 1 << 26)(chunks)
    return new_object, new_probe


def solution(mesh):
    placed = (P(None, "row", "col"), P(), P(("row", "col"), None, None), P())
    return jax.shard_map(local, mesh=mesh, in_specs=placed, out_specs=(P(None, "row", "col"), P()), check_vma=False)
```

```python
import functools

import jax
import jax.numpy as jnp
import numpy as np
from jax import lax
from jax.experimental import pallas as pl
from jax.experimental.pallas import tpu as pltpu
from jax.sharding import PartitionSpec as P

ITERS = 2
SEND = 2

amplitude_floor = 0.1
object_regular = 0.5
probe_regular = 1.0

LANES = 128
SUBLANES = 8
LEVELS = 32767.0
CHUNK = 32
VMEM = pl.BlockSpec(memory_space=pltpu.VMEM)
SMEM = pl.BlockSpec(memory_space=pltpu.SMEM)
HBM = pl.BlockSpec(memory_space=pltpu.HBM)
LOAD = object()
FREE = pl.BlockSpec(memory_space=pl.ANY)
f32 = jnp.float32
bf16 = jnp.bfloat16


def tables(order):
    half = order // 2
    counter = np.arange(half)
    angles = 2.0 * np.pi * ((counter[:, None] * counter[None, :]) % half) / half
    cos, sin = np.cos(angles), np.sin(angles)
    scale = 1.0 / np.sqrt(order)
    turns = []
    for block in ([[cos, -sin], [sin, cos]], [[cos, sin], [-sin, cos]]):
        matrix = np.block(block) * scale
        high = matrix.astype(jnp.bfloat16)
        turns.append(np.stack([high, (matrix - high.astype(np.float64)).astype(jnp.bfloat16)]))
    turn = 2.0 * np.pi * counter / order
    twiddle = np.stack([np.cos(turn), -np.sin(turn)]).astype(np.float32)
    twiddles = np.concatenate(
        [np.broadcast_to(twiddle[:, :, None], (2, half, half)), np.broadcast_to(twiddle[:, None, :], (2, SUBLANES, half))], axis=1
    )
    sorting = np.zeros((order, order), np.float32)
    sorting[np.arange(half), 2 * np.arange(half)] = 1.0
    sorting[half + np.arange(half), 2 * np.arange(half) + 1] = 1.0
    return (
        jnp.asarray(np.stack(turns)),
        jnp.asarray(np.ascontiguousarray(twiddles)),
        jnp.asarray(np.stack([sorting, sorting.T]).astype(jnp.bfloat16)),
    )


def list_patterns(dims, pos_ref, me_ref, ys_ref, xs_ref, slots_ref):
    tile_rows, tile_cols, pat_count, col_count, capacity = dims
    my_row, my_col = me_ref[0], me_ref[1]
    band_count = pat_count * col_count
    first = my_row * band_count
    total = pos_ref.shape[0] // 2

    def visit(index, carry):
        found, source, rank = carry
        y = pos_ref[first + index]
        x = pos_ref[total + first + index]
        here = lax.div(x, tile_cols) == my_col
        holder = lax.div(index, pat_count)
        rank = jnp.where(holder == source, rank, 0)

        @pl.when(here & (found < capacity))
        def _():
            ys_ref[found] = y - my_row * tile_rows
            xs_ref[found] = x - my_col * tile_cols
            slots_ref[found] = holder * SEND + jnp.minimum(rank, SEND - 1)

        step = here.astype(jnp.int32)
        return found + step, holder, rank + step

    found, _, _ = lax.fori_loop(0, band_count, visit, (jnp.int32(0), jnp.int32(-1), jnp.int32(0)))
    return jnp.minimum(found, capacity)


def lane_index(rows):
    return lax.broadcasted_iota(jnp.int32, (rows, LANES), 1)


def shifted_left(tiles, shift):
    lane = lane_index(tiles[0].shape[0])
    turn = lax.rem(LANES - shift, LANES)
    rolled = [pltpu.roll(tile, turn, axis=1) for tile in tiles]
    inside = lane < LANES - shift
    return [jnp.where(inside, a, b) for a, b in zip(rolled[:-1], rolled[1:])]


def shifted_right(tiles, shift):
    lane = lane_index(tiles[0].shape[0])
    rolled = [pltpu.roll(tile, shift, axis=1) for tile in tiles]
    outside = lane < shift
    zero = jnp.zeros_like(rolled[0])
    firsts = [zero] + rolled
    seconds = rolled + [zero]
    return [jnp.where(outside, a, b) for a, b in zip(firsts, seconds)]


def row_groups(tile):
    return [tile[k : k + SUBLANES] for k in range(0, tile.shape[0], SUBLANES)]


def shifted_up(tile, shift):
    row = lax.broadcasted_iota(jnp.int32, (SUBLANES, LANES), 0)
    turn = lax.rem(SUBLANES - shift, SUBLANES)
    rolled = [pltpu.roll(group, turn, axis=0) for group in row_groups(tile)]
    inside = row < SUBLANES - shift
    return jnp.concatenate([jnp.where(inside, a, b) for a, b in zip(rolled[:-1], rolled[1:])], axis=0)


def shifted_down(before, tile, shift):
    row = lax.broadcasted_iota(jnp.int32, (SUBLANES, LANES), 0)
    rolled = [before] + [pltpu.roll(group, shift, axis=0) for group in row_groups(tile)]
    outside = row < shift
    return rolled[-1], jnp.concatenate([jnp.where(outside, a, b) for a, b in zip(rolled[:-1], rolled[1:])], axis=0)


class Deposit:
    def __init__(self, add, top, left):
        self.add = add
        self.row = pl.multiple_of(lax.div(top, SUBLANES) * SUBLANES, SUBLANES)
        self.col = pl.multiple_of(lax.div(left, LANES) * LANES, LANES)
        self.down = lax.rem(top, SUBLANES)
        self.right = lax.rem(left, LANES)
        self.carried = None

    def place(self, first, tiles):
        moved = jnp.concatenate(shifted_right(tiles, self.right), axis=1)
        self.add(pl.ds(self.row + first, tiles[0].shape[0]), pl.ds(self.col, moved.shape[1]), moved)

    def put(self, first, tiles):
        if self.carried is None:
            self.carried = [jnp.zeros((SUBLANES, LANES), f32) for _ in tiles]
        pairs = [shifted_down(before, tile, self.down) for before, tile in zip(self.carried, tiles)]
        self.carried = [carried for carried, _ in pairs]
        self.place(first, [tile for _, tile in pairs])

    def finish(self, first):
        row = lax.broadcasted_iota(jnp.int32, (SUBLANES, LANES), 0)
        self.place(first, [jnp.where(row < self.down, tile, 0.0) for tile in self.carried])


def lane_tiles(value):
    return [value[:, k : k + LANES] for k in range(0, value.shape[1], LANES)]


def store_split(ref, rows, cols, value):
    high = value.astype(bf16)
    ref[0, rows, cols] = high
    ref[1, rows, cols] = (value - high.astype(f32)).astype(bf16)


def right_dot(x_ref, table_ref):
    left = jnp.concatenate([x_ref[0], x_ref[1], x_ref[0]], axis=1)
    right = jnp.concatenate([table_ref[0], table_ref[0], table_ref[1]], axis=0)
    return jnp.dot(left, right, preferred_element_type=f32)


def left_dot(table_ref, x_ref):
    left = jnp.concatenate([table_ref[0], table_ref[0], table_ref[1]], axis=1)
    right = jnp.concatenate([x_ref[0], x_ref[1], x_ref[0]], axis=0)
    return jnp.dot(left, right, preferred_element_type=f32)


def repeated(group, rows):
    return jnp.concatenate([group] * (rows // SUBLANES), axis=0)


def encode(read, out_ref, rows, first, last):
    for col in range(0, out_ref.shape[1], LANES):
        cols = pl.ds(col, LANES)
        largest = jnp.full((SUBLANES, LANES), 1e-30, f32)
        for start in range(0, rows, CHUNK):
            for comp in range(2):
                for group in row_groups(jnp.abs(read(comp, pl.ds(start, CHUNK), cols))):
                    largest = jnp.maximum(largest, group)
        exponent = jnp.ceil(jnp.log2(largest))
        out_ref[last : last + SUBLANES, cols] = exponent.astype(jnp.int32)
        scale = repeated(jnp.exp2(-exponent) * LEVELS, CHUNK)
        for start in range(0, rows, CHUNK):
            codes = []
            for comp in range(2):
                scaled = jnp.clip(read(comp, pl.ds(start, CHUNK), cols) * scale, -LEVELS, LEVELS)
                codes.append(jnp.round(scaled).astype(jnp.int32))
            out_ref[pl.ds(first + start, CHUNK), cols] = (codes[0] << 16) | (codes[1] & 0xFFFF)


def decode(ref, start, last, col):
    cols = pl.ds(col, LANES)
    words = ref[pl.ds(start, CHUNK), cols]
    scale = repeated(jnp.exp2(ref[last : last + SUBLANES, cols].astype(f32)) * (1.0 / LEVELS), CHUNK)
    return (words >> 16).astype(f32) * scale, ((words << 16) >> 16).astype(f32) * scale


def largest_exponent(values):
    largest = jnp.full((SUBLANES, LANES), 1e-30, f32)
    for value in values:
        for group in row_groups(jnp.abs(value)):
            largest = jnp.maximum(largest, group)
    return jnp.ceil(jnp.log2(largest))


def fixed(value, exponent):
    scaled = value * repeated(jnp.exp2(-exponent) * LEVELS, value.shape[0])
    return jnp.round(jnp.clip(scaled, -LEVELS, LEVELS)).astype(jnp.int32)


def paired(first, second):
    return (first << 16) | (second & 0xFFFF)


def unpaired(words):
    return words >> 16, (words << 16) >> 16


def scaled_back(codes, exponent):
    return codes.astype(f32) * repeated(jnp.exp2(exponent.astype(f32)) * (1.0 / LEVELS), codes.shape[0])


def sums_rows(rows):
    return rows + rows // 2 + SUBLANES


def encode_sums(out_ref, cols, u_re, u_im, v):
    rows = v.shape[0]
    half = rows // 2
    of_u, of_v = largest_exponent([u_re, u_im]), largest_exponent([v])
    out_ref[0:rows, cols] = paired(fixed(u_re, of_u), fixed(u_im, of_u))
    codes = fixed(v, of_v)
    out_ref[rows : rows + half, cols] = paired(codes[:half], codes[half:])
    out_ref[rows + half : rows + half + SUBLANES, cols] = paired(of_u.astype(jnp.int32), of_v.astype(jnp.int32))


def decode_sums(ref, cols, rows):
    half = rows // 2
    of_u, of_v = unpaired(ref[rows + half : rows + half + SUBLANES, cols])
    u_re, u_im = unpaired(ref[0:rows, cols])
    v = jnp.concatenate(unpaired(ref[rows : rows + half, cols]), axis=0)
    return scaled_back(u_re, of_u), scaled_back(u_im, of_u), scaled_back(v, of_v)


def decode_probe(out_ref, chunks_ref):
    chunks = chunks_ref.shape[0]
    rows = out_ref.shape[1] // chunks
    for chunk in range(chunks):
        for col in range(0, out_ref.shape[2], LANES):
            cols = pl.ds(col, LANES)
            exponent = chunks_ref[chunk, rows : rows + SUBLANES, cols]
            for comp, codes in enumerate(unpaired(chunks_ref[chunk, 0:rows, cols])):
                out_ref[comp, chunk * rows : (chunk + 1) * rows, cols] = scaled_back(codes, exponent)


def cut_chunk(ext_ref, comp, first, top, left, rows):
    row = pl.multiple_of(lax.div(top, SUBLANES) * SUBLANES, SUBLANES)
    col = pl.multiple_of(lax.div(left, LANES) * LANES, LANES)
    block = ext_ref[comp, pl.ds(row + first, rows + SUBLANES), pl.ds(col, 3 * LANES)]
    tiles = shifted_left(lane_tiles(block), lax.rem(left, LANES))
    return [shifted_up(tile, lax.rem(top, SUBLANES)) for tile in tiles]


def forward(order, ext_ref, probe_ref, consts, y, x, win_ref, power_ref, weight, xa_ref, xb_ref, ya_ref, yb_ref, far_ref):
    turns, twiddles = consts
    half = order // 2
    tw_re = repeated(twiddles[0, half : half + SUBLANES, :], CHUNK)
    tw_im = repeated(twiddles[1, half : half + SUBLANES, :], CHUNK)
    for first in range(0, order, CHUNK):
        rows = pl.ds(first, CHUNK)
        win_re = cut_chunk(ext_ref, 0, first, y, x, CHUNK)
        win_im = cut_chunk(ext_ref, 1, first, y, x, CHUNK)
        exits = []
        for k in range(2):
            cols = pl.ds(k * half, half)
            win_ref[0, rows, cols] = win_re[k]
            win_ref[1, rows, cols] = win_im[k]
            power_ref[rows, cols] += weight * (win_re[k] * win_re[k] + win_im[k] * win_im[k])
            p_re, p_im = probe_ref[0, rows, cols], probe_ref[1, rows, cols]
            exits.append((p_re * win_re[k] - p_im * win_im[k], p_re * win_im[k] + p_im * win_re[k]))
        (lo_re, lo_im), (hi_re, hi_im) = exits
        store_split(xa_ref, rows, pl.ds(0, half), lo_re + hi_re)
        store_split(xa_ref, rows, pl.ds(half, half), lo_im + hi_im)
        d_re, d_im = lo_re - hi_re, lo_im - hi_im
        store_split(xb_ref, rows, pl.ds(0, half), d_re * tw_re - d_im * tw_im)
        store_split(xb_ref, rows, pl.ds(half, half), d_re * tw_im + d_im * tw_re)
    yield
    ya_ref[...] = right_dot(xa_ref, turns.at[0])
    yb_ref[...] = right_dot(xb_ref, turns.at[0])
    yield
    for first in range(0, half, CHUNK):
        rows = pl.ds(first, CHUNK)
        below = pl.ds(half + first, CHUNK)
        t_re, t_im = twiddles[0, rows, :], twiddles[1, rows, :]
        for k, y_ref in enumerate((ya_ref, yb_ref)):
            cols = pl.ds(k * half, half)
            up_re, up_im = y_ref[rows, 0:half], y_ref[rows, half:order]
            dn_re, dn_im = y_ref[below, 0:half], y_ref[below, half:order]
            store_split(xa_ref, rows, cols, up_re + dn_re)
            store_split(xa_ref, below, cols, up_im + dn_im)
            d_re, d_im = up_re - dn_re, up_im - dn_im
            store_split(xb_ref, rows, cols, d_re * t_re - d_im * t_im)
            store_split(xb_ref, below, cols, d_re * t_im + d_im * t_re)
    yield
    far_ref[0] = left_dot(turns.at[1], xa_ref)
    far_ref[1] = left_dot(turns.at[1], xb_ref)
    yield


def backward(order, far_ref, amp_ref, consts, y, x, weight, probe_ref, win_ref, xa_ref, xb_ref, ya_ref, yb_ref, grad_ref, numer_ref):
    turns, twiddles = consts
    half = order // 2
    tw_re = repeated(twiddles[0, half : half + SUBLANES, :], CHUNK)
    tw_im = repeated(twiddles[1, half : half + SUBLANES, :], CHUNK)
    for k, x_ref in enumerate((xa_ref, xb_ref)):
        for first in range(0, half, CHUNK):
            rows = pl.ds(first, CHUNK)
            below = pl.ds(half + first, CHUNK)
            far_re, far_im = far_ref[k, rows, :], far_ref[k, below, :]
            amp = amp_ref[pl.ds(k * half + first, CHUNK), :].astype(f32)
            factor = amp * lax.rsqrt(far_re * far_re + far_im * far_im + amplitude_floor)
            store_split(x_ref, rows, slice(None), far_re * factor)
            store_split(x_ref, below, slice(None), far_im * factor)
    yield
    ya_ref[...] = left_dot(turns.at[0], xa_ref)
    yb_ref[...] = left_dot(turns.at[0], xb_ref)
    yield
    for first in range(0, half, CHUNK):
        rows = pl.ds(first, CHUNK)
        below = pl.ds(half + first, CHUNK)
        t_re, t_im = twiddles[0, rows, :], twiddles[1, rows, :]
        for k, x_ref in enumerate((xa_ref, xb_ref)):
            cols = slice(k * half, (k + 1) * half)
            a_re, a_im = ya_ref[rows, cols], ya_ref[below, cols]
            b_re, b_im = yb_ref[rows, cols], yb_ref[below, cols]
            c_re, c_im = b_re * t_re + b_im * t_im, b_im * t_re - b_re * t_im
            store_split(x_ref, rows, pl.ds(0, half), a_re + c_re)
            store_split(x_ref, rows, pl.ds(half, half), a_im + c_im)
            store_split(x_ref, below, pl.ds(0, half), a_re - c_re)
            store_split(x_ref, below, pl.ds(half, half), a_im - c_im)
    yield
    ya_ref[...] = right_dot(xa_ref, turns.at[1])
    yb_ref[...] = right_dot(xb_ref, turns.at[1])
    yield

    def adder(comp):
        def add(rows, cols, moved):
            grad_ref[comp, rows, cols] += moved

        return add

    deposits = [Deposit(adder(comp), y, x) for comp in range(2)]
    for first in range(0, order, CHUNK):
        rows = pl.ds(first, CHUNK)
        a_re, a_im = ya_ref[rows, 0:half], ya_ref[rows, half:order]
        b_re, b_im = yb_ref[rows, 0:half], yb_ref[rows, half:order]
        c_re, c_im = b_re * tw_re + b_im * tw_im, b_im * tw_re - b_re * tw_im
        waves = [(a_re + c_re, a_im + c_im), (a_re - c_re, a_im - c_im)]
        terms = ([], [])
        for k, (wave_re, wave_im) in enumerate(waves):
            cols = pl.ds(k * half, half)
            wave_re, wave_im = weight * wave_re, weight * wave_im
            p_re, p_im = probe_ref[0, rows, cols], probe_ref[1, rows, cols]
            w_re, w_im = win_ref[0, rows, cols], win_ref[1, rows, cols]
            terms[0].append(p_re * wave_re + p_im * wave_im)
            terms[1].append(p_re * wave_im - p_im * wave_re)
            numer_ref[0, rows, cols] += w_re * wave_re + w_im * wave_im
            numer_ref[1, rows, cols] += w_re * wave_im - w_im * wave_re
        for comp in range(2):
            deposits[comp].put(first, terms[comp])
    for deposit in deposits:
        deposit.finish(order)
    yield


def interleaved(*stages):
    live = list(stages)
    while live:
        still = []
        for stage in live:
            try:
                next(stage)
                still.append(stage)
            except StopIteration:
                pass
        live = still


def outgoing_kernel(dims, pos_ref, me_ref, amp_ref, after_ref, also_ref, out_ref, sems):
    tile_rows, tile_cols, pat_count, col_count, capacity = dims
    first = (me_ref[0] * col_count + me_ref[1]) * pat_count
    total = pos_ref.shape[0] // 2
    owners = [lax.div(pos_ref[total + first + k], tile_cols) for k in range(pat_count)]
    copies = []
    for k in range(pat_count):
        rank = sum(((owners[e] == owners[k]).astype(jnp.int32) for e in range(k)), jnp.int32(0))
        slot = owners[k] * SEND + jnp.minimum(rank, SEND - 1)
        copies.append(pltpu.make_async_copy(amp_ref.at[k], out_ref.at[slot], sems.at[k]))
        copies[-1].start()
    for copy in copies:
        copy.wait()


def weights_kernel(dims, span, pos_ref, me_ref, probe_ref, out_ref, sums_ref, power_ref):
    tile_rows, tile_cols, pat_count, col_count, capacity = dims
    order = probe_ref.shape[1]
    top = (me_ref[0] - 1) * tile_rows
    left = (me_ref[1] - 1) * tile_cols
    total = pos_ref.shape[0] // 2
    for first in range(0, sums_ref.shape[0], order):
        sums_ref[pl.ds(first, order), :] = jnp.zeros((order, sums_ref.shape[1]), f32)
    power_ref[...] = probe_ref[0] * probe_ref[0] + probe_ref[1] * probe_ref[1]

    def visit(index, carry):
        y = pos_ref[index] - top
        x = pos_ref[total + index] - left

        @pl.when((y > 0) & (y < (span + 1) * tile_rows) & (x > 0) & (x < (span + 1) * tile_cols))
        def _():
            def add(rows, cols, moved):
                sums_ref[rows, cols] += moved

            deposit = Deposit(add, y, x)
            for first in range(0, order, CHUNK):
                deposit.put(first, lane_tiles(power_ref[pl.ds(first, CHUNK), :]))
            deposit.finish(order)

        return carry

    lax.fori_loop(0, total, visit, 0)
    pltpu.sync_copy(sums_ref.at[pl.ds(tile_rows, span * tile_rows), pl.ds(tile_cols, span * tile_cols)], out_ref)


def encode_kernel(obj_ref, out_ref):
    rows = obj_ref.shape[1]
    encode(lambda comp, at, cols: obj_ref[comp, at, cols], out_ref, rows, 0, rows)


def unfold(dims, ext_ref, own_ref, coded_refs):
    tile_rows, tile_cols = dims[:2]
    ext_ref[:, 0:tile_rows, 0:tile_cols] = own_ref[...]
    for (i, j), ref in zip(((0, 1), (1, 0), (1, 1)), coded_refs):
        for col in range(0, tile_cols, LANES):
            for start in range(0, tile_rows, CHUNK):
                parts = decode(ref, start, tile_rows, col)
                for comp in range(2):
                    ext_ref[comp, pl.ds(i * tile_rows + start, CHUNK), pl.ds(j * tile_cols + col, LANES)] = parts[comp]


def spread_sums(out_ref, u_ref, v_ref):
    chunks = out_ref.shape[0]
    rows = v_ref.shape[0] // chunks
    for chunk in range(chunks):
        at = pl.ds(chunk * rows, rows)
        for col in range(0, v_ref.shape[1], LANES):
            cols = pl.ds(col, LANES)
            encode_sums(out_ref.at[chunk], cols, u_ref[0, at, cols], u_ref[1, at, cols], v_ref[at, cols])


def added(parts):
    while len(parts) > 1:
        parts = [tuple(x + y for x, y in zip(a, b)) for a, b in zip(parts[::2], parts[1::2])]
    return parts[0]


def sums_kernel(rows, parts_ref, *refs):
    out_ref = refs[-1]
    for col in range(0, out_ref.shape[1], LANES):
        cols = pl.ds(col, LANES)
        total = added([decode_sums(parts_ref.at[k], cols, rows) for k in range(parts_ref.shape[0])])
        encode_sums(out_ref, cols, *total)


def update_kernel(rows, me_ref, probe_ref, *refs):
    *parts, out_ref = refs
    first = pl.multiple_of(me_ref[1] * rows, SUBLANES)
    for col in range(0, out_ref.shape[2], LANES):
        cols = pl.ds(col, LANES)
        u_re, u_im, v = added([decode_sums(ref, cols, rows) for ref in parts])
        scale = 1.0 / (v + probe_regular)
        re = (probe_ref[0, pl.ds(first, rows), cols] + u_re) * scale
        im = (probe_ref[1, pl.ds(first, rows), cols] + u_im) * scale
        exponent = largest_exponent([re, im])
        words = paired(fixed(re, exponent), fixed(im, exponent))
        for chunk in range(out_ref.shape[0]):
            out_ref[chunk, 0:rows, cols] = words
            out_ref[chunk, rows : rows + SUBLANES, cols] = exponent.astype(jnp.int32)


def probe_kernel(chunks_ref, out_ref):
    decode_probe(out_ref, chunks_ref)


def first_half_kernel(dims, pos_ref, me_ref, own_ref, right_ref, below_ref, diag_ref, probe_ref, turns, twiddles,
                      far_out, power_out, ext_out, ext_ref, win_ref, xa_ref, xb_ref, ya_ref, yb_ref, far_ref, ys_ref, xs_ref, slots_ref, sems, ext_sem):
    tile_rows, tile_cols, pat_count, col_count, capacity = dims
    order = probe_ref.shape[1]
    count = list_patterns(dims, pos_ref, me_ref, ys_ref, xs_ref, slots_ref)
    unfold(dims, ext_ref, own_ref, (right_ref, below_ref, diag_ref))
    keep = pltpu.make_async_copy(ext_ref, ext_out, ext_sem)
    keep.start()
    power_out[...] = jnp.zeros_like(power_out)
    consts = (turns, twiddles)

    def pair(step, carry):
        stages = []
        for k in range(2):
            listed = 2 * step + k
            weight = (listed < count).astype(f32)
            index = jnp.minimum(listed, count - 1)
            stages.append(forward(order, ext_ref, probe_ref, consts, ys_ref[index], xs_ref[index], win_ref.at[k], power_out, weight,
                                  xa_ref.at[k], xb_ref.at[k], ya_ref.at[k], yb_ref.at[k], far_ref.at[listed]))
        interleaved(*stages)
        for k in range(2):
            listed = 2 * step + k
            pltpu.make_async_copy(far_ref.at[listed], far_out.at[listed], sems.at[listed]).start()
        return carry

    pairs = lax.div(count + 1, 2)
    lax.fori_loop(0, pairs, pair, 0)

    def settle(listed, carry):
        pltpu.make_async_copy(far_ref.at[listed], far_out.at[listed], sems.at[listed]).wait()
        return carry

    lax.fori_loop(0, 2 * pairs, settle, 0)
    keep.wait()


def second_half_kernel(dims, pos_ref, me_ref, ext_ref, probe_ref, power_ref, weights_ref, far_in, amp_in, turns, twiddles, sorting,
                       share_out, top_out, bottom_out, numer_out, amp_out,
                       sum_ref, win_ref, xa_ref, xb_ref, ya_ref, yb_ref, numer_ref, far_ref, amp_ref, sorted_ref, ys_ref, xs_ref, slots_ref, far_sems, amp_sems, out_sems, sum_sem):
    tile_rows, tile_cols, pat_count, col_count, capacity = dims
    order = probe_ref.shape[1]
    half = order // 2
    count = list_patterns(dims, pos_ref, me_ref, ys_ref, xs_ref, slots_ref)
    pairs = lax.div(count + 1, 2)

    def copies(listed):
        return (
            pltpu.make_async_copy(far_in.at[listed], far_ref.at[listed], far_sems.at[listed]),
            pltpu.make_async_copy(amp_in.at[slots_ref[jnp.minimum(listed, count - 1)]], amp_ref.at[listed], amp_sems.at[listed]),
        )

    def begin(listed, carry):
        for copy in copies(listed):
            copy.start()
        return carry

    lax.fori_loop(0, 2 * pairs, begin, 0)
    sum_ref[...] = jnp.zeros_like(sum_ref)
    numer_ref[...] = jnp.zeros_like(numer_ref)
    consts = (turns, twiddles)

    def pair(step, carry):
        stages = []
        for k in range(2):
            listed = 2 * step + k
            for copy in copies(listed):
                copy.wait()
        for k in range(2):
            listed = 2 * step + k
            weight = (listed < count).astype(f32)
            index = jnp.minimum(listed, count - 1)
            y, x = ys_ref[index], xs_ref[index]
            rows_sorted = jnp.dot(sorting[0], amp_ref[listed], preferred_element_type=f32).astype(bf16)
            sorted_ref[listed] = jnp.dot(rows_sorted, sorting[1], preferred_element_type=f32).astype(bf16)
            for first in range(0, order, CHUNK):
                for comp in range(2):
                    for c, tile in enumerate(cut_chunk(ext_ref, comp, first, y, x, CHUNK)):
                        win_ref[k, comp, pl.ds(first, CHUNK), pl.ds(c * half, half)] = tile
            stages.append(backward(order, far_ref.at[listed], sorted_ref.at[listed], consts, y, x, weight, probe_ref, win_ref.at[k],
                                   xa_ref.at[k], xb_ref.at[k], ya_ref.at[k], yb_ref.at[k], sum_ref, numer_ref))
        interleaved(*stages)
        for k in range(2):
            listed = 2 * step + k
            pltpu.make_async_copy(sorted_ref.at[listed], amp_out.at[listed], out_sems.at[listed]).start()
        return carry

    lax.fori_loop(0, pairs, pair, 0)
    for first in range(0, 2 * tile_rows, CHUNK):
        rows = pl.ds(first, CHUNK)
        scale = 1.0 / (weights_ref[rows, :] + object_regular)
        for comp in range(2):
            sum_ref[comp, rows, :] = sum_ref[comp, rows, :] * scale
    keep = pltpu.make_async_copy(sum_ref, share_out, sum_sem)
    keep.start()
    encode(lambda comp, at, cols: sum_ref[comp, at, cols], top_out, tile_rows, 0, tile_rows)
    encode(lambda comp, at, cols: sum_ref[comp, pl.ds(tile_rows + at.start, at.size), cols], bottom_out, tile_rows, 0, tile_rows)
    spread_sums(numer_out, numer_ref, power_ref)

    def settle(listed, carry):
        pltpu.make_async_copy(sorted_ref.at[listed], amp_out.at[listed], out_sems.at[listed]).wait()
        return carry

    lax.fori_loop(0, 2 * pairs, settle, 0)
    keep.wait()


def rows_sum_kernel(dims, share_ref, above_ref, below_ref, after_ref, sum_out, left_out, right_out):
    tile_rows, tile_cols = dims[:2]
    for i, ref in enumerate((above_ref, below_ref)):
        for col in range(0, 2 * tile_cols, LANES):
            for start in range(0, tile_rows, CHUNK):
                rows, cols = pl.ds(i * tile_rows + start, CHUNK), pl.ds(col, LANES)
                parts = decode(ref, start, tile_rows, col)
                for comp in range(2):
                    sum_out[comp, rows, cols] = share_ref[comp, rows, cols] + parts[comp]
    for j, ref in enumerate((left_out, right_out)):
        for i in range(2):

            def read(comp, at, cols, i=i, j=j):
                return sum_out[comp, pl.ds(i * tile_rows + at.start, at.size), pl.ds(j * tile_cols + cols.start, cols.size)]

            encode(read, ref, tile_rows, i * tile_rows, 2 * tile_rows + i * SUBLANES)


def whole_kernel(dims, pos_ref, me_ref, old_ref, sum_ref, from_left_ref, from_right_ref, weights_ref,
                 chunks_ref, amp_in, turns, twiddles,
                 current_out, own_out, right_out, below_out, diag_out, numer_out, probe_ref,
                 ext_ref, grad_ref, win_ref, xa_ref, xb_ref, ya_ref, yb_ref, numer_ref, far_ref, amp_ref, ys_ref, xs_ref, slots_ref, amp_sems, own_sem):
    tile_rows, tile_cols, pat_count, col_count, capacity = dims
    order = probe_ref.shape[1]
    count = list_patterns(dims, pos_ref, me_ref, ys_ref, xs_ref, slots_ref)
    pairs = lax.div(count + 1, 2)
    decode_probe(probe_ref, chunks_ref)

    def fetch(listed):
        return pltpu.make_async_copy(amp_in.at[jnp.minimum(listed, count - 1)], amp_ref.at[listed], amp_sems.at[listed])

    def begin(listed, carry):
        fetch(listed).start()
        return carry

    lax.fori_loop(0, 2 * pairs, begin, 0)
    for j, ref in enumerate((from_left_ref, from_right_ref)):
        for i in range(2):
            for col in range(0, tile_cols, LANES):
                for start in range(0, tile_rows, CHUNK):
                    rows, cols = pl.ds(i * tile_rows + start, CHUNK), pl.ds(j * tile_cols + col, LANES)
                    parts = decode(ref, i * tile_rows + start, 2 * tile_rows + i * SUBLANES, col)
                    scale = object_regular / (weights_ref[rows, cols] + object_regular)
                    for comp in range(2):
                        ext_ref[comp, rows, cols] = old_ref[comp, rows, cols] * scale + (sum_ref[comp, rows, cols] + parts[comp])
    keep = pltpu.make_async_copy(ext_ref.at[:, pl.ds(0, tile_rows), pl.ds(0, tile_cols)], current_out, own_sem)
    keep.start()
    grad_ref[...] = jnp.zeros_like(grad_ref)
    numer_ref[...] = jnp.zeros_like(numer_ref)
    consts = (turns, twiddles)

    def pair(step, carry):
        stages = []
        for k in range(2):
            fetch(2 * step + k).wait()
        for k in range(2):
            listed = 2 * step + k
            weight = (listed < count).astype(f32)
            index = jnp.minimum(listed, count - 1)
            y, x = ys_ref[index], xs_ref[index]

            def both(k=k, listed=listed, weight=weight, y=y, x=x):
                yield from forward(order, ext_ref, probe_ref, consts, y, x, win_ref.at[k], numer_ref.at[2], weight,
                                   xa_ref.at[k], xb_ref.at[k], ya_ref.at[k], yb_ref.at[k], far_ref.at[k])
                yield from backward(order, far_ref.at[k], amp_ref.at[listed], consts, y, x, weight, probe_ref, win_ref.at[k],
                                    xa_ref.at[k], xb_ref.at[k], ya_ref.at[k], yb_ref.at[k], grad_ref, numer_ref)

            stages.append(both())
        interleaved(*stages)
        return carry

    lax.fori_loop(0, pairs, pair, 0)
    own_out[...] = grad_ref[:, 0:tile_rows, 0:tile_cols]
    for (i, j), ref in zip(((0, 1), (1, 0), (1, 1)), (right_out, below_out, diag_out)):

        def read(comp, at, cols, i=i, j=j):
            rows, cols = pl.ds(i * tile_rows + at.start, at.size), pl.ds(j * tile_cols + cols.start, cols.size)
            return grad_ref[comp, rows, cols] / (weights_ref[rows, cols] + object_regular)

        encode(read, ref, tile_rows, 0, tile_rows)
    spread_sums(numer_out, numer_ref, numer_ref.at[2])
    keep.wait()


def object_kernel(dims, current_ref, own_ref, left_ref, above_ref, diag_ref, before_ref, weights_ref, out_ref):
    tile_rows, tile_cols = dims[:2]
    for col in range(0, tile_cols, LANES):
        for start in range(0, tile_rows, CHUNK):
            rows, cols = pl.ds(start, CHUNK), pl.ds(col, LANES)
            scale = 1.0 / (weights_ref[rows, cols] + object_regular)
            back = (before_ref[rows, cols] + object_regular) * scale
            parts = [decode(ref, start, tile_rows, col) for ref in (left_ref, above_ref, diag_ref)]
            for comp in range(2):
                coded = parts[0][comp] + parts[1][comp] + parts[2][comp]
                old = object_regular * current_ref[comp, rows, cols] + own_ref[comp, rows, cols]
                out_ref[comp, rows, cols] = old * scale + coded * back


def shape(dims, dtype=f32):
    return jax.ShapeDtypeStruct(dims, dtype)


def work_scratch(order):
    return [
        pltpu.VMEM((2, 2, order, order), f32),
        pltpu.VMEM((2, 2, order, order), bf16),
        pltpu.VMEM((2, 2, order, order), bf16),
        pltpu.VMEM((2, order, order), f32),
        pltpu.VMEM((2, order, order), f32),
    ]


def list_scratch(capacity):
    return [pltpu.SMEM((capacity,), jnp.int32)] * 3


def call(kernel, outs, out_specs, in_specs, scratch, flops, limit=26 << 20):
    several = isinstance(outs, tuple)
    out_count = len(outs) if several else 1
    in_count = len(in_specs)
    loaded = [k for k, spec in enumerate(in_specs) if spec is LOAD]

    def body(*refs):
        ins, rest = list(refs[:in_count]), refs[in_count:]
        given, kept = rest[: out_count + len(scratch)], rest[out_count + len(scratch) :]
        copies = [pltpu.make_async_copy(ins[k], kept[n], kept[-1].at[n]) for n, k in enumerate(loaded)]
        for copy in copies:
            copy.start()
        for n, k in enumerate(loaded):
            copies[n].wait()
            ins[k] = kept[n]
        kernel(*ins, *given)

    fixed_outs = [
        pltpu.HBM(out.shape, out.dtype) if spec is HBM else out
        for out, spec in zip(outs if several else (outs,), out_specs if several else (out_specs,))
    ]
    stay = [spec is LOAD or spec is HBM for spec in in_specs]

    def called(*args):
        args = [pltpu.with_memory_space_constraint(arg, pltpu.HBM) if kept else arg for arg, kept in zip(args, stay)]
        own = [pltpu.VMEM(args[k].shape, args[k].dtype) for k in loaded]
        if loaded:
            own.append(pltpu.SemaphoreType.DMA((len(loaded),)))
        return pl.pallas_call(
            body,
            out_shape=tuple(fixed_outs) if several else fixed_outs[0],
            out_specs=out_specs,
            in_specs=[HBM if spec is LOAD else spec for spec in in_specs],
            scratch_shapes=list(scratch) + own,
            compiler_params=pltpu.CompilerParams(vmem_limit_bytes=limit),
            cost_estimate=pl.CostEstimate(flops=flops, bytes_accessed=8 << 20, transcendentals=0),
        )(*args)

    return called


def passed_along(value, axis, steps):
    count = lax.axis_size(axis)
    leading, last = (max(0, -steps), min(count, count - steps))
    return lax.ppermute(value, axis, [(source, source + steps) for source in range(leading, last)])


def passed_both(value, row_steps, col_steps):
    rows, cols = lax.axis_size("row"), lax.axis_size("col")
    pairs = []
    for r in range(rows):
        for c in range(cols):
            if 0 <= r + row_steps < rows and 0 <= c + col_steps < cols:
                pairs.append((r * cols + c, (r + row_steps) * cols + c + col_steps))
    return lax.ppermute(value, ("row", "col"), pairs)


def swapped(value, axis, mask):
    return lax.ppermute(value, axis, [(k, k ^ mask) for k in range(lax.axis_size(axis))])


def probe_update(me, probe, numer, kind, *after):
    cols, order = lax.axis_size("col"), probe.shape[1]
    rows = order // cols
    parts = lax.all_to_all(numer, "col", split_axis=0, concat_axis=0, tiled=True)
    total = call(functools.partial(sums_kernel, rows), shape((sums_rows(rows), order), jnp.int32), VMEM, [VMEM] + [FREE] * len(after), [], 1 << 26)(parts, *after)
    totals = [total] + [swapped(total, "row", mask) for mask in range(1, lax.axis_size("row"))]
    fresh = call(
        functools.partial(update_kernel, rows), shape((cols, rows + SUBLANES, order), jnp.int32), VMEM,
        [SMEM, kind] + [VMEM] * len(totals), [], 1 << 26,
    )(me, probe, *totals)
    return total, lax.all_to_all(fresh, "col", split_axis=0, concat_axis=0, tiled=True)


def local(obj, probe, amplitudes, positions):
    col_count = lax.axis_size("col")
    tile_rows, tile_cols = obj.shape[1], obj.shape[2]
    order = probe.shape[1]
    pat_count = amplitudes.shape[0]
    capacity = 2 * pat_count
    dims = (tile_rows, tile_cols, pat_count, col_count, capacity)
    me = jnp.stack([lax.axis_index("row"), lax.axis_index("col")]).astype(jnp.int32)
    pos = positions.T.reshape(-1)
    turns, twiddles, sorting = tables(order)
    tile = (2, tile_rows, tile_cols)
    window = (2, order, order)
    wide = (2, 2 * tile_rows, 2 * tile_cols)
    shares = shape((col_count, sums_rows(order // col_count), order), jnp.int32)
    coded_tile = shape((tile_rows + SUBLANES, tile_cols), jnp.int32)
    coded_row = shape((tile_rows + SUBLANES, 2 * tile_cols), jnp.int32)
    coded_col = shape((2 * (tile_rows + SUBLANES), tile_cols), jnp.int32)
    one_pattern = 24 * 2 * order**3

    coded = call(encode_kernel, coded_tile, VMEM, [LOAD], [], 1 << 26)(obj)
    right = passed_along(coded, "col", -1)
    below = passed_along(coded, "row", -1)
    diag = passed_along(right, "row", -1)

    outgoing = call(
        functools.partial(outgoing_kernel, dims), shape((col_count * SEND, order, order), bf16), HBM, [SMEM, SMEM, HBM, FREE, FREE],
        [pltpu.SemaphoreType.DMA((pat_count,))], 1 << 20,
    )(pos, me, amplitudes, right, below)
    incoming = lax.all_to_all(outgoing, "col", split_axis=0, concat_axis=0, tiled=True)

    def weights(probe_now, span, kind):
        return call(
            functools.partial(weights_kernel, dims, span), shape((span * tile_rows, span * tile_cols)), HBM, [SMEM, SMEM, kind],
            [pltpu.VMEM(((span + 2) * tile_rows, (span + 2) * tile_cols), f32), pltpu.VMEM((order, order), f32)], 8 << 30,
        )(pos, me, probe_now)

    weights_old = weights(probe, 2, LOAD)

    far, power, ext = call(
        functools.partial(first_half_kernel, dims), (shape((capacity,) + window), shape((order, order)), shape(wide)), (HBM, VMEM, HBM),
        [SMEM, SMEM, LOAD] + [VMEM] * 3 + [LOAD] * 3,
        [pltpu.VMEM(wide, f32)] + work_scratch(order) + [pltpu.VMEM((capacity,) + window, f32)] + list_scratch(capacity)
        + [pltpu.SemaphoreType.DMA((capacity,)), pltpu.SemaphoreType.DMA],
        capacity * one_pattern // 2,
    )(pos, me, obj, right, below, diag, probe, turns, twiddles)

    share, top, bottom, numer, sorted_amps = call(
        functools.partial(second_half_kernel, dims),
        (shape(wide), coded_row, coded_row, shares, shape((capacity, order, order), bf16)),
        (HBM, VMEM, VMEM, VMEM, HBM),
        [SMEM, SMEM, LOAD, LOAD, VMEM, LOAD, HBM, HBM] + [LOAD] * 3,
        [pltpu.VMEM(wide, f32)] + work_scratch(order)
        + [pltpu.VMEM(window, f32), pltpu.VMEM((capacity,) + window, f32), pltpu.VMEM((capacity, order, order), bf16), pltpu.VMEM((capacity, order, order), bf16)]
        + list_scratch(capacity) + [pltpu.SemaphoreType.DMA((capacity,))] * 3 + [pltpu.SemaphoreType.DMA],
        capacity * one_pattern // 2,
    )(pos, me, ext, probe, power, weights_old, far, incoming, turns, twiddles, sorting)

    from_above = passed_along(bottom, "row", 1)
    from_below = passed_along(top, "row", -1)
    total, chunks = probe_update(me, probe, numer, LOAD)
    sums, to_left, to_right = call(
        functools.partial(rows_sum_kernel, dims), (shape(wide), coded_col, coded_col), (VMEM,) * 3, [LOAD, VMEM, VMEM, FREE], [], 1 << 26,
    )(share, from_above, from_below, total)
    from_left = passed_along(to_right, "col", 1)
    from_right = passed_along(to_left, "col", -1)

    current, own, to_right, to_below, to_diag, numer, probe_now = call(
        functools.partial(whole_kernel, dims), (shape(tile), shape(tile), coded_tile, coded_tile, coded_tile, shares, shape(window)), (HBM,) + (VMEM,) * 6,
        [SMEM, SMEM, LOAD] + [VMEM] * 3 + [LOAD, VMEM, HBM, LOAD, LOAD],
        [pltpu.VMEM(wide, f32), pltpu.VMEM(wide, f32)] + work_scratch(order)
        + [pltpu.VMEM((3, order, order), f32), pltpu.VMEM((2,) + window, f32), pltpu.VMEM((capacity, order, order), bf16)]
        + list_scratch(capacity) + [pltpu.SemaphoreType.DMA((capacity,)), pltpu.SemaphoreType.DMA],
        capacity * one_pattern,
    )(pos, me, ext, sums, from_left, from_right, weights_old, chunks, sorted_amps, turns, twiddles)

    from_left = passed_along(to_right, "col", 1)
    from_above = passed_along(to_below, "row", 1)
    from_diag = passed_both(to_diag, 1, 1)
    weights_new = weights(probe_now, 1, VMEM)
    new_object = call(functools.partial(object_kernel, dims), shape(tile), VMEM, [LOAD] + [VMEM] * 4 + [LOAD, LOAD], [], 1 << 26)(
        current, own, from_left, from_above, from_diag, weights_old, weights_new
    )
    _, chunks = probe_update(me, probe_now, numer, VMEM, weights_new)
    new_probe = call(probe_kernel, shape(window), VMEM, [VMEM], [], 1 << 26)(chunks)
    return new_object, new_probe


def solution(mesh):
    placed = (P(None, "row", "col"), P(), P(("row", "col"), None, None), P())
    return jax.shard_map(local, mesh=mesh, in_specs=placed, out_specs=(P(None, "row", "col"), P()), check_vma=False)
```

```python
import functools

import jax
import jax.numpy as jnp
import numpy as np
from jax import lax
from jax.experimental import pallas as pl
from jax.experimental.pallas import tpu as pltpu
from jax.sharding import PartitionSpec as P

ITERS = 2
SEND = 2

amplitude_floor = 0.1
object_regular = 0.5
probe_regular = 1.0

LANES = 128
SUBLANES = 8
LEVELS = 32767.0
CHUNK = 32
VMEM = pl.BlockSpec(memory_space=pltpu.VMEM)
SMEM = pl.BlockSpec(memory_space=pltpu.SMEM)
HBM = pl.BlockSpec(memory_space=pltpu.HBM)
LOAD = object()
FREE = pl.BlockSpec(memory_space=pl.ANY)
f32 = jnp.float32
bf16 = jnp.bfloat16


def tables(order):
    half = order // 2
    counter = np.arange(half)
    angles = 2.0 * np.pi * ((counter[:, None] * counter[None, :]) % half) / half
    cos, sin = np.cos(angles), np.sin(angles)
    scale = 1.0 / np.sqrt(order)
    turns = []
    for block in ([[cos, -sin], [sin, cos]], [[cos, sin], [-sin, cos]]):
        matrix = np.block(block) * scale
        high = matrix.astype(jnp.bfloat16)
        turns.append(np.stack([high, (matrix - high.astype(np.float64)).astype(jnp.bfloat16)]))
    turn = 2.0 * np.pi * counter / order
    twiddle = np.stack([np.cos(turn), -np.sin(turn)]).astype(np.float32)
    twiddles = np.concatenate(
        [np.broadcast_to(twiddle[:, :, None], (2, half, half)), np.broadcast_to(twiddle[:, None, :], (2, SUBLANES, half))], axis=1
    )
    sorting = np.zeros((order, order), np.float32)
    sorting[np.arange(half), 2 * np.arange(half)] = 1.0
    sorting[half + np.arange(half), 2 * np.arange(half) + 1] = 1.0
    return (
        jnp.asarray(np.stack(turns)),
        jnp.asarray(np.ascontiguousarray(twiddles)),
        jnp.asarray(np.stack([sorting, sorting.T]).astype(jnp.bfloat16)),
    )


def list_patterns(dims, pos_ref, me_ref, ys_ref, xs_ref, slots_ref):
    tile_rows, tile_cols, pat_count, col_count, capacity = dims
    my_row, my_col = me_ref[0], me_ref[1]
    band_count = pat_count * col_count
    first = my_row * band_count
    total = pos_ref.shape[0] // 2

    def visit(index, carry):
        found, source, rank = carry
        y = pos_ref[first + index]
        x = pos_ref[total + first + index]
        here = lax.div(x, tile_cols) == my_col
        holder = lax.div(index, pat_count)
        rank = jnp.where(holder == source, rank, 0)

        @pl.when(here & (found < capacity))
        def _():
            ys_ref[found] = y - my_row * tile_rows
            xs_ref[found] = x - my_col * tile_cols
            slots_ref[found] = holder * SEND + jnp.minimum(rank, SEND - 1)

        step = here.astype(jnp.int32)
        return found + step, holder, rank + step

    found, _, _ = lax.fori_loop(0, band_count, visit, (jnp.int32(0), jnp.int32(-1), jnp.int32(0)))
    return jnp.minimum(found, capacity)


def lane_index(rows):
    return lax.broadcasted_iota(jnp.int32, (rows, LANES), 1)


def shifted_left(tiles, shift):
    lane = lane_index(tiles[0].shape[0])
    turn = lax.rem(LANES - shift, LANES)
    rolled = [pltpu.roll(tile, turn, axis=1) for tile in tiles]
    inside = lane < LANES - shift
    return [jnp.where(inside, a, b) for a, b in zip(rolled[:-1], rolled[1:])]


def shifted_right(tiles, shift):
    lane = lane_index(tiles[0].shape[0])
    rolled = [pltpu.roll(tile, shift, axis=1) for tile in tiles]
    outside = lane < shift
    zero = jnp.zeros_like(rolled[0])
    firsts = [zero] + rolled
    seconds = rolled + [zero]
    return [jnp.where(outside, a, b) for a, b in zip(firsts, seconds)]


def row_groups(tile):
    return [tile[k : k + SUBLANES] for k in range(0, tile.shape[0], SUBLANES)]


def shifted_up(tile, shift):
    row = lax.broadcasted_iota(jnp.int32, (SUBLANES, LANES), 0)
    turn = lax.rem(SUBLANES - shift, SUBLANES)
    rolled = [pltpu.roll(group, turn, axis=0) for group in row_groups(tile)]
    inside = row < SUBLANES - shift
    return jnp.concatenate([jnp.where(inside, a, b) for a, b in zip(rolled[:-1], rolled[1:])], axis=0)


def shifted_down(before, tile, shift):
    row = lax.broadcasted_iota(jnp.int32, (SUBLANES, LANES), 0)
    rolled = [before] + [pltpu.roll(group, shift, axis=0) for group in row_groups(tile)]
    outside = row < shift
    return rolled[-1], jnp.concatenate([jnp.where(outside, a, b) for a, b in zip(rolled[:-1], rolled[1:])], axis=0)


class Deposit:
    def __init__(self, add, top, left):
        self.add = add
        self.row = pl.multiple_of(lax.div(top, SUBLANES) * SUBLANES, SUBLANES)
        self.col = pl.multiple_of(lax.div(left, LANES) * LANES, LANES)
        self.down = lax.rem(top, SUBLANES)
        self.right = lax.rem(left, LANES)
        self.carried = None

    def place(self, first, tiles):
        moved = jnp.concatenate(shifted_right(tiles, self.right), axis=1)
        self.add(pl.ds(self.row + first, tiles[0].shape[0]), pl.ds(self.col, moved.shape[1]), moved)

    def put(self, first, tiles):
        if self.carried is None:
            self.carried = [jnp.zeros((SUBLANES, LANES), f32) for _ in tiles]
        pairs = [shifted_down(before, tile, self.down) for before, tile in zip(self.carried, tiles)]
        self.carried = [carried for carried, _ in pairs]
        self.place(first, [tile for _, tile in pairs])

    def finish(self, first):
        row = lax.broadcasted_iota(jnp.int32, (SUBLANES, LANES), 0)
        self.place(first, [jnp.where(row < self.down, tile, 0.0) for tile in self.carried])


def lane_tiles(value):
    return [value[:, k : k + LANES] for k in range(0, value.shape[1], LANES)]


def store_split(ref, rows, cols, value):
    high = value.astype(bf16)
    ref[0, rows, cols] = high
    ref[1, rows, cols] = (value - high.astype(f32)).astype(bf16)


def right_dot(x_ref, table_ref):
    left = jnp.concatenate([x_ref[0], x_ref[1], x_ref[0]], axis=1)
    right = jnp.concatenate([table_ref[0], table_ref[0], table_ref[1]], axis=0)
    return jnp.dot(left, right, preferred_element_type=f32)


def left_dot(table_ref, x_ref):
    left = jnp.concatenate([table_ref[0], table_ref[0], table_ref[1]], axis=1)
    right = jnp.concatenate([x_ref[0], x_ref[1], x_ref[0]], axis=0)
    return jnp.dot(left, right, preferred_element_type=f32)


def repeated(group, rows):
    return jnp.concatenate([group] * (rows // SUBLANES), axis=0)


def encode(read, out_ref, rows, first, last):
    for col in range(0, out_ref.shape[1], LANES):
        cols = pl.ds(col, LANES)
        largest = jnp.full((SUBLANES, LANES), 1e-30, f32)
        for start in range(0, rows, CHUNK):
            for comp in range(2):
                for group in row_groups(jnp.abs(read(comp, pl.ds(start, CHUNK), cols))):
                    largest = jnp.maximum(largest, group)
        exponent = jnp.ceil(jnp.log2(largest))
        out_ref[last : last + SUBLANES, cols] = exponent.astype(jnp.int32)
        scale = repeated(jnp.exp2(-exponent) * LEVELS, CHUNK)
        for start in range(0, rows, CHUNK):
            codes = []
            for comp in range(2):
                scaled = jnp.clip(read(comp, pl.ds(start, CHUNK), cols) * scale, -LEVELS, LEVELS)
                codes.append(jnp.round(scaled).astype(jnp.int32))
            out_ref[pl.ds(first + start, CHUNK), cols] = (codes[0] << 16) | (codes[1] & 0xFFFF)


def decode(ref, start, last, col):
    cols = pl.ds(col, LANES)
    words = ref[pl.ds(start, CHUNK), cols]
    scale = repeated(jnp.exp2(ref[last : last + SUBLANES, cols].astype(f32)) * (1.0 / LEVELS), CHUNK)
    return (words >> 16).astype(f32) * scale, ((words << 16) >> 16).astype(f32) * scale


def largest_exponent(values):
    largest = jnp.full((SUBLANES, LANES), 1e-30, f32)
    for value in values:
        for group in row_groups(jnp.abs(value)):
            largest = jnp.maximum(largest, group)
    return jnp.ceil(jnp.log2(largest))


def fixed(value, exponent):
    scaled = value * repeated(jnp.exp2(-exponent) * LEVELS, value.shape[0])
    return jnp.round(jnp.clip(scaled, -LEVELS, LEVELS)).astype(jnp.int32)


def paired(first, second):
    return (first << 16) | (second & 0xFFFF)


def unpaired(words):
    return words >> 16, (words << 16) >> 16


def scaled_back(codes, exponent):
    return codes.astype(f32) * repeated(jnp.exp2(exponent.astype(f32)) * (1.0 / LEVELS), codes.shape[0])


def sums_rows(rows):
    return rows + rows // 2 + SUBLANES


def encode_sums(out_ref, cols, u_re, u_im, v):
    rows = v.shape[0]
    half = rows // 2
    of_u, of_v = largest_exponent([u_re, u_im]), largest_exponent([v])
    out_ref[0:rows, cols] = paired(fixed(u_re, of_u), fixed(u_im, of_u))
    codes = fixed(v, of_v)
    out_ref[rows : rows + half, cols] = paired(codes[:half], codes[half:])
    out_ref[rows + half : rows + half + SUBLANES, cols] = paired(of_u.astype(jnp.int32), of_v.astype(jnp.int32))


def decode_sums(ref, cols, rows):
    half = rows // 2
    of_u, of_v = unpaired(ref[rows + half : rows + half + SUBLANES, cols])
    u_re, u_im = unpaired(ref[0:rows, cols])
    v = jnp.concatenate(unpaired(ref[rows : rows + half, cols]), axis=0)
    return scaled_back(u_re, of_u), scaled_back(u_im, of_u), scaled_back(v, of_v)


def decode_probe(out_ref, chunks_ref):
    chunks = chunks_ref.shape[0]
    rows = out_ref.shape[1] // chunks
    for chunk in range(chunks):
        for col in range(0, out_ref.shape[2], LANES):
            cols = pl.ds(col, LANES)
            exponent = chunks_ref[chunk, rows : rows + SUBLANES, cols]
            for comp, codes in enumerate(unpaired(chunks_ref[chunk, 0:rows, cols])):
                out_ref[comp, chunk * rows : (chunk + 1) * rows, cols] = scaled_back(codes, exponent)


def cut_chunk(ext_ref, comp, first, top, left, rows):
    row = pl.multiple_of(lax.div(top, SUBLANES) * SUBLANES, SUBLANES)
    col = pl.multiple_of(lax.div(left, LANES) * LANES, LANES)
    block = ext_ref[comp, pl.ds(row + first, rows + SUBLANES), pl.ds(col, 3 * LANES)]
    tiles = shifted_left(lane_tiles(block), lax.rem(left, LANES))
    return [shifted_up(tile, lax.rem(top, SUBLANES)) for tile in tiles]


def forward(order, ext_ref, probe_ref, consts, y, x, win_ref, power_ref, weight, xa_ref, xb_ref, ya_ref, yb_ref, far_ref):
    turns, twiddles = consts
    half = order // 2
    tw_re = repeated(twiddles[0, half : half + SUBLANES, :], CHUNK)
    tw_im = repeated(twiddles[1, half : half + SUBLANES, :], CHUNK)
    for first in range(0, order, CHUNK):
        rows = pl.ds(first, CHUNK)
        win_re = cut_chunk(ext_ref, 0, first, y, x, CHUNK)
        win_im = cut_chunk(ext_ref, 1, first, y, x, CHUNK)
        exits = []
        for k in range(2):
            cols = pl.ds(k * half, half)
            win_ref[0, rows, cols] = win_re[k]
            win_ref[1, rows, cols] = win_im[k]
            power_ref[rows, cols] += weight * (win_re[k] * win_re[k] + win_im[k] * win_im[k])
            p_re, p_im = probe_ref[0, rows, cols], probe_ref[1, rows, cols]
            exits.append((p_re * win_re[k] - p_im * win_im[k], p_re * win_im[k] + p_im * win_re[k]))
        (lo_re, lo_im), (hi_re, hi_im) = exits
        store_split(xa_ref, rows, pl.ds(0, half), lo_re + hi_re)
        store_split(xa_ref, rows, pl.ds(half, half), lo_im + hi_im)
        d_re, d_im = lo_re - hi_re, lo_im - hi_im
        store_split(xb_ref, rows, pl.ds(0, half), d_re * tw_re - d_im * tw_im)
        store_split(xb_ref, rows, pl.ds(half, half), d_re * tw_im + d_im * tw_re)
    yield
    ya_ref[...] = right_dot(xa_ref, turns.at[0])
    yb_ref[...] = right_dot(xb_ref, turns.at[0])
    yield
    for first in range(0, half, CHUNK):
        rows = pl.ds(first, CHUNK)
        below = pl.ds(half + first, CHUNK)
        t_re, t_im = twiddles[0, rows, :], twiddles[1, rows, :]
        for k, y_ref in enumerate((ya_ref, yb_ref)):
            cols = pl.ds(k * half, half)
            up_re, up_im = y_ref[rows, 0:half], y_ref[rows, half:order]
            dn_re, dn_im = y_ref[below, 0:half], y_ref[below, half:order]
            store_split(xa_ref, rows, cols, up_re + dn_re)
            store_split(xa_ref, below, cols, up_im + dn_im)
            d_re, d_im = up_re - dn_re, up_im - dn_im
            store_split(xb_ref, rows, cols, d_re * t_re - d_im * t_im)
            store_split(xb_ref, below, cols, d_re * t_im + d_im * t_re)
    yield
    far_ref[0] = left_dot(turns.at[1], xa_ref)
    far_ref[1] = left_dot(turns.at[1], xb_ref)
    yield


def backward(order, far_ref, amp_ref, consts, y, x, weight, probe_ref, win_ref, xa_ref, xb_ref, ya_ref, yb_ref, grad_ref, numer_ref):
    turns, twiddles = consts
    half = order // 2
    tw_re = repeated(twiddles[0, half : half + SUBLANES, :], CHUNK)
    tw_im = repeated(twiddles[1, half : half + SUBLANES, :], CHUNK)
    for k, x_ref in enumerate((xa_ref, xb_ref)):
        for first in range(0, half, CHUNK):
            rows = pl.ds(first, CHUNK)
            below = pl.ds(half + first, CHUNK)
            far_re, far_im = far_ref[k, rows, :], far_ref[k, below, :]
            amp = amp_ref[pl.ds(k * half + first, CHUNK), :].astype(f32)
            factor = amp * lax.rsqrt(far_re * far_re + far_im * far_im + amplitude_floor)
            store_split(x_ref, rows, slice(None), far_re * factor)
            store_split(x_ref, below, slice(None), far_im * factor)
    yield
    ya_ref[...] = left_dot(turns.at[0], xa_ref)
    yb_ref[...] = left_dot(turns.at[0], xb_ref)
    yield
    for first in range(0, half, CHUNK):
        rows = pl.ds(first, CHUNK)
        below = pl.ds(half + first, CHUNK)
        t_re, t_im = twiddles[0, rows, :], twiddles[1, rows, :]
        for k, x_ref in enumerate((xa_ref, xb_ref)):
            cols = slice(k * half, (k + 1) * half)
            a_re, a_im = ya_ref[rows, cols], ya_ref[below, cols]
            b_re, b_im = yb_ref[rows, cols], yb_ref[below, cols]
            c_re, c_im = b_re * t_re + b_im * t_im, b_im * t_re - b_re * t_im
            store_split(x_ref, rows, pl.ds(0, half), a_re + c_re)
            store_split(x_ref, rows, pl.ds(half, half), a_im + c_im)
            store_split(x_ref, below, pl.ds(0, half), a_re - c_re)
            store_split(x_ref, below, pl.ds(half, half), a_im - c_im)
    yield
    ya_ref[...] = right_dot(xa_ref, turns.at[1])
    yb_ref[...] = right_dot(xb_ref, turns.at[1])
    yield

    def adder(comp):
        def add(rows, cols, moved):
            grad_ref[comp, rows, cols] += moved

        return add

    deposits = [Deposit(adder(comp), y, x) for comp in range(2)]
    for first in range(0, order, CHUNK):
        rows = pl.ds(first, CHUNK)
        a_re, a_im = ya_ref[rows, 0:half], ya_ref[rows, half:order]
        b_re, b_im = yb_ref[rows, 0:half], yb_ref[rows, half:order]
        c_re, c_im = b_re * tw_re + b_im * tw_im, b_im * tw_re - b_re * tw_im
        waves = [(a_re + c_re, a_im + c_im), (a_re - c_re, a_im - c_im)]
        terms = ([], [])
        for k, (wave_re, wave_im) in enumerate(waves):
            cols = pl.ds(k * half, half)
            wave_re, wave_im = weight * wave_re, weight * wave_im
            p_re, p_im = probe_ref[0, rows, cols], probe_ref[1, rows, cols]
            w_re, w_im = win_ref[0, rows, cols], win_ref[1, rows, cols]
            terms[0].append(p_re * wave_re + p_im * wave_im)
            terms[1].append(p_re * wave_im - p_im * wave_re)
            numer_ref[0, rows, cols] += w_re * wave_re + w_im * wave_im
            numer_ref[1, rows, cols] += w_re * wave_im - w_im * wave_re
        for comp in range(2):
            deposits[comp].put(first, terms[comp])
    for deposit in deposits:
        deposit.finish(order)
    yield


def interleaved(*stages):
    live = list(stages)
    while live:
        still = []
        for stage in live:
            try:
                next(stage)
                still.append(stage)
            except StopIteration:
                pass
        live = still


def outgoing_kernel(dims, pos_ref, me_ref, amp_ref, after_ref, also_ref, out_ref, sems):
    tile_rows, tile_cols, pat_count, col_count, capacity = dims
    first = (me_ref[0] * col_count + me_ref[1]) * pat_count
    total = pos_ref.shape[0] // 2
    owners = [lax.div(pos_ref[total + first + k], tile_cols) for k in range(pat_count)]
    copies = []
    for k in range(pat_count):
        rank = sum(((owners[e] == owners[k]).astype(jnp.int32) for e in range(k)), jnp.int32(0))
        slot = owners[k] * SEND + jnp.minimum(rank, SEND - 1)
        copies.append(pltpu.make_async_copy(amp_ref.at[k], out_ref.at[slot], sems.at[k]))
        copies[-1].start()
    for copy in copies:
        copy.wait()


def weights_kernel(dims, span, pos_ref, me_ref, probe_ref, out_ref, sums_ref, power_ref):
    tile_rows, tile_cols, pat_count, col_count, capacity = dims
    order = probe_ref.shape[1]
    top = (me_ref[0] - 1) * tile_rows
    left = (me_ref[1] - 1) * tile_cols
    total = pos_ref.shape[0] // 2
    for first in range(0, sums_ref.shape[0], order):
        sums_ref[pl.ds(first, order), :] = jnp.zeros((order, sums_ref.shape[1]), f32)
    power_ref[...] = probe_ref[0] * probe_ref[0] + probe_ref[1] * probe_ref[1]

    def visit(index, carry):
        y = pos_ref[index] - top
        x = pos_ref[total + index] - left

        @pl.when((y > 0) & (y < (span + 1) * tile_rows) & (x > 0) & (x < (span + 1) * tile_cols))
        def _():
            def add(rows, cols, moved):
                sums_ref[rows, cols] += moved

            deposit = Deposit(add, y, x)
            for first in range(0, order, CHUNK):
                deposit.put(first, lane_tiles(power_ref[pl.ds(first, CHUNK), :]))
            deposit.finish(order)

        return carry

    lax.fori_loop(0, total, visit, 0)
    pltpu.sync_copy(sums_ref.at[pl.ds(tile_rows, span * tile_rows), pl.ds(tile_cols, span * tile_cols)], out_ref)


def encode_kernel(obj_ref, out_ref):
    rows = obj_ref.shape[1]
    encode(lambda comp, at, cols: obj_ref[comp, at, cols], out_ref, rows, 0, rows)


def unfold(dims, ext_ref, own_ref, coded_refs):
    tile_rows, tile_cols = dims[:2]
    ext_ref[:, 0:tile_rows, 0:tile_cols] = own_ref[...]
    for (i, j), ref in zip(((0, 1), (1, 0), (1, 1)), coded_refs):
        for col in range(0, tile_cols, LANES):
            for start in range(0, tile_rows, CHUNK):
                parts = decode(ref, start, tile_rows, col)
                for comp in range(2):
                    ext_ref[comp, pl.ds(i * tile_rows + start, CHUNK), pl.ds(j * tile_cols + col, LANES)] = parts[comp]


def spread_sums(out_ref, u_ref, v_ref):
    chunks = out_ref.shape[0]
    rows = v_ref.shape[0] // chunks
    for chunk in range(chunks):
        at = pl.ds(chunk * rows, rows)
        for col in range(0, v_ref.shape[1], LANES):
            cols = pl.ds(col, LANES)
            encode_sums(out_ref.at[chunk], cols, u_ref[0, at, cols], u_ref[1, at, cols], v_ref[at, cols])


def added(parts):
    while len(parts) > 1:
        parts = [tuple(x + y for x, y in zip(a, b)) for a, b in zip(parts[::2], parts[1::2])]
    return parts[0]


def sums_kernel(rows, parts_ref, out_ref):
    for col in range(0, out_ref.shape[2], LANES):
        cols = pl.ds(col, LANES)
        total = added([decode_sums(parts_ref.at[k], cols, rows) for k in range(parts_ref.shape[0])])
        encode_sums(out_ref.at[0], cols, *total)
        for k in range(1, out_ref.shape[0]):
            out_ref[k, :, cols] = out_ref[0, :, cols]


def update_kernel(rows, me_ref, probe_ref, parts_ref, *refs):
    out_ref = refs[-1]
    first = pl.multiple_of(me_ref[1] * rows, SUBLANES)
    for col in range(0, out_ref.shape[2], LANES):
        cols = pl.ds(col, LANES)
        u_re, u_im, v = added([decode_sums(parts_ref.at[k], cols, rows) for k in range(parts_ref.shape[0])])
        scale = 1.0 / (v + probe_regular)
        re = (probe_ref[0, pl.ds(first, rows), cols] + u_re) * scale
        im = (probe_ref[1, pl.ds(first, rows), cols] + u_im) * scale
        exponent = largest_exponent([re, im])
        words = paired(fixed(re, exponent), fixed(im, exponent))
        for chunk in range(out_ref.shape[0]):
            out_ref[chunk, 0:rows, cols] = words
            out_ref[chunk, rows : rows + SUBLANES, cols] = exponent.astype(jnp.int32)


def probe_kernel(chunks_ref, out_ref):
    decode_probe(out_ref, chunks_ref)


def first_half_kernel(dims, pos_ref, me_ref, own_ref, right_ref, below_ref, diag_ref, probe_ref, turns, twiddles,
                      far_out, power_out, ext_out, ext_ref, win_ref, xa_ref, xb_ref, ya_ref, yb_ref, far_ref, ys_ref, xs_ref, slots_ref, sems, ext_sem):
    tile_rows, tile_cols, pat_count, col_count, capacity = dims
    order = probe_ref.shape[1]
    count = list_patterns(dims, pos_ref, me_ref, ys_ref, xs_ref, slots_ref)
    unfold(dims, ext_ref, own_ref, (right_ref, below_ref, diag_ref))
    keep = pltpu.make_async_copy(ext_ref, ext_out, ext_sem)
    keep.start()
    power_out[...] = jnp.zeros_like(power_out)
    consts = (turns, twiddles)

    def pair(step, carry):
        stages = []
        for k in range(2):
            listed = 2 * step + k
            weight = (listed < count).astype(f32)
            index = jnp.minimum(listed, count - 1)
            stages.append(forward(order, ext_ref, probe_ref, consts, ys_ref[index], xs_ref[index], win_ref.at[k], power_out, weight,
                                  xa_ref.at[k], xb_ref.at[k], ya_ref.at[k], yb_ref.at[k], far_ref.at[listed]))
        interleaved(*stages)
        for k in range(2):
            listed = 2 * step + k
            pltpu.make_async_copy(far_ref.at[listed], far_out.at[listed], sems.at[listed]).start()
        return carry

    pairs = lax.div(count + 1, 2)
    lax.fori_loop(0, pairs, pair, 0)

    def settle(listed, carry):
        pltpu.make_async_copy(far_ref.at[listed], far_out.at[listed], sems.at[listed]).wait()
        return carry

    lax.fori_loop(0, 2 * pairs, settle, 0)
    keep.wait()


def second_half_kernel(dims, pos_ref, me_ref, ext_ref, probe_ref, power_ref, weights_ref, far_in, amp_in, turns, twiddles, sorting,
                       share_out, top_out, bottom_out, numer_out, amp_out,
                       sum_ref, win_ref, xa_ref, xb_ref, ya_ref, yb_ref, numer_ref, far_ref, amp_ref, sorted_ref, ys_ref, xs_ref, slots_ref, far_sems, amp_sems, out_sems, sum_sem):
    tile_rows, tile_cols, pat_count, col_count, capacity = dims
    order = probe_ref.shape[1]
    half = order // 2
    count = list_patterns(dims, pos_ref, me_ref, ys_ref, xs_ref, slots_ref)
    pairs = lax.div(count + 1, 2)

    def copies(listed):
        return (
            pltpu.make_async_copy(far_in.at[listed], far_ref.at[listed], far_sems.at[listed]),
            pltpu.make_async_copy(amp_in.at[slots_ref[jnp.minimum(listed, count - 1)]], amp_ref.at[listed], amp_sems.at[listed]),
        )

    def begin(listed, carry):
        for copy in copies(listed):
            copy.start()
        return carry

    lax.fori_loop(0, 2 * pairs, begin, 0)
    sum_ref[...] = jnp.zeros_like(sum_ref)
    numer_ref[...] = jnp.zeros_like(numer_ref)
    consts = (turns, twiddles)

    def pair(step, carry):
        stages = []
        for k in range(2):
            listed = 2 * step + k
            for copy in copies(listed):
                copy.wait()
        for k in range(2):
            listed = 2 * step + k
            weight = (listed < count).astype(f32)
            index = jnp.minimum(listed, count - 1)
            y, x = ys_ref[index], xs_ref[index]
            rows_sorted = jnp.dot(sorting[0], amp_ref[listed], preferred_element_type=f32).astype(bf16)
            sorted_ref[listed] = jnp.dot(rows_sorted, sorting[1], preferred_element_type=f32).astype(bf16)
            for first in range(0, order, CHUNK):
                for comp in range(2):
                    for c, tile in enumerate(cut_chunk(ext_ref, comp, first, y, x, CHUNK)):
                        win_ref[k, comp, pl.ds(first, CHUNK), pl.ds(c * half, half)] = tile
            stages.append(backward(order, far_ref.at[listed], sorted_ref.at[listed], consts, y, x, weight, probe_ref, win_ref.at[k],
                                   xa_ref.at[k], xb_ref.at[k], ya_ref.at[k], yb_ref.at[k], sum_ref, numer_ref))
        interleaved(*stages)
        for k in range(2):
            listed = 2 * step + k
            pltpu.make_async_copy(sorted_ref.at[listed], amp_out.at[listed], out_sems.at[listed]).start()
        return carry

    lax.fori_loop(0, pairs, pair, 0)
    for first in range(0, 2 * tile_rows, CHUNK):
        rows = pl.ds(first, CHUNK)
        scale = 1.0 / (weights_ref[rows, :] + object_regular)
        for comp in range(2):
            sum_ref[comp, rows, :] = sum_ref[comp, rows, :] * scale
    keep = pltpu.make_async_copy(sum_ref, share_out, sum_sem)
    keep.start()
    encode(lambda comp, at, cols: sum_ref[comp, at, cols], top_out, tile_rows, 0, tile_rows)
    encode(lambda comp, at, cols: sum_ref[comp, pl.ds(tile_rows + at.start, at.size), cols], bottom_out, tile_rows, 0, tile_rows)
    spread_sums(numer_out, numer_ref, power_ref)

    def settle(listed, carry):
        pltpu.make_async_copy(sorted_ref.at[listed], amp_out.at[listed], out_sems.at[listed]).wait()
        return carry

    lax.fori_loop(0, 2 * pairs, settle, 0)
    keep.wait()


def rows_sum_kernel(dims, share_ref, above_ref, below_ref, after_ref, sum_out, left_out, right_out):
    tile_rows, tile_cols = dims[:2]
    for i, ref in enumerate((above_ref, below_ref)):
        for col in range(0, 2 * tile_cols, LANES):
            for start in range(0, tile_rows, CHUNK):
                rows, cols = pl.ds(i * tile_rows + start, CHUNK), pl.ds(col, LANES)
                parts = decode(ref, start, tile_rows, col)
                for comp in range(2):
                    sum_out[comp, rows, cols] = share_ref[comp, rows, cols] + parts[comp]
    for j, ref in enumerate((left_out, right_out)):
        for i in range(2):

            def read(comp, at, cols, i=i, j=j):
                return sum_out[comp, pl.ds(i * tile_rows + at.start, at.size), pl.ds(j * tile_cols + cols.start, cols.size)]

            encode(read, ref, tile_rows, i * tile_rows, 2 * tile_rows + i * SUBLANES)


def whole_kernel(dims, pos_ref, me_ref, old_ref, sum_ref, from_left_ref, from_right_ref, weights_ref,
                 chunks_ref, amp_in, turns, twiddles,
                 current_out, own_out, right_out, below_out, diag_out, numer_out, probe_ref,
                 ext_ref, grad_ref, win_ref, xa_ref, xb_ref, ya_ref, yb_ref, numer_ref, far_ref, amp_ref, ys_ref, xs_ref, slots_ref, amp_sems, own_sem):
    tile_rows, tile_cols, pat_count, col_count, capacity = dims
    order = probe_ref.shape[1]
    count = list_patterns(dims, pos_ref, me_ref, ys_ref, xs_ref, slots_ref)
    pairs = lax.div(count + 1, 2)
    decode_probe(probe_ref, chunks_ref)

    def fetch(listed):
        return pltpu.make_async_copy(amp_in.at[jnp.minimum(listed, count - 1)], amp_ref.at[listed], amp_sems.at[listed])

    def begin(listed, carry):
        fetch(listed).start()
        return carry

    lax.fori_loop(0, 2 * pairs, begin, 0)
    for j, ref in enumerate((from_left_ref, from_right_ref)):
        for i in range(2):
            for col in range(0, tile_cols, LANES):
                for start in range(0, tile_rows, CHUNK):
                    rows, cols = pl.ds(i * tile_rows + start, CHUNK), pl.ds(j * tile_cols + col, LANES)
                    parts = decode(ref, i * tile_rows + start, 2 * tile_rows + i * SUBLANES, col)
                    scale = object_regular / (weights_ref[rows, cols] + object_regular)
                    for comp in range(2):
                        ext_ref[comp, rows, cols] = old_ref[comp, rows, cols] * scale + (sum_ref[comp, rows, cols] + parts[comp])
    keep = pltpu.make_async_copy(ext_ref.at[:, pl.ds(0, tile_rows), pl.ds(0, tile_cols)], current_out, own_sem)
    keep.start()
    grad_ref[...] = jnp.zeros_like(grad_ref)
    numer_ref[...] = jnp.zeros_like(numer_ref)
    consts = (turns, twiddles)

    def pair(step, carry):
        stages = []
        for k in range(2):
            fetch(2 * step + k).wait()
        for k in range(2):
            listed = 2 * step + k
            weight = (listed < count).astype(f32)
            index = jnp.minimum(listed, count - 1)
            y, x = ys_ref[index], xs_ref[index]

            def both(k=k, listed=listed, weight=weight, y=y, x=x):
                yield from forward(order, ext_ref, probe_ref, consts, y, x, win_ref.at[k], numer_ref.at[2], weight,
                                   xa_ref.at[k], xb_ref.at[k], ya_ref.at[k], yb_ref.at[k], far_ref.at[k])
                yield from backward(order, far_ref.at[k], amp_ref.at[listed], consts, y, x, weight, probe_ref, win_ref.at[k],
                                    xa_ref.at[k], xb_ref.at[k], ya_ref.at[k], yb_ref.at[k], grad_ref, numer_ref)

            stages.append(both())
        interleaved(*stages)
        return carry

    lax.fori_loop(0, pairs, pair, 0)
    own_out[...] = grad_ref[:, 0:tile_rows, 0:tile_cols]
    for (i, j), ref in zip(((0, 1), (1, 0), (1, 1)), (right_out, below_out, diag_out)):

        def read(comp, at, cols, i=i, j=j):
            rows, cols = pl.ds(i * tile_rows + at.start, at.size), pl.ds(j * tile_cols + cols.start, cols.size)
            return grad_ref[comp, rows, cols] / (weights_ref[rows, cols] + object_regular)

        encode(read, ref, tile_rows, 0, tile_rows)
    spread_sums(numer_out, numer_ref, numer_ref.at[2])
    keep.wait()


def object_kernel(dims, current_ref, own_ref, left_ref, above_ref, diag_ref, before_ref, weights_ref, out_ref):
    tile_rows, tile_cols = dims[:2]
    for col in range(0, tile_cols, LANES):
        for start in range(0, tile_rows, CHUNK):
            rows, cols = pl.ds(start, CHUNK), pl.ds(col, LANES)
            scale = 1.0 / (weights_ref[rows, cols] + object_regular)
            back = (before_ref[rows, cols] + object_regular) * scale
            parts = [decode(ref, start, tile_rows, col) for ref in (left_ref, above_ref, diag_ref)]
            for comp in range(2):
                coded = parts[0][comp] + parts[1][comp] + parts[2][comp]
                old = object_regular * current_ref[comp, rows, cols] + own_ref[comp, rows, cols]
                out_ref[comp, rows, cols] = old * scale + coded * back


def shape(dims, dtype=f32):
    return jax.ShapeDtypeStruct(dims, dtype)


def work_scratch(order):
    return [
        pltpu.VMEM((2, 2, order, order), f32),
        pltpu.VMEM((2, 2, order, order), bf16),
        pltpu.VMEM((2, 2, order, order), bf16),
        pltpu.VMEM((2, order, order), f32),
        pltpu.VMEM((2, order, order), f32),
    ]


def list_scratch(capacity):
    return [pltpu.SMEM((capacity,), jnp.int32)] * 3


def call(kernel, outs, out_specs, in_specs, scratch, flops, limit=26 << 20):
    several = isinstance(outs, tuple)
    out_count = len(outs) if several else 1
    in_count = len(in_specs)
    loaded = [k for k, spec in enumerate(in_specs) if spec is LOAD]

    def body(*refs):
        ins, rest = list(refs[:in_count]), refs[in_count:]
        given, kept = rest[: out_count + len(scratch)], rest[out_count + len(scratch) :]
        copies = [pltpu.make_async_copy(ins[k], kept[n], kept[-1].at[n]) for n, k in enumerate(loaded)]
        for copy in copies:
            copy.start()
        for n, k in enumerate(loaded):
            copies[n].wait()
            ins[k] = kept[n]
        kernel(*ins, *given)

    fixed_outs = [
        pltpu.HBM(out.shape, out.dtype) if spec is HBM else out
        for out, spec in zip(outs if several else (outs,), out_specs if several else (out_specs,))
    ]
    stay = [spec is LOAD or spec is HBM for spec in in_specs]

    def called(*args):
        args = [pltpu.with_memory_space_constraint(arg, pltpu.HBM) if kept else arg for arg, kept in zip(args, stay)]
        own = [pltpu.VMEM(args[k].shape, args[k].dtype) for k in loaded]
        if loaded:
            own.append(pltpu.SemaphoreType.DMA((len(loaded),)))
        return pl.pallas_call(
            body,
            out_shape=tuple(fixed_outs) if several else fixed_outs[0],
            out_specs=out_specs,
            in_specs=[HBM if spec is LOAD else spec for spec in in_specs],
            scratch_shapes=list(scratch) + own,
            compiler_params=pltpu.CompilerParams(vmem_limit_bytes=limit),
            cost_estimate=pl.CostEstimate(flops=flops, bytes_accessed=8 << 20, transcendentals=0),
        )(*args)

    return called


def passed_along(value, axis, steps):
    count = lax.axis_size(axis)
    leading, last = (max(0, -steps), min(count, count - steps))
    return lax.ppermute(value, axis, [(source, source + steps) for source in range(leading, last)])


def passed_both(value, row_steps, col_steps):
    rows, cols = lax.axis_size("row"), lax.axis_size("col")
    pairs = []
    for r in range(rows):
        for c in range(cols):
            if 0 <= r + row_steps < rows and 0 <= c + col_steps < cols:
                pairs.append((r * cols + c, (r + row_steps) * cols + c + col_steps))
    return lax.ppermute(value, ("row", "col"), pairs)


def probe_update(me, probe, numer, kind, *after):
    cols, order = lax.axis_size("col"), probe.shape[1]
    rows = order // cols
    parts = lax.all_to_all(numer, "col", split_axis=0, concat_axis=0, tiled=True)
    total = call(
        functools.partial(sums_kernel, rows), shape((lax.axis_size("row"), sums_rows(rows), order), jnp.int32), VMEM, [VMEM], [], 1 << 26,
    )(parts)
    parts = lax.all_to_all(total, "row", split_axis=0, concat_axis=0, tiled=True)
    fresh = call(
        functools.partial(update_kernel, rows), shape((cols, rows + SUBLANES, order), jnp.int32), VMEM,
        [SMEM, kind, VMEM] + [spec for spec, _ in after], [], 1 << 26,
    )(me, probe, parts, *[value for _, value in after])
    return total, lax.all_to_all(fresh, "col", split_axis=0, concat_axis=0, tiled=True)


def local(obj, probe, amplitudes, positions):
    col_count = lax.axis_size("col")
    tile_rows, tile_cols = obj.shape[1], obj.shape[2]
    order = probe.shape[1]
    pat_count = amplitudes.shape[0]
    capacity = 2 * pat_count
    dims = (tile_rows, tile_cols, pat_count, col_count, capacity)
    me = jnp.stack([lax.axis_index("row"), lax.axis_index("col")]).astype(jnp.int32)
    pos = positions.T.reshape(-1)
    turns, twiddles, sorting = tables(order)
    tile = (2, tile_rows, tile_cols)
    window = (2, order, order)
    wide = (2, 2 * tile_rows, 2 * tile_cols)
    shares = shape((col_count, sums_rows(order // col_count), order), jnp.int32)
    coded_tile = shape((tile_rows + SUBLANES, tile_cols), jnp.int32)
    coded_row = shape((tile_rows + SUBLANES, 2 * tile_cols), jnp.int32)
    coded_col = shape((2 * (tile_rows + SUBLANES), tile_cols), jnp.int32)
    one_pattern = 24 * 2 * order**3

    coded = call(encode_kernel, coded_tile, VMEM, [LOAD], [], 1 << 26)(obj)
    right = passed_along(coded, "col", -1)
    below = passed_along(coded, "row", -1)
    diag = passed_along(right, "row", -1)

    outgoing = call(
        functools.partial(outgoing_kernel, dims), shape((col_count * SEND, order, order), bf16), HBM, [SMEM, SMEM, LOAD, FREE, FREE],
        [pltpu.SemaphoreType.DMA((pat_count,))], 1 << 20,
    )(pos, me, amplitudes, right, below)
    incoming = lax.all_to_all(outgoing, "col", split_axis=0, concat_axis=0, tiled=True)

    def weights(probe_now, span, kind):
        return call(
            functools.partial(weights_kernel, dims, span), shape((span * tile_rows, span * tile_cols)), HBM, [SMEM, SMEM, kind],
            [pltpu.VMEM(((span + 2) * tile_rows, (span + 2) * tile_cols), f32), pltpu.VMEM((order, order), f32)], 8 << 30,
        )(pos, me, probe_now)

    weights_old = weights(probe, 2, LOAD)

    far, power, ext = call(
        functools.partial(first_half_kernel, dims), (shape((capacity,) + window), shape((order, order)), shape(wide)), (HBM, VMEM, HBM),
        [SMEM, SMEM, LOAD] + [VMEM] * 3 + [LOAD] * 3,
        [pltpu.VMEM(wide, f32)] + work_scratch(order) + [pltpu.VMEM((capacity,) + window, f32)] + list_scratch(capacity)
        + [pltpu.SemaphoreType.DMA((capacity,)), pltpu.SemaphoreType.DMA],
        capacity * one_pattern // 2,
    )(pos, me, obj, right, below, diag, probe, turns, twiddles)

    share, top, bottom, numer, sorted_amps = call(
        functools.partial(second_half_kernel, dims),
        (shape(wide), coded_row, coded_row, shares, shape((capacity, order, order), bf16)),
        (HBM, VMEM, VMEM, VMEM, HBM),
        [SMEM, SMEM, LOAD, LOAD, VMEM, LOAD, HBM, HBM] + [LOAD] * 3,
        [pltpu.VMEM(wide, f32)] + work_scratch(order)
        + [pltpu.VMEM(window, f32), pltpu.VMEM((capacity,) + window, f32), pltpu.VMEM((capacity, order, order), bf16), pltpu.VMEM((capacity, order, order), bf16)]
        + list_scratch(capacity) + [pltpu.SemaphoreType.DMA((capacity,))] * 3 + [pltpu.SemaphoreType.DMA],
        capacity * one_pattern // 2,
    )(pos, me, ext, probe, power, weights_old, far, incoming, turns, twiddles, sorting)

    from_above = passed_along(bottom, "row", 1)
    from_below = passed_along(top, "row", -1)
    total, chunks = probe_update(me, probe, numer, LOAD)
    sums, to_left, to_right = call(
        functools.partial(rows_sum_kernel, dims), (shape(wide), coded_col, coded_col), (VMEM,) * 3, [LOAD, VMEM, VMEM, FREE], [], 1 << 26,
    )(share, from_above, from_below, total)
    from_left = passed_along(to_right, "col", 1)
    from_right = passed_along(to_left, "col", -1)

    current, own, to_right, to_below, to_diag, numer, probe_now = call(
        functools.partial(whole_kernel, dims), (shape(tile), shape(tile), coded_tile, coded_tile, coded_tile, shares, shape(window)), (HBM,) + (VMEM,) * 6,
        [SMEM, SMEM, LOAD] + [VMEM] * 3 + [LOAD, VMEM, HBM, LOAD, LOAD],
        [pltpu.VMEM(wide, f32), pltpu.VMEM(wide, f32)] + work_scratch(order)
        + [pltpu.VMEM((3, order, order), f32), pltpu.VMEM((2,) + window, f32), pltpu.VMEM((capacity, order, order), bf16)]
        + list_scratch(capacity) + [pltpu.SemaphoreType.DMA((capacity,)), pltpu.SemaphoreType.DMA],
        capacity * one_pattern,
    )(pos, me, ext, sums, from_left, from_right, weights_old, chunks, sorted_amps, turns, twiddles)

    from_left = passed_along(to_right, "col", 1)
    from_above = passed_along(to_below, "row", 1)
    from_diag = passed_both(to_diag, 1, 1)
    weights_new = weights(probe_now, 1, VMEM)
    new_object = call(functools.partial(object_kernel, dims), shape(tile), VMEM, [LOAD] + [VMEM] * 4 + [LOAD, LOAD], [], 1 << 26)(
        current, own, from_left, from_above, from_diag, weights_old, weights_new
    )
    _, chunks = probe_update(me, probe_now, numer, VMEM, (HBM, weights_new), (FREE, from_left), (FREE, from_above), (FREE, from_diag))
    new_probe = call(probe_kernel, shape(window), VMEM, [VMEM], [], 1 << 26)(chunks)
    return new_object, new_probe


def solution(mesh):
    placed = (P(None, "row", "col"), P(), P(("row", "col"), None, None), P())
    return jax.shard_map(local, mesh=mesh, in_specs=placed, out_specs=(P(None, "row", "col"), P()), check_vma=False)
```

```python
import functools

import jax
import jax.numpy as jnp
import numpy as np
from jax import lax
from jax.experimental import pallas as pl
from jax.experimental.pallas import tpu as pltpu
from jax.sharding import PartitionSpec as P

ITERS = 2
SEND = 2

amplitude_floor = 0.1
object_regular = 0.5
probe_regular = 1.0

LANES = 128
SUBLANES = 8
LEVELS = 32767.0
CHUNK = 32
VMEM = pl.BlockSpec(memory_space=pltpu.VMEM)
SMEM = pl.BlockSpec(memory_space=pltpu.SMEM)
HBM = pl.BlockSpec(memory_space=pltpu.HBM)
LOAD = object()
FREE = pl.BlockSpec(memory_space=pl.ANY)
PIN = pl.BlockSpec(memory_space=pltpu.VMEM)
f32 = jnp.float32
bf16 = jnp.bfloat16


def tables(order):
    half = order // 2
    counter = np.arange(half)
    angles = 2.0 * np.pi * ((counter[:, None] * counter[None, :]) % half) / half
    cos, sin = np.cos(angles), np.sin(angles)
    scale = 1.0 / np.sqrt(order)
    turns = []
    for block in ([[cos, -sin], [sin, cos]], [[cos, sin], [-sin, cos]]):
        matrix = np.block(block) * scale
        high = matrix.astype(jnp.bfloat16)
        turns.append(np.stack([high, (matrix - high.astype(np.float64)).astype(jnp.bfloat16)]))
    turn = 2.0 * np.pi * counter / order
    twiddle = np.stack([np.cos(turn), -np.sin(turn)]).astype(np.float32)
    twiddles = np.concatenate(
        [np.broadcast_to(twiddle[:, :, None], (2, half, half)), np.broadcast_to(twiddle[:, None, :], (2, SUBLANES, half))], axis=1
    )
    sorting = np.zeros((order, order), np.float32)
    sorting[np.arange(half), 2 * np.arange(half)] = 1.0
    sorting[half + np.arange(half), 2 * np.arange(half) + 1] = 1.0
    return (
        jnp.asarray(np.stack(turns)),
        jnp.asarray(np.ascontiguousarray(twiddles)),
        jnp.asarray(np.stack([sorting, sorting.T]).astype(jnp.bfloat16)),
    )


def list_patterns(dims, pos_ref, me_ref, ys_ref, xs_ref, slots_ref):
    tile_rows, tile_cols, pat_count, col_count, capacity = dims
    my_row, my_col = me_ref[0], me_ref[1]
    band_count = pat_count * col_count
    first = my_row * band_count
    total = pos_ref.shape[0] // 2

    def visit(index, carry):
        found, source, rank = carry
        y = pos_ref[first + index]
        x = pos_ref[total + first + index]
        here = lax.div(x, tile_cols) == my_col
        holder = lax.div(index, pat_count)
        rank = jnp.where(holder == source, rank, 0)

        @pl.when(here & (found < capacity))
        def _():
            ys_ref[found] = y - my_row * tile_rows
            xs_ref[found] = x - my_col * tile_cols
            slots_ref[found] = holder * SEND + jnp.minimum(rank, SEND - 1)

        step = here.astype(jnp.int32)
        return found + step, holder, rank + step

    found, _, _ = lax.fori_loop(0, band_count, visit, (jnp.int32(0), jnp.int32(-1), jnp.int32(0)))
    return jnp.minimum(found, capacity)


def lane_index(rows):
    return lax.broadcasted_iota(jnp.int32, (rows, LANES), 1)


def shifted_left(tiles, shift):
    lane = lane_index(tiles[0].shape[0])
    turn = lax.rem(LANES - shift, LANES)
    rolled = [pltpu.roll(tile, turn, axis=1) for tile in tiles]
    inside = lane < LANES - shift
    return [jnp.where(inside, a, b) for a, b in zip(rolled[:-1], rolled[1:])]


def shifted_right(tiles, shift):
    lane = lane_index(tiles[0].shape[0])
    rolled = [pltpu.roll(tile, shift, axis=1) for tile in tiles]
    outside = lane < shift
    zero = jnp.zeros_like(rolled[0])
    firsts = [zero] + rolled
    seconds = rolled + [zero]
    return [jnp.where(outside, a, b) for a, b in zip(firsts, seconds)]


def row_groups(tile):
    return [tile[k : k + SUBLANES] for k in range(0, tile.shape[0], SUBLANES)]


def shifted_up(tile, shift):
    row = lax.broadcasted_iota(jnp.int32, (SUBLANES, LANES), 0)
    turn = lax.rem(SUBLANES - shift, SUBLANES)
    rolled = [pltpu.roll(group, turn, axis=0) for group in row_groups(tile)]
    inside = row < SUBLANES - shift
    return jnp.concatenate([jnp.where(inside, a, b) for a, b in zip(rolled[:-1], rolled[1:])], axis=0)


def shifted_down(before, tile, shift):
    row = lax.broadcasted_iota(jnp.int32, (SUBLANES, LANES), 0)
    rolled = [before] + [pltpu.roll(group, shift, axis=0) for group in row_groups(tile)]
    outside = row < shift
    return rolled[-1], jnp.concatenate([jnp.where(outside, a, b) for a, b in zip(rolled[:-1], rolled[1:])], axis=0)


class Deposit:
    def __init__(self, add, top, left):
        self.add = add
        self.row = pl.multiple_of(lax.div(top, SUBLANES) * SUBLANES, SUBLANES)
        self.col = pl.multiple_of(lax.div(left, LANES) * LANES, LANES)
        self.down = lax.rem(top, SUBLANES)
        self.right = lax.rem(left, LANES)
        self.carried = None

    def place(self, first, tiles):
        moved = jnp.concatenate(shifted_right(tiles, self.right), axis=1)
        self.add(pl.ds(self.row + first, tiles[0].shape[0]), pl.ds(self.col, moved.shape[1]), moved)

    def put(self, first, tiles):
        if self.carried is None:
            self.carried = [jnp.zeros((SUBLANES, LANES), f32) for _ in tiles]
        pairs = [shifted_down(before, tile, self.down) for before, tile in zip(self.carried, tiles)]
        self.carried = [carried for carried, _ in pairs]
        self.place(first, [tile for _, tile in pairs])

    def finish(self, first):
        row = lax.broadcasted_iota(jnp.int32, (SUBLANES, LANES), 0)
        self.place(first, [jnp.where(row < self.down, tile, 0.0) for tile in self.carried])


def lane_tiles(value):
    return [value[:, k : k + LANES] for k in range(0, value.shape[1], LANES)]


def store_split(ref, rows, cols, value):
    high = value.astype(bf16)
    ref[0, rows, cols] = high
    ref[1, rows, cols] = (value - high.astype(f32)).astype(bf16)


def right_dot(x_ref, table_ref):
    left = jnp.concatenate([x_ref[0], x_ref[1], x_ref[0]], axis=1)
    right = jnp.concatenate([table_ref[0], table_ref[0], table_ref[1]], axis=0)
    return jnp.dot(left, right, preferred_element_type=f32)


def left_dot(table_ref, x_ref):
    left = jnp.concatenate([table_ref[0], table_ref[0], table_ref[1]], axis=1)
    right = jnp.concatenate([x_ref[0], x_ref[1], x_ref[0]], axis=0)
    return jnp.dot(left, right, preferred_element_type=f32)


def repeated(group, rows):
    return jnp.concatenate([group] * (rows // SUBLANES), axis=0)


def encode(read, out_ref, rows, first, last):
    for col in range(0, out_ref.shape[1], LANES):
        cols = pl.ds(col, LANES)
        largest = jnp.full((SUBLANES, LANES), 1e-30, f32)
        for start in range(0, rows, CHUNK):
            for comp in range(2):
                for group in row_groups(jnp.abs(read(comp, pl.ds(start, CHUNK), cols))):
                    largest = jnp.maximum(largest, group)
        exponent = jnp.ceil(jnp.log2(largest))
        out_ref[last : last + SUBLANES, cols] = exponent.astype(jnp.int32)
        scale = repeated(jnp.exp2(-exponent) * LEVELS, CHUNK)
        for start in range(0, rows, CHUNK):
            codes = []
            for comp in range(2):
                scaled = jnp.clip(read(comp, pl.ds(start, CHUNK), cols) * scale, -LEVELS, LEVELS)
                codes.append(jnp.round(scaled).astype(jnp.int32))
            out_ref[pl.ds(first + start, CHUNK), cols] = (codes[0] << 16) | (codes[1] & 0xFFFF)


def decode(ref, start, last, col):
    cols = pl.ds(col, LANES)
    words = ref[pl.ds(start, CHUNK), cols]
    scale = repeated(jnp.exp2(ref[last : last + SUBLANES, cols].astype(f32)) * (1.0 / LEVELS), CHUNK)
    return (words >> 16).astype(f32) * scale, ((words << 16) >> 16).astype(f32) * scale


def largest_exponent(values):
    largest = jnp.full((SUBLANES, LANES), 1e-30, f32)
    for value in values:
        for group in row_groups(jnp.abs(value)):
            largest = jnp.maximum(largest, group)
    return jnp.ceil(jnp.log2(largest))


def fixed(value, exponent):
    scaled = value * repeated(jnp.exp2(-exponent) * LEVELS, value.shape[0])
    return jnp.round(jnp.clip(scaled, -LEVELS, LEVELS)).astype(jnp.int32)


def paired(first, second):
    return (first << 16) | (second & 0xFFFF)


def unpaired(words):
    return words >> 16, (words << 16) >> 16


def scaled_back(codes, exponent):
    return codes.astype(f32) * repeated(jnp.exp2(exponent.astype(f32)) * (1.0 / LEVELS), codes.shape[0])


def sums_rows(rows):
    return rows + rows // 2 + SUBLANES


def encode_sums(out_ref, cols, u_re, u_im, v):
    rows = v.shape[0]
    half = rows // 2
    of_u, of_v = largest_exponent([u_re, u_im]), largest_exponent([v])
    out_ref[0:rows, cols] = paired(fixed(u_re, of_u), fixed(u_im, of_u))
    codes = fixed(v, of_v)
    out_ref[rows : rows + half, cols] = paired(codes[:half], codes[half:])
    out_ref[rows + half : rows + half + SUBLANES, cols] = paired(of_u.astype(jnp.int32), of_v.astype(jnp.int32))


def decode_sums(ref, cols, rows):
    half = rows // 2
    of_u, of_v = unpaired(ref[rows + half : rows + half + SUBLANES, cols])
    u_re, u_im = unpaired(ref[0:rows, cols])
    v = jnp.concatenate(unpaired(ref[rows : rows + half, cols]), axis=0)
    return scaled_back(u_re, of_u), scaled_back(u_im, of_u), scaled_back(v, of_v)


def decode_probe(out_ref, chunks_ref):
    chunks = chunks_ref.shape[0]
    rows = out_ref.shape[1] // chunks
    for chunk in range(chunks):
        for col in range(0, out_ref.shape[2], LANES):
            cols = pl.ds(col, LANES)
            exponent = chunks_ref[chunk, rows : rows + SUBLANES, cols]
            for comp, codes in enumerate(unpaired(chunks_ref[chunk, 0:rows, cols])):
                out_ref[comp, chunk * rows : (chunk + 1) * rows, cols] = scaled_back(codes, exponent)


def cut_chunk(ext_ref, comp, first, top, left, rows):
    row = pl.multiple_of(lax.div(top, SUBLANES) * SUBLANES, SUBLANES)
    col = pl.multiple_of(lax.div(left, LANES) * LANES, LANES)
    block = ext_ref[comp, pl.ds(row + first, rows + SUBLANES), pl.ds(col, 3 * LANES)]
    tiles = shifted_left(lane_tiles(block), lax.rem(left, LANES))
    return [shifted_up(tile, lax.rem(top, SUBLANES)) for tile in tiles]


def forward(order, ext_ref, probe_ref, consts, y, x, win_ref, power_ref, weight, xa_ref, xb_ref, ya_ref, yb_ref, far_ref):
    turns, twiddles = consts
    half = order // 2
    tw_re = repeated(twiddles[0, half : half + SUBLANES, :], CHUNK)
    tw_im = repeated(twiddles[1, half : half + SUBLANES, :], CHUNK)
    for first in range(0, order, CHUNK):
        rows = pl.ds(first, CHUNK)
        win_re = cut_chunk(ext_ref, 0, first, y, x, CHUNK)
        win_im = cut_chunk(ext_ref, 1, first, y, x, CHUNK)
        exits = []
        for k in range(2):
            cols = pl.ds(k * half, half)
            win_ref[0, rows, cols] = win_re[k]
            win_ref[1, rows, cols] = win_im[k]
            power_ref[rows, cols] += weight * (win_re[k] * win_re[k] + win_im[k] * win_im[k])
            p_re, p_im = probe_ref[0, rows, cols], probe_ref[1, rows, cols]
            exits.append((p_re * win_re[k] - p_im * win_im[k], p_re * win_im[k] + p_im * win_re[k]))
        (lo_re, lo_im), (hi_re, hi_im) = exits
        store_split(xa_ref, rows, pl.ds(0, half), lo_re + hi_re)
        store_split(xa_ref, rows, pl.ds(half, half), lo_im + hi_im)
        d_re, d_im = lo_re - hi_re, lo_im - hi_im
        store_split(xb_ref, rows, pl.ds(0, half), d_re * tw_re - d_im * tw_im)
        store_split(xb_ref, rows, pl.ds(half, half), d_re * tw_im + d_im * tw_re)
    yield
    ya_ref[...] = right_dot(xa_ref, turns.at[0])
    yb_ref[...] = right_dot(xb_ref, turns.at[0])
    yield
    for first in range(0, half, CHUNK):
        rows = pl.ds(first, CHUNK)
        below = pl.ds(half + first, CHUNK)
        t_re, t_im = twiddles[0, rows, :], twiddles[1, rows, :]
        for k, y_ref in enumerate((ya_ref, yb_ref)):
            cols = pl.ds(k * half, half)
            up_re, up_im = y_ref[rows, 0:half], y_ref[rows, half:order]
            dn_re, dn_im = y_ref[below, 0:half], y_ref[below, half:order]
            store_split(xa_ref, rows, cols, up_re + dn_re)
            store_split(xa_ref, below, cols, up_im + dn_im)
            d_re, d_im = up_re - dn_re, up_im - dn_im
            store_split(xb_ref, rows, cols, d_re * t_re - d_im * t_im)
            store_split(xb_ref, below, cols, d_re * t_im + d_im * t_re)
    yield
    far_ref[0] = left_dot(turns.at[1], xa_ref)
    far_ref[1] = left_dot(turns.at[1], xb_ref)
    yield


def backward(order, far_ref, amp_ref, consts, y, x, weight, probe_ref, win_ref, xa_ref, xb_ref, ya_ref, yb_ref, grad_ref, numer_ref):
    turns, twiddles = consts
    half = order // 2
    tw_re = repeated(twiddles[0, half : half + SUBLANES, :], CHUNK)
    tw_im = repeated(twiddles[1, half : half + SUBLANES, :], CHUNK)
    for k, x_ref in enumerate((xa_ref, xb_ref)):
        for first in range(0, half, CHUNK):
            rows = pl.ds(first, CHUNK)
            below = pl.ds(half + first, CHUNK)
            far_re, far_im = far_ref[k, rows, :], far_ref[k, below, :]
            amp = amp_ref[pl.ds(k * half + first, CHUNK), :].astype(f32)
            factor = amp * lax.rsqrt(far_re * far_re + far_im * far_im + amplitude_floor)
            store_split(x_ref, rows, slice(None), far_re * factor)
            store_split(x_ref, below, slice(None), far_im * factor)
    yield
    ya_ref[...] = left_dot(turns.at[0], xa_ref)
    yb_ref[...] = left_dot(turns.at[0], xb_ref)
    yield
    for first in range(0, half, CHUNK):
        rows = pl.ds(first, CHUNK)
        below = pl.ds(half + first, CHUNK)
        t_re, t_im = twiddles[0, rows, :], twiddles[1, rows, :]
        for k, x_ref in enumerate((xa_ref, xb_ref)):
            cols = slice(k * half, (k + 1) * half)
            a_re, a_im = ya_ref[rows, cols], ya_ref[below, cols]
            b_re, b_im = yb_ref[rows, cols], yb_ref[below, cols]
            c_re, c_im = b_re * t_re + b_im * t_im, b_im * t_re - b_re * t_im
            store_split(x_ref, rows, pl.ds(0, half), a_re + c_re)
            store_split(x_ref, rows, pl.ds(half, half), a_im + c_im)
            store_split(x_ref, below, pl.ds(0, half), a_re - c_re)
            store_split(x_ref, below, pl.ds(half, half), a_im - c_im)
    yield
    ya_ref[...] = right_dot(xa_ref, turns.at[1])
    yb_ref[...] = right_dot(xb_ref, turns.at[1])
    yield

    def adder(comp):
        def add(rows, cols, moved):
            grad_ref[comp, rows, cols] += moved

        return add

    deposits = [Deposit(adder(comp), y, x) for comp in range(2)]
    for first in range(0, order, CHUNK):
        rows = pl.ds(first, CHUNK)
        a_re, a_im = ya_ref[rows, 0:half], ya_ref[rows, half:order]
        b_re, b_im = yb_ref[rows, 0:half], yb_ref[rows, half:order]
        c_re, c_im = b_re * tw_re + b_im * tw_im, b_im * tw_re - b_re * tw_im
        waves = [(a_re + c_re, a_im + c_im), (a_re - c_re, a_im - c_im)]
        terms = ([], [])
        for k, (wave_re, wave_im) in enumerate(waves):
            cols = pl.ds(k * half, half)
            wave_re, wave_im = weight * wave_re, weight * wave_im
            p_re, p_im = probe_ref[0, rows, cols], probe_ref[1, rows, cols]
            w_re, w_im = win_ref[0, rows, cols], win_ref[1, rows, cols]
            terms[0].append(p_re * wave_re + p_im * wave_im)
            terms[1].append(p_re * wave_im - p_im * wave_re)
            numer_ref[0, rows, cols] += w_re * wave_re + w_im * wave_im
            numer_ref[1, rows, cols] += w_re * wave_im - w_im * wave_re
        for comp in range(2):
            deposits[comp].put(first, terms[comp])
    for deposit in deposits:
        deposit.finish(order)
    yield


def interleaved(*stages):
    live = list(stages)
    while live:
        still = []
        for stage in live:
            try:
                next(stage)
                still.append(stage)
            except StopIteration:
                pass
        live = still


def outgoing_kernel(dims, pos_ref, me_ref, amp_ref, after_ref, also_ref, out_ref, sems):
    tile_rows, tile_cols, pat_count, col_count, capacity = dims
    first = (me_ref[0] * col_count + me_ref[1]) * pat_count
    total = pos_ref.shape[0] // 2
    owners = [lax.div(pos_ref[total + first + k], tile_cols) for k in range(pat_count)]
    copies = []
    for k in range(pat_count):
        rank = sum(((owners[e] == owners[k]).astype(jnp.int32) for e in range(k)), jnp.int32(0))
        slot = owners[k] * SEND + jnp.minimum(rank, SEND - 1)
        copies.append(pltpu.make_async_copy(amp_ref.at[k], out_ref.at[slot], sems.at[k]))
        copies[-1].start()
    for copy in copies:
        copy.wait()


def weights_kernel(dims, span, pos_ref, me_ref, probe_ref, out_ref, sums_ref, power_ref):
    tile_rows, tile_cols, pat_count, col_count, capacity = dims
    order = probe_ref.shape[1]
    top = (me_ref[0] - 1) * tile_rows
    left = (me_ref[1] - 1) * tile_cols
    total = pos_ref.shape[0] // 2
    for first in range(0, sums_ref.shape[0], order):
        sums_ref[pl.ds(first, order), :] = jnp.zeros((order, sums_ref.shape[1]), f32)
    power_ref[...] = probe_ref[0] * probe_ref[0] + probe_ref[1] * probe_ref[1]

    def visit(index, carry):
        y = pos_ref[index] - top
        x = pos_ref[total + index] - left

        @pl.when((y > 0) & (y < (span + 1) * tile_rows) & (x > 0) & (x < (span + 1) * tile_cols))
        def _():
            def add(rows, cols, moved):
                sums_ref[rows, cols] += moved

            deposit = Deposit(add, y, x)
            for first in range(0, order, CHUNK):
                deposit.put(first, lane_tiles(power_ref[pl.ds(first, CHUNK), :]))
            deposit.finish(order)

        return carry

    lax.fori_loop(0, total, visit, 0)
    pltpu.sync_copy(sums_ref.at[pl.ds(tile_rows, span * tile_rows), pl.ds(tile_cols, span * tile_cols)], out_ref)


def encode_kernel(obj_ref, out_ref):
    rows = obj_ref.shape[1]
    encode(lambda comp, at, cols: obj_ref[comp, at, cols], out_ref, rows, 0, rows)


def unfold(dims, ext_ref, own_ref, coded_refs):
    tile_rows, tile_cols = dims[:2]
    ext_ref[:, 0:tile_rows, 0:tile_cols] = own_ref[...]
    for (i, j), ref in zip(((0, 1), (1, 0), (1, 1)), coded_refs):
        for col in range(0, tile_cols, LANES):
            for start in range(0, tile_rows, CHUNK):
                parts = decode(ref, start, tile_rows, col)
                for comp in range(2):
                    ext_ref[comp, pl.ds(i * tile_rows + start, CHUNK), pl.ds(j * tile_cols + col, LANES)] = parts[comp]


def spread_sums(out_ref, u_ref, v_ref):
    chunks = out_ref.shape[0]
    rows = v_ref.shape[0] // chunks
    for chunk in range(chunks):
        at = pl.ds(chunk * rows, rows)
        for col in range(0, v_ref.shape[1], LANES):
            cols = pl.ds(col, LANES)
            encode_sums(out_ref.at[chunk], cols, u_ref[0, at, cols], u_ref[1, at, cols], v_ref[at, cols])


def added(parts):
    while len(parts) > 1:
        parts = [tuple(x + y for x, y in zip(a, b)) for a, b in zip(parts[::2], parts[1::2])]
    return parts[0]


def sums_kernel(rows, parts_ref, *refs):
    out_ref = refs[-1]
    for col in range(0, out_ref.shape[2], LANES):
        cols = pl.ds(col, LANES)
        total = added([decode_sums(parts_ref.at[k], cols, rows) for k in range(parts_ref.shape[0])])
        encode_sums(out_ref.at[0], cols, *total)
        for k in range(1, out_ref.shape[0]):
            out_ref[k, :, cols] = out_ref[0, :, cols]


def update_kernel(rows, me_ref, probe_ref, parts_ref, *refs):
    out_ref = refs[-1]
    first = pl.multiple_of(me_ref[1] * rows, SUBLANES)
    for col in range(0, out_ref.shape[2], LANES):
        cols = pl.ds(col, LANES)
        u_re, u_im, v = added([decode_sums(parts_ref.at[k], cols, rows) for k in range(parts_ref.shape[0])])
        scale = 1.0 / (v + probe_regular)
        re = (probe_ref[0, pl.ds(first, rows), cols] + u_re) * scale
        im = (probe_ref[1, pl.ds(first, rows), cols] + u_im) * scale
        exponent = largest_exponent([re, im])
        words = paired(fixed(re, exponent), fixed(im, exponent))
        for chunk in range(out_ref.shape[0]):
            out_ref[chunk, 0:rows, cols] = words
            out_ref[chunk, rows : rows + SUBLANES, cols] = exponent.astype(jnp.int32)


def probe_kernel(chunks_ref, out_ref):
    decode_probe(out_ref, chunks_ref)


def first_half_kernel(dims, pos_ref, me_ref, own_ref, right_ref, below_ref, diag_ref, probe_ref, turns, twiddles,
                      far_out, power_out, ext_out, ext_ref, win_ref, xa_ref, xb_ref, ya_ref, yb_ref, far_ref, ys_ref, xs_ref, slots_ref, sems, ext_sem):
    tile_rows, tile_cols, pat_count, col_count, capacity = dims
    order = probe_ref.shape[1]
    count = list_patterns(dims, pos_ref, me_ref, ys_ref, xs_ref, slots_ref)
    unfold(dims, ext_ref, own_ref, (right_ref, below_ref, diag_ref))
    keep = pltpu.make_async_copy(ext_ref, ext_out, ext_sem)
    keep.start()
    power_out[...] = jnp.zeros_like(power_out)
    consts = (turns, twiddles)

    def pair(step, carry):
        stages = []
        for k in range(2):
            listed = 2 * step + k
            weight = (listed < count).astype(f32)
            index = jnp.minimum(listed, count - 1)
            stages.append(forward(order, ext_ref, probe_ref, consts, ys_ref[index], xs_ref[index], win_ref.at[k], power_out, weight,
                                  xa_ref.at[k], xb_ref.at[k], ya_ref.at[k], yb_ref.at[k], far_ref.at[listed]))
        interleaved(*stages)
        for k in range(2):
            listed = 2 * step + k
            pltpu.make_async_copy(far_ref.at[listed], far_out.at[listed], sems.at[listed]).start()
        return carry

    pairs = lax.div(count + 1, 2)
    lax.fori_loop(0, pairs, pair, 0)

    def settle(listed, carry):
        pltpu.make_async_copy(far_ref.at[listed], far_out.at[listed], sems.at[listed]).wait()
        return carry

    lax.fori_loop(0, 2 * pairs, settle, 0)
    keep.wait()


def second_half_kernel(dims, pos_ref, me_ref, ext_ref, probe_ref, power_ref, weights_ref, far_in, amp_in, turns, twiddles, sorting,
                       share_out, numer_out, amp_out,
                       sum_ref, win_ref, xa_ref, xb_ref, ya_ref, yb_ref, numer_ref, far_ref, amp_ref, sorted_ref, ys_ref, xs_ref, slots_ref, far_sems, amp_sems, out_sems, sum_sem):
    tile_rows, tile_cols, pat_count, col_count, capacity = dims
    order = probe_ref.shape[1]
    half = order // 2
    count = list_patterns(dims, pos_ref, me_ref, ys_ref, xs_ref, slots_ref)
    pairs = lax.div(count + 1, 2)

    def copies(listed):
        return (
            pltpu.make_async_copy(far_in.at[listed], far_ref.at[listed], far_sems.at[listed]),
            pltpu.make_async_copy(amp_in.at[slots_ref[jnp.minimum(listed, count - 1)]], amp_ref.at[listed], amp_sems.at[listed]),
        )

    def begin(listed, carry):
        for copy in copies(listed):
            copy.start()
        return carry

    lax.fori_loop(0, 2 * pairs, begin, 0)
    sum_ref[...] = jnp.zeros_like(sum_ref)
    numer_ref[...] = jnp.zeros_like(numer_ref)
    consts = (turns, twiddles)

    def pair(step, carry):
        stages = []
        for k in range(2):
            listed = 2 * step + k
            for copy in copies(listed):
                copy.wait()
        for k in range(2):
            listed = 2 * step + k
            weight = (listed < count).astype(f32)
            index = jnp.minimum(listed, count - 1)
            y, x = ys_ref[index], xs_ref[index]
            rows_sorted = jnp.dot(sorting[0], amp_ref[listed], preferred_element_type=f32).astype(bf16)
            sorted_ref[listed] = jnp.dot(rows_sorted, sorting[1], preferred_element_type=f32).astype(bf16)
            for first in range(0, order, CHUNK):
                for comp in range(2):
                    for c, tile in enumerate(cut_chunk(ext_ref, comp, first, y, x, CHUNK)):
                        win_ref[k, comp, pl.ds(first, CHUNK), pl.ds(c * half, half)] = tile
            stages.append(backward(order, far_ref.at[listed], sorted_ref.at[listed], consts, y, x, weight, probe_ref, win_ref.at[k],
                                   xa_ref.at[k], xb_ref.at[k], ya_ref.at[k], yb_ref.at[k], sum_ref, numer_ref))
        interleaved(*stages)
        for k in range(2):
            listed = 2 * step + k
            pltpu.make_async_copy(sorted_ref.at[listed], amp_out.at[listed], out_sems.at[listed]).start()
        return carry

    lax.fori_loop(0, pairs, pair, 0)
    for first in range(0, 2 * tile_rows, CHUNK):
        rows = pl.ds(first, CHUNK)
        scale = 1.0 / (weights_ref[rows, :] + object_regular)
        for comp in range(2):
            sum_ref[comp, rows, :] = sum_ref[comp, rows, :] * scale
    keep = pltpu.make_async_copy(sum_ref, share_out, sum_sem)
    keep.start()
    spread_sums(numer_out, numer_ref, power_ref)

    def settle(listed, carry):
        pltpu.make_async_copy(sorted_ref.at[listed], amp_out.at[listed], out_sems.at[listed]).wait()
        return carry

    lax.fori_loop(0, 2 * pairs, settle, 0)
    keep.wait()


def rows_code_kernel(dims, share_ref, top_out, bottom_out):
    tile_rows = dims[0]
    encode(lambda comp, at, cols: share_ref[comp, at, cols], top_out, tile_rows, 0, tile_rows)
    encode(lambda comp, at, cols: share_ref[comp, pl.ds(tile_rows + at.start, at.size), cols], bottom_out, tile_rows, 0, tile_rows)


def rows_sum_kernel(dims, share_ref, above_ref, below_ref, after_ref, sum_out, left_out, right_out):
    tile_rows, tile_cols = dims[:2]
    for i, ref in enumerate((above_ref, below_ref)):
        for col in range(0, 2 * tile_cols, LANES):
            for start in range(0, tile_rows, CHUNK):
                rows, cols = pl.ds(i * tile_rows + start, CHUNK), pl.ds(col, LANES)
                parts = decode(ref, start, tile_rows, col)
                for comp in range(2):
                    sum_out[comp, rows, cols] = share_ref[comp, rows, cols] + parts[comp]
    for j, ref in enumerate((left_out, right_out)):
        for i in range(2):

            def read(comp, at, cols, i=i, j=j):
                return sum_out[comp, pl.ds(i * tile_rows + at.start, at.size), pl.ds(j * tile_cols + cols.start, cols.size)]

            encode(read, ref, tile_rows, i * tile_rows, 2 * tile_rows + i * SUBLANES)


def whole_kernel(dims, pos_ref, me_ref, old_ref, sum_ref, from_left_ref, from_right_ref, weights_ref,
                 chunks_ref, amp_in, turns, twiddles,
                 current_out, top_out, bottom_out, numer_out, probe_ref,
                 ext_ref, grad_ref, win_ref, xa_ref, xb_ref, ya_ref, yb_ref, numer_ref, far_ref, amp_ref, ys_ref, xs_ref, slots_ref, amp_sems, own_sem, top_sem):
    tile_rows, tile_cols, pat_count, col_count, capacity = dims
    order = probe_ref.shape[1]
    count = list_patterns(dims, pos_ref, me_ref, ys_ref, xs_ref, slots_ref)
    pairs = lax.div(count + 1, 2)
    decode_probe(probe_ref, chunks_ref)

    def fetch(listed):
        return pltpu.make_async_copy(amp_in.at[jnp.minimum(listed, count - 1)], amp_ref.at[listed], amp_sems.at[listed])

    def begin(listed, carry):
        fetch(listed).start()
        return carry

    lax.fori_loop(0, 2 * pairs, begin, 0)
    for j, ref in enumerate((from_left_ref, from_right_ref)):
        for i in range(2):
            for col in range(0, tile_cols, LANES):
                for start in range(0, tile_rows, CHUNK):
                    rows, cols = pl.ds(i * tile_rows + start, CHUNK), pl.ds(j * tile_cols + col, LANES)
                    parts = decode(ref, i * tile_rows + start, 2 * tile_rows + i * SUBLANES, col)
                    scale = object_regular / (weights_ref[rows, cols] + object_regular)
                    for comp in range(2):
                        ext_ref[comp, rows, cols] = old_ref[comp, rows, cols] * scale + (sum_ref[comp, rows, cols] + parts[comp])
    keep = pltpu.make_async_copy(ext_ref.at[:, pl.ds(0, tile_rows), pl.ds(0, tile_cols)], current_out, own_sem)
    keep.start()
    grad_ref[...] = jnp.zeros_like(grad_ref)
    numer_ref[...] = jnp.zeros_like(numer_ref)
    consts = (turns, twiddles)

    def pair(step, carry):
        stages = []
        for k in range(2):
            fetch(2 * step + k).wait()
        for k in range(2):
            listed = 2 * step + k
            weight = (listed < count).astype(f32)
            index = jnp.minimum(listed, count - 1)
            y, x = ys_ref[index], xs_ref[index]

            def both(k=k, listed=listed, weight=weight, y=y, x=x):
                yield from forward(order, ext_ref, probe_ref, consts, y, x, win_ref.at[k], numer_ref.at[2], weight,
                                   xa_ref.at[k], xb_ref.at[k], ya_ref.at[k], yb_ref.at[k], far_ref.at[k])
                yield from backward(order, far_ref.at[k], amp_ref.at[listed], consts, y, x, weight, probe_ref, win_ref.at[k],
                                    xa_ref.at[k], xb_ref.at[k], ya_ref.at[k], yb_ref.at[k], grad_ref, numer_ref)

            stages.append(both())
        interleaved(*stages)
        return carry

    lax.fori_loop(0, pairs, pair, 0)
    for first in range(0, tile_rows, CHUNK):
        rows = pl.ds(first, CHUNK)
        scale = 1.0 / (weights_ref[rows, :] + object_regular)
        for comp in range(2):
            grad_ref[comp, rows, :] = grad_ref[comp, rows, :] * scale
    give = pltpu.make_async_copy(grad_ref.at[:, pl.ds(0, tile_rows), :], top_out, top_sem)
    give.start()

    def read(comp, at, cols):
        rows = pl.ds(tile_rows + at.start, at.size)
        return grad_ref[comp, rows, cols] / (weights_ref[rows, cols] + object_regular)

    encode(read, bottom_out, tile_rows, 0, tile_rows)
    spread_sums(numer_out, numer_ref, numer_ref.at[2])
    keep.wait()
    give.wait()


def fold_kernel(dims, top_ref, above_ref, own_out, right_out, own_ref, sem):
    tile_rows, tile_cols = dims[:2]
    for col in range(0, 2 * tile_cols, LANES):
        for start in range(0, tile_rows, CHUNK):
            rows, cols = pl.ds(start, CHUNK), pl.ds(col, LANES)
            parts = decode(above_ref, start, tile_rows, col)
            for comp in range(2):
                if col < tile_cols:
                    own_ref[comp, rows, cols] = top_ref[comp, rows, cols] + parts[comp]
                else:
                    top_ref[comp, rows, cols] += parts[comp]
    keep = pltpu.make_async_copy(own_ref, own_out, sem)
    keep.start()
    encode(lambda comp, at, cols: top_ref[comp, at, pl.ds(tile_cols + cols.start, cols.size)], right_out, tile_rows, 0, tile_rows)
    keep.wait()


def object_kernel(dims, current_ref, own_ref, left_ref, before_ref, weights_ref, out_ref):
    tile_rows, tile_cols = dims[:2]
    for col in range(0, tile_cols, LANES):
        for start in range(0, tile_rows, CHUNK):
            rows, cols = pl.ds(start, CHUNK), pl.ds(col, LANES)
            scale = 1.0 / (weights_ref[rows, cols] + object_regular)
            back = (before_ref[rows, cols] + object_regular) * scale
            parts = decode(left_ref, start, tile_rows, col)
            for comp in range(2):
                old = object_regular * scale * current_ref[comp, rows, cols]
                out_ref[comp, rows, cols] = old + (own_ref[comp, rows, cols] + parts[comp]) * back


def shape(dims, dtype=f32):
    return jax.ShapeDtypeStruct(dims, dtype)


def work_scratch(order):
    return [
        pltpu.VMEM((2, 2, order, order), f32),
        pltpu.VMEM((2, 2, order, order), bf16),
        pltpu.VMEM((2, 2, order, order), bf16),
        pltpu.VMEM((2, order, order), f32),
        pltpu.VMEM((2, order, order), f32),
    ]


def list_scratch(capacity):
    return [pltpu.SMEM((capacity,), jnp.int32)] * 3


def call(kernel, outs, out_specs, in_specs, scratch, flops, limit=26 << 20):
    several = isinstance(outs, tuple)
    out_count = len(outs) if several else 1
    in_count = len(in_specs)
    loaded = [k for k, spec in enumerate(in_specs) if spec is LOAD]

    def body(*refs):
        ins, rest = list(refs[:in_count]), refs[in_count:]
        given, kept = rest[: out_count + len(scratch)], rest[out_count + len(scratch) :]
        copies = [pltpu.make_async_copy(ins[k], kept[n], kept[-1].at[n]) for n, k in enumerate(loaded)]
        for copy in copies:
            copy.start()
        for n, k in enumerate(loaded):
            copies[n].wait()
            ins[k] = kept[n]
        kernel(*ins, *given)

    fixed_outs = [
        pltpu.HBM(out.shape, out.dtype) if spec is HBM else pltpu.VMEM(out.shape, out.dtype) if spec is PIN else out
        for out, spec in zip(outs if several else (outs,), out_specs if several else (out_specs,))
    ]
    places = [pltpu.HBM if spec is LOAD or spec is HBM else pltpu.VMEM if spec is PIN else None for spec in in_specs]

    def called(*args):
        args = [arg if place is None else pltpu.with_memory_space_constraint(arg, place) for arg, place in zip(args, places)]
        own = [pltpu.VMEM(args[k].shape, args[k].dtype) for k in loaded]
        if loaded:
            own.append(pltpu.SemaphoreType.DMA((len(loaded),)))
        return pl.pallas_call(
            body,
            out_shape=tuple(fixed_outs) if several else fixed_outs[0],
            out_specs=out_specs,
            in_specs=[HBM if spec is LOAD else spec for spec in in_specs],
            scratch_shapes=list(scratch) + own,
            compiler_params=pltpu.CompilerParams(vmem_limit_bytes=limit),
            cost_estimate=pl.CostEstimate(flops=flops, bytes_accessed=8 << 20, transcendentals=0),
        )(*args)

    return called


def passed_along(value, axis, steps):
    count = lax.axis_size(axis)
    leading, last = (max(0, -steps), min(count, count - steps))
    return lax.ppermute(value, axis, [(source, source + steps) for source in range(leading, last)])


def probe_update(me, probe, numer, kind, weights=None, fold=None):
    cols, order = lax.axis_size("col"), probe.shape[1]
    rows = order // cols
    before_sum = [] if weights is None else [weights]
    before_update = [] if fold is None else [fold]
    parts = lax.all_to_all(numer, "col", split_axis=0, concat_axis=0, tiled=True)
    total = call(
        functools.partial(sums_kernel, rows), shape((lax.axis_size("row"), sums_rows(rows), order), jnp.int32), VMEM,
        [VMEM] + [HBM] * len(before_sum), [], 1 << 26,
    )(parts, *before_sum)
    parts = lax.all_to_all(total, "row", split_axis=0, concat_axis=0, tiled=True)
    fresh = call(
        functools.partial(update_kernel, rows), shape((cols, rows + SUBLANES, order), jnp.int32), VMEM,
        [SMEM, kind, VMEM] + [FREE] * len(before_update), [], 1 << 26,
    )(me, probe, parts, *before_update)
    return total, lax.all_to_all(fresh, "col", split_axis=0, concat_axis=0, tiled=True)


def local(obj, probe, amplitudes, positions):
    col_count = lax.axis_size("col")
    tile_rows, tile_cols = obj.shape[1], obj.shape[2]
    order = probe.shape[1]
    pat_count = amplitudes.shape[0]
    capacity = 2 * pat_count
    dims = (tile_rows, tile_cols, pat_count, col_count, capacity)
    me = jnp.stack([lax.axis_index("row"), lax.axis_index("col")]).astype(jnp.int32)
    pos = positions.T.reshape(-1)
    turns, twiddles, sorting = tables(order)
    tile = (2, tile_rows, tile_cols)
    window = (2, order, order)
    wide = (2, 2 * tile_rows, 2 * tile_cols)
    shares = shape((col_count, sums_rows(order // col_count), order), jnp.int32)
    coded_tile = shape((tile_rows + SUBLANES, tile_cols), jnp.int32)
    coded_row = shape((tile_rows + SUBLANES, 2 * tile_cols), jnp.int32)
    coded_col = shape((2 * (tile_rows + SUBLANES), tile_cols), jnp.int32)
    one_pattern = 24 * 2 * order**3

    coded = call(encode_kernel, coded_tile, VMEM, [LOAD], [], 1 << 26)(obj)
    right = passed_along(coded, "col", -1)
    below = passed_along(coded, "row", -1)
    diag = passed_along(right, "row", -1)

    outgoing = call(
        functools.partial(outgoing_kernel, dims), shape((col_count * SEND, order, order), bf16), HBM, [SMEM, SMEM, LOAD, FREE, FREE],
        [pltpu.SemaphoreType.DMA((pat_count,))], 1 << 20,
    )(pos, me, amplitudes, right, below)
    incoming = lax.all_to_all(outgoing, "col", split_axis=0, concat_axis=0, tiled=True)

    def weights(probe_now, span, kind):
        return call(
            functools.partial(weights_kernel, dims, span), shape((span * tile_rows, span * tile_cols)), HBM, [SMEM, SMEM, kind],
            [pltpu.VMEM(((span + 2) * tile_rows, (span + 2) * tile_cols), f32), pltpu.VMEM((order, order), f32)], 8 << 30,
        )(pos, me, probe_now)

    weights_old = weights(probe, 2, LOAD)

    far, power, ext = call(
        functools.partial(first_half_kernel, dims), (shape((capacity,) + window), shape((order, order)), shape(wide)), (HBM, VMEM, HBM),
        [SMEM, SMEM, LOAD] + [VMEM] * 3 + [LOAD] * 3,
        [pltpu.VMEM(wide, f32)] + work_scratch(order) + [pltpu.VMEM((capacity,) + window, f32)] + list_scratch(capacity)
        + [pltpu.SemaphoreType.DMA((capacity,)), pltpu.SemaphoreType.DMA],
        capacity * one_pattern // 2,
    )(pos, me, obj, right, below, diag, probe, turns, twiddles)

    share, numer, sorted_amps = call(
        functools.partial(second_half_kernel, dims),
        (shape(wide), shares, shape((capacity, order, order), bf16)),
        (HBM, VMEM, HBM),
        [SMEM, SMEM, LOAD, LOAD, VMEM, LOAD, HBM, HBM] + [LOAD] * 3,
        [pltpu.VMEM(wide, f32)] + work_scratch(order)
        + [pltpu.VMEM(window, f32), pltpu.VMEM((capacity,) + window, f32), pltpu.VMEM((capacity, order, order), bf16), pltpu.VMEM((capacity, order, order), bf16)]
        + list_scratch(capacity) + [pltpu.SemaphoreType.DMA((capacity,))] * 3 + [pltpu.SemaphoreType.DMA],
        capacity * one_pattern // 2,
    )(pos, me, ext, probe, power, weights_old, far, incoming, turns, twiddles, sorting)

    top, bottom = call(functools.partial(rows_code_kernel, dims), (coded_row, coded_row), (VMEM, VMEM), [LOAD], [], 1 << 26)(share)
    from_above = passed_along(bottom, "row", 1)
    from_below = passed_along(top, "row", -1)
    total, chunks = probe_update(me, probe, numer, LOAD)
    sums, to_left, to_right = call(
        functools.partial(rows_sum_kernel, dims), (shape(wide), coded_col, coded_col), (PIN, VMEM, VMEM), [LOAD, VMEM, VMEM, FREE], [], 1 << 26,
    )(share, from_above, from_below, total)
    from_left = passed_along(to_right, "col", 1)
    from_right = passed_along(to_left, "col", -1)

    current, top, bottom, numer, probe_now = call(
        functools.partial(whole_kernel, dims), (shape(tile), shape((2, tile_rows, 2 * tile_cols)), coded_row, shares, shape(window)), (HBM, HBM) + (VMEM,) * 3,
        [SMEM, SMEM, LOAD, PIN, VMEM, VMEM, LOAD, VMEM, HBM, LOAD, LOAD],
        [pltpu.VMEM(wide, f32), pltpu.VMEM(wide, f32)] + work_scratch(order)
        + [pltpu.VMEM((3, order, order), f32), pltpu.VMEM((2,) + window, f32), pltpu.VMEM((capacity, order, order), bf16)]
        + list_scratch(capacity) + [pltpu.SemaphoreType.DMA((capacity,)), pltpu.SemaphoreType.DMA, pltpu.SemaphoreType.DMA],
        capacity * one_pattern,
    )(pos, me, ext, sums, from_left, from_right, weights_old, chunks, sorted_amps, turns, twiddles)

    from_above = passed_along(bottom, "row", 1)
    weights_new = weights(probe_now, 1, VMEM)
    own, to_right = call(
        functools.partial(fold_kernel, dims), (shape(tile), coded_tile), (HBM, VMEM), [LOAD, VMEM], [pltpu.VMEM(tile, f32), pltpu.SemaphoreType.DMA], 1 << 26,
    )(top, from_above)
    from_left = passed_along(to_right, "col", 1)
    new_object = call(functools.partial(object_kernel, dims), shape(tile), VMEM, [LOAD, LOAD, VMEM, LOAD, LOAD], [], 1 << 26)(
        current, own, from_left, weights_old, weights_new
    )
    _, chunks = probe_update(me, probe_now, numer, VMEM, weights_new, to_right)
    new_probe = call(probe_kernel, shape(window), VMEM, [VMEM], [], 1 << 26)(chunks)
    return new_object, new_probe


def solution(mesh):
    placed = (P(None, "row", "col"), P(), P(("row", "col"), None, None), P())
    return jax.shard_map(local, mesh=mesh, in_specs=placed, out_specs=(P(None, "row", "col"), P()), check_vma=False)
```

```python
import functools

import jax
import jax.numpy as jnp
import numpy as np
from jax import lax
from jax.experimental import pallas as pl
from jax.experimental.pallas import tpu as pltpu
from jax.sharding import PartitionSpec as P

ITERS = 2
SEND = 2

amplitude_floor = 0.1
object_regular = 0.5
probe_regular = 1.0

LANES = 128
SUBLANES = 8
LEVELS = 32767.0
CHUNK = 32
VMEM = pl.BlockSpec(memory_space=pltpu.VMEM)
SMEM = pl.BlockSpec(memory_space=pltpu.SMEM)
HBM = pl.BlockSpec(memory_space=pltpu.HBM)
LOAD = object()
FREE = pl.BlockSpec(memory_space=pl.ANY)
PIN = pl.BlockSpec(memory_space=pltpu.VMEM)
f32 = jnp.float32
bf16 = jnp.bfloat16


def tables(order):
    half = order // 2
    counter = np.arange(half)
    angles = 2.0 * np.pi * ((counter[:, None] * counter[None, :]) % half) / half
    cos, sin = np.cos(angles), np.sin(angles)
    scale = 1.0 / np.sqrt(order)
    turns = []
    for block in ([[cos, -sin], [sin, cos]], [[cos, sin], [-sin, cos]]):
        matrix = np.block(block) * scale
        high = matrix.astype(jnp.bfloat16)
        turns.append(np.stack([high, (matrix - high.astype(np.float64)).astype(jnp.bfloat16)]))
    turn = 2.0 * np.pi * counter / order
    twiddle = np.stack([np.cos(turn), -np.sin(turn)]).astype(np.float32)
    twiddles = np.concatenate(
        [np.broadcast_to(twiddle[:, :, None], (2, half, half)), np.broadcast_to(twiddle[:, None, :], (2, SUBLANES, half))], axis=1
    )
    sorting = np.zeros((order, order), np.float32)
    sorting[np.arange(half), 2 * np.arange(half)] = 1.0
    sorting[half + np.arange(half), 2 * np.arange(half) + 1] = 1.0
    return (
        jnp.asarray(np.stack(turns)),
        jnp.asarray(np.ascontiguousarray(twiddles)),
        jnp.asarray(np.stack([sorting, sorting.T]).astype(jnp.bfloat16)),
    )


def list_patterns(dims, pos_ref, me_ref, ys_ref, xs_ref, slots_ref):
    tile_rows, tile_cols, pat_count, col_count, capacity = dims
    my_row, my_col = me_ref[0], me_ref[1]
    band_count = pat_count * col_count
    first = my_row * band_count
    total = pos_ref.shape[0] // 2

    def visit(index, carry):
        found, source, rank = carry
        y = pos_ref[first + index]
        x = pos_ref[total + first + index]
        here = lax.div(x, tile_cols) == my_col
        holder = lax.div(index, pat_count)
        rank = jnp.where(holder == source, rank, 0)

        @pl.when(here & (found < capacity))
        def _():
            ys_ref[found] = y - my_row * tile_rows
            xs_ref[found] = x - my_col * tile_cols
            slots_ref[found] = holder * SEND + jnp.minimum(rank, SEND - 1)

        step = here.astype(jnp.int32)
        return found + step, holder, rank + step

    found, _, _ = lax.fori_loop(0, band_count, visit, (jnp.int32(0), jnp.int32(-1), jnp.int32(0)))
    return jnp.minimum(found, capacity)


def lane_index(rows):
    return lax.broadcasted_iota(jnp.int32, (rows, LANES), 1)


def shifted_left(tiles, shift):
    lane = lane_index(tiles[0].shape[0])
    turn = lax.rem(LANES - shift, LANES)
    rolled = [pltpu.roll(tile, turn, axis=1) for tile in tiles]
    inside = lane < LANES - shift
    return [jnp.where(inside, a, b) for a, b in zip(rolled[:-1], rolled[1:])]


def shifted_right(tiles, shift):
    lane = lane_index(tiles[0].shape[0])
    rolled = [pltpu.roll(tile, shift, axis=1) for tile in tiles]
    outside = lane < shift
    zero = jnp.zeros_like(rolled[0])
    firsts = [zero] + rolled
    seconds = rolled + [zero]
    return [jnp.where(outside, a, b) for a, b in zip(firsts, seconds)]


def row_groups(tile):
    return [tile[k : k + SUBLANES] for k in range(0, tile.shape[0], SUBLANES)]


def shifted_up(tile, shift):
    row = lax.broadcasted_iota(jnp.int32, (SUBLANES, LANES), 0)
    turn = lax.rem(SUBLANES - shift, SUBLANES)
    rolled = [pltpu.roll(group, turn, axis=0) for group in row_groups(tile)]
    inside = row < SUBLANES - shift
    return jnp.concatenate([jnp.where(inside, a, b) for a, b in zip(rolled[:-1], rolled[1:])], axis=0)


def shifted_down(before, tile, shift):
    row = lax.broadcasted_iota(jnp.int32, (SUBLANES, LANES), 0)
    rolled = [before] + [pltpu.roll(group, shift, axis=0) for group in row_groups(tile)]
    outside = row < shift
    return rolled[-1], jnp.concatenate([jnp.where(outside, a, b) for a, b in zip(rolled[:-1], rolled[1:])], axis=0)


class Deposit:
    def __init__(self, add, top, left):
        self.add = add
        self.row = pl.multiple_of(lax.div(top, SUBLANES) * SUBLANES, SUBLANES)
        self.col = pl.multiple_of(lax.div(left, LANES) * LANES, LANES)
        self.down = lax.rem(top, SUBLANES)
        self.right = lax.rem(left, LANES)
        self.carried = None

    def place(self, first, tiles):
        moved = jnp.concatenate(shifted_right(tiles, self.right), axis=1)
        self.add(pl.ds(self.row + first, tiles[0].shape[0]), pl.ds(self.col, moved.shape[1]), moved)

    def put(self, first, tiles):
        if self.carried is None:
            self.carried = [jnp.zeros((SUBLANES, LANES), f32) for _ in tiles]
        pairs = [shifted_down(before, tile, self.down) for before, tile in zip(self.carried, tiles)]
        self.carried = [carried for carried, _ in pairs]
        self.place(first, [tile for _, tile in pairs])

    def finish(self, first):
        row = lax.broadcasted_iota(jnp.int32, (SUBLANES, LANES), 0)
        self.place(first, [jnp.where(row < self.down, tile, 0.0) for tile in self.carried])


def lane_tiles(value):
    return [value[:, k : k + LANES] for k in range(0, value.shape[1], LANES)]


def store_split(ref, rows, cols, value):
    high = value.astype(bf16)
    ref[0, rows, cols] = high
    ref[1, rows, cols] = (value - high.astype(f32)).astype(bf16)


def right_dot(x_ref, table_ref):
    left = jnp.concatenate([x_ref[0], x_ref[1], x_ref[0]], axis=1)
    right = jnp.concatenate([table_ref[0], table_ref[0], table_ref[1]], axis=0)
    return jnp.dot(left, right, preferred_element_type=f32)


def left_dot(table_ref, x_ref):
    left = jnp.concatenate([table_ref[0], table_ref[0], table_ref[1]], axis=1)
    right = jnp.concatenate([x_ref[0], x_ref[1], x_ref[0]], axis=0)
    return jnp.dot(left, right, preferred_element_type=f32)


def repeated(group, rows):
    return jnp.concatenate([group] * (rows // SUBLANES), axis=0)


def encode(read, out_ref, rows, first, last):
    for col in range(0, out_ref.shape[1], LANES):
        cols = pl.ds(col, LANES)
        largest = jnp.full((SUBLANES, LANES), 1e-30, f32)
        for start in range(0, rows, CHUNK):
            for comp in range(2):
                for group in row_groups(jnp.abs(read(comp, pl.ds(start, CHUNK), cols))):
                    largest = jnp.maximum(largest, group)
        exponent = jnp.ceil(jnp.log2(largest))
        out_ref[last : last + SUBLANES, cols] = exponent.astype(jnp.int32)
        scale = repeated(jnp.exp2(-exponent) * LEVELS, CHUNK)
        for start in range(0, rows, CHUNK):
            codes = []
            for comp in range(2):
                scaled = jnp.clip(read(comp, pl.ds(start, CHUNK), cols) * scale, -LEVELS, LEVELS)
                codes.append(jnp.round(scaled).astype(jnp.int32))
            out_ref[pl.ds(first + start, CHUNK), cols] = (codes[0] << 16) | (codes[1] & 0xFFFF)


def decode(ref, start, last, col):
    cols = pl.ds(col, LANES)
    words = ref[pl.ds(start, CHUNK), cols]
    scale = repeated(jnp.exp2(ref[last : last + SUBLANES, cols].astype(f32)) * (1.0 / LEVELS), CHUNK)
    return (words >> 16).astype(f32) * scale, ((words << 16) >> 16).astype(f32) * scale


def largest_exponent(values):
    largest = jnp.full((SUBLANES, LANES), 1e-30, f32)
    for value in values:
        for group in row_groups(jnp.abs(value)):
            largest = jnp.maximum(largest, group)
    return jnp.ceil(jnp.log2(largest))


def fixed(value, exponent):
    scaled = value * repeated(jnp.exp2(-exponent) * LEVELS, value.shape[0])
    return jnp.round(jnp.clip(scaled, -LEVELS, LEVELS)).astype(jnp.int32)


def paired(first, second):
    return (first << 16) | (second & 0xFFFF)


def unpaired(words):
    return words >> 16, (words << 16) >> 16


def scaled_back(codes, exponent):
    return codes.astype(f32) * repeated(jnp.exp2(exponent.astype(f32)) * (1.0 / LEVELS), codes.shape[0])


def sums_rows(rows):
    return rows + rows // 2 + SUBLANES


def encode_sums(out_ref, cols, u_re, u_im, v):
    rows = v.shape[0]
    half = rows // 2
    of_u, of_v = largest_exponent([u_re, u_im]), largest_exponent([v])
    out_ref[0:rows, cols] = paired(fixed(u_re, of_u), fixed(u_im, of_u))
    codes = fixed(v, of_v)
    out_ref[rows : rows + half, cols] = paired(codes[:half], codes[half:])
    out_ref[rows + half : rows + half + SUBLANES, cols] = paired(of_u.astype(jnp.int32), of_v.astype(jnp.int32))


def decode_sums(ref, cols, rows):
    half = rows // 2
    of_u, of_v = unpaired(ref[rows + half : rows + half + SUBLANES, cols])
    u_re, u_im = unpaired(ref[0:rows, cols])
    v = jnp.concatenate(unpaired(ref[rows : rows + half, cols]), axis=0)
    return scaled_back(u_re, of_u), scaled_back(u_im, of_u), scaled_back(v, of_v)


def decode_probe(out_ref, chunks_ref):
    chunks = chunks_ref.shape[0]
    rows = out_ref.shape[1] // chunks
    for chunk in range(chunks):
        for col in range(0, out_ref.shape[2], LANES):
            cols = pl.ds(col, LANES)
            exponent = chunks_ref[chunk, rows : rows + SUBLANES, cols]
            for comp, codes in enumerate(unpaired(chunks_ref[chunk, 0:rows, cols])):
                out_ref[comp, chunk * rows : (chunk + 1) * rows, cols] = scaled_back(codes, exponent)


def cut_chunk(ext_ref, comp, first, top, left, rows):
    row = pl.multiple_of(lax.div(top, SUBLANES) * SUBLANES, SUBLANES)
    col = pl.multiple_of(lax.div(left, LANES) * LANES, LANES)
    block = ext_ref[comp, pl.ds(row + first, rows + SUBLANES), pl.ds(col, 3 * LANES)]
    tiles = shifted_left(lane_tiles(block), lax.rem(left, LANES))
    return [shifted_up(tile, lax.rem(top, SUBLANES)) for tile in tiles]


def forward(order, ext_ref, probe_ref, consts, y, x, win_ref, power_ref, weight, xa_ref, xb_ref, ya_ref, yb_ref, far_ref):
    turns, twiddles = consts
    half = order // 2
    tw_re = repeated(twiddles[0, half : half + SUBLANES, :], CHUNK)
    tw_im = repeated(twiddles[1, half : half + SUBLANES, :], CHUNK)
    for first in range(0, order, CHUNK):
        rows = pl.ds(first, CHUNK)
        win_re = cut_chunk(ext_ref, 0, first, y, x, CHUNK)
        win_im = cut_chunk(ext_ref, 1, first, y, x, CHUNK)
        exits = []
        for k in range(2):
            cols = pl.ds(k * half, half)
            win_ref[0, rows, cols] = win_re[k]
            win_ref[1, rows, cols] = win_im[k]
            power_ref[rows, cols] += weight * (win_re[k] * win_re[k] + win_im[k] * win_im[k])
            p_re, p_im = probe_ref[0, rows, cols], probe_ref[1, rows, cols]
            exits.append((p_re * win_re[k] - p_im * win_im[k], p_re * win_im[k] + p_im * win_re[k]))
        (lo_re, lo_im), (hi_re, hi_im) = exits
        store_split(xa_ref, rows, pl.ds(0, half), lo_re + hi_re)
        store_split(xa_ref, rows, pl.ds(half, half), lo_im + hi_im)
        d_re, d_im = lo_re - hi_re, lo_im - hi_im
        store_split(xb_ref, rows, pl.ds(0, half), d_re * tw_re - d_im * tw_im)
        store_split(xb_ref, rows, pl.ds(half, half), d_re * tw_im + d_im * tw_re)
    yield
    ya_ref[...] = right_dot(xa_ref, turns.at[0])
    yb_ref[...] = right_dot(xb_ref, turns.at[0])
    yield
    for first in range(0, half, CHUNK):
        rows = pl.ds(first, CHUNK)
        below = pl.ds(half + first, CHUNK)
        t_re, t_im = twiddles[0, rows, :], twiddles[1, rows, :]
        for k, y_ref in enumerate((ya_ref, yb_ref)):
            cols = pl.ds(k * half, half)
            up_re, up_im = y_ref[rows, 0:half], y_ref[rows, half:order]
            dn_re, dn_im = y_ref[below, 0:half], y_ref[below, half:order]
            store_split(xa_ref, rows, cols, up_re + dn_re)
            store_split(xa_ref, below, cols, up_im + dn_im)
            d_re, d_im = up_re - dn_re, up_im - dn_im
            store_split(xb_ref, rows, cols, d_re * t_re - d_im * t_im)
            store_split(xb_ref, below, cols, d_re * t_im + d_im * t_re)
    yield
    far_ref[0] = left_dot(turns.at[1], xa_ref)
    far_ref[1] = left_dot(turns.at[1], xb_ref)
    yield


def backward(order, far_ref, amp_ref, consts, y, x, weight, probe_ref, win_ref, xa_ref, xb_ref, ya_ref, yb_ref, grad_ref, numer_ref):
    turns, twiddles = consts
    half = order // 2
    tw_re = repeated(twiddles[0, half : half + SUBLANES, :], CHUNK)
    tw_im = repeated(twiddles[1, half : half + SUBLANES, :], CHUNK)
    for k, x_ref in enumerate((xa_ref, xb_ref)):
        for first in range(0, half, CHUNK):
            rows = pl.ds(first, CHUNK)
            below = pl.ds(half + first, CHUNK)
            far_re, far_im = far_ref[k, rows, :], far_ref[k, below, :]
            amp = amp_ref[pl.ds(k * half + first, CHUNK), :].astype(f32)
            factor = amp * lax.rsqrt(far_re * far_re + far_im * far_im + amplitude_floor)
            store_split(x_ref, rows, slice(None), far_re * factor)
            store_split(x_ref, below, slice(None), far_im * factor)
    yield
    ya_ref[...] = left_dot(turns.at[0], xa_ref)
    yb_ref[...] = left_dot(turns.at[0], xb_ref)
    yield
    for first in range(0, half, CHUNK):
        rows = pl.ds(first, CHUNK)
        below = pl.ds(half + first, CHUNK)
        t_re, t_im = twiddles[0, rows, :], twiddles[1, rows, :]
        for k, x_ref in enumerate((xa_ref, xb_ref)):
            cols = slice(k * half, (k + 1) * half)
            a_re, a_im = ya_ref[rows, cols], ya_ref[below, cols]
            b_re, b_im = yb_ref[rows, cols], yb_ref[below, cols]
            c_re, c_im = b_re * t_re + b_im * t_im, b_im * t_re - b_re * t_im
            store_split(x_ref, rows, pl.ds(0, half), a_re + c_re)
            store_split(x_ref, rows, pl.ds(half, half), a_im + c_im)
            store_split(x_ref, below, pl.ds(0, half), a_re - c_re)
            store_split(x_ref, below, pl.ds(half, half), a_im - c_im)
    yield
    ya_ref[...] = right_dot(xa_ref, turns.at[1])
    yb_ref[...] = right_dot(xb_ref, turns.at[1])
    yield

    def adder(comp):
        def add(rows, cols, moved):
            grad_ref[comp, rows, cols] += moved

        return add

    deposits = [Deposit(adder(comp), y, x) for comp in range(2)]
    for first in range(0, order, CHUNK):
        rows = pl.ds(first, CHUNK)
        a_re, a_im = ya_ref[rows, 0:half], ya_ref[rows, half:order]
        b_re, b_im = yb_ref[rows, 0:half], yb_ref[rows, half:order]
        c_re, c_im = b_re * tw_re + b_im * tw_im, b_im * tw_re - b_re * tw_im
        waves = [(a_re + c_re, a_im + c_im), (a_re - c_re, a_im - c_im)]
        terms = ([], [])
        for k, (wave_re, wave_im) in enumerate(waves):
            cols = pl.ds(k * half, half)
            wave_re, wave_im = weight * wave_re, weight * wave_im
            p_re, p_im = probe_ref[0, rows, cols], probe_ref[1, rows, cols]
            w_re, w_im = win_ref[0, rows, cols], win_ref[1, rows, cols]
            terms[0].append(p_re * wave_re + p_im * wave_im)
            terms[1].append(p_re * wave_im - p_im * wave_re)
            numer_ref[0, rows, cols] += w_re * wave_re + w_im * wave_im
            numer_ref[1, rows, cols] += w_re * wave_im - w_im * wave_re
        for comp in range(2):
            deposits[comp].put(first, terms[comp])
    for deposit in deposits:
        deposit.finish(order)
    yield


def interleaved(*stages):
    live = list(stages)
    while live:
        still = []
        for stage in live:
            try:
                next(stage)
                still.append(stage)
            except StopIteration:
                pass
        live = still


def outgoing_kernel(dims, pos_ref, me_ref, amp_ref, after_ref, also_ref, out_ref, sems):
    tile_rows, tile_cols, pat_count, col_count, capacity = dims
    first = (me_ref[0] * col_count + me_ref[1]) * pat_count
    total = pos_ref.shape[0] // 2
    owners = [lax.div(pos_ref[total + first + k], tile_cols) for k in range(pat_count)]
    copies = []
    for k in range(pat_count):
        rank = sum(((owners[e] == owners[k]).astype(jnp.int32) for e in range(k)), jnp.int32(0))
        slot = owners[k] * SEND + jnp.minimum(rank, SEND - 1)
        copies.append(pltpu.make_async_copy(amp_ref.at[k], out_ref.at[slot], sems.at[k]))
        copies[-1].start()
    for copy in copies:
        copy.wait()


def weights_kernel(dims, span, pos_ref, me_ref, probe_ref, out_ref, sums_ref, power_ref):
    tile_rows, tile_cols, pat_count, col_count, capacity = dims
    order = probe_ref.shape[1]
    top = (me_ref[0] - 1) * tile_rows
    left = (me_ref[1] - 1) * tile_cols
    total = pos_ref.shape[0] // 2
    for first in range(0, sums_ref.shape[0], order):
        sums_ref[pl.ds(first, order), :] = jnp.zeros((order, sums_ref.shape[1]), f32)
    power_ref[...] = probe_ref[0] * probe_ref[0] + probe_ref[1] * probe_ref[1]

    def visit(index, carry):
        y = pos_ref[index] - top
        x = pos_ref[total + index] - left

        @pl.when((y > 0) & (y < (span + 1) * tile_rows) & (x > 0) & (x < (span + 1) * tile_cols))
        def _():
            def add(rows, cols, moved):
                sums_ref[rows, cols] += moved

            deposit = Deposit(add, y, x)
            for first in range(0, order, CHUNK):
                deposit.put(first, lane_tiles(power_ref[pl.ds(first, CHUNK), :]))
            deposit.finish(order)

        return carry

    lax.fori_loop(0, total, visit, 0)
    pltpu.sync_copy(sums_ref.at[pl.ds(tile_rows, span * tile_rows), pl.ds(tile_cols, span * tile_cols)], out_ref)


def encode_kernel(obj_ref, out_ref):
    rows = obj_ref.shape[1]
    encode(lambda comp, at, cols: obj_ref[comp, at, cols], out_ref, rows, 0, rows)


def unfold(dims, ext_ref, own_ref, coded_refs):
    tile_rows, tile_cols = dims[:2]
    ext_ref[:, 0:tile_rows, 0:tile_cols] = own_ref[...]
    for (i, j), ref in zip(((0, 1), (1, 0), (1, 1)), coded_refs):
        for col in range(0, tile_cols, LANES):
            for start in range(0, tile_rows, CHUNK):
                parts = decode(ref, start, tile_rows, col)
                for comp in range(2):
                    ext_ref[comp, pl.ds(i * tile_rows + start, CHUNK), pl.ds(j * tile_cols + col, LANES)] = parts[comp]


def spread_sums(out_ref, u_ref, v_ref):
    chunks = out_ref.shape[0]
    rows = v_ref.shape[0] // chunks
    for chunk in range(chunks):
        at = pl.ds(chunk * rows, rows)
        for col in range(0, v_ref.shape[1], LANES):
            cols = pl.ds(col, LANES)
            encode_sums(out_ref.at[chunk], cols, u_ref[0, at, cols], u_ref[1, at, cols], v_ref[at, cols])


def added(parts):
    while len(parts) > 1:
        parts = [tuple(x + y for x, y in zip(a, b)) for a, b in zip(parts[::2], parts[1::2])]
    return parts[0]


def sums_kernel(rows, parts_ref, *refs):
    out_ref = refs[-1]
    for col in range(0, out_ref.shape[2], LANES):
        cols = pl.ds(col, LANES)
        total = added([decode_sums(parts_ref.at[k], cols, rows) for k in range(parts_ref.shape[0])])
        encode_sums(out_ref.at[0], cols, *total)
        for k in range(1, out_ref.shape[0]):
            out_ref[k, :, cols] = out_ref[0, :, cols]


def update_kernel(rows, count, me_ref, probe_ref, *refs):
    out_ref = refs[-1]
    first = pl.multiple_of(me_ref[1] * rows, SUBLANES)
    for col in range(0, out_ref.shape[2], LANES):
        cols = pl.ds(col, LANES)
        u_re, u_im, v = added([decode_sums(ref.at[k], cols, rows) for ref in refs[:count] for k in range(ref.shape[0])])
        scale = 1.0 / (v + probe_regular)
        re = (probe_ref[0, pl.ds(first, rows), cols] + u_re) * scale
        im = (probe_ref[1, pl.ds(first, rows), cols] + u_im) * scale
        exponent = largest_exponent([re, im])
        words = paired(fixed(re, exponent), fixed(im, exponent))
        for chunk in range(out_ref.shape[0]):
            out_ref[chunk, 0:rows, cols] = words
            out_ref[chunk, rows : rows + SUBLANES, cols] = exponent.astype(jnp.int32)


def probe_kernel(chunks_ref, out_ref):
    decode_probe(out_ref, chunks_ref)


def first_half_kernel(dims, pos_ref, me_ref, own_ref, right_ref, below_ref, diag_ref, probe_ref, turns, twiddles,
                      far_out, power_out, ext_out, ext_ref, win_ref, xa_ref, xb_ref, ya_ref, yb_ref, far_ref, ys_ref, xs_ref, slots_ref, sems, ext_sem):
    tile_rows, tile_cols, pat_count, col_count, capacity = dims
    order = probe_ref.shape[1]
    count = list_patterns(dims, pos_ref, me_ref, ys_ref, xs_ref, slots_ref)
    unfold(dims, ext_ref, own_ref, (right_ref, below_ref, diag_ref))
    keep = pltpu.make_async_copy(ext_ref, ext_out, ext_sem)
    keep.start()
    power_out[...] = jnp.zeros_like(power_out)
    consts = (turns, twiddles)

    def pair(step, carry):
        stages = []
        for k in range(2):
            listed = 2 * step + k
            weight = (listed < count).astype(f32)
            index = jnp.minimum(listed, count - 1)
            stages.append(forward(order, ext_ref, probe_ref, consts, ys_ref[index], xs_ref[index], win_ref.at[k], power_out, weight,
                                  xa_ref.at[k], xb_ref.at[k], ya_ref.at[k], yb_ref.at[k], far_ref.at[listed]))
        interleaved(*stages)
        for k in range(2):
            listed = 2 * step + k
            pltpu.make_async_copy(far_ref.at[listed], far_out.at[listed], sems.at[listed]).start()
        return carry

    pairs = lax.div(count + 1, 2)
    lax.fori_loop(0, pairs, pair, 0)

    def settle(listed, carry):
        pltpu.make_async_copy(far_ref.at[listed], far_out.at[listed], sems.at[listed]).wait()
        return carry

    lax.fori_loop(0, 2 * pairs, settle, 0)
    keep.wait()


def second_half_kernel(dims, pos_ref, me_ref, ext_ref, probe_ref, power_ref, weights_ref, far_in, amp_in, turns, twiddles, sorting,
                       share_out, numer_out, amp_out,
                       sum_ref, win_ref, xa_ref, xb_ref, ya_ref, yb_ref, numer_ref, far_ref, amp_ref, sorted_ref, ys_ref, xs_ref, slots_ref, far_sems, amp_sems, out_sems, sum_sem):
    tile_rows, tile_cols, pat_count, col_count, capacity = dims
    order = probe_ref.shape[1]
    half = order // 2
    count = list_patterns(dims, pos_ref, me_ref, ys_ref, xs_ref, slots_ref)
    pairs = lax.div(count + 1, 2)

    def copies(listed):
        return (
            pltpu.make_async_copy(far_in.at[listed], far_ref.at[listed], far_sems.at[listed]),
            pltpu.make_async_copy(amp_in.at[slots_ref[jnp.minimum(listed, count - 1)]], amp_ref.at[listed], amp_sems.at[listed]),
        )

    def begin(listed, carry):
        for copy in copies(listed):
            copy.start()
        return carry

    lax.fori_loop(0, 2 * pairs, begin, 0)
    sum_ref[...] = jnp.zeros_like(sum_ref)
    numer_ref[...] = jnp.zeros_like(numer_ref)
    consts = (turns, twiddles)

    def pair(step, carry):
        stages = []
        for k in range(2):
            listed = 2 * step + k
            for copy in copies(listed):
                copy.wait()
        for k in range(2):
            listed = 2 * step + k
            weight = (listed < count).astype(f32)
            index = jnp.minimum(listed, count - 1)
            y, x = ys_ref[index], xs_ref[index]
            rows_sorted = jnp.dot(sorting[0], amp_ref[listed], preferred_element_type=f32).astype(bf16)
            sorted_ref[listed] = jnp.dot(rows_sorted, sorting[1], preferred_element_type=f32).astype(bf16)
            for first in range(0, order, CHUNK):
                for comp in range(2):
                    for c, tile in enumerate(cut_chunk(ext_ref, comp, first, y, x, CHUNK)):
                        win_ref[k, comp, pl.ds(first, CHUNK), pl.ds(c * half, half)] = tile
            stages.append(backward(order, far_ref.at[listed], sorted_ref.at[listed], consts, y, x, weight, probe_ref, win_ref.at[k],
                                   xa_ref.at[k], xb_ref.at[k], ya_ref.at[k], yb_ref.at[k], sum_ref, numer_ref))
        interleaved(*stages)
        for k in range(2):
            listed = 2 * step + k
            pltpu.make_async_copy(sorted_ref.at[listed], amp_out.at[listed], out_sems.at[listed]).start()
        return carry

    lax.fori_loop(0, pairs, pair, 0)
    for first in range(0, 2 * tile_rows, CHUNK):
        rows = pl.ds(first, CHUNK)
        scale = 1.0 / (weights_ref[rows, :] + object_regular)
        for comp in range(2):
            sum_ref[comp, rows, :] = sum_ref[comp, rows, :] * scale
    keep = pltpu.make_async_copy(sum_ref, share_out, sum_sem)
    keep.start()
    spread_sums(numer_out, numer_ref, power_ref)

    def settle(listed, carry):
        pltpu.make_async_copy(sorted_ref.at[listed], amp_out.at[listed], out_sems.at[listed]).wait()
        return carry

    lax.fori_loop(0, 2 * pairs, settle, 0)
    keep.wait()


def rows_code_kernel(dims, share_ref, top_out, bottom_out):
    tile_rows = dims[0]
    encode(lambda comp, at, cols: share_ref[comp, at, cols], top_out, tile_rows, 0, tile_rows)
    encode(lambda comp, at, cols: share_ref[comp, pl.ds(tile_rows + at.start, at.size), cols], bottom_out, tile_rows, 0, tile_rows)


def rows_sum_kernel(dims, share_ref, above_ref, below_ref, after_ref, sum_out, left_out, right_out, sem):
    tile_rows, tile_cols = dims[:2]
    for i, ref in enumerate((above_ref, below_ref)):
        for col in range(0, 2 * tile_cols, LANES):
            for start in range(0, tile_rows, CHUNK):
                rows, cols = pl.ds(i * tile_rows + start, CHUNK), pl.ds(col, LANES)
                parts = decode(ref, start, tile_rows, col)
                for comp in range(2):
                    share_ref[comp, rows, cols] += parts[comp]
    keep = pltpu.make_async_copy(share_ref, sum_out, sem)
    keep.start()
    for j, ref in enumerate((left_out, right_out)):
        for i in range(2):

            def read(comp, at, cols, i=i, j=j):
                return share_ref[comp, pl.ds(i * tile_rows + at.start, at.size), pl.ds(j * tile_cols + cols.start, cols.size)]

            encode(read, ref, tile_rows, i * tile_rows, 2 * tile_rows + i * SUBLANES)
    keep.wait()


def whole_kernel(dims, pos_ref, me_ref, old_ref, sum_ref, from_left_ref, from_right_ref, weights_ref,
                 chunks_ref, amp_in, turns, twiddles,
                 current_out, top_out, bottom_out, numer_out, probe_ref,
                 ext_ref, grad_ref, win_ref, xa_ref, xb_ref, ya_ref, yb_ref, numer_ref, far_ref, amp_ref, ys_ref, xs_ref, slots_ref, amp_sems, own_sem, top_sem):
    tile_rows, tile_cols, pat_count, col_count, capacity = dims
    order = probe_ref.shape[1]
    count = list_patterns(dims, pos_ref, me_ref, ys_ref, xs_ref, slots_ref)
    pairs = lax.div(count + 1, 2)
    decode_probe(probe_ref, chunks_ref)

    def fetch(listed):
        return pltpu.make_async_copy(amp_in.at[jnp.minimum(listed, count - 1)], amp_ref.at[listed], amp_sems.at[listed])

    def begin(listed, carry):
        fetch(listed).start()
        return carry

    lax.fori_loop(0, 2 * pairs, begin, 0)
    for j, ref in enumerate((from_left_ref, from_right_ref)):
        for i in range(2):
            for col in range(0, tile_cols, LANES):
                for start in range(0, tile_rows, CHUNK):
                    rows, cols = pl.ds(i * tile_rows + start, CHUNK), pl.ds(j * tile_cols + col, LANES)
                    parts = decode(ref, i * tile_rows + start, 2 * tile_rows + i * SUBLANES, col)
                    scale = object_regular / (weights_ref[rows, cols] + object_regular)
                    for comp in range(2):
                        ext_ref[comp, rows, cols] = old_ref[comp, rows, cols] * scale + (sum_ref[comp, rows, cols] + parts[comp])
    keep = pltpu.make_async_copy(ext_ref.at[:, pl.ds(0, tile_rows), pl.ds(0, tile_cols)], current_out, own_sem)
    keep.start()
    grad_ref[...] = jnp.zeros_like(grad_ref)
    numer_ref[...] = jnp.zeros_like(numer_ref)
    consts = (turns, twiddles)

    def pair(step, carry):
        stages = []
        for k in range(2):
            fetch(2 * step + k).wait()
        for k in range(2):
            listed = 2 * step + k
            weight = (listed < count).astype(f32)
            index = jnp.minimum(listed, count - 1)
            y, x = ys_ref[index], xs_ref[index]

            def both(k=k, listed=listed, weight=weight, y=y, x=x):
                yield from forward(order, ext_ref, probe_ref, consts, y, x, win_ref.at[k], numer_ref.at[2], weight,
                                   xa_ref.at[k], xb_ref.at[k], ya_ref.at[k], yb_ref.at[k], far_ref.at[k])
                yield from backward(order, far_ref.at[k], amp_ref.at[listed], consts, y, x, weight, probe_ref, win_ref.at[k],
                                    xa_ref.at[k], xb_ref.at[k], ya_ref.at[k], yb_ref.at[k], grad_ref, numer_ref)

            stages.append(both())
        interleaved(*stages)
        return carry

    lax.fori_loop(0, pairs, pair, 0)
    for first in range(0, tile_rows, CHUNK):
        rows = pl.ds(first, CHUNK)
        scale = 1.0 / (weights_ref[rows, :] + object_regular)
        for comp in range(2):
            grad_ref[comp, rows, :] = grad_ref[comp, rows, :] * scale
    give = pltpu.make_async_copy(grad_ref.at[:, pl.ds(0, tile_rows), :], top_out, top_sem)
    give.start()

    def read(comp, at, cols):
        rows = pl.ds(tile_rows + at.start, at.size)
        return grad_ref[comp, rows, cols] / (weights_ref[rows, cols] + object_regular)

    encode(read, bottom_out, tile_rows, 0, tile_rows)
    spread_sums(numer_out, numer_ref, numer_ref.at[2])
    keep.wait()
    give.wait()


def fold_kernel(dims, top_ref, above_ref, own_out, right_out, own_ref, sem):
    tile_rows, tile_cols = dims[:2]
    for col in range(0, 2 * tile_cols, LANES):
        for start in range(0, tile_rows, CHUNK):
            rows, cols = pl.ds(start, CHUNK), pl.ds(col, LANES)
            parts = decode(above_ref, start, tile_rows, col)
            for comp in range(2):
                if col < tile_cols:
                    own_ref[comp, rows, cols] = top_ref[comp, rows, cols] + parts[comp]
                else:
                    top_ref[comp, rows, cols] += parts[comp]
    keep = pltpu.make_async_copy(own_ref, own_out, sem)
    keep.start()
    encode(lambda comp, at, cols: top_ref[comp, at, pl.ds(tile_cols + cols.start, cols.size)], right_out, tile_rows, 0, tile_rows)
    keep.wait()


def object_kernel(dims, current_ref, own_ref, left_ref, before_ref, weights_ref, out_ref):
    tile_rows, tile_cols = dims[:2]
    for col in range(0, tile_cols, LANES):
        for start in range(0, tile_rows, CHUNK):
            rows, cols = pl.ds(start, CHUNK), pl.ds(col, LANES)
            scale = 1.0 / (weights_ref[rows, cols] + object_regular)
            back = (before_ref[rows, cols] + object_regular) * scale
            parts = decode(left_ref, start, tile_rows, col)
            for comp in range(2):
                old = object_regular * scale * current_ref[comp, rows, cols]
                out_ref[comp, rows, cols] = old + (own_ref[comp, rows, cols] + parts[comp]) * back


def shape(dims, dtype=f32):
    return jax.ShapeDtypeStruct(dims, dtype)


def work_scratch(order):
    return [
        pltpu.VMEM((2, 2, order, order), f32),
        pltpu.VMEM((2, 2, order, order), bf16),
        pltpu.VMEM((2, 2, order, order), bf16),
        pltpu.VMEM((2, order, order), f32),
        pltpu.VMEM((2, order, order), f32),
    ]


def list_scratch(capacity):
    return [pltpu.SMEM((capacity,), jnp.int32)] * 3


def call(kernel, outs, out_specs, in_specs, scratch, flops, limit=26 << 20):
    several = isinstance(outs, tuple)
    out_count = len(outs) if several else 1
    in_count = len(in_specs)
    loaded = [k for k, spec in enumerate(in_specs) if spec is LOAD]

    def body(*refs):
        ins, rest = list(refs[:in_count]), refs[in_count:]
        given, kept = rest[: out_count + len(scratch)], rest[out_count + len(scratch) :]
        copies = [pltpu.make_async_copy(ins[k], kept[n], kept[-1].at[n]) for n, k in enumerate(loaded)]
        for copy in copies:
            copy.start()
        for n, k in enumerate(loaded):
            copies[n].wait()
            ins[k] = kept[n]
        kernel(*ins, *given)

    fixed_outs = [
        pltpu.HBM(out.shape, out.dtype) if spec is HBM else pltpu.VMEM(out.shape, out.dtype) if spec is PIN else out
        for out, spec in zip(outs if several else (outs,), out_specs if several else (out_specs,))
    ]
    places = [pltpu.HBM if spec is LOAD or spec is HBM else pltpu.VMEM if spec is PIN else None for spec in in_specs]

    def called(*args):
        args = [arg if place is None else pltpu.with_memory_space_constraint(arg, place) for arg, place in zip(args, places)]
        own = [pltpu.VMEM(args[k].shape, args[k].dtype) for k in loaded]
        if loaded:
            own.append(pltpu.SemaphoreType.DMA((len(loaded),)))
        return pl.pallas_call(
            body,
            out_shape=tuple(fixed_outs) if several else fixed_outs[0],
            out_specs=out_specs,
            in_specs=[HBM if spec is LOAD else spec for spec in in_specs],
            scratch_shapes=list(scratch) + own,
            compiler_params=pltpu.CompilerParams(vmem_limit_bytes=limit),
            cost_estimate=pl.CostEstimate(flops=flops, bytes_accessed=8 << 20, transcendentals=0),
        )(*args)

    return called


def passed_along(value, axis, steps):
    count = lax.axis_size(axis)
    leading, last = (max(0, -steps), min(count, count - steps))
    return lax.ppermute(value, axis, [(source, source + steps) for source in range(leading, last)])


def swapped(value, axis, mask):
    return lax.ppermute(value, axis, [(k, k ^ mask) for k in range(lax.axis_size(axis))])


def probe_update(me, probe, numer, kind, at_once, before_sum, before_update):
    cols, order = lax.axis_size("col"), probe.shape[1]
    rows = order // cols
    parts = lax.all_to_all(numer, "col", split_axis=0, concat_axis=0, tiled=True)
    blocks = lax.axis_size("row") if at_once else 1
    total = call(
        functools.partial(sums_kernel, rows), shape((blocks, sums_rows(rows), order), jnp.int32), VMEM,
        [VMEM] + [spec for spec, _ in before_sum], [], 1 << 26,
    )(parts, *[value for _, value in before_sum])
    if at_once:
        totals = [lax.all_to_all(total, "row", split_axis=0, concat_axis=0, tiled=True)]
    else:
        totals = [total] + [swapped(total, "row", mask) for mask in range(1, lax.axis_size("row"))]
    fresh = call(
        functools.partial(update_kernel, rows, len(totals)), shape((cols, rows + SUBLANES, order), jnp.int32), VMEM,
        [SMEM, kind] + [VMEM] * len(totals) + [FREE] * len(before_update), [], 1 << 26,
    )(me, probe, *totals, *before_update)
    return total, lax.all_to_all(fresh, "col", split_axis=0, concat_axis=0, tiled=True)


def local(obj, probe, amplitudes, positions):
    col_count = lax.axis_size("col")
    tile_rows, tile_cols = obj.shape[1], obj.shape[2]
    order = probe.shape[1]
    pat_count = amplitudes.shape[0]
    capacity = 2 * pat_count
    dims = (tile_rows, tile_cols, pat_count, col_count, capacity)
    me = jnp.stack([lax.axis_index("row"), lax.axis_index("col")]).astype(jnp.int32)
    pos = positions.T.reshape(-1)
    turns, twiddles, sorting = tables(order)
    tile = (2, tile_rows, tile_cols)
    window = (2, order, order)
    wide = (2, 2 * tile_rows, 2 * tile_cols)
    shares = shape((col_count, sums_rows(order // col_count), order), jnp.int32)
    coded_tile = shape((tile_rows + SUBLANES, tile_cols), jnp.int32)
    coded_row = shape((tile_rows + SUBLANES, 2 * tile_cols), jnp.int32)
    coded_col = shape((2 * (tile_rows + SUBLANES), tile_cols), jnp.int32)
    one_pattern = 24 * 2 * order**3

    coded = call(encode_kernel, coded_tile, VMEM, [LOAD], [], 1 << 26)(obj)
    right = passed_along(coded, "col", -1)
    below = passed_along(coded, "row", -1)
    diag = passed_along(right, "row", -1)

    outgoing = call(
        functools.partial(outgoing_kernel, dims), shape((col_count * SEND, order, order), bf16), HBM, [SMEM, SMEM, LOAD, FREE, FREE],
        [pltpu.SemaphoreType.DMA((pat_count,))], 1 << 20,
    )(pos, me, amplitudes, right, below)
    incoming = lax.all_to_all(outgoing, "col", split_axis=0, concat_axis=0, tiled=True)

    def weights(probe_now, span, kind):
        return call(
            functools.partial(weights_kernel, dims, span), shape((span * tile_rows, span * tile_cols)), HBM, [SMEM, SMEM, kind],
            [pltpu.VMEM(((span + 2) * tile_rows, (span + 2) * tile_cols), f32), pltpu.VMEM((order, order), f32)], 8 << 30,
        )(pos, me, probe_now)

    weights_old = weights(probe, 2, LOAD)

    far, power, ext = call(
        functools.partial(first_half_kernel, dims), (shape((capacity,) + window), shape((order, order)), shape(wide)), (HBM, VMEM, HBM),
        [SMEM, SMEM, LOAD] + [VMEM] * 3 + [LOAD] * 3,
        [pltpu.VMEM(wide, f32)] + work_scratch(order) + [pltpu.VMEM((capacity,) + window, f32)] + list_scratch(capacity)
        + [pltpu.SemaphoreType.DMA((capacity,)), pltpu.SemaphoreType.DMA],
        capacity * one_pattern // 2,
    )(pos, me, obj, right, below, diag, probe, turns, twiddles)

    share, numer, sorted_amps = call(
        functools.partial(second_half_kernel, dims),
        (shape(wide), shares, shape((capacity, order, order), bf16)),
        (HBM, VMEM, HBM),
        [SMEM, SMEM, LOAD, LOAD, VMEM, LOAD, HBM, FREE] + [LOAD] * 3,
        [pltpu.VMEM(wide, f32)] + work_scratch(order)
        + [pltpu.VMEM(window, f32), pltpu.VMEM((capacity,) + window, f32), pltpu.VMEM((capacity, order, order), bf16), pltpu.VMEM((capacity, order, order), bf16)]
        + list_scratch(capacity) + [pltpu.SemaphoreType.DMA((capacity,))] * 3 + [pltpu.SemaphoreType.DMA],
        capacity * one_pattern // 2,
    )(pos, me, ext, probe, power, weights_old, far, incoming, turns, twiddles, sorting)

    top, bottom = call(functools.partial(rows_code_kernel, dims), (coded_row, coded_row), (VMEM, VMEM), [LOAD], [], 1 << 26)(share)
    from_above = passed_along(bottom, "row", 1)
    from_below = passed_along(top, "row", -1)
    total, chunks = probe_update(me, probe, numer, LOAD, True, [(FREE, top)], [])
    sums, to_left, to_right = call(
        functools.partial(rows_sum_kernel, dims), (shape(wide), coded_col, coded_col), (HBM, VMEM, VMEM), [LOAD, VMEM, VMEM, FREE], [pltpu.SemaphoreType.DMA], 1 << 26,
    )(share, from_above, from_below, total)
    from_left = passed_along(to_right, "col", 1)
    from_right = passed_along(to_left, "col", -1)

    current, top, bottom, numer, probe_now = call(
        functools.partial(whole_kernel, dims), (shape(tile), shape((2, tile_rows, 2 * tile_cols)), coded_row, shares, shape(window)), (HBM, HBM) + (VMEM,) * 3,
        [SMEM, SMEM, LOAD, LOAD, VMEM, VMEM, LOAD, VMEM, HBM, LOAD, LOAD],
        [pltpu.VMEM(wide, f32), pltpu.VMEM(wide, f32)] + work_scratch(order)
        + [pltpu.VMEM((3, order, order), f32), pltpu.VMEM((2,) + window, f32), pltpu.VMEM((capacity, order, order), bf16)]
        + list_scratch(capacity) + [pltpu.SemaphoreType.DMA((capacity,)), pltpu.SemaphoreType.DMA, pltpu.SemaphoreType.DMA],
        capacity * one_pattern,
    )(pos, me, ext, sums, from_left, from_right, weights_old, chunks, sorted_amps, turns, twiddles)

    from_above = passed_along(bottom, "row", 1)
    weights_new = weights(probe_now, 1, VMEM)
    own, to_right = call(
        functools.partial(fold_kernel, dims), (shape(tile), coded_tile), (HBM, VMEM), [LOAD, VMEM], [pltpu.VMEM(tile, f32), pltpu.SemaphoreType.DMA], 1 << 26,
    )(top, from_above)
    from_left = passed_along(to_right, "col", 1)
    new_object = call(functools.partial(object_kernel, dims), shape(tile), VMEM, [LOAD, LOAD, VMEM, LOAD, LOAD], [], 1 << 26)(
        current, own, from_left, weights_old, weights_new
    )
    _, chunks = probe_update(me, probe_now, numer, VMEM, False, [(HBM, weights_new)], [to_right])
    new_probe = call(probe_kernel, shape(window), VMEM, [VMEM], [], 1 << 26)(chunks)
    return new_object, new_probe


def solution(mesh):
    placed = (P(None, "row", "col"), P(), P(("row", "col"), None, None), P())
    return jax.shard_map(local, mesh=mesh, in_specs=placed, out_specs=(P(None, "row", "col"), P()), check_vma=False)
```

```python
import functools

import jax
import jax.numpy as jnp
import numpy as np
from jax import lax
from jax.experimental import pallas as pl
from jax.experimental.pallas import tpu as pltpu
from jax.sharding import PartitionSpec as P

ITERS = 2
SEND = 2

amplitude_floor = 0.1
object_regular = 0.5
probe_regular = 1.0

LANES = 128
SUBLANES = 8
LEVELS = 32767.0
CHUNK = 32
VMEM = pl.BlockSpec(memory_space=pltpu.VMEM)
SMEM = pl.BlockSpec(memory_space=pltpu.SMEM)
HBM = pl.BlockSpec(memory_space=pltpu.HBM)
LOAD = object()
LATE = object()
FREE = pl.BlockSpec(memory_space=pl.ANY)
PIN = pl.BlockSpec(memory_space=pltpu.VMEM)
f32 = jnp.float32
bf16 = jnp.bfloat16


def tables(order):
    half = order // 2
    counter = np.arange(half)
    angles = 2.0 * np.pi * ((counter[:, None] * counter[None, :]) % half) / half
    cos, sin = np.cos(angles), np.sin(angles)
    scale = 1.0 / np.sqrt(order)
    turns = []
    for block in ([[cos, -sin], [sin, cos]], [[cos, sin], [-sin, cos]]):
        matrix = np.block(block) * scale
        high = matrix.astype(jnp.bfloat16)
        turns.append(np.stack([high, (matrix - high.astype(np.float64)).astype(jnp.bfloat16)]))
    turn = 2.0 * np.pi * counter / order
    twiddle = np.stack([np.cos(turn), -np.sin(turn)]).astype(np.float32)
    twiddles = np.concatenate(
        [np.broadcast_to(twiddle[:, :, None], (2, half, half)), np.broadcast_to(twiddle[:, None, :], (2, SUBLANES, half))], axis=1
    )
    sorting = np.zeros((order, order), np.float32)
    sorting[np.arange(half), 2 * np.arange(half)] = 1.0
    sorting[half + np.arange(half), 2 * np.arange(half) + 1] = 1.0
    return (
        jnp.asarray(np.stack(turns)),
        jnp.asarray(np.ascontiguousarray(twiddles)),
        jnp.asarray(np.stack([sorting, sorting.T]).astype(jnp.bfloat16)),
    )


def list_patterns(dims, pos_ref, me_ref, ys_ref, xs_ref, slots_ref):
    tile_rows, tile_cols, pat_count, col_count, capacity = dims
    my_row, my_col = me_ref[0], me_ref[1]
    band_count = pat_count * col_count
    first = my_row * band_count
    total = pos_ref.shape[0] // 2

    def visit(index, carry):
        found, source, rank = carry
        y = pos_ref[first + index]
        x = pos_ref[total + first + index]
        here = lax.div(x, tile_cols) == my_col
        holder = lax.div(index, pat_count)
        rank = jnp.where(holder == source, rank, 0)

        @pl.when(here & (found < capacity))
        def _():
            ys_ref[found] = y - my_row * tile_rows
            xs_ref[found] = x - my_col * tile_cols
            slots_ref[found] = holder * SEND + jnp.minimum(rank, SEND - 1)

        step = here.astype(jnp.int32)
        return found + step, holder, rank + step

    found, _, _ = lax.fori_loop(0, band_count, visit, (jnp.int32(0), jnp.int32(-1), jnp.int32(0)))
    return jnp.minimum(found, capacity)


def lane_index(rows):
    return lax.broadcasted_iota(jnp.int32, (rows, LANES), 1)


def shifted_left(tiles, shift):
    lane = lane_index(tiles[0].shape[0])
    turn = lax.rem(LANES - shift, LANES)
    rolled = [pltpu.roll(tile, turn, axis=1) for tile in tiles]
    inside = lane < LANES - shift
    return [jnp.where(inside, a, b) for a, b in zip(rolled[:-1], rolled[1:])]


def shifted_right(tiles, shift):
    lane = lane_index(tiles[0].shape[0])
    rolled = [pltpu.roll(tile, shift, axis=1) for tile in tiles]
    outside = lane < shift
    zero = jnp.zeros_like(rolled[0])
    firsts = [zero] + rolled
    seconds = rolled + [zero]
    return [jnp.where(outside, a, b) for a, b in zip(firsts, seconds)]


def row_groups(tile):
    return [tile[k : k + SUBLANES] for k in range(0, tile.shape[0], SUBLANES)]


def shifted_up(tile, shift):
    row = lax.broadcasted_iota(jnp.int32, (SUBLANES, LANES), 0)
    turn = lax.rem(SUBLANES - shift, SUBLANES)
    rolled = [pltpu.roll(group, turn, axis=0) for group in row_groups(tile)]
    inside = row < SUBLANES - shift
    return jnp.concatenate([jnp.where(inside, a, b) for a, b in zip(rolled[:-1], rolled[1:])], axis=0)


def shifted_down(before, tile, shift):
    row = lax.broadcasted_iota(jnp.int32, (SUBLANES, LANES), 0)
    rolled = [before] + [pltpu.roll(group, shift, axis=0) for group in row_groups(tile)]
    outside = row < shift
    return rolled[-1], jnp.concatenate([jnp.where(outside, a, b) for a, b in zip(rolled[:-1], rolled[1:])], axis=0)


class Deposit:
    def __init__(self, add, top, left):
        self.add = add
        self.row = pl.multiple_of(lax.div(top, SUBLANES) * SUBLANES, SUBLANES)
        self.col = pl.multiple_of(lax.div(left, LANES) * LANES, LANES)
        self.down = lax.rem(top, SUBLANES)
        self.right = lax.rem(left, LANES)
        self.carried = None

    def place(self, first, tiles):
        moved = jnp.concatenate(shifted_right(tiles, self.right), axis=1)
        self.add(pl.ds(self.row + first, tiles[0].shape[0]), pl.ds(self.col, moved.shape[1]), moved)

    def put(self, first, tiles):
        if self.carried is None:
            self.carried = [jnp.zeros((SUBLANES, LANES), f32) for _ in tiles]
        pairs = [shifted_down(before, tile, self.down) for before, tile in zip(self.carried, tiles)]
        self.carried = [carried for carried, _ in pairs]
        self.place(first, [tile for _, tile in pairs])

    def finish(self, first):
        row = lax.broadcasted_iota(jnp.int32, (SUBLANES, LANES), 0)
        self.place(first, [jnp.where(row < self.down, tile, 0.0) for tile in self.carried])


def lane_tiles(value):
    return [value[:, k : k + LANES] for k in range(0, value.shape[1], LANES)]


def store_split(ref, rows, cols, value):
    high = value.astype(bf16)
    ref[0, rows, cols] = high
    ref[1, rows, cols] = (value - high.astype(f32)).astype(bf16)


def right_dot(x_ref, table_ref):
    left = jnp.concatenate([x_ref[0], x_ref[1], x_ref[0]], axis=1)
    right = jnp.concatenate([table_ref[0], table_ref[0], table_ref[1]], axis=0)
    return jnp.dot(left, right, preferred_element_type=f32)


def left_dot(table_ref, x_ref):
    left = jnp.concatenate([table_ref[0], table_ref[0], table_ref[1]], axis=1)
    right = jnp.concatenate([x_ref[0], x_ref[1], x_ref[0]], axis=0)
    return jnp.dot(left, right, preferred_element_type=f32)


def repeated(group, rows):
    return jnp.concatenate([group] * (rows // SUBLANES), axis=0)


def encode(read, out_ref, rows, first, last):
    for col in range(0, out_ref.shape[1], LANES):
        cols = pl.ds(col, LANES)
        largest = jnp.full((SUBLANES, LANES), 1e-30, f32)
        for start in range(0, rows, CHUNK):
            for comp in range(2):
                for group in row_groups(jnp.abs(read(comp, pl.ds(start, CHUNK), cols))):
                    largest = jnp.maximum(largest, group)
        exponent = jnp.ceil(jnp.log2(largest))
        out_ref[last : last + SUBLANES, cols] = exponent.astype(jnp.int32)
        scale = repeated(jnp.exp2(-exponent) * LEVELS, CHUNK)
        for start in range(0, rows, CHUNK):
            codes = []
            for comp in range(2):
                scaled = jnp.clip(read(comp, pl.ds(start, CHUNK), cols) * scale, -LEVELS, LEVELS)
                codes.append(jnp.round(scaled).astype(jnp.int32))
            out_ref[pl.ds(first + start, CHUNK), cols] = (codes[0] << 16) | (codes[1] & 0xFFFF)


def decode(ref, start, last, col):
    cols = pl.ds(col, LANES)
    words = ref[pl.ds(start, CHUNK), cols]
    scale = repeated(jnp.exp2(ref[last : last + SUBLANES, cols].astype(f32)) * (1.0 / LEVELS), CHUNK)
    return (words >> 16).astype(f32) * scale, ((words << 16) >> 16).astype(f32) * scale


def largest_exponent(values):
    largest = jnp.full((SUBLANES, LANES), 1e-30, f32)
    for value in values:
        for group in row_groups(jnp.abs(value)):
            largest = jnp.maximum(largest, group)
    return jnp.ceil(jnp.log2(largest))


def fixed(value, exponent):
    scaled = value * repeated(jnp.exp2(-exponent) * LEVELS, value.shape[0])
    return jnp.round(jnp.clip(scaled, -LEVELS, LEVELS)).astype(jnp.int32)


def paired(first, second):
    return (first << 16) | (second & 0xFFFF)


def unpaired(words):
    return words >> 16, (words << 16) >> 16


def scaled_back(codes, exponent):
    return codes.astype(f32) * repeated(jnp.exp2(exponent.astype(f32)) * (1.0 / LEVELS), codes.shape[0])


def sums_rows(rows):
    return rows + rows // 2 + SUBLANES


def encode_sums(out_ref, cols, u_re, u_im, v):
    rows = v.shape[0]
    half = rows // 2
    of_u, of_v = largest_exponent([u_re, u_im]), largest_exponent([v])
    out_ref[0:rows, cols] = paired(fixed(u_re, of_u), fixed(u_im, of_u))
    codes = fixed(v, of_v)
    out_ref[rows : rows + half, cols] = paired(codes[:half], codes[half:])
    out_ref[rows + half : rows + half + SUBLANES, cols] = paired(of_u.astype(jnp.int32), of_v.astype(jnp.int32))


def decode_sums(ref, cols, rows):
    half = rows // 2
    of_u, of_v = unpaired(ref[rows + half : rows + half + SUBLANES, cols])
    u_re, u_im = unpaired(ref[0:rows, cols])
    v = jnp.concatenate(unpaired(ref[rows : rows + half, cols]), axis=0)
    return scaled_back(u_re, of_u), scaled_back(u_im, of_u), scaled_back(v, of_v)


def decode_probe(out_ref, chunks_ref):
    chunks = chunks_ref.shape[0]
    rows = out_ref.shape[1] // chunks
    for chunk in range(chunks):
        for col in range(0, out_ref.shape[2], LANES):
            cols = pl.ds(col, LANES)
            exponent = chunks_ref[chunk, rows : rows + SUBLANES, cols]
            for comp, codes in enumerate(unpaired(chunks_ref[chunk, 0:rows, cols])):
                out_ref[comp, chunk * rows : (chunk + 1) * rows, cols] = scaled_back(codes, exponent)


def cut_chunk(ext_ref, comp, first, top, left, rows):
    row = pl.multiple_of(lax.div(top, SUBLANES) * SUBLANES, SUBLANES)
    col = pl.multiple_of(lax.div(left, LANES) * LANES, LANES)
    block = ext_ref[comp, pl.ds(row + first, rows + SUBLANES), pl.ds(col, 3 * LANES)]
    tiles = shifted_left(lane_tiles(block), lax.rem(left, LANES))
    return [shifted_up(tile, lax.rem(top, SUBLANES)) for tile in tiles]


def forward(order, ext_ref, probe_ref, consts, y, x, win_ref, power_ref, weight, xa_ref, xb_ref, ya_ref, yb_ref, far_ref):
    turns, twiddles = consts
    half = order // 2
    tw_re = repeated(twiddles[0, half : half + SUBLANES, :], CHUNK)
    tw_im = repeated(twiddles[1, half : half + SUBLANES, :], CHUNK)
    for first in range(0, order, CHUNK):
        rows = pl.ds(first, CHUNK)
        win_re = cut_chunk(ext_ref, 0, first, y, x, CHUNK)
        win_im = cut_chunk(ext_ref, 1, first, y, x, CHUNK)
        exits = []
        for k in range(2):
            cols = pl.ds(k * half, half)
            win_ref[0, rows, cols] = win_re[k]
            win_ref[1, rows, cols] = win_im[k]
            power_ref[rows, cols] += weight * (win_re[k] * win_re[k] + win_im[k] * win_im[k])
            p_re, p_im = probe_ref[0, rows, cols], probe_ref[1, rows, cols]
            exits.append((p_re * win_re[k] - p_im * win_im[k], p_re * win_im[k] + p_im * win_re[k]))
        (lo_re, lo_im), (hi_re, hi_im) = exits
        store_split(xa_ref, rows, pl.ds(0, half), lo_re + hi_re)
        store_split(xa_ref, rows, pl.ds(half, half), lo_im + hi_im)
        d_re, d_im = lo_re - hi_re, lo_im - hi_im
        store_split(xb_ref, rows, pl.ds(0, half), d_re * tw_re - d_im * tw_im)
        store_split(xb_ref, rows, pl.ds(half, half), d_re * tw_im + d_im * tw_re)
    yield
    ya_ref[...] = right_dot(xa_ref, turns.at[0])
    yb_ref[...] = right_dot(xb_ref, turns.at[0])
    yield
    for first in range(0, half, CHUNK):
        rows = pl.ds(first, CHUNK)
        below = pl.ds(half + first, CHUNK)
        t_re, t_im = twiddles[0, rows, :], twiddles[1, rows, :]
        for k, y_ref in enumerate((ya_ref, yb_ref)):
            cols = pl.ds(k * half, half)
            up_re, up_im = y_ref[rows, 0:half], y_ref[rows, half:order]
            dn_re, dn_im = y_ref[below, 0:half], y_ref[below, half:order]
            store_split(xa_ref, rows, cols, up_re + dn_re)
            store_split(xa_ref, below, cols, up_im + dn_im)
            d_re, d_im = up_re - dn_re, up_im - dn_im
            store_split(xb_ref, rows, cols, d_re * t_re - d_im * t_im)
            store_split(xb_ref, below, cols, d_re * t_im + d_im * t_re)
    yield
    far_ref[0] = left_dot(turns.at[1], xa_ref)
    far_ref[1] = left_dot(turns.at[1], xb_ref)
    yield


def backward(order, far_ref, amp_ref, consts, y, x, weight, probe_ref, win_ref, xa_ref, xb_ref, ya_ref, yb_ref, grad_ref, numer_ref):
    turns, twiddles = consts
    half = order // 2
    tw_re = repeated(twiddles[0, half : half + SUBLANES, :], CHUNK)
    tw_im = repeated(twiddles[1, half : half + SUBLANES, :], CHUNK)
    for k, x_ref in enumerate((xa_ref, xb_ref)):
        for first in range(0, half, CHUNK):
            rows = pl.ds(first, CHUNK)
            below = pl.ds(half + first, CHUNK)
            far_re, far_im = far_ref[k, rows, :], far_ref[k, below, :]
            amp = amp_ref[pl.ds(k * half + first, CHUNK), :].astype(f32) * weight
            factor = amp * lax.rsqrt(far_re * far_re + far_im * far_im + amplitude_floor)
            store_split(x_ref, rows, slice(None), far_re * factor)
            store_split(x_ref, below, slice(None), far_im * factor)
    yield
    ya_ref[...] = left_dot(turns.at[0], xa_ref)
    yb_ref[...] = left_dot(turns.at[0], xb_ref)
    yield
    for first in range(0, half, CHUNK):
        rows = pl.ds(first, CHUNK)
        below = pl.ds(half + first, CHUNK)
        t_re, t_im = twiddles[0, rows, :], twiddles[1, rows, :]
        for k, x_ref in enumerate((xa_ref, xb_ref)):
            cols = slice(k * half, (k + 1) * half)
            a_re, a_im = ya_ref[rows, cols], ya_ref[below, cols]
            b_re, b_im = yb_ref[rows, cols], yb_ref[below, cols]
            c_re, c_im = b_re * t_re + b_im * t_im, b_im * t_re - b_re * t_im
            store_split(x_ref, rows, pl.ds(0, half), a_re + c_re)
            store_split(x_ref, rows, pl.ds(half, half), a_im + c_im)
            store_split(x_ref, below, pl.ds(0, half), a_re - c_re)
            store_split(x_ref, below, pl.ds(half, half), a_im - c_im)
    yield
    ya_ref[...] = right_dot(xa_ref, turns.at[1])
    yb_ref[...] = right_dot(xb_ref, turns.at[1])
    yield

    def adder(comp):
        def add(rows, cols, moved):
            grad_ref[comp, rows, cols] += moved

        return add

    deposits = [Deposit(adder(comp), y, x) for comp in range(2)]
    for first in range(0, order, CHUNK):
        rows = pl.ds(first, CHUNK)
        a_re, a_im = ya_ref[rows, 0:half], ya_ref[rows, half:order]
        b_re, b_im = yb_ref[rows, 0:half], yb_ref[rows, half:order]
        c_re, c_im = b_re * tw_re + b_im * tw_im, b_im * tw_re - b_re * tw_im
        waves = [(a_re + c_re, a_im + c_im), (a_re - c_re, a_im - c_im)]
        terms = ([], [])
        for k, (wave_re, wave_im) in enumerate(waves):
            cols = pl.ds(k * half, half)
            p_re, p_im = probe_ref[0, rows, cols], probe_ref[1, rows, cols]
            w_re, w_im = win_ref[0, rows, cols], win_ref[1, rows, cols]
            terms[0].append(p_re * wave_re + p_im * wave_im)
            terms[1].append(p_re * wave_im - p_im * wave_re)
            numer_ref[0, rows, cols] += w_re * wave_re + w_im * wave_im
            numer_ref[1, rows, cols] += w_re * wave_im - w_im * wave_re
        for comp in range(2):
            deposits[comp].put(first, terms[comp])
    for deposit in deposits:
        deposit.finish(order)
    yield


def interleaved(*stages):
    live = list(stages)
    while live:
        still = []
        for stage in live:
            try:
                next(stage)
                still.append(stage)
            except StopIteration:
                pass
        live = still


def outgoing_kernel(dims, pos_ref, me_ref, amp_ref, after_ref, also_ref, out_ref, sems):
    tile_rows, tile_cols, pat_count, col_count, capacity = dims
    first = (me_ref[0] * col_count + me_ref[1]) * pat_count
    total = pos_ref.shape[0] // 2
    owners = [lax.div(pos_ref[total + first + k], tile_cols) for k in range(pat_count)]
    copies = []
    for k in range(pat_count):
        rank = sum(((owners[e] == owners[k]).astype(jnp.int32) for e in range(k)), jnp.int32(0))
        slot = owners[k] * SEND + jnp.minimum(rank, SEND - 1)
        copies.append(pltpu.make_async_copy(amp_ref.at[k], out_ref.at[slot], sems.at[k]))
        copies[-1].start()
    for copy in copies:
        copy.wait()


def weights_kernel(dims, span, pos_ref, me_ref, probe_ref, out_ref, sums_ref, power_ref):
    tile_rows, tile_cols, pat_count, col_count, capacity = dims
    order = probe_ref.shape[1]
    top = (me_ref[0] - 1) * tile_rows
    left = (me_ref[1] - 1) * tile_cols
    total = pos_ref.shape[0] // 2
    for first in range(0, sums_ref.shape[0], order):
        sums_ref[pl.ds(first, order), :] = jnp.zeros((order, sums_ref.shape[1]), f32)
    power_ref[...] = probe_ref[0] * probe_ref[0] + probe_ref[1] * probe_ref[1]

    def visit(index, carry):
        y = pos_ref[index] - top
        x = pos_ref[total + index] - left

        @pl.when((y > 0) & (y < (span + 1) * tile_rows) & (x > 0) & (x < (span + 1) * tile_cols))
        def _():
            def add(rows, cols, moved):
                sums_ref[rows, cols] += moved

            deposit = Deposit(add, y, x)
            for first in range(0, order, CHUNK):
                deposit.put(first, lane_tiles(power_ref[pl.ds(first, CHUNK), :]))
            deposit.finish(order)

        return carry

    lax.fori_loop(0, total, visit, 0)
    pltpu.sync_copy(sums_ref.at[pl.ds(tile_rows, span * tile_rows), pl.ds(tile_cols, span * tile_cols)], out_ref)


def encode_kernel(obj_ref, out_ref):
    rows = obj_ref.shape[1]
    encode(lambda comp, at, cols: obj_ref[comp, at, cols], out_ref, rows, 0, rows)


def unfold(dims, ext_ref, own_ref, coded_refs):
    tile_rows, tile_cols = dims[:2]
    ext_ref[:, 0:tile_rows, 0:tile_cols] = own_ref[...]
    for (i, j), ref in zip(((0, 1), (1, 0), (1, 1)), coded_refs):
        for col in range(0, tile_cols, LANES):
            for start in range(0, tile_rows, CHUNK):
                parts = decode(ref, start, tile_rows, col)
                for comp in range(2):
                    ext_ref[comp, pl.ds(i * tile_rows + start, CHUNK), pl.ds(j * tile_cols + col, LANES)] = parts[comp]


def spread_sums(out_ref, u_ref, v_ref):
    chunks = out_ref.shape[0]
    rows = v_ref.shape[0] // chunks
    for chunk in range(chunks):
        at = pl.ds(chunk * rows, rows)
        for col in range(0, v_ref.shape[1], LANES):
            cols = pl.ds(col, LANES)
            encode_sums(out_ref.at[chunk], cols, u_ref[0, at, cols], u_ref[1, at, cols], v_ref[at, cols])


def added(parts):
    while len(parts) > 1:
        parts = [tuple(x + y for x, y in zip(a, b)) for a, b in zip(parts[::2], parts[1::2])]
    return parts[0]


def sums_kernel(rows, parts_ref, *refs):
    out_ref = refs[-1]
    for col in range(0, out_ref.shape[2], LANES):
        cols = pl.ds(col, LANES)
        total = added([decode_sums(parts_ref.at[k], cols, rows) for k in range(parts_ref.shape[0])])
        encode_sums(out_ref.at[0], cols, *total)
        for k in range(1, out_ref.shape[0]):
            out_ref[k, :, cols] = out_ref[0, :, cols]


def update_kernel(rows, count, me_ref, probe_ref, *refs):
    out_ref = refs[-1]
    first = pl.multiple_of(me_ref[1] * rows, SUBLANES)
    for col in range(0, out_ref.shape[2], LANES):
        cols = pl.ds(col, LANES)
        u_re, u_im, v = added([decode_sums(ref.at[k], cols, rows) for ref in refs[:count] for k in range(ref.shape[0])])
        scale = 1.0 / (v + probe_regular)
        re = (probe_ref[0, pl.ds(first, rows), cols] + u_re) * scale
        im = (probe_ref[1, pl.ds(first, rows), cols] + u_im) * scale
        exponent = largest_exponent([re, im])
        words = paired(fixed(re, exponent), fixed(im, exponent))
        for chunk in range(out_ref.shape[0]):
            out_ref[chunk, 0:rows, cols] = words
            out_ref[chunk, rows : rows + SUBLANES, cols] = exponent.astype(jnp.int32)


def probe_kernel(chunks_ref, out_ref):
    decode_probe(out_ref, chunks_ref)


def first_half_kernel(dims, pos_ref, me_ref, own_ref, right_ref, below_ref, diag_ref, probe_ref, turns, twiddles,
                      far_out, win_out, power_out, ext_out, ext_ref, xa_ref, xb_ref, ya_ref, yb_ref, far_ref, win_ref, ys_ref, xs_ref, slots_ref, sems, win_sems, ext_sem):
    tile_rows, tile_cols, pat_count, col_count, capacity = dims
    order = probe_ref.shape[1]
    count = list_patterns(dims, pos_ref, me_ref, ys_ref, xs_ref, slots_ref)
    unfold(dims, ext_ref, own_ref, (right_ref, below_ref, diag_ref))
    keep = pltpu.make_async_copy(ext_ref, ext_out, ext_sem)
    keep.start()
    power_out[...] = jnp.zeros_like(power_out)
    consts = (turns, twiddles)

    def pair(step, carry):
        stages = []
        for k in range(2):
            listed = 2 * step + k
            weight = (listed < count).astype(f32)
            index = jnp.minimum(listed, count - 1)
            stages.append(forward(order, ext_ref, probe_ref, consts, ys_ref[index], xs_ref[index], win_ref.at[listed], power_out, weight,
                                  xa_ref.at[k], xb_ref.at[k], ya_ref.at[k], yb_ref.at[k], far_ref.at[listed]))
        interleaved(*stages)
        for k in range(2):
            listed = 2 * step + k
            pltpu.make_async_copy(far_ref.at[listed], far_out.at[listed], sems.at[listed]).start()
            pltpu.make_async_copy(win_ref.at[listed], win_out.at[listed], win_sems.at[listed]).start()
        return carry

    pairs = lax.div(count + 1, 2)
    lax.fori_loop(0, pairs, pair, 0)

    def settle(listed, carry):
        pltpu.make_async_copy(far_ref.at[listed], far_out.at[listed], sems.at[listed]).wait()
        pltpu.make_async_copy(win_ref.at[listed], win_out.at[listed], win_sems.at[listed]).wait()
        return carry

    lax.fori_loop(0, 2 * pairs, settle, 0)
    keep.wait()


def second_half_kernel(dims, pos_ref, me_ref, probe_ref, power_ref, late_weights, far_in, win_in, amp_in, turns, twiddles, sorting,
                       share_out, top_out, bottom_out, numer_out, amp_out,
                       sum_ref, xa_ref, xb_ref, ya_ref, yb_ref, numer_ref, far_ref, win_ref, amp_ref, sorted_ref, ys_ref, xs_ref, slots_ref, far_sems, win_sems, amp_sems, out_sems, sum_sem):
    tile_rows, tile_cols, pat_count, col_count, capacity = dims
    order = probe_ref.shape[1]
    count = list_patterns(dims, pos_ref, me_ref, ys_ref, xs_ref, slots_ref)
    pairs = lax.div(count + 1, 2)

    def copies(listed):
        return (
            pltpu.make_async_copy(far_in.at[listed], far_ref.at[listed], far_sems.at[listed]),
            pltpu.make_async_copy(win_in.at[listed], win_ref.at[listed], win_sems.at[listed]),
            pltpu.make_async_copy(amp_in.at[slots_ref[jnp.minimum(listed, count - 1)]], amp_ref.at[listed], amp_sems.at[listed]),
        )

    def begin(listed, carry):
        for copy in copies(listed):
            copy.start()
        return carry

    lax.fori_loop(0, 2 * pairs, begin, 0)
    sum_ref[...] = jnp.zeros_like(sum_ref)
    numer_ref[...] = jnp.zeros_like(numer_ref)
    consts = (turns, twiddles)

    def pair(step, carry):
        stages = []
        for k in range(2):
            listed = 2 * step + k
            for copy in copies(listed):
                copy.wait()
        for k in range(2):
            listed = 2 * step + k
            weight = (listed < count).astype(f32)
            index = jnp.minimum(listed, count - 1)
            y, x = ys_ref[index], xs_ref[index]
            rows_sorted = jnp.dot(sorting[0], amp_ref[listed], preferred_element_type=f32).astype(bf16)
            sorted_ref[listed] = jnp.dot(rows_sorted, sorting[1], preferred_element_type=f32).astype(bf16)
            stages.append(backward(order, far_ref.at[listed], sorted_ref.at[listed], consts, y, x, weight, probe_ref, win_ref.at[listed],
                                   xa_ref.at[k], xb_ref.at[k], ya_ref.at[k], yb_ref.at[k], sum_ref, numer_ref))
        interleaved(*stages)
        for k in range(2):
            listed = 2 * step + k
            pltpu.make_async_copy(sorted_ref.at[listed], amp_out.at[listed], out_sems.at[listed]).start()
        return carry

    lax.fori_loop(0, pairs, pair, 0)
    weights_ref, weights_come = late_weights
    weights_come()
    for first in range(0, 2 * tile_rows, CHUNK):
        rows = pl.ds(first, CHUNK)
        scale = 1.0 / (weights_ref[rows, :] + object_regular)
        for comp in range(2):
            sum_ref[comp, rows, :] = sum_ref[comp, rows, :] * scale
    keep = pltpu.make_async_copy(sum_ref, share_out, sum_sem)
    keep.start()
    encode(lambda comp, at, cols: sum_ref[comp, at, cols], top_out, tile_rows, 0, tile_rows)
    encode(lambda comp, at, cols: sum_ref[comp, pl.ds(tile_rows + at.start, at.size), cols], bottom_out, tile_rows, 0, tile_rows)
    spread_sums(numer_out, numer_ref, power_ref)

    def settle(listed, carry):
        pltpu.make_async_copy(sorted_ref.at[listed], amp_out.at[listed], out_sems.at[listed]).wait()
        return carry

    lax.fori_loop(0, 2 * pairs, settle, 0)
    keep.wait()


def rows_sum_kernel(dims, share_ref, above_ref, below_ref, after_ref, sum_out, left_out, right_out, sem):
    tile_rows, tile_cols = dims[:2]
    for i, ref in enumerate((above_ref, below_ref)):
        for col in range(0, 2 * tile_cols, LANES):
            for start in range(0, tile_rows, CHUNK):
                rows, cols = pl.ds(i * tile_rows + start, CHUNK), pl.ds(col, LANES)
                parts = decode(ref, start, tile_rows, col)
                for comp in range(2):
                    share_ref[comp, rows, cols] += parts[comp]
    keep = pltpu.make_async_copy(share_ref, sum_out, sem)
    keep.start()
    for j, ref in enumerate((left_out, right_out)):
        for i in range(2):

            def read(comp, at, cols, i=i, j=j):
                return share_ref[comp, pl.ds(i * tile_rows + at.start, at.size), pl.ds(j * tile_cols + cols.start, cols.size)]

            encode(read, ref, tile_rows, i * tile_rows, 2 * tile_rows + i * SUBLANES)
    keep.wait()


def whole_kernel(dims, pos_ref, me_ref, old_ref, sum_ref, from_left_ref, from_right_ref, weights_ref,
                 chunks_ref, amp_in, turns, twiddles,
                 current_out, top_out, bottom_out, numer_out, probe_ref,
                 ext_ref, grad_ref, win_ref, xa_ref, xb_ref, ya_ref, yb_ref, numer_ref, far_ref, amp_ref, ys_ref, xs_ref, slots_ref, amp_sems, own_sem, top_sem):
    tile_rows, tile_cols, pat_count, col_count, capacity = dims
    order = probe_ref.shape[1]
    count = list_patterns(dims, pos_ref, me_ref, ys_ref, xs_ref, slots_ref)
    pairs = lax.div(count + 1, 2)
    decode_probe(probe_ref, chunks_ref)

    def fetch(listed):
        return pltpu.make_async_copy(amp_in.at[jnp.minimum(listed, count - 1)], amp_ref.at[listed], amp_sems.at[listed])

    def begin(listed, carry):
        fetch(listed).start()
        return carry

    lax.fori_loop(0, 2 * pairs, begin, 0)
    for j, ref in enumerate((from_left_ref, from_right_ref)):
        for i in range(2):
            for col in range(0, tile_cols, LANES):
                for start in range(0, tile_rows, CHUNK):
                    rows, cols = pl.ds(i * tile_rows + start, CHUNK), pl.ds(j * tile_cols + col, LANES)
                    parts = decode(ref, i * tile_rows + start, 2 * tile_rows + i * SUBLANES, col)
                    scale = object_regular / (weights_ref[rows, cols] + object_regular)
                    for comp in range(2):
                        ext_ref[comp, rows, cols] = old_ref[comp, rows, cols] * scale + (sum_ref[comp, rows, cols] + parts[comp])
    keep = pltpu.make_async_copy(ext_ref.at[:, pl.ds(0, tile_rows), pl.ds(0, tile_cols)], current_out, own_sem)
    keep.start()
    grad_ref[...] = jnp.zeros_like(grad_ref)
    numer_ref[...] = jnp.zeros_like(numer_ref)
    consts = (turns, twiddles)

    def pair(step, carry):
        stages = []
        for k in range(2):
            fetch(2 * step + k).wait()
        for k in range(2):
            listed = 2 * step + k
            weight = (listed < count).astype(f32)
            index = jnp.minimum(listed, count - 1)
            y, x = ys_ref[index], xs_ref[index]

            def both(k=k, listed=listed, weight=weight, y=y, x=x):
                yield from forward(order, ext_ref, probe_ref, consts, y, x, win_ref.at[k], numer_ref.at[2], weight,
                                   xa_ref.at[k], xb_ref.at[k], ya_ref.at[k], yb_ref.at[k], far_ref.at[k])
                yield from backward(order, far_ref.at[k], amp_ref.at[listed], consts, y, x, weight, probe_ref, win_ref.at[k],
                                    xa_ref.at[k], xb_ref.at[k], ya_ref.at[k], yb_ref.at[k], grad_ref, numer_ref)

            stages.append(both())
        interleaved(*stages)
        return carry

    lax.fori_loop(0, pairs, pair, 0)
    for first in range(0, tile_rows, CHUNK):
        rows = pl.ds(first, CHUNK)
        scale = 1.0 / (weights_ref[rows, :] + object_regular)
        for comp in range(2):
            grad_ref[comp, rows, :] = grad_ref[comp, rows, :] * scale
    give = pltpu.make_async_copy(grad_ref.at[:, pl.ds(0, tile_rows), :], top_out, top_sem)
    give.start()

    def read(comp, at, cols):
        rows = pl.ds(tile_rows + at.start, at.size)
        return grad_ref[comp, rows, cols] / (weights_ref[rows, cols] + object_regular)

    encode(read, bottom_out, tile_rows, 0, tile_rows)
    spread_sums(numer_out, numer_ref, numer_ref.at[2])
    keep.wait()
    give.wait()


def fold_kernel(dims, top_ref, above_ref, own_out, right_out, own_ref, sem):
    tile_rows, tile_cols = dims[:2]
    for col in range(0, 2 * tile_cols, LANES):
        for start in range(0, tile_rows, CHUNK):
            rows, cols = pl.ds(start, CHUNK), pl.ds(col, LANES)
            parts = decode(above_ref, start, tile_rows, col)
            for comp in range(2):
                if col < tile_cols:
                    own_ref[comp, rows, cols] = top_ref[comp, rows, cols] + parts[comp]
                else:
                    top_ref[comp, rows, cols] += parts[comp]
    keep = pltpu.make_async_copy(own_ref, own_out, sem)
    keep.start()
    encode(lambda comp, at, cols: top_ref[comp, at, pl.ds(tile_cols + cols.start, cols.size)], right_out, tile_rows, 0, tile_rows)
    keep.wait()


def object_kernel(dims, current_ref, own_ref, left_ref, before_ref, weights_ref, out_ref):
    tile_rows, tile_cols = dims[:2]
    for col in range(0, tile_cols, LANES):
        for start in range(0, tile_rows, CHUNK):
            rows, cols = pl.ds(start, CHUNK), pl.ds(col, LANES)
            scale = 1.0 / (weights_ref[rows, cols] + object_regular)
            back = (before_ref[rows, cols] + object_regular) * scale
            parts = decode(left_ref, start, tile_rows, col)
            for comp in range(2):
                old = object_regular * scale * current_ref[comp, rows, cols]
                out_ref[comp, rows, cols] = old + (own_ref[comp, rows, cols] + parts[comp]) * back


def shape(dims, dtype=f32):
    return jax.ShapeDtypeStruct(dims, dtype)


def work_scratch(order):
    return [
        pltpu.VMEM((2, 2, order, order), bf16),
        pltpu.VMEM((2, 2, order, order), bf16),
        pltpu.VMEM((2, order, order), f32),
        pltpu.VMEM((2, order, order), f32),
    ]


def list_scratch(capacity):
    return [pltpu.SMEM((capacity,), jnp.int32)] * 3


def call(kernel, outs, out_specs, in_specs, scratch, flops, limit=26 << 20):
    several = isinstance(outs, tuple)
    out_count = len(outs) if several else 1
    in_count = len(in_specs)
    loaded = [k for k, spec in enumerate(in_specs) if spec is LOAD or spec is LATE]

    def body(*refs):
        ins, rest = list(refs[:in_count]), refs[in_count:]
        given, kept = rest[: out_count + len(scratch)], rest[out_count + len(scratch) :]
        copies = [pltpu.make_async_copy(ins[k], kept[n], kept[-1].at[n]) for n, k in enumerate(loaded)]
        for copy in copies:
            copy.start()
        for n, k in enumerate(loaded):
            if in_specs[k] is LOAD:
                copies[n].wait()
                ins[k] = kept[n]
            else:
                ins[k] = (kept[n], copies[n].wait)
        kernel(*ins, *given)

    fixed_outs = [
        pltpu.HBM(out.shape, out.dtype) if spec is HBM else pltpu.VMEM(out.shape, out.dtype) if spec is PIN else out
        for out, spec in zip(outs if several else (outs,), out_specs if several else (out_specs,))
    ]
    places = [pltpu.HBM if spec in (LOAD, LATE, HBM) else pltpu.VMEM if spec is PIN else None for spec in in_specs]

    def called(*args):
        args = [arg if place is None else pltpu.with_memory_space_constraint(arg, place) for arg, place in zip(args, places)]
        own = [pltpu.VMEM(args[k].shape, args[k].dtype) for k in loaded]
        if loaded:
            own.append(pltpu.SemaphoreType.DMA((len(loaded),)))
        return pl.pallas_call(
            body,
            out_shape=tuple(fixed_outs) if several else fixed_outs[0],
            out_specs=out_specs,
            in_specs=[HBM if spec in (LOAD, LATE) else spec for spec in in_specs],
            scratch_shapes=list(scratch) + own,
            compiler_params=pltpu.CompilerParams(vmem_limit_bytes=limit),
            cost_estimate=pl.CostEstimate(flops=flops, bytes_accessed=8 << 20, transcendentals=0),
        )(*args)

    return called


def passed_along(value, axis, steps):
    count = lax.axis_size(axis)
    leading, last = (max(0, -steps), min(count, count - steps))
    return lax.ppermute(value, axis, [(source, source + steps) for source in range(leading, last)])


def swapped(value, axis, mask):
    return lax.ppermute(value, axis, [(k, k ^ mask) for k in range(lax.axis_size(axis))])


def probe_update(me, probe, numer, kind, at_once, before_sum, before_update):
    cols, order = lax.axis_size("col"), probe.shape[1]
    rows = order // cols
    parts = lax.all_to_all(numer, "col", split_axis=0, concat_axis=0, tiled=True)
    blocks = lax.axis_size("row") if at_once else 1
    total = call(
        functools.partial(sums_kernel, rows), shape((blocks, sums_rows(rows), order), jnp.int32), VMEM,
        [VMEM] + [spec for spec, _ in before_sum], [], 1 << 26,
    )(parts, *[value for _, value in before_sum])
    if at_once:
        totals = [lax.all_to_all(total, "row", split_axis=0, concat_axis=0, tiled=True)]
    else:
        totals = [total] + [swapped(total, "row", mask) for mask in range(1, lax.axis_size("row"))]
    fresh = call(
        functools.partial(update_kernel, rows, len(totals)), shape((cols, rows + SUBLANES, order), jnp.int32), VMEM,
        [SMEM, kind] + [VMEM] * len(totals) + [FREE] * len(before_update), [], 1 << 26,
    )(me, probe, *totals, *before_update)
    return total, lax.all_to_all(fresh, "col", split_axis=0, concat_axis=0, tiled=True)


def local(obj, probe, amplitudes, positions):
    col_count = lax.axis_size("col")
    tile_rows, tile_cols = obj.shape[1], obj.shape[2]
    order = probe.shape[1]
    pat_count = amplitudes.shape[0]
    capacity = 2 * pat_count
    dims = (tile_rows, tile_cols, pat_count, col_count, capacity)
    me = jnp.stack([lax.axis_index("row"), lax.axis_index("col")]).astype(jnp.int32)
    pos = positions.T.reshape(-1)
    turns, twiddles, sorting = tables(order)
    tile = (2, tile_rows, tile_cols)
    window = (2, order, order)
    wide = (2, 2 * tile_rows, 2 * tile_cols)
    shares = shape((col_count, sums_rows(order // col_count), order), jnp.int32)
    coded_tile = shape((tile_rows + SUBLANES, tile_cols), jnp.int32)
    coded_row = shape((tile_rows + SUBLANES, 2 * tile_cols), jnp.int32)
    coded_col = shape((2 * (tile_rows + SUBLANES), tile_cols), jnp.int32)
    one_pattern = 24 * 2 * order**3

    coded = call(encode_kernel, coded_tile, VMEM, [LOAD], [], 1 << 26)(obj)
    right = passed_along(coded, "col", -1)
    below = passed_along(coded, "row", -1)
    diag = passed_along(right, "row", -1)

    outgoing = call(
        functools.partial(outgoing_kernel, dims), shape((col_count * SEND, order, order), bf16), HBM, [SMEM, SMEM, LOAD, FREE, FREE],
        [pltpu.SemaphoreType.DMA((pat_count,))], 1 << 20,
    )(pos, me, amplitudes, right, below)
    incoming = lax.all_to_all(outgoing, "col", split_axis=0, concat_axis=0, tiled=True)

    def weights(probe_now, span, kind):
        return call(
            functools.partial(weights_kernel, dims, span), shape((span * tile_rows, span * tile_cols)), HBM, [SMEM, SMEM, kind],
            [pltpu.VMEM(((span + 2) * tile_rows, (span + 2) * tile_cols), f32), pltpu.VMEM((order, order), f32)], 8 << 30,
        )(pos, me, probe_now)

    weights_old = weights(probe, 2, LOAD)

    far, wins, power, ext = call(
        functools.partial(first_half_kernel, dims), (shape((capacity,) + window), shape((capacity,) + window), shape((order, order)), shape(wide)), (HBM, HBM, VMEM, HBM),
        [SMEM, SMEM, LOAD] + [VMEM] * 3 + [LOAD] * 3,
        [pltpu.VMEM(wide, f32)] + work_scratch(order) + [pltpu.VMEM((capacity,) + window, f32)] * 2 + list_scratch(capacity)
        + [pltpu.SemaphoreType.DMA((capacity,))] * 2 + [pltpu.SemaphoreType.DMA],
        capacity * one_pattern // 2,
    )(pos, me, obj, right, below, diag, probe, turns, twiddles)

    share, top, bottom, numer, sorted_amps = call(
        functools.partial(second_half_kernel, dims),
        (shape(wide), coded_row, coded_row, shares, shape((capacity, order, order), bf16)),
        (HBM, VMEM, VMEM, VMEM, HBM),
        [SMEM, SMEM, LOAD, VMEM, LATE, HBM, HBM, FREE] + [LOAD] * 3,
        [pltpu.VMEM(wide, f32)] + work_scratch(order)
        + [pltpu.VMEM(window, f32)] + [pltpu.VMEM((capacity,) + window, f32)] * 2 + [pltpu.VMEM((capacity, order, order), bf16)] * 2
        + list_scratch(capacity) + [pltpu.SemaphoreType.DMA((capacity,))] * 4 + [pltpu.SemaphoreType.DMA],
        capacity * one_pattern // 2,
    )(pos, me, probe, power, weights_old, far, wins, incoming, turns, twiddles, sorting)

    from_above = passed_along(bottom, "row", 1)
    from_below = passed_along(top, "row", -1)
    total, chunks = probe_update(me, probe, numer, LOAD, True, [], [])
    sums, to_left, to_right = call(
        functools.partial(rows_sum_kernel, dims), (shape(wide), coded_col, coded_col), (HBM, VMEM, VMEM), [LOAD, VMEM, VMEM, FREE], [pltpu.SemaphoreType.DMA], 1 << 26,
    )(share, from_above, from_below, total)
    from_left = passed_along(to_right, "col", 1)
    from_right = passed_along(to_left, "col", -1)

    current, top, bottom, numer, probe_now = call(
        functools.partial(whole_kernel, dims), (shape(tile), shape((2, tile_rows, 2 * tile_cols)), coded_row, shares, shape(window)), (HBM, HBM) + (VMEM,) * 3,
        [SMEM, SMEM, LOAD, LOAD, VMEM, VMEM, LOAD, VMEM, HBM, LOAD, LOAD],
        [pltpu.VMEM(wide, f32), pltpu.VMEM(wide, f32), pltpu.VMEM((2,) + window, f32)] + work_scratch(order)
        + [pltpu.VMEM((3, order, order), f32), pltpu.VMEM((2,) + window, f32), pltpu.VMEM((capacity, order, order), bf16)]
        + list_scratch(capacity) + [pltpu.SemaphoreType.DMA((capacity,)), pltpu.SemaphoreType.DMA, pltpu.SemaphoreType.DMA],
        capacity * one_pattern,
    )(pos, me, ext, sums, from_left, from_right, weights_old, chunks, sorted_amps, turns, twiddles)

    from_above = passed_along(bottom, "row", 1)
    weights_new = weights(probe_now, 1, VMEM)
    own, to_right = call(
        functools.partial(fold_kernel, dims), (shape(tile), coded_tile), (HBM, VMEM), [LOAD, VMEM], [pltpu.VMEM(tile, f32), pltpu.SemaphoreType.DMA], 1 << 26,
    )(top, from_above)
    from_left = passed_along(to_right, "col", 1)
    new_object = call(functools.partial(object_kernel, dims), shape(tile), VMEM, [LOAD, LOAD, VMEM, LOAD, LOAD], [], 1 << 26)(
        current, own, from_left, weights_old, weights_new
    )
    _, chunks = probe_update(me, probe_now, numer, VMEM, False, [(HBM, weights_new)], [from_left])
    new_probe = call(probe_kernel, shape(window), VMEM, [VMEM], [], 1 << 26)(chunks)
    return new_object, new_probe


def solution(mesh):
    placed = (P(None, "row", "col"), P(), P(("row", "col"), None, None), P())
    return jax.shard_map(local, mesh=mesh, in_specs=placed, out_specs=(P(None, "row", "col"), P()), check_vma=False)
```

```python
import functools

import jax
import jax.numpy as jnp
import numpy as np
from jax import lax
from jax.experimental import pallas as pl
from jax.experimental.pallas import tpu as pltpu
from jax.sharding import PartitionSpec as P

ITERS = 2
SEND = 2

amplitude_floor = 0.1
object_regular = 0.5
probe_regular = 1.0

LANES = 128
SUBLANES = 8
LEVELS = 32767.0
CHUNK = 32
VMEM = pl.BlockSpec(memory_space=pltpu.VMEM)
SMEM = pl.BlockSpec(memory_space=pltpu.SMEM)
HBM = pl.BlockSpec(memory_space=pltpu.HBM)
LOAD = object()
LATE = object()
FREE = pl.BlockSpec(memory_space=pl.ANY)
PIN = pl.BlockSpec(memory_space=pltpu.VMEM)
f32 = jnp.float32
bf16 = jnp.bfloat16


def tables(order):
    half = order // 2
    counter = np.arange(half)
    angles = 2.0 * np.pi * ((counter[:, None] * counter[None, :]) % half) / half
    cos, sin = np.cos(angles), np.sin(angles)
    scale = 1.0 / np.sqrt(order)
    turns = []
    for block in ([[cos, -sin], [sin, cos]], [[cos, sin], [-sin, cos]]):
        matrix = np.block(block) * scale
        high = matrix.astype(jnp.bfloat16)
        turns.append(np.stack([high, (matrix - high.astype(np.float64)).astype(jnp.bfloat16)]))
    turn = 2.0 * np.pi * counter / order
    twiddle = np.stack([np.cos(turn), -np.sin(turn)]).astype(np.float32)
    twiddles = np.concatenate(
        [np.broadcast_to(twiddle[:, :, None], (2, half, half)), np.broadcast_to(twiddle[:, None, :], (2, SUBLANES, half))], axis=1
    )
    sorting = np.zeros((order, order), np.float32)
    sorting[np.arange(half), 2 * np.arange(half)] = 1.0
    sorting[half + np.arange(half), 2 * np.arange(half) + 1] = 1.0
    return (
        jnp.asarray(np.stack(turns)),
        jnp.asarray(np.ascontiguousarray(twiddles)),
        jnp.asarray(np.stack([sorting, sorting.T]).astype(jnp.bfloat16)),
    )


def list_patterns(dims, pos_ref, me_ref, ys_ref, xs_ref, slots_ref):
    tile_rows, tile_cols, pat_count, col_count, capacity = dims
    my_row, my_col = me_ref[0], me_ref[1]
    band_count = pat_count * col_count
    first = my_row * band_count
    total = pos_ref.shape[0] // 2

    def visit(index, carry):
        found, source, rank = carry
        y = pos_ref[first + index]
        x = pos_ref[total + first + index]
        here = lax.div(x, tile_cols) == my_col
        holder = lax.div(index, pat_count)
        rank = jnp.where(holder == source, rank, 0)

        @pl.when(here & (found < capacity))
        def _():
            ys_ref[found] = y - my_row * tile_rows
            xs_ref[found] = x - my_col * tile_cols
            slots_ref[found] = holder * SEND + jnp.minimum(rank, SEND - 1)

        step = here.astype(jnp.int32)
        return found + step, holder, rank + step

    found, _, _ = lax.fori_loop(0, band_count, visit, (jnp.int32(0), jnp.int32(-1), jnp.int32(0)))
    return jnp.minimum(found, capacity)


def lane_index(rows):
    return lax.broadcasted_iota(jnp.int32, (rows, LANES), 1)


def shifted_left(tiles, shift):
    lane = lane_index(tiles[0].shape[0])
    turn = lax.rem(LANES - shift, LANES)
    rolled = [pltpu.roll(tile, turn, axis=1) for tile in tiles]
    inside = lane < LANES - shift
    return [jnp.where(inside, a, b) for a, b in zip(rolled[:-1], rolled[1:])]


def shifted_right(tiles, shift):
    lane = lane_index(tiles[0].shape[0])
    rolled = [pltpu.roll(tile, shift, axis=1) for tile in tiles]
    outside = lane < shift
    zero = jnp.zeros_like(rolled[0])
    firsts = [zero] + rolled
    seconds = rolled + [zero]
    return [jnp.where(outside, a, b) for a, b in zip(firsts, seconds)]


def row_groups(tile):
    return [tile[k : k + SUBLANES] for k in range(0, tile.shape[0], SUBLANES)]


def shifted_up(tile, shift):
    row = lax.broadcasted_iota(jnp.int32, (SUBLANES, LANES), 0)
    turn = lax.rem(SUBLANES - shift, SUBLANES)
    rolled = [pltpu.roll(group, turn, axis=0) for group in row_groups(tile)]
    inside = row < SUBLANES - shift
    return jnp.concatenate([jnp.where(inside, a, b) for a, b in zip(rolled[:-1], rolled[1:])], axis=0)


def shifted_down(before, tile, shift):
    row = lax.broadcasted_iota(jnp.int32, (SUBLANES, LANES), 0)
    rolled = [before] + [pltpu.roll(group, shift, axis=0) for group in row_groups(tile)]
    outside = row < shift
    return rolled[-1], jnp.concatenate([jnp.where(outside, a, b) for a, b in zip(rolled[:-1], rolled[1:])], axis=0)


class Deposit:
    def __init__(self, add, top, left):
        self.add = add
        self.row = pl.multiple_of(lax.div(top, SUBLANES) * SUBLANES, SUBLANES)
        self.col = pl.multiple_of(lax.div(left, LANES) * LANES, LANES)
        self.down = lax.rem(top, SUBLANES)
        self.right = lax.rem(left, LANES)
        self.carried = None

    def place(self, first, tiles):
        moved = jnp.concatenate(shifted_right(tiles, self.right), axis=1)
        self.add(pl.ds(self.row + first, tiles[0].shape[0]), pl.ds(self.col, moved.shape[1]), moved)

    def put(self, first, tiles):
        if self.carried is None:
            self.carried = [jnp.zeros((SUBLANES, LANES), f32) for _ in tiles]
        pairs = [shifted_down(before, tile, self.down) for before, tile in zip(self.carried, tiles)]
        self.carried = [carried for carried, _ in pairs]
        self.place(first, [tile for _, tile in pairs])

    def finish(self, first):
        row = lax.broadcasted_iota(jnp.int32, (SUBLANES, LANES), 0)
        self.place(first, [jnp.where(row < self.down, tile, 0.0) for tile in self.carried])


def lane_tiles(value):
    return [value[:, k : k + LANES] for k in range(0, value.shape[1], LANES)]


def store_split(ref, rows, cols, value):
    high = value.astype(bf16)
    ref[0, rows, cols] = high
    ref[1, rows, cols] = (value - high.astype(f32)).astype(bf16)


def right_dot(x_ref, table_ref):
    left = jnp.concatenate([x_ref[0], x_ref[1], x_ref[0]], axis=1)
    right = jnp.concatenate([table_ref[0], table_ref[0], table_ref[1]], axis=0)
    return jnp.dot(left, right, preferred_element_type=f32)


def left_dot(table_ref, x_ref):
    left = jnp.concatenate([table_ref[0], table_ref[0], table_ref[1]], axis=1)
    right = jnp.concatenate([x_ref[0], x_ref[1], x_ref[0]], axis=0)
    return jnp.dot(left, right, preferred_element_type=f32)


def repeated(group, rows):
    return jnp.concatenate([group] * (rows // SUBLANES), axis=0)


def encode(read, out_ref, rows, first, last):
    for col in range(0, out_ref.shape[1], LANES):
        cols = pl.ds(col, LANES)
        largest = jnp.full((SUBLANES, LANES), 1e-30, f32)
        for start in range(0, rows, CHUNK):
            for comp in range(2):
                for group in row_groups(jnp.abs(read(comp, pl.ds(start, CHUNK), cols))):
                    largest = jnp.maximum(largest, group)
        exponent = jnp.ceil(jnp.log2(largest))
        out_ref[last : last + SUBLANES, cols] = exponent.astype(jnp.int32)
        scale = repeated(jnp.exp2(-exponent) * LEVELS, CHUNK)
        for start in range(0, rows, CHUNK):
            codes = []
            for comp in range(2):
                scaled = jnp.clip(read(comp, pl.ds(start, CHUNK), cols) * scale, -LEVELS, LEVELS)
                codes.append(jnp.round(scaled).astype(jnp.int32))
            out_ref[pl.ds(first + start, CHUNK), cols] = (codes[0] << 16) | (codes[1] & 0xFFFF)


def decode(ref, start, last, col):
    cols = pl.ds(col, LANES)
    words = ref[pl.ds(start, CHUNK), cols]
    scale = repeated(jnp.exp2(ref[last : last + SUBLANES, cols].astype(f32)) * (1.0 / LEVELS), CHUNK)
    return (words >> 16).astype(f32) * scale, ((words << 16) >> 16).astype(f32) * scale


def largest_exponent(values):
    largest = jnp.full((SUBLANES, LANES), 1e-30, f32)
    for value in values:
        for group in row_groups(jnp.abs(value)):
            largest = jnp.maximum(largest, group)
    return jnp.ceil(jnp.log2(largest))


def fixed(value, exponent):
    scaled = value * repeated(jnp.exp2(-exponent) * LEVELS, value.shape[0])
    return jnp.round(jnp.clip(scaled, -LEVELS, LEVELS)).astype(jnp.int32)


def paired(first, second):
    return (first << 16) | (second & 0xFFFF)


def unpaired(words):
    return words >> 16, (words << 16) >> 16


def scaled_back(codes, exponent):
    return codes.astype(f32) * repeated(jnp.exp2(exponent.astype(f32)) * (1.0 / LEVELS), codes.shape[0])


def sums_rows(rows):
    return rows + rows // 2 + SUBLANES


def encode_sums(out_ref, cols, u_re, u_im, v):
    rows = v.shape[0]
    half = rows // 2
    of_u, of_v = largest_exponent([u_re, u_im]), largest_exponent([v])
    out_ref[0:rows, cols] = paired(fixed(u_re, of_u), fixed(u_im, of_u))
    codes = fixed(v, of_v)
    out_ref[rows : rows + half, cols] = paired(codes[:half], codes[half:])
    out_ref[rows + half : rows + half + SUBLANES, cols] = paired(of_u.astype(jnp.int32), of_v.astype(jnp.int32))


def decode_sums(ref, cols, rows):
    half = rows // 2
    of_u, of_v = unpaired(ref[rows + half : rows + half + SUBLANES, cols])
    u_re, u_im = unpaired(ref[0:rows, cols])
    v = jnp.concatenate(unpaired(ref[rows : rows + half, cols]), axis=0)
    return scaled_back(u_re, of_u), scaled_back(u_im, of_u), scaled_back(v, of_v)


def decode_probe(out_ref, chunks_ref):
    chunks = chunks_ref.shape[0]
    rows = out_ref.shape[1] // chunks
    for chunk in range(chunks):
        for col in range(0, out_ref.shape[2], LANES):
            cols = pl.ds(col, LANES)
            exponent = chunks_ref[chunk, rows : rows + SUBLANES, cols]
            for comp, codes in enumerate(unpaired(chunks_ref[chunk, 0:rows, cols])):
                out_ref[comp, chunk * rows : (chunk + 1) * rows, cols] = scaled_back(codes, exponent)


def cut_chunk(ext_ref, comp, first, top, left, rows):
    row = pl.multiple_of(lax.div(top, SUBLANES) * SUBLANES, SUBLANES)
    col = pl.multiple_of(lax.div(left, LANES) * LANES, LANES)
    block = ext_ref[comp, pl.ds(row + first, rows + SUBLANES), pl.ds(col, 3 * LANES)]
    tiles = shifted_left(lane_tiles(block), lax.rem(left, LANES))
    return [shifted_up(tile, lax.rem(top, SUBLANES)) for tile in tiles]


def forward(order, ext_ref, probe_ref, consts, y, x, win_ref, power_ref, weight, xa_ref, xb_ref, ya_ref, yb_ref, far_ref):
    turns, twiddles = consts
    half = order // 2
    tw_re = repeated(twiddles[0, half : half + SUBLANES, :], CHUNK)
    tw_im = repeated(twiddles[1, half : half + SUBLANES, :], CHUNK)
    for first in range(0, order, CHUNK):
        rows = pl.ds(first, CHUNK)
        win_re = cut_chunk(ext_ref, 0, first, y, x, CHUNK)
        win_im = cut_chunk(ext_ref, 1, first, y, x, CHUNK)
        exits = []
        for k in range(2):
            cols = pl.ds(k * half, half)
            win_ref[0, rows, cols] = win_re[k]
            win_ref[1, rows, cols] = win_im[k]
            power_ref[rows, cols] += weight * (win_re[k] * win_re[k] + win_im[k] * win_im[k])
            p_re, p_im = probe_ref[0, rows, cols], probe_ref[1, rows, cols]
            exits.append((p_re * win_re[k] - p_im * win_im[k], p_re * win_im[k] + p_im * win_re[k]))
        (lo_re, lo_im), (hi_re, hi_im) = exits
        store_split(xa_ref, rows, pl.ds(0, half), lo_re + hi_re)
        store_split(xa_ref, rows, pl.ds(half, half), lo_im + hi_im)
        d_re, d_im = lo_re - hi_re, lo_im - hi_im
        store_split(xb_ref, rows, pl.ds(0, half), d_re * tw_re - d_im * tw_im)
        store_split(xb_ref, rows, pl.ds(half, half), d_re * tw_im + d_im * tw_re)
    yield
    ya_ref[...] = right_dot(xa_ref, turns.at[0])
    yb_ref[...] = right_dot(xb_ref, turns.at[0])
    yield
    for first in range(0, half, CHUNK):
        rows = pl.ds(first, CHUNK)
        below = pl.ds(half + first, CHUNK)
        t_re, t_im = twiddles[0, rows, :], twiddles[1, rows, :]
        for k, y_ref in enumerate((ya_ref, yb_ref)):
            cols = pl.ds(k * half, half)
            up_re, up_im = y_ref[rows, 0:half], y_ref[rows, half:order]
            dn_re, dn_im = y_ref[below, 0:half], y_ref[below, half:order]
            store_split(xa_ref, rows, cols, up_re + dn_re)
            store_split(xa_ref, below, cols, up_im + dn_im)
            d_re, d_im = up_re - dn_re, up_im - dn_im
            store_split(xb_ref, rows, cols, d_re * t_re - d_im * t_im)
            store_split(xb_ref, below, cols, d_re * t_im + d_im * t_re)
    yield
    far_ref[0] = left_dot(turns.at[1], xa_ref)
    far_ref[1] = left_dot(turns.at[1], xb_ref)
    yield


def backward(order, far_ref, amp_ref, consts, y, x, weight, probe_ref, win_ref, xa_ref, xb_ref, ya_ref, yb_ref, grad_ref, numer_ref):
    turns, twiddles = consts
    half = order // 2
    tw_re = repeated(twiddles[0, half : half + SUBLANES, :], CHUNK)
    tw_im = repeated(twiddles[1, half : half + SUBLANES, :], CHUNK)
    for k, x_ref in enumerate((xa_ref, xb_ref)):
        for first in range(0, half, CHUNK):
            rows = pl.ds(first, CHUNK)
            below = pl.ds(half + first, CHUNK)
            far_re, far_im = far_ref[k, rows, :], far_ref[k, below, :]
            amp = amp_ref[pl.ds(k * half + first, CHUNK), :].astype(f32) * weight
            factor = amp * lax.rsqrt(far_re * far_re + far_im * far_im + amplitude_floor)
            store_split(x_ref, rows, slice(None), far_re * factor)
            store_split(x_ref, below, slice(None), far_im * factor)
    yield
    ya_ref[...] = left_dot(turns.at[0], xa_ref)
    yb_ref[...] = left_dot(turns.at[0], xb_ref)
    yield
    for first in range(0, half, CHUNK):
        rows = pl.ds(first, CHUNK)
        below = pl.ds(half + first, CHUNK)
        t_re, t_im = twiddles[0, rows, :], twiddles[1, rows, :]
        for k, x_ref in enumerate((xa_ref, xb_ref)):
            cols = slice(k * half, (k + 1) * half)
            a_re, a_im = ya_ref[rows, cols], ya_ref[below, cols]
            b_re, b_im = yb_ref[rows, cols], yb_ref[below, cols]
            c_re, c_im = b_re * t_re + b_im * t_im, b_im * t_re - b_re * t_im
            store_split(x_ref, rows, pl.ds(0, half), a_re + c_re)
            store_split(x_ref, rows, pl.ds(half, half), a_im + c_im)
            store_split(x_ref, below, pl.ds(0, half), a_re - c_re)
            store_split(x_ref, below, pl.ds(half, half), a_im - c_im)
    yield
    ya_ref[...] = right_dot(xa_ref, turns.at[1])
    yb_ref[...] = right_dot(xb_ref, turns.at[1])
    yield

    def adder(comp):
        def add(rows, cols, moved):
            grad_ref[comp, rows, cols] += moved

        return add

    deposits = [Deposit(adder(comp), y, x) for comp in range(2)]
    for first in range(0, order, CHUNK):
        rows = pl.ds(first, CHUNK)
        a_re, a_im = ya_ref[rows, 0:half], ya_ref[rows, half:order]
        b_re, b_im = yb_ref[rows, 0:half], yb_ref[rows, half:order]
        c_re, c_im = b_re * tw_re + b_im * tw_im, b_im * tw_re - b_re * tw_im
        waves = [(a_re + c_re, a_im + c_im), (a_re - c_re, a_im - c_im)]
        terms = ([], [])
        for k, (wave_re, wave_im) in enumerate(waves):
            cols = pl.ds(k * half, half)
            p_re, p_im = probe_ref[0, rows, cols], probe_ref[1, rows, cols]
            w_re, w_im = win_ref[0, rows, cols], win_ref[1, rows, cols]
            terms[0].append(p_re * wave_re + p_im * wave_im)
            terms[1].append(p_re * wave_im - p_im * wave_re)
            numer_ref[0, rows, cols] += w_re * wave_re + w_im * wave_im
            numer_ref[1, rows, cols] += w_re * wave_im - w_im * wave_re
        for comp in range(2):
            deposits[comp].put(first, terms[comp])
    for deposit in deposits:
        deposit.finish(order)
    yield


def interleaved(*stages):
    live = list(stages)
    while live:
        still = []
        for stage in live:
            try:
                next(stage)
                still.append(stage)
            except StopIteration:
                pass
        live = still


def outgoing_kernel(dims, pos_ref, me_ref, amp_ref, after_ref, also_ref, out_ref, sems):
    tile_rows, tile_cols, pat_count, col_count, capacity = dims
    first = (me_ref[0] * col_count + me_ref[1]) * pat_count
    total = pos_ref.shape[0] // 2
    owners = [lax.div(pos_ref[total + first + k], tile_cols) for k in range(pat_count)]
    copies = []
    for k in range(pat_count):
        rank = sum(((owners[e] == owners[k]).astype(jnp.int32) for e in range(k)), jnp.int32(0))
        slot = owners[k] * SEND + jnp.minimum(rank, SEND - 1)
        copies.append(pltpu.make_async_copy(amp_ref.at[k], out_ref.at[slot], sems.at[k]))
        copies[-1].start()
    for copy in copies:
        copy.wait()


def weights_kernel(dims, span, pos_ref, me_ref, probe_ref, out_ref, sums_ref, power_ref):
    tile_rows, tile_cols, pat_count, col_count, capacity = dims
    order = probe_ref.shape[1]
    top = (me_ref[0] - 1) * tile_rows
    left = (me_ref[1] - 1) * tile_cols
    total = pos_ref.shape[0] // 2
    for first in range(0, sums_ref.shape[0], order):
        sums_ref[pl.ds(first, order), :] = jnp.zeros((order, sums_ref.shape[1]), f32)
    power_ref[...] = probe_ref[0] * probe_ref[0] + probe_ref[1] * probe_ref[1]

    def visit(index, carry):
        y = pos_ref[index] - top
        x = pos_ref[total + index] - left

        @pl.when((y > 0) & (y < (span + 1) * tile_rows) & (x > 0) & (x < (span + 1) * tile_cols))
        def _():
            def add(rows, cols, moved):
                sums_ref[rows, cols] += moved

            deposit = Deposit(add, y, x)
            for first in range(0, order, CHUNK):
                deposit.put(first, lane_tiles(power_ref[pl.ds(first, CHUNK), :]))
            deposit.finish(order)

        return carry

    lax.fori_loop(0, total, visit, 0)
    pltpu.sync_copy(sums_ref.at[pl.ds(tile_rows, span * tile_rows), pl.ds(tile_cols, span * tile_cols)], out_ref)


def encode_kernel(obj_ref, out_ref):
    rows = obj_ref.shape[1]
    encode(lambda comp, at, cols: obj_ref[comp, at, cols], out_ref, rows, 0, rows)


def unfold(dims, ext_ref, own_ref, coded_refs):
    tile_rows, tile_cols = dims[:2]
    ext_ref[:, 0:tile_rows, 0:tile_cols] = own_ref[...]
    for (i, j), ref in zip(((0, 1), (1, 0), (1, 1)), coded_refs):
        for col in range(0, tile_cols, LANES):
            for start in range(0, tile_rows, CHUNK):
                parts = decode(ref, start, tile_rows, col)
                for comp in range(2):
                    ext_ref[comp, pl.ds(i * tile_rows + start, CHUNK), pl.ds(j * tile_cols + col, LANES)] = parts[comp]


def spread_sums(out_ref, u_ref, v_ref):
    chunks = out_ref.shape[0]
    rows = v_ref.shape[0] // chunks
    for chunk in range(chunks):
        at = pl.ds(chunk * rows, rows)
        for col in range(0, v_ref.shape[1], LANES):
            cols = pl.ds(col, LANES)
            encode_sums(out_ref.at[chunk], cols, u_ref[0, at, cols], u_ref[1, at, cols], v_ref[at, cols])


def added(parts):
    while len(parts) > 1:
        parts = [tuple(x + y for x, y in zip(a, b)) for a, b in zip(parts[::2], parts[1::2])]
    return parts[0]


def sums_kernel(rows, parts_ref, *refs):
    out_ref = refs[-1]
    for col in range(0, out_ref.shape[2], LANES):
        cols = pl.ds(col, LANES)
        total = added([decode_sums(parts_ref.at[k], cols, rows) for k in range(parts_ref.shape[0])])
        encode_sums(out_ref.at[0], cols, *total)
        for k in range(1, out_ref.shape[0]):
            out_ref[k, :, cols] = out_ref[0, :, cols]


def update_kernel(rows, count, me_ref, probe_ref, *refs):
    out_ref = refs[-1]
    first = pl.multiple_of(me_ref[1] * rows, SUBLANES)
    for col in range(0, out_ref.shape[2], LANES):
        cols = pl.ds(col, LANES)
        u_re, u_im, v = added([decode_sums(ref.at[k], cols, rows) for ref in refs[:count] for k in range(ref.shape[0])])
        scale = 1.0 / (v + probe_regular)
        re = (probe_ref[0, pl.ds(first, rows), cols] + u_re) * scale
        im = (probe_ref[1, pl.ds(first, rows), cols] + u_im) * scale
        exponent = largest_exponent([re, im])
        words = paired(fixed(re, exponent), fixed(im, exponent))
        for chunk in range(out_ref.shape[0]):
            out_ref[chunk, 0:rows, cols] = words
            out_ref[chunk, rows : rows + SUBLANES, cols] = exponent.astype(jnp.int32)


def probe_kernel(chunks_ref, out_ref):
    decode_probe(out_ref, chunks_ref)


def first_half_kernel(dims, pos_ref, me_ref, own_ref, right_ref, below_ref, diag_ref, probe_ref, turns, twiddles,
                      far_out, win_out, power_out, ext_out, ext_ref, xa_ref, xb_ref, ya_ref, yb_ref, far_ref, win_ref, ys_ref, xs_ref, slots_ref, sems, win_sems, ext_sem):
    tile_rows, tile_cols, pat_count, col_count, capacity = dims
    order = probe_ref.shape[1]
    count = list_patterns(dims, pos_ref, me_ref, ys_ref, xs_ref, slots_ref)
    unfold(dims, ext_ref, own_ref, (right_ref, below_ref, diag_ref))
    keep = pltpu.make_async_copy(ext_ref, ext_out, ext_sem)
    keep.start()
    power_out[...] = jnp.zeros_like(power_out)
    consts = (turns, twiddles)

    def pair(step, carry):
        stages = []
        for k in range(2):
            listed = 2 * step + k
            weight = (listed < count).astype(f32)
            index = jnp.minimum(listed, count - 1)
            stages.append(forward(order, ext_ref, probe_ref, consts, ys_ref[index], xs_ref[index], win_ref.at[listed], power_out, weight,
                                  xa_ref.at[k], xb_ref.at[k], ya_ref.at[k], yb_ref.at[k], far_ref.at[listed]))
        interleaved(*stages)
        for k in range(2):
            listed = 2 * step + k
            pltpu.make_async_copy(far_ref.at[listed], far_out.at[listed], sems.at[listed]).start()
            pltpu.make_async_copy(win_ref.at[listed], win_out.at[listed], win_sems.at[listed]).start()
        return carry

    pairs = lax.div(count + 1, 2)
    lax.fori_loop(0, pairs, pair, 0)

    def settle(listed, carry):
        pltpu.make_async_copy(far_ref.at[listed], far_out.at[listed], sems.at[listed]).wait()
        pltpu.make_async_copy(win_ref.at[listed], win_out.at[listed], win_sems.at[listed]).wait()
        return carry

    lax.fori_loop(0, 2 * pairs, settle, 0)
    keep.wait()


def second_half_kernel(dims, pos_ref, me_ref, probe_ref, power_ref, late_weights, far_in, win_in, amp_in, turns, twiddles, sorting,
                       share_out, top_out, bottom_out, numer_out, amp_out,
                       sum_ref, xa_ref, xb_ref, ya_ref, yb_ref, numer_ref, far_ref, win_ref, amp_ref, sorted_ref, ys_ref, xs_ref, slots_ref, far_sems, win_sems, amp_sems, out_sems, sum_sem):
    tile_rows, tile_cols, pat_count, col_count, capacity = dims
    order = probe_ref.shape[1]
    count = list_patterns(dims, pos_ref, me_ref, ys_ref, xs_ref, slots_ref)
    pairs = lax.div(count + 1, 2)

    def copies(listed):
        return (
            pltpu.make_async_copy(far_in.at[listed], far_ref.at[listed], far_sems.at[listed]),
            pltpu.make_async_copy(win_in.at[listed], win_ref.at[listed], win_sems.at[listed]),
            pltpu.make_async_copy(amp_in.at[slots_ref[jnp.minimum(listed, count - 1)]], amp_ref.at[listed], amp_sems.at[listed]),
        )

    def begin(listed, carry):
        for copy in copies(listed):
            copy.start()
        return carry

    lax.fori_loop(0, 2 * pairs, begin, 0)
    sum_ref[...] = jnp.zeros_like(sum_ref)
    numer_ref[...] = jnp.zeros_like(numer_ref)
    consts = (turns, twiddles)

    def pair(step, carry):
        stages = []
        for k in range(2):
            listed = 2 * step + k
            for copy in copies(listed):
                copy.wait()
        for k in range(2):
            listed = 2 * step + k
            weight = (listed < count).astype(f32)
            index = jnp.minimum(listed, count - 1)
            y, x = ys_ref[index], xs_ref[index]
            rows_sorted = jnp.dot(sorting[0], amp_ref[listed], preferred_element_type=f32).astype(bf16)
            sorted_ref[listed] = jnp.dot(rows_sorted, sorting[1], preferred_element_type=f32).astype(bf16)
            stages.append(backward(order, far_ref.at[listed], sorted_ref.at[listed], consts, y, x, weight, probe_ref, win_ref.at[listed],
                                   xa_ref.at[k], xb_ref.at[k], ya_ref.at[k], yb_ref.at[k], sum_ref, numer_ref))
        interleaved(*stages)
        for k in range(2):
            listed = 2 * step + k
            pltpu.make_async_copy(sorted_ref.at[listed], amp_out.at[listed], out_sems.at[listed]).start()
        return carry

    lax.fori_loop(0, pairs, pair, 0)
    weights_ref, weights_come = late_weights
    weights_come()
    for first in range(0, 2 * tile_rows, CHUNK):
        rows = pl.ds(first, CHUNK)
        scale = 1.0 / (weights_ref[rows, :] + object_regular)
        for comp in range(2):
            sum_ref[comp, rows, :] = sum_ref[comp, rows, :] * scale
    keep = pltpu.make_async_copy(sum_ref, share_out, sum_sem)
    keep.start()
    encode(lambda comp, at, cols: sum_ref[comp, at, cols], top_out, tile_rows, 0, tile_rows)
    encode(lambda comp, at, cols: sum_ref[comp, pl.ds(tile_rows + at.start, at.size), cols], bottom_out, tile_rows, 0, tile_rows)
    spread_sums(numer_out, numer_ref, power_ref)

    def settle(listed, carry):
        pltpu.make_async_copy(sorted_ref.at[listed], amp_out.at[listed], out_sems.at[listed]).wait()
        return carry

    lax.fori_loop(0, 2 * pairs, settle, 0)
    keep.wait()


def rows_sum_kernel(dims, share_ref, above_ref, below_ref, after_ref, sum_out, left_out, right_out, sem):
    tile_rows, tile_cols = dims[:2]
    for i, ref in enumerate((above_ref, below_ref)):
        for col in range(0, 2 * tile_cols, LANES):
            for start in range(0, tile_rows, CHUNK):
                rows, cols = pl.ds(i * tile_rows + start, CHUNK), pl.ds(col, LANES)
                parts = decode(ref, start, tile_rows, col)
                for comp in range(2):
                    share_ref[comp, rows, cols] += parts[comp]
    keep = pltpu.make_async_copy(share_ref, sum_out, sem)
    keep.start()
    for j, ref in enumerate((left_out, right_out)):
        for i in range(2):

            def read(comp, at, cols, i=i, j=j):
                return share_ref[comp, pl.ds(i * tile_rows + at.start, at.size), pl.ds(j * tile_cols + cols.start, cols.size)]

            encode(read, ref, tile_rows, i * tile_rows, 2 * tile_rows + i * SUBLANES)
    keep.wait()


def whole_kernel(dims, pos_ref, me_ref, old_ref, sum_ref, from_left_ref, from_right_ref, weights_ref,
                 chunks_ref, amp_in, turns, twiddles,
                 current_out, top_out, bottom_out, numer_out, probe_ref,
                 ext_ref, grad_ref, win_ref, xa_ref, xb_ref, ya_ref, yb_ref, numer_ref, far_ref, amp_ref, ys_ref, xs_ref, slots_ref, amp_sems, own_sem, top_sem):
    tile_rows, tile_cols, pat_count, col_count, capacity = dims
    order = probe_ref.shape[1]
    count = list_patterns(dims, pos_ref, me_ref, ys_ref, xs_ref, slots_ref)
    pairs = lax.div(count + 1, 2)
    decode_probe(probe_ref, chunks_ref)

    def fetch(listed):
        return pltpu.make_async_copy(amp_in.at[jnp.minimum(listed, count - 1)], amp_ref.at[listed], amp_sems.at[listed])

    def begin(listed, carry):
        fetch(listed).start()
        return carry

    lax.fori_loop(0, 2 * pairs, begin, 0)
    for j, ref in enumerate((from_left_ref, from_right_ref)):
        for i in range(2):
            for col in range(0, tile_cols, LANES):
                for start in range(0, tile_rows, CHUNK):
                    rows, cols = pl.ds(i * tile_rows + start, CHUNK), pl.ds(j * tile_cols + col, LANES)
                    parts = decode(ref, i * tile_rows + start, 2 * tile_rows + i * SUBLANES, col)
                    scale = object_regular / (weights_ref[rows, cols] + object_regular)
                    for comp in range(2):
                        ext_ref[comp, rows, cols] = old_ref[comp, rows, cols] * scale + (sum_ref[comp, rows, cols] + parts[comp])
    keep = pltpu.make_async_copy(ext_ref.at[:, pl.ds(0, tile_rows), pl.ds(0, tile_cols)], current_out, own_sem)
    keep.start()
    grad_ref[...] = jnp.zeros_like(grad_ref)
    numer_ref[...] = jnp.zeros_like(numer_ref)
    consts = (turns, twiddles)

    def pair(step, carry):
        stages = []
        for k in range(2):
            fetch(2 * step + k).wait()
        for k in range(2):
            listed = 2 * step + k
            weight = (listed < count).astype(f32)
            index = jnp.minimum(listed, count - 1)
            y, x = ys_ref[index], xs_ref[index]

            def both(k=k, listed=listed, weight=weight, y=y, x=x):
                yield from forward(order, ext_ref, probe_ref, consts, y, x, win_ref.at[k], numer_ref.at[2], weight,
                                   xa_ref.at[k], xb_ref.at[k], ya_ref.at[k], yb_ref.at[k], far_ref.at[k])
                yield from backward(order, far_ref.at[k], amp_ref.at[listed], consts, y, x, weight, probe_ref, win_ref.at[k],
                                    xa_ref.at[k], xb_ref.at[k], ya_ref.at[k], yb_ref.at[k], grad_ref, numer_ref)

            stages.append(both())
        interleaved(*stages)
        return carry

    lax.fori_loop(0, pairs, pair, 0)
    for first in range(0, tile_rows, CHUNK):
        rows = pl.ds(first, CHUNK)
        scale = 1.0 / (weights_ref[rows, :] + object_regular)
        for comp in range(2):
            grad_ref[comp, rows, :] = grad_ref[comp, rows, :] * scale
    give = pltpu.make_async_copy(grad_ref.at[:, pl.ds(0, tile_rows), :], top_out, top_sem)
    give.start()

    def read(comp, at, cols):
        rows = pl.ds(tile_rows + at.start, at.size)
        return grad_ref[comp, rows, cols] / (weights_ref[rows, cols] + object_regular)

    encode(read, bottom_out, tile_rows, 0, tile_rows)
    spread_sums(numer_out, numer_ref, numer_ref.at[2])
    keep.wait()
    give.wait()


def fold_kernel(dims, top_ref, above_ref, own_out, right_out, own_ref, sem):
    tile_rows, tile_cols = dims[:2]
    for col in range(0, 2 * tile_cols, LANES):
        for start in range(0, tile_rows, CHUNK):
            rows, cols = pl.ds(start, CHUNK), pl.ds(col, LANES)
            parts = decode(above_ref, start, tile_rows, col)
            for comp in range(2):
                if col < tile_cols:
                    own_ref[comp, rows, cols] = top_ref[comp, rows, cols] + parts[comp]
                else:
                    top_ref[comp, rows, cols] += parts[comp]
    keep = pltpu.make_async_copy(own_ref, own_out, sem)
    keep.start()
    encode(lambda comp, at, cols: top_ref[comp, at, pl.ds(tile_cols + cols.start, cols.size)], right_out, tile_rows, 0, tile_rows)
    keep.wait()


def object_kernel(dims, current_ref, own_ref, left_ref, before_ref, weights_ref, out_ref):
    tile_rows, tile_cols = dims[:2]
    for col in range(0, tile_cols, LANES):
        for start in range(0, tile_rows, CHUNK):
            rows, cols = pl.ds(start, CHUNK), pl.ds(col, LANES)
            scale = 1.0 / (weights_ref[rows, cols] + object_regular)
            back = (before_ref[rows, cols] + object_regular) * scale
            parts = decode(left_ref, start, tile_rows, col)
            for comp in range(2):
                old = object_regular * scale * current_ref[comp, rows, cols]
                out_ref[comp, rows, cols] = old + (own_ref[comp, rows, cols] + parts[comp]) * back


def shape(dims, dtype=f32):
    return jax.ShapeDtypeStruct(dims, dtype)


def work_scratch(order):
    return [
        pltpu.VMEM((2, 2, order, order), bf16),
        pltpu.VMEM((2, 2, order, order), bf16),
        pltpu.VMEM((2, order, order), f32),
        pltpu.VMEM((2, order, order), f32),
    ]


def list_scratch(capacity):
    return [pltpu.SMEM((capacity,), jnp.int32)] * 3


def call(kernel, outs, out_specs, in_specs, scratch, flops, limit=26 << 20):
    several = isinstance(outs, tuple)
    out_count = len(outs) if several else 1
    in_count = len(in_specs)
    loaded = [k for k, spec in enumerate(in_specs) if spec is LOAD or spec is LATE]

    def body(*refs):
        ins, rest = list(refs[:in_count]), refs[in_count:]
        given, kept = rest[: out_count + len(scratch)], rest[out_count + len(scratch) :]
        copies = [pltpu.make_async_copy(ins[k], kept[n], kept[-1].at[n]) for n, k in enumerate(loaded)]
        for copy in copies:
            copy.start()
        for n, k in enumerate(loaded):
            if in_specs[k] is LOAD:
                copies[n].wait()
                ins[k] = kept[n]
            else:
                ins[k] = (kept[n], copies[n].wait)
        kernel(*ins, *given)

    fixed_outs = [
        pltpu.HBM(out.shape, out.dtype) if spec is HBM else pltpu.VMEM(out.shape, out.dtype) if spec is PIN else out
        for out, spec in zip(outs if several else (outs,), out_specs if several else (out_specs,))
    ]
    places = [pltpu.HBM if spec in (LOAD, LATE, HBM) else pltpu.VMEM if spec is PIN else None for spec in in_specs]

    def called(*args):
        args = [arg if place is None else pltpu.with_memory_space_constraint(arg, place) for arg, place in zip(args, places)]
        own = [pltpu.VMEM(args[k].shape, args[k].dtype) for k in loaded]
        if loaded:
            own.append(pltpu.SemaphoreType.DMA((len(loaded),)))
        return pl.pallas_call(
            body,
            out_shape=tuple(fixed_outs) if several else fixed_outs[0],
            out_specs=out_specs,
            in_specs=[HBM if spec in (LOAD, LATE) else spec for spec in in_specs],
            scratch_shapes=list(scratch) + own,
            compiler_params=pltpu.CompilerParams(vmem_limit_bytes=limit),
            cost_estimate=pl.CostEstimate(flops=flops, bytes_accessed=8 << 20, transcendentals=0),
        )(*args)

    return called


def passed_along(value, axis, steps):
    count = lax.axis_size(axis)
    leading, last = (max(0, -steps), min(count, count - steps))
    return lax.ppermute(value, axis, [(source, source + steps) for source in range(leading, last)])


def swapped(value, axis, mask):
    return lax.ppermute(value, axis, [(k, k ^ mask) for k in range(lax.axis_size(axis))])


def probe_update(me, probe, numer, kind, at_once, before_sum, before_update):
    cols, order = lax.axis_size("col"), probe.shape[1]
    rows = order // cols
    parts = lax.all_to_all(numer, "col", split_axis=0, concat_axis=0, tiled=True)
    blocks = lax.axis_size("row") if at_once else 1
    total = call(
        functools.partial(sums_kernel, rows), shape((blocks, sums_rows(rows), order), jnp.int32), VMEM,
        [VMEM] + [spec for spec, _ in before_sum], [], 1 << 26,
    )(parts, *[value for _, value in before_sum])
    if at_once:
        totals = [lax.all_to_all(total, "row", split_axis=0, concat_axis=0, tiled=True)]
    else:
        totals = [total] + [swapped(total, "row", mask) for mask in range(1, lax.axis_size("row"))]
    fresh = call(
        functools.partial(update_kernel, rows, len(totals)), shape((cols, rows + SUBLANES, order), jnp.int32), VMEM,
        [SMEM, kind] + [VMEM] * len(totals) + [spec for spec, _ in before_update], [], 1 << 26,
    )(me, probe, *totals, *[value for _, value in before_update])
    return total, lax.all_to_all(fresh, "col", split_axis=0, concat_axis=0, tiled=True)


def local(obj, probe, amplitudes, positions):
    col_count = lax.axis_size("col")
    tile_rows, tile_cols = obj.shape[1], obj.shape[2]
    order = probe.shape[1]
    pat_count = amplitudes.shape[0]
    capacity = 2 * pat_count
    dims = (tile_rows, tile_cols, pat_count, col_count, capacity)
    me = jnp.stack([lax.axis_index("row"), lax.axis_index("col")]).astype(jnp.int32)
    pos = positions.T.reshape(-1)
    turns, twiddles, sorting = tables(order)
    tile = (2, tile_rows, tile_cols)
    window = (2, order, order)
    wide = (2, 2 * tile_rows, 2 * tile_cols)
    shares = shape((col_count, sums_rows(order // col_count), order), jnp.int32)
    coded_tile = shape((tile_rows + SUBLANES, tile_cols), jnp.int32)
    coded_row = shape((tile_rows + SUBLANES, 2 * tile_cols), jnp.int32)
    coded_col = shape((2 * (tile_rows + SUBLANES), tile_cols), jnp.int32)
    one_pattern = 24 * 2 * order**3

    coded = call(encode_kernel, coded_tile, VMEM, [LOAD], [], 1 << 26)(obj)
    right = passed_along(coded, "col", -1)
    below = passed_along(coded, "row", -1)
    diag = passed_along(right, "row", -1)

    outgoing = call(
        functools.partial(outgoing_kernel, dims), shape((col_count * SEND, order, order), bf16), HBM, [SMEM, SMEM, LOAD, FREE, FREE],
        [pltpu.SemaphoreType.DMA((pat_count,))], 1 << 20,
    )(pos, me, amplitudes, right, below)
    incoming = lax.all_to_all(outgoing, "col", split_axis=0, concat_axis=0, tiled=True)

    def weights(probe_now, span, kind):
        return call(
            functools.partial(weights_kernel, dims, span), shape((span * tile_rows, span * tile_cols)), HBM, [SMEM, SMEM, kind],
            [pltpu.VMEM(((span + 2) * tile_rows, (span + 2) * tile_cols), f32), pltpu.VMEM((order, order), f32)], 8 << 30,
        )(pos, me, probe_now)

    weights_old = weights(probe, 2, LOAD)

    far, wins, power, ext = call(
        functools.partial(first_half_kernel, dims), (shape((capacity,) + window), shape((capacity,) + window), shape((order, order)), shape(wide)), (HBM, HBM, VMEM, HBM),
        [SMEM, SMEM, LOAD] + [VMEM] * 3 + [LOAD] * 3,
        [pltpu.VMEM(wide, f32)] + work_scratch(order) + [pltpu.VMEM((capacity,) + window, f32)] * 2 + list_scratch(capacity)
        + [pltpu.SemaphoreType.DMA((capacity,))] * 2 + [pltpu.SemaphoreType.DMA],
        capacity * one_pattern // 2,
    )(pos, me, obj, right, below, diag, probe, turns, twiddles)

    share, top, bottom, numer, sorted_amps = call(
        functools.partial(second_half_kernel, dims),
        (shape(wide), coded_row, coded_row, shares, shape((capacity, order, order), bf16)),
        (HBM, VMEM, VMEM, VMEM, HBM),
        [SMEM, SMEM, LOAD, VMEM, LATE, HBM, HBM, FREE] + [LOAD] * 3,
        [pltpu.VMEM(wide, f32)] + work_scratch(order)
        + [pltpu.VMEM(window, f32)] + [pltpu.VMEM((capacity,) + window, f32)] * 2 + [pltpu.VMEM((capacity, order, order), bf16)] * 2
        + list_scratch(capacity) + [pltpu.SemaphoreType.DMA((capacity,))] * 4 + [pltpu.SemaphoreType.DMA],
        capacity * one_pattern // 2,
    )(pos, me, probe, power, weights_old, far, wins, incoming, turns, twiddles, sorting)

    from_above = passed_along(bottom, "row", 1)
    from_below = passed_along(top, "row", -1)
    total, chunks = probe_update(me, probe, numer, LOAD, True, [], [])
    sums, to_left, to_right = call(
        functools.partial(rows_sum_kernel, dims), (shape(wide), coded_col, coded_col), (HBM, VMEM, VMEM), [LOAD, VMEM, VMEM, FREE], [pltpu.SemaphoreType.DMA], 1 << 26,
    )(share, from_above, from_below, total)
    from_left = passed_along(to_right, "col", 1)
    from_right = passed_along(to_left, "col", -1)

    current, top, bottom, numer, probe_now = call(
        functools.partial(whole_kernel, dims), (shape(tile), shape((2, tile_rows, 2 * tile_cols)), coded_row, shares, shape(window)), (HBM, HBM) + (VMEM,) * 3,
        [SMEM, SMEM, LOAD, LOAD, VMEM, VMEM, LOAD, VMEM, HBM, LOAD, LOAD],
        [pltpu.VMEM(wide, f32), pltpu.VMEM(wide, f32), pltpu.VMEM((2,) + window, f32)] + work_scratch(order)
        + [pltpu.VMEM((3, order, order), f32), pltpu.VMEM((2,) + window, f32), pltpu.VMEM((capacity, order, order), bf16)]
        + list_scratch(capacity) + [pltpu.SemaphoreType.DMA((capacity,)), pltpu.SemaphoreType.DMA, pltpu.SemaphoreType.DMA],
        capacity * one_pattern,
    )(pos, me, ext, sums, from_left, from_right, weights_old, chunks, sorted_amps, turns, twiddles)

    from_above = passed_along(bottom, "row", 1)
    weights_new = weights(probe_now, 1, VMEM)
    own, to_right = call(
        functools.partial(fold_kernel, dims), (shape(tile), coded_tile), (HBM, VMEM), [LOAD, VMEM], [pltpu.VMEM(tile, f32), pltpu.SemaphoreType.DMA], 1 << 26,
    )(top, from_above)
    from_left = passed_along(to_right, "col", 1)
    new_object = call(functools.partial(object_kernel, dims), shape(tile), VMEM, [LOAD, LOAD, VMEM, LOAD, LOAD], [], 1 << 26)(
        current, own, from_left, weights_old, weights_new
    )
    _, chunks = probe_update(me, probe_now, numer, VMEM, False, [(FREE, to_right)], [(FREE, from_left), (HBM, weights_new)])
    new_probe = call(probe_kernel, shape(window), VMEM, [VMEM], [], 1 << 26)(chunks)
    return new_object, new_probe


def solution(mesh):
    placed = (P(None, "row", "col"), P(), P(("row", "col"), None, None), P())
    return jax.shard_map(local, mesh=mesh, in_specs=placed, out_specs=(P(None, "row", "col"), P()), check_vma=False)
```

```python
import functools

import jax
import jax.numpy as jnp
import numpy as np
from jax import lax
from jax.experimental import pallas as pl
from jax.experimental.pallas import tpu as pltpu
from jax.sharding import PartitionSpec as P

ITERS = 2
SEND = 2

amplitude_floor = 0.1
object_regular = 0.5
probe_regular = 1.0

LANES = 128
SUBLANES = 8
LEVELS = 32767.0
CHUNK = 32
VMEM = pl.BlockSpec(memory_space=pltpu.VMEM)
SMEM = pl.BlockSpec(memory_space=pltpu.SMEM)
HBM = pl.BlockSpec(memory_space=pltpu.HBM)
LOAD = object()
LATE = object()
FREE = pl.BlockSpec(memory_space=pl.ANY)
PIN = pl.BlockSpec(memory_space=pltpu.VMEM)
f32 = jnp.float32
bf16 = jnp.bfloat16


def tables(order):
    half = order // 2
    counter = np.arange(half)
    angles = 2.0 * np.pi * ((counter[:, None] * counter[None, :]) % half) / half
    cos, sin = np.cos(angles), np.sin(angles)
    scale = 1.0 / np.sqrt(order)
    turns = []
    for block in ([[cos, -sin], [sin, cos]], [[cos, sin], [-sin, cos]]):
        matrix = np.block(block) * scale
        high = matrix.astype(jnp.bfloat16)
        turns.append(np.stack([high, (matrix - high.astype(np.float64)).astype(jnp.bfloat16)]))
    turn = 2.0 * np.pi * counter / order
    twiddle = np.stack([np.cos(turn), -np.sin(turn)]).astype(np.float32)
    twiddles = np.concatenate(
        [np.broadcast_to(twiddle[:, :, None], (2, half, half)), np.broadcast_to(twiddle[:, None, :], (2, SUBLANES, half))], axis=1
    )
    sorting = np.zeros((order, order), np.float32)
    sorting[np.arange(half), 2 * np.arange(half)] = 1.0
    sorting[half + np.arange(half), 2 * np.arange(half) + 1] = 1.0
    return (
        jnp.asarray(np.stack(turns)),
        jnp.asarray(np.ascontiguousarray(twiddles)),
        jnp.asarray(np.stack([sorting, sorting.T]).astype(jnp.bfloat16)),
    )


def list_patterns(dims, pos_ref, me_ref, ys_ref, xs_ref, slots_ref):
    tile_rows, tile_cols, pat_count, col_count, capacity = dims
    my_row, my_col = me_ref[0], me_ref[1]
    band_count = pat_count * col_count
    first = my_row * band_count
    total = pos_ref.shape[0] // 2

    def visit(index, carry):
        found, source, rank = carry
        y = pos_ref[first + index]
        x = pos_ref[total + first + index]
        here = lax.div(x, tile_cols) == my_col
        holder = lax.div(index, pat_count)
        rank = jnp.where(holder == source, rank, 0)

        @pl.when(here & (found < capacity))
        def _():
            ys_ref[found] = y - my_row * tile_rows
            xs_ref[found] = x - my_col * tile_cols
            slots_ref[found] = holder * SEND + jnp.minimum(rank, SEND - 1)

        step = here.astype(jnp.int32)
        return found + step, holder, rank + step

    found, _, _ = lax.fori_loop(0, band_count, visit, (jnp.int32(0), jnp.int32(-1), jnp.int32(0)))
    return jnp.minimum(found, capacity)


def lane_index(rows):
    return lax.broadcasted_iota(jnp.int32, (rows, LANES), 1)


def shifted_left(tiles, shift):
    lane = lane_index(tiles[0].shape[0])
    turn = lax.rem(LANES - shift, LANES)
    rolled = [pltpu.roll(tile, turn, axis=1) for tile in tiles]
    inside = lane < LANES - shift
    return [jnp.where(inside, a, b) for a, b in zip(rolled[:-1], rolled[1:])]


def shifted_right(tiles, shift):
    lane = lane_index(tiles[0].shape[0])
    rolled = [pltpu.roll(tile, shift, axis=1) for tile in tiles]
    outside = lane < shift
    zero = jnp.zeros_like(rolled[0])
    firsts = [zero] + rolled
    seconds = rolled + [zero]
    return [jnp.where(outside, a, b) for a, b in zip(firsts, seconds)]


def row_groups(tile):
    return [tile[k : k + SUBLANES] for k in range(0, tile.shape[0], SUBLANES)]


def shifted_up(tile, shift):
    row = lax.broadcasted_iota(jnp.int32, (SUBLANES, LANES), 0)
    turn = lax.rem(SUBLANES - shift, SUBLANES)
    rolled = [pltpu.roll(group, turn, axis=0) for group in row_groups(tile)]
    inside = row < SUBLANES - shift
    return jnp.concatenate([jnp.where(inside, a, b) for a, b in zip(rolled[:-1], rolled[1:])], axis=0)


def shifted_down(before, tile, shift):
    row = lax.broadcasted_iota(jnp.int32, (SUBLANES, LANES), 0)
    rolled = [before] + [pltpu.roll(group, shift, axis=0) for group in row_groups(tile)]
    outside = row < shift
    return rolled[-1], jnp.concatenate([jnp.where(outside, a, b) for a, b in zip(rolled[:-1], rolled[1:])], axis=0)


class Deposit:
    def __init__(self, add, top, left):
        self.add = add
        self.row = pl.multiple_of(lax.div(top, SUBLANES) * SUBLANES, SUBLANES)
        self.col = pl.multiple_of(lax.div(left, LANES) * LANES, LANES)
        self.down = lax.rem(top, SUBLANES)
        self.right = lax.rem(left, LANES)
        self.carried = None

    def place(self, first, tiles):
        moved = jnp.concatenate(shifted_right(tiles, self.right), axis=1)
        self.add(pl.ds(self.row + first, tiles[0].shape[0]), pl.ds(self.col, moved.shape[1]), moved)

    def put(self, first, tiles):
        if self.carried is None:
            self.carried = [jnp.zeros((SUBLANES, LANES), f32) for _ in tiles]
        pairs = [shifted_down(before, tile, self.down) for before, tile in zip(self.carried, tiles)]
        self.carried = [carried for carried, _ in pairs]
        self.place(first, [tile for _, tile in pairs])

    def finish(self, first):
        row = lax.broadcasted_iota(jnp.int32, (SUBLANES, LANES), 0)
        self.place(first, [jnp.where(row < self.down, tile, 0.0) for tile in self.carried])


def lane_tiles(value):
    return [value[:, k : k + LANES] for k in range(0, value.shape[1], LANES)]


def store_split(ref, rows, cols, value):
    high = value.astype(bf16)
    ref[0, rows, cols] = high
    ref[1, rows, cols] = (value - high.astype(f32)).astype(bf16)


def right_dot(x_ref, table_ref):
    left = jnp.concatenate([x_ref[0], x_ref[1], x_ref[0]], axis=1)
    right = jnp.concatenate([table_ref[0], table_ref[0], table_ref[1]], axis=0)
    return jnp.dot(left, right, preferred_element_type=f32)


def left_dot(table_ref, x_ref):
    left = jnp.concatenate([table_ref[0], table_ref[0], table_ref[1]], axis=1)
    right = jnp.concatenate([x_ref[0], x_ref[1], x_ref[0]], axis=0)
    return jnp.dot(left, right, preferred_element_type=f32)


def repeated(group, rows):
    return jnp.concatenate([group] * (rows // SUBLANES), axis=0)


def encode(read, out_ref, rows, first, last):
    for col in range(0, out_ref.shape[1], LANES):
        cols = pl.ds(col, LANES)
        largest = jnp.full((SUBLANES, LANES), 1e-30, f32)
        for start in range(0, rows, CHUNK):
            for comp in range(2):
                for group in row_groups(jnp.abs(read(comp, pl.ds(start, CHUNK), cols))):
                    largest = jnp.maximum(largest, group)
        exponent = jnp.ceil(jnp.log2(largest))
        out_ref[last : last + SUBLANES, cols] = exponent.astype(jnp.int32)
        scale = repeated(jnp.exp2(-exponent) * LEVELS, CHUNK)
        for start in range(0, rows, CHUNK):
            codes = []
            for comp in range(2):
                scaled = jnp.clip(read(comp, pl.ds(start, CHUNK), cols) * scale, -LEVELS, LEVELS)
                codes.append(jnp.round(scaled).astype(jnp.int32))
            out_ref[pl.ds(first + start, CHUNK), cols] = (codes[0] << 16) | (codes[1] & 0xFFFF)


def decode(ref, start, last, col):
    cols = pl.ds(col, LANES)
    words = ref[pl.ds(start, CHUNK), cols]
    scale = repeated(jnp.exp2(ref[last : last + SUBLANES, cols].astype(f32)) * (1.0 / LEVELS), CHUNK)
    return (words >> 16).astype(f32) * scale, ((words << 16) >> 16).astype(f32) * scale


def largest_exponent(values):
    largest = jnp.full((SUBLANES, LANES), 1e-30, f32)
    for value in values:
        for group in row_groups(jnp.abs(value)):
            largest = jnp.maximum(largest, group)
    return jnp.ceil(jnp.log2(largest))


def fixed(value, exponent):
    scaled = value * repeated(jnp.exp2(-exponent) * LEVELS, value.shape[0])
    return jnp.round(jnp.clip(scaled, -LEVELS, LEVELS)).astype(jnp.int32)


def paired(first, second):
    return (first << 16) | (second & 0xFFFF)


def unpaired(words):
    return words >> 16, (words << 16) >> 16


def scaled_back(codes, exponent):
    return codes.astype(f32) * repeated(jnp.exp2(exponent.astype(f32)) * (1.0 / LEVELS), codes.shape[0])


def sums_rows(rows):
    return rows + rows // 2 + SUBLANES


def encode_sums(out_ref, cols, u_re, u_im, v):
    rows = v.shape[0]
    half = rows // 2
    of_u, of_v = largest_exponent([u_re, u_im]), largest_exponent([v])
    out_ref[0:rows, cols] = paired(fixed(u_re, of_u), fixed(u_im, of_u))
    codes = fixed(v, of_v)
    out_ref[rows : rows + half, cols] = paired(codes[:half], codes[half:])
    out_ref[rows + half : rows + half + SUBLANES, cols] = paired(of_u.astype(jnp.int32), of_v.astype(jnp.int32))


def decode_sums(ref, cols, rows):
    half = rows // 2
    of_u, of_v = unpaired(ref[rows + half : rows + half + SUBLANES, cols])
    u_re, u_im = unpaired(ref[0:rows, cols])
    v = jnp.concatenate(unpaired(ref[rows : rows + half, cols]), axis=0)
    return scaled_back(u_re, of_u), scaled_back(u_im, of_u), scaled_back(v, of_v)


def decode_probe(out_ref, chunks_ref):
    chunks = chunks_ref.shape[0]
    rows = out_ref.shape[1] // chunks
    for chunk in range(chunks):
        for col in range(0, out_ref.shape[2], LANES):
            cols = pl.ds(col, LANES)
            exponent = chunks_ref[chunk, rows : rows + SUBLANES, cols]
            for comp, codes in enumerate(unpaired(chunks_ref[chunk, 0:rows, cols])):
                out_ref[comp, chunk * rows : (chunk + 1) * rows, cols] = scaled_back(codes, exponent)


def cut_chunk(ext_ref, comp, first, top, left, rows):
    row = pl.multiple_of(lax.div(top, SUBLANES) * SUBLANES, SUBLANES)
    col = pl.multiple_of(lax.div(left, LANES) * LANES, LANES)
    block = ext_ref[comp, pl.ds(row + first, rows + SUBLANES), pl.ds(col, 3 * LANES)]
    tiles = shifted_left(lane_tiles(block), lax.rem(left, LANES))
    return [shifted_up(tile, lax.rem(top, SUBLANES)) for tile in tiles]


def forward(order, ext_ref, probe_ref, consts, y, x, win_ref, power_ref, weight, xa_ref, xb_ref, ya_ref, yb_ref, far_ref):
    turns, twiddles = consts
    half = order // 2
    tw_re = repeated(twiddles[0, half : half + SUBLANES, :], CHUNK)
    tw_im = repeated(twiddles[1, half : half + SUBLANES, :], CHUNK)
    for first in range(0, order, CHUNK):
        rows = pl.ds(first, CHUNK)
        win_re = cut_chunk(ext_ref, 0, first, y, x, CHUNK)
        win_im = cut_chunk(ext_ref, 1, first, y, x, CHUNK)
        exits = []
        for k in range(2):
            cols = pl.ds(k * half, half)
            win_ref[0, rows, cols] = win_re[k]
            win_ref[1, rows, cols] = win_im[k]
            power_ref[rows, cols] += weight * (win_re[k] * win_re[k] + win_im[k] * win_im[k])
            p_re, p_im = probe_ref[0, rows, cols], probe_ref[1, rows, cols]
            exits.append((p_re * win_re[k] - p_im * win_im[k], p_re * win_im[k] + p_im * win_re[k]))
        (lo_re, lo_im), (hi_re, hi_im) = exits
        store_split(xa_ref, rows, pl.ds(0, half), lo_re + hi_re)
        store_split(xa_ref, rows, pl.ds(half, half), lo_im + hi_im)
        d_re, d_im = lo_re - hi_re, lo_im - hi_im
        store_split(xb_ref, rows, pl.ds(0, half), d_re * tw_re - d_im * tw_im)
        store_split(xb_ref, rows, pl.ds(half, half), d_re * tw_im + d_im * tw_re)
    yield
    ya_ref[...] = right_dot(xa_ref, turns.at[0])
    yb_ref[...] = right_dot(xb_ref, turns.at[0])
    yield
    for first in range(0, half, CHUNK):
        rows = pl.ds(first, CHUNK)
        below = pl.ds(half + first, CHUNK)
        t_re, t_im = twiddles[0, rows, :], twiddles[1, rows, :]
        for k, y_ref in enumerate((ya_ref, yb_ref)):
            cols = pl.ds(k * half, half)
            up_re, up_im = y_ref[rows, 0:half], y_ref[rows, half:order]
            dn_re, dn_im = y_ref[below, 0:half], y_ref[below, half:order]
            store_split(xa_ref, rows, cols, up_re + dn_re)
            store_split(xa_ref, below, cols, up_im + dn_im)
            d_re, d_im = up_re - dn_re, up_im - dn_im
            store_split(xb_ref, rows, cols, d_re * t_re - d_im * t_im)
            store_split(xb_ref, below, cols, d_re * t_im + d_im * t_re)
    yield
    far_ref[0] = left_dot(turns.at[1], xa_ref)
    far_ref[1] = left_dot(turns.at[1], xb_ref)
    yield


def backward(order, far_ref, amp_ref, consts, y, x, weight, probe_ref, win_ref, xa_ref, xb_ref, ya_ref, yb_ref, grad_ref, numer_ref):
    turns, twiddles = consts
    half = order // 2
    tw_re = repeated(twiddles[0, half : half + SUBLANES, :], CHUNK)
    tw_im = repeated(twiddles[1, half : half + SUBLANES, :], CHUNK)
    for k, x_ref in enumerate((xa_ref, xb_ref)):
        for first in range(0, half, CHUNK):
            rows = pl.ds(first, CHUNK)
            below = pl.ds(half + first, CHUNK)
            far_re, far_im = far_ref[k, rows, :], far_ref[k, below, :]
            amp = amp_ref[pl.ds(k * half + first, CHUNK), :].astype(f32) * weight
            factor = amp * lax.rsqrt(far_re * far_re + far_im * far_im + amplitude_floor)
            store_split(x_ref, rows, slice(None), far_re * factor)
            store_split(x_ref, below, slice(None), far_im * factor)
    yield
    ya_ref[...] = left_dot(turns.at[0], xa_ref)
    yb_ref[...] = left_dot(turns.at[0], xb_ref)
    yield
    for first in range(0, half, CHUNK):
        rows = pl.ds(first, CHUNK)
        below = pl.ds(half + first, CHUNK)
        t_re, t_im = twiddles[0, rows, :], twiddles[1, rows, :]
        for k, x_ref in enumerate((xa_ref, xb_ref)):
            cols = slice(k * half, (k + 1) * half)
            a_re, a_im = ya_ref[rows, cols], ya_ref[below, cols]
            b_re, b_im = yb_ref[rows, cols], yb_ref[below, cols]
            c_re, c_im = b_re * t_re + b_im * t_im, b_im * t_re - b_re * t_im
            store_split(x_ref, rows, pl.ds(0, half), a_re + c_re)
            store_split(x_ref, rows, pl.ds(half, half), a_im + c_im)
            store_split(x_ref, below, pl.ds(0, half), a_re - c_re)
            store_split(x_ref, below, pl.ds(half, half), a_im - c_im)
    yield
    ya_ref[...] = right_dot(xa_ref, turns.at[1])
    yb_ref[...] = right_dot(xb_ref, turns.at[1])
    yield

    def adder(comp):
        def add(rows, cols, moved):
            grad_ref[comp, rows, cols] += moved

        return add

    deposits = [Deposit(adder(comp), y, x) for comp in range(2)]
    for first in range(0, order, CHUNK):
        rows = pl.ds(first, CHUNK)
        a_re, a_im = ya_ref[rows, 0:half], ya_ref[rows, half:order]
        b_re, b_im = yb_ref[rows, 0:half], yb_ref[rows, half:order]
        c_re, c_im = b_re * tw_re + b_im * tw_im, b_im * tw_re - b_re * tw_im
        waves = [(a_re + c_re, a_im + c_im), (a_re - c_re, a_im - c_im)]
        terms = ([], [])
        for k, (wave_re, wave_im) in enumerate(waves):
            cols = pl.ds(k * half, half)
            p_re, p_im = probe_ref[0, rows, cols], probe_ref[1, rows, cols]
            w_re, w_im = win_ref[0, rows, cols], win_ref[1, rows, cols]
            terms[0].append(p_re * wave_re + p_im * wave_im)
            terms[1].append(p_re * wave_im - p_im * wave_re)
            numer_ref[0, rows, cols] += w_re * wave_re + w_im * wave_im
            numer_ref[1, rows, cols] += w_re * wave_im - w_im * wave_re
        for comp in range(2):
            deposits[comp].put(first, terms[comp])
    for deposit in deposits:
        deposit.finish(order)
    yield


def interleaved(*stages):
    live = list(stages)
    while live:
        still = []
        for stage in live:
            try:
                next(stage)
                still.append(stage)
            except StopIteration:
                pass
        live = still


def outgoing_kernel(dims, pos_ref, me_ref, amp_ref, after_ref, also_ref, out_ref, sems):
    tile_rows, tile_cols, pat_count, col_count, capacity = dims
    first = (me_ref[0] * col_count + me_ref[1]) * pat_count
    total = pos_ref.shape[0] // 2
    owners = [lax.div(pos_ref[total + first + k], tile_cols) for k in range(pat_count)]
    copies = []
    for k in range(pat_count):
        rank = sum(((owners[e] == owners[k]).astype(jnp.int32) for e in range(k)), jnp.int32(0))
        slot = owners[k] * SEND + jnp.minimum(rank, SEND - 1)
        copies.append(pltpu.make_async_copy(amp_ref.at[k], out_ref.at[slot], sems.at[k]))
        copies[-1].start()
    for copy in copies:
        copy.wait()


def weights_kernel(dims, span, pos_ref, me_ref, probe_ref, out_ref, sums_ref, power_ref):
    tile_rows, tile_cols, pat_count, col_count, capacity = dims
    order = probe_ref.shape[1]
    top = (me_ref[0] - 1) * tile_rows
    left = (me_ref[1] - 1) * tile_cols
    total = pos_ref.shape[0] // 2
    for first in range(0, sums_ref.shape[0], order):
        sums_ref[pl.ds(first, order), :] = jnp.zeros((order, sums_ref.shape[1]), f32)
    power_ref[...] = probe_ref[0] * probe_ref[0] + probe_ref[1] * probe_ref[1]

    def visit(index, carry):
        y = pos_ref[index] - top
        x = pos_ref[total + index] - left

        @pl.when((y > 0) & (y < (span + 1) * tile_rows) & (x > 0) & (x < (span + 1) * tile_cols))
        def _():
            def add(rows, cols, moved):
                sums_ref[rows, cols] += moved

            deposit = Deposit(add, y, x)
            for first in range(0, order, CHUNK):
                deposit.put(first, lane_tiles(power_ref[pl.ds(first, CHUNK), :]))
            deposit.finish(order)

        return carry

    lax.fori_loop(0, total, visit, 0)
    pltpu.sync_copy(sums_ref.at[pl.ds(tile_rows, span * tile_rows), pl.ds(tile_cols, span * tile_cols)], out_ref)


def encode_kernel(obj_ref, out_ref):
    rows = obj_ref.shape[1]
    encode(lambda comp, at, cols: obj_ref[comp, at, cols], out_ref, rows, 0, rows)


def unfold(dims, ext_ref, own_ref, coded_refs):
    tile_rows, tile_cols = dims[:2]
    ext_ref[:, 0:tile_rows, 0:tile_cols] = own_ref[...]
    for (i, j), ref in zip(((0, 1), (1, 0), (1, 1)), coded_refs):
        for col in range(0, tile_cols, LANES):
            for start in range(0, tile_rows, CHUNK):
                parts = decode(ref, start, tile_rows, col)
                for comp in range(2):
                    ext_ref[comp, pl.ds(i * tile_rows + start, CHUNK), pl.ds(j * tile_cols + col, LANES)] = parts[comp]


def spread_sums(out_ref, u_ref, v_ref):
    chunks = out_ref.shape[0]
    rows = v_ref.shape[0] // chunks
    for chunk in range(chunks):
        at = pl.ds(chunk * rows, rows)
        for col in range(0, v_ref.shape[1], LANES):
            cols = pl.ds(col, LANES)
            encode_sums(out_ref.at[chunk], cols, u_ref[0, at, cols], u_ref[1, at, cols], v_ref[at, cols])


def added(parts):
    while len(parts) > 1:
        parts = [tuple(x + y for x, y in zip(a, b)) for a, b in zip(parts[::2], parts[1::2])]
    return parts[0]


def sums_kernel(rows, parts_ref, *refs):
    out_ref = refs[-1]
    for col in range(0, out_ref.shape[2], LANES):
        cols = pl.ds(col, LANES)
        total = added([decode_sums(parts_ref.at[k], cols, rows) for k in range(parts_ref.shape[0])])
        encode_sums(out_ref.at[0], cols, *total)
        for k in range(1, out_ref.shape[0]):
            out_ref[k, :, cols] = out_ref[0, :, cols]


def update_kernel(rows, count, me_ref, probe_ref, *refs):
    out_ref = refs[-1]
    first = pl.multiple_of(me_ref[1] * rows, SUBLANES)
    for col in range(0, out_ref.shape[2], LANES):
        cols = pl.ds(col, LANES)
        u_re, u_im, v = added([decode_sums(ref.at[k], cols, rows) for ref in refs[:count] for k in range(ref.shape[0])])
        scale = 1.0 / (v + probe_regular)
        re = (probe_ref[0, pl.ds(first, rows), cols] + u_re) * scale
        im = (probe_ref[1, pl.ds(first, rows), cols] + u_im) * scale
        exponent = largest_exponent([re, im])
        words = paired(fixed(re, exponent), fixed(im, exponent))
        for chunk in range(out_ref.shape[0]):
            out_ref[chunk, 0:rows, cols] = words
            out_ref[chunk, rows : rows + SUBLANES, cols] = exponent.astype(jnp.int32)


def probe_kernel(chunks_ref, out_ref):
    decode_probe(out_ref, chunks_ref)


def first_half_kernel(dims, pos_ref, me_ref, own_ref, right_ref, below_ref, diag_ref, probe_ref, turns, twiddles,
                      far_out, win_out, power_out, ext_out, ext_ref, xa_ref, xb_ref, ya_ref, yb_ref, far_ref, win_ref, ys_ref, xs_ref, slots_ref, sems, win_sems, ext_sem):
    tile_rows, tile_cols, pat_count, col_count, capacity = dims
    order = probe_ref.shape[1]
    count = list_patterns(dims, pos_ref, me_ref, ys_ref, xs_ref, slots_ref)
    unfold(dims, ext_ref, own_ref, (right_ref, below_ref, diag_ref))
    keep = pltpu.make_async_copy(ext_ref, ext_out, ext_sem)
    keep.start()
    power_out[...] = jnp.zeros_like(power_out)
    consts = (turns, twiddles)

    def pair(step, carry):
        stages = []
        for k in range(2):
            listed = 2 * step + k
            weight = (listed < count).astype(f32)
            index = jnp.minimum(listed, count - 1)
            stages.append(forward(order, ext_ref, probe_ref, consts, ys_ref[index], xs_ref[index], win_ref.at[listed], power_out, weight,
                                  xa_ref.at[k], xb_ref.at[k], ya_ref.at[k], yb_ref.at[k], far_ref.at[listed]))
        interleaved(*stages)
        for k in range(2):
            listed = 2 * step + k
            pltpu.make_async_copy(far_ref.at[listed], far_out.at[listed], sems.at[listed]).start()
            pltpu.make_async_copy(win_ref.at[listed], win_out.at[listed], win_sems.at[listed]).start()
        return carry

    pairs = lax.div(count + 1, 2)
    lax.fori_loop(0, pairs, pair, 0)

    def settle(listed, carry):
        pltpu.make_async_copy(far_ref.at[listed], far_out.at[listed], sems.at[listed]).wait()
        pltpu.make_async_copy(win_ref.at[listed], win_out.at[listed], win_sems.at[listed]).wait()
        return carry

    lax.fori_loop(0, 2 * pairs, settle, 0)
    keep.wait()


def second_half_kernel(dims, pos_ref, me_ref, probe_ref, power_ref, late_weights, far_in, win_in, amp_in, turns, twiddles, sorting,
                       share_out, top_out, bottom_out, numer_out, amp_out,
                       sum_ref, xa_ref, xb_ref, ya_ref, yb_ref, numer_ref, far_ref, win_ref, amp_ref, sorted_ref, ys_ref, xs_ref, slots_ref, far_sems, win_sems, amp_sems, out_sems, sum_sem):
    tile_rows, tile_cols, pat_count, col_count, capacity = dims
    order = probe_ref.shape[1]
    count = list_patterns(dims, pos_ref, me_ref, ys_ref, xs_ref, slots_ref)
    pairs = lax.div(count + 1, 2)

    def copies(listed):
        return (
            pltpu.make_async_copy(far_in.at[listed], far_ref.at[listed], far_sems.at[listed]),
            pltpu.make_async_copy(win_in.at[listed], win_ref.at[listed], win_sems.at[listed]),
            pltpu.make_async_copy(amp_in.at[slots_ref[jnp.minimum(listed, count - 1)]], amp_ref.at[listed], amp_sems.at[listed]),
        )

    def begin(listed, carry):
        for copy in copies(listed):
            copy.start()
        return carry

    lax.fori_loop(0, 2 * pairs, begin, 0)
    sum_ref[...] = jnp.zeros_like(sum_ref)
    numer_ref[...] = jnp.zeros_like(numer_ref)
    consts = (turns, twiddles)

    def pair(step, carry):
        stages = []
        for k in range(2):
            listed = 2 * step + k
            for copy in copies(listed):
                copy.wait()
        for k in range(2):
            listed = 2 * step + k
            weight = (listed < count).astype(f32)
            index = jnp.minimum(listed, count - 1)
            y, x = ys_ref[index], xs_ref[index]
            rows_sorted = jnp.dot(sorting[0], amp_ref[listed], preferred_element_type=f32).astype(bf16)
            sorted_ref[listed] = jnp.dot(rows_sorted, sorting[1], preferred_element_type=f32).astype(bf16)
            stages.append(backward(order, far_ref.at[listed], sorted_ref.at[listed], consts, y, x, weight, probe_ref, win_ref.at[listed],
                                   xa_ref.at[k], xb_ref.at[k], ya_ref.at[k], yb_ref.at[k], sum_ref, numer_ref))
        interleaved(*stages)
        for k in range(2):
            listed = 2 * step + k
            pltpu.make_async_copy(sorted_ref.at[listed], amp_out.at[listed], out_sems.at[listed]).start()
        return carry

    lax.fori_loop(0, pairs, pair, 0)
    weights_ref, weights_come = late_weights
    weights_come()
    for first in range(0, 2 * tile_rows, CHUNK):
        rows = pl.ds(first, CHUNK)
        scale = 1.0 / (weights_ref[rows, :] + object_regular)
        for comp in range(2):
            sum_ref[comp, rows, :] = sum_ref[comp, rows, :] * scale
    keep = pltpu.make_async_copy(sum_ref, share_out, sum_sem)
    keep.start()
    encode(lambda comp, at, cols: sum_ref[comp, at, cols], top_out, tile_rows, 0, tile_rows)
    encode(lambda comp, at, cols: sum_ref[comp, pl.ds(tile_rows + at.start, at.size), cols], bottom_out, tile_rows, 0, tile_rows)
    spread_sums(numer_out, numer_ref, power_ref)

    def settle(listed, carry):
        pltpu.make_async_copy(sorted_ref.at[listed], amp_out.at[listed], out_sems.at[listed]).wait()
        return carry

    lax.fori_loop(0, 2 * pairs, settle, 0)
    keep.wait()


def rows_sum_kernel(dims, share_ref, above_ref, below_ref, sum_out, left_out, right_out, sem):
    tile_rows, tile_cols = dims[:2]
    for i, ref in enumerate((above_ref, below_ref)):
        for col in range(0, 2 * tile_cols, LANES):
            for start in range(0, tile_rows, CHUNK):
                rows, cols = pl.ds(i * tile_rows + start, CHUNK), pl.ds(col, LANES)
                parts = decode(ref, start, tile_rows, col)
                for comp in range(2):
                    share_ref[comp, rows, cols] += parts[comp]
    keep = pltpu.make_async_copy(share_ref, sum_out, sem)
    keep.start()
    for j, ref in enumerate((left_out, right_out)):
        for i in range(2):

            def read(comp, at, cols, i=i, j=j):
                return share_ref[comp, pl.ds(i * tile_rows + at.start, at.size), pl.ds(j * tile_cols + cols.start, cols.size)]

            encode(read, ref, tile_rows, i * tile_rows, 2 * tile_rows + i * SUBLANES)
    keep.wait()


def whole_kernel(dims, pos_ref, me_ref, old_ref, sum_ref, from_left_ref, from_right_ref, weights_ref,
                 chunks_ref, amp_in, turns, twiddles,
                 current_out, top_out, bottom_out, numer_out, probe_ref,
                 ext_ref, grad_ref, win_ref, xa_ref, xb_ref, ya_ref, yb_ref, numer_ref, far_ref, amp_ref, ys_ref, xs_ref, slots_ref, amp_sems, own_sem, top_sem):
    tile_rows, tile_cols, pat_count, col_count, capacity = dims
    order = probe_ref.shape[1]
    count = list_patterns(dims, pos_ref, me_ref, ys_ref, xs_ref, slots_ref)
    pairs = lax.div(count + 1, 2)
    decode_probe(probe_ref, chunks_ref)

    def fetch(listed):
        return pltpu.make_async_copy(amp_in.at[jnp.minimum(listed, count - 1)], amp_ref.at[listed], amp_sems.at[listed])

    def begin(listed, carry):
        fetch(listed).start()
        return carry

    lax.fori_loop(0, 2 * pairs, begin, 0)
    for j, ref in enumerate((from_left_ref, from_right_ref)):
        for i in range(2):
            for col in range(0, tile_cols, LANES):
                for start in range(0, tile_rows, CHUNK):
                    rows, cols = pl.ds(i * tile_rows + start, CHUNK), pl.ds(j * tile_cols + col, LANES)
                    parts = decode(ref, i * tile_rows + start, 2 * tile_rows + i * SUBLANES, col)
                    scale = object_regular / (weights_ref[rows, cols] + object_regular)
                    for comp in range(2):
                        ext_ref[comp, rows, cols] = old_ref[comp, rows, cols] * scale + (sum_ref[comp, rows, cols] + parts[comp])
    keep = pltpu.make_async_copy(ext_ref.at[:, pl.ds(0, tile_rows), pl.ds(0, tile_cols)], current_out, own_sem)
    keep.start()
    grad_ref[...] = jnp.zeros_like(grad_ref)
    numer_ref[...] = jnp.zeros_like(numer_ref)
    consts = (turns, twiddles)

    def pair(step, carry):
        stages = []
        for k in range(2):
            fetch(2 * step + k).wait()
        for k in range(2):
            listed = 2 * step + k
            weight = (listed < count).astype(f32)
            index = jnp.minimum(listed, count - 1)
            y, x = ys_ref[index], xs_ref[index]

            def both(k=k, listed=listed, weight=weight, y=y, x=x):
                yield from forward(order, ext_ref, probe_ref, consts, y, x, win_ref.at[k], numer_ref.at[2], weight,
                                   xa_ref.at[k], xb_ref.at[k], ya_ref.at[k], yb_ref.at[k], far_ref.at[k])
                yield from backward(order, far_ref.at[k], amp_ref.at[listed], consts, y, x, weight, probe_ref, win_ref.at[k],
                                    xa_ref.at[k], xb_ref.at[k], ya_ref.at[k], yb_ref.at[k], grad_ref, numer_ref)

            stages.append(both())
        interleaved(*stages)
        return carry

    lax.fori_loop(0, pairs, pair, 0)
    for first in range(0, tile_rows, CHUNK):
        rows = pl.ds(first, CHUNK)
        scale = 1.0 / (weights_ref[rows, :] + object_regular)
        for comp in range(2):
            grad_ref[comp, rows, :] = grad_ref[comp, rows, :] * scale
    give = pltpu.make_async_copy(grad_ref.at[:, pl.ds(0, tile_rows), :], top_out, top_sem)
    give.start()

    def read(comp, at, cols):
        rows = pl.ds(tile_rows + at.start, at.size)
        return grad_ref[comp, rows, cols] / (weights_ref[rows, cols] + object_regular)

    encode(read, bottom_out, tile_rows, 0, tile_rows)
    spread_sums(numer_out, numer_ref, numer_ref.at[2])
    keep.wait()
    give.wait()


def fold_kernel(dims, top_ref, above_ref, after_ref, own_out, right_out, own_ref, sem):
    tile_rows, tile_cols = dims[:2]
    for col in range(0, 2 * tile_cols, LANES):
        for start in range(0, tile_rows, CHUNK):
            rows, cols = pl.ds(start, CHUNK), pl.ds(col, LANES)
            parts = decode(above_ref, start, tile_rows, col)
            for comp in range(2):
                if col < tile_cols:
                    own_ref[comp, rows, cols] = top_ref[comp, rows, cols] + parts[comp]
                else:
                    top_ref[comp, rows, cols] += parts[comp]
    keep = pltpu.make_async_copy(own_ref, own_out, sem)
    keep.start()
    encode(lambda comp, at, cols: top_ref[comp, at, pl.ds(tile_cols + cols.start, cols.size)], right_out, tile_rows, 0, tile_rows)
    keep.wait()


def object_kernel(dims, current_ref, own_ref, left_ref, before_ref, weights_ref, out_ref):
    tile_rows, tile_cols = dims[:2]
    for col in range(0, tile_cols, LANES):
        for start in range(0, tile_rows, CHUNK):
            rows, cols = pl.ds(start, CHUNK), pl.ds(col, LANES)
            scale = 1.0 / (weights_ref[rows, cols] + object_regular)
            back = (before_ref[rows, cols] + object_regular) * scale
            parts = decode(left_ref, start, tile_rows, col)
            for comp in range(2):
                old = object_regular * scale * current_ref[comp, rows, cols]
                out_ref[comp, rows, cols] = old + (own_ref[comp, rows, cols] + parts[comp]) * back


def shape(dims, dtype=f32):
    return jax.ShapeDtypeStruct(dims, dtype)


def work_scratch(order):
    return [
        pltpu.VMEM((2, 2, order, order), bf16),
        pltpu.VMEM((2, 2, order, order), bf16),
        pltpu.VMEM((2, order, order), f32),
        pltpu.VMEM((2, order, order), f32),
    ]


def list_scratch(capacity):
    return [pltpu.SMEM((capacity,), jnp.int32)] * 3


def call(kernel, outs, out_specs, in_specs, scratch, flops, limit=26 << 20):
    several = isinstance(outs, tuple)
    out_count = len(outs) if several else 1
    in_count = len(in_specs)
    loaded = [k for k, spec in enumerate(in_specs) if spec is LOAD or spec is LATE]

    def body(*refs):
        ins, rest = list(refs[:in_count]), refs[in_count:]
        given, kept = rest[: out_count + len(scratch)], rest[out_count + len(scratch) :]
        copies = [pltpu.make_async_copy(ins[k], kept[n], kept[-1].at[n]) for n, k in enumerate(loaded)]
        for copy in copies:
            copy.start()
        for n, k in enumerate(loaded):
            if in_specs[k] is LOAD:
                copies[n].wait()
                ins[k] = kept[n]
            else:
                ins[k] = (kept[n], copies[n].wait)
        kernel(*ins, *given)

    fixed_outs = [
        pltpu.HBM(out.shape, out.dtype) if spec is HBM else pltpu.VMEM(out.shape, out.dtype) if spec is PIN else out
        for out, spec in zip(outs if several else (outs,), out_specs if several else (out_specs,))
    ]
    places = [pltpu.HBM if spec in (LOAD, LATE, HBM) else pltpu.VMEM if spec is PIN else None for spec in in_specs]

    def called(*args):
        args = [arg if place is None else pltpu.with_memory_space_constraint(arg, place) for arg, place in zip(args, places)]
        own = [pltpu.VMEM(args[k].shape, args[k].dtype) for k in loaded]
        if loaded:
            own.append(pltpu.SemaphoreType.DMA((len(loaded),)))
        return pl.pallas_call(
            body,
            out_shape=tuple(fixed_outs) if several else fixed_outs[0],
            out_specs=out_specs,
            in_specs=[HBM if spec in (LOAD, LATE) else spec for spec in in_specs],
            scratch_shapes=list(scratch) + own,
            compiler_params=pltpu.CompilerParams(vmem_limit_bytes=limit),
            cost_estimate=pl.CostEstimate(flops=flops, bytes_accessed=8 << 20, transcendentals=0),
        )(*args)

    return called


def passed_along(value, axis, steps):
    count = lax.axis_size(axis)
    leading, last = (max(0, -steps), min(count, count - steps))
    return lax.ppermute(value, axis, [(source, source + steps) for source in range(leading, last)])


def swapped(value, axis, mask):
    return lax.ppermute(value, axis, [(k, k ^ mask) for k in range(lax.axis_size(axis))])


def probe_update(me, probe, numer, kind, before_sum, before_update):
    cols, order = lax.axis_size("col"), probe.shape[1]
    rows = order // cols
    parts = lax.all_to_all(numer, "col", split_axis=0, concat_axis=0, tiled=True)
    total = call(
        functools.partial(sums_kernel, rows), shape((1, sums_rows(rows), order), jnp.int32), VMEM,
        [VMEM] + [spec for spec, _ in before_sum], [], 1 << 26,
    )(parts, *[value for _, value in before_sum])
    totals = [total] + [swapped(total, "row", mask) for mask in range(1, lax.axis_size("row"))]
    fresh = call(
        functools.partial(update_kernel, rows, len(totals)), shape((cols, rows + SUBLANES, order), jnp.int32), VMEM,
        [SMEM, kind] + [VMEM] * len(totals) + [spec for spec, _ in before_update], [], 1 << 26,
    )(me, probe, *totals, *[value for _, value in before_update])
    return lax.all_to_all(fresh, "col", split_axis=0, concat_axis=0, tiled=True)


def local(obj, probe, amplitudes, positions):
    col_count = lax.axis_size("col")
    tile_rows, tile_cols = obj.shape[1], obj.shape[2]
    order = probe.shape[1]
    pat_count = amplitudes.shape[0]
    capacity = 2 * pat_count
    dims = (tile_rows, tile_cols, pat_count, col_count, capacity)
    me = jnp.stack([lax.axis_index("row"), lax.axis_index("col")]).astype(jnp.int32)
    pos = positions.T.reshape(-1)
    turns, twiddles, sorting = tables(order)
    tile = (2, tile_rows, tile_cols)
    window = (2, order, order)
    wide = (2, 2 * tile_rows, 2 * tile_cols)
    shares = shape((col_count, sums_rows(order // col_count), order), jnp.int32)
    coded_tile = shape((tile_rows + SUBLANES, tile_cols), jnp.int32)
    coded_row = shape((tile_rows + SUBLANES, 2 * tile_cols), jnp.int32)
    coded_col = shape((2 * (tile_rows + SUBLANES), tile_cols), jnp.int32)
    one_pattern = 24 * 2 * order**3

    coded = call(encode_kernel, coded_tile, VMEM, [LOAD], [], 1 << 26)(obj)
    right = passed_along(coded, "col", -1)
    below = passed_along(coded, "row", -1)
    diag = passed_along(right, "row", -1)

    outgoing = call(
        functools.partial(outgoing_kernel, dims), shape((col_count * SEND, order, order), bf16), HBM, [SMEM, SMEM, LOAD, FREE, FREE],
        [pltpu.SemaphoreType.DMA((pat_count,))], 1 << 20,
    )(pos, me, amplitudes, right, below)
    incoming = lax.all_to_all(outgoing, "col", split_axis=0, concat_axis=0, tiled=True)

    def weights(probe_now, span, kind):
        return call(
            functools.partial(weights_kernel, dims, span), shape((span * tile_rows, span * tile_cols)), HBM, [SMEM, SMEM, kind],
            [pltpu.VMEM(((span + 2) * tile_rows, (span + 2) * tile_cols), f32), pltpu.VMEM((order, order), f32)], 8 << 30,
        )(pos, me, probe_now)

    weights_old = weights(probe, 2, LOAD)

    far, wins, power, ext = call(
        functools.partial(first_half_kernel, dims), (shape((capacity,) + window), shape((capacity,) + window), shape((order, order)), shape(wide)), (HBM, HBM, VMEM, HBM),
        [SMEM, SMEM, LOAD] + [VMEM] * 3 + [LOAD] * 3,
        [pltpu.VMEM(wide, f32)] + work_scratch(order) + [pltpu.VMEM((capacity,) + window, f32)] * 2 + list_scratch(capacity)
        + [pltpu.SemaphoreType.DMA((capacity,))] * 2 + [pltpu.SemaphoreType.DMA],
        capacity * one_pattern // 2,
    )(pos, me, obj, right, below, diag, probe, turns, twiddles)

    share, top, bottom, numer, sorted_amps = call(
        functools.partial(second_half_kernel, dims),
        (shape(wide), coded_row, coded_row, shares, shape((capacity, order, order), bf16)),
        (HBM, VMEM, VMEM, VMEM, HBM),
        [SMEM, SMEM, LOAD, VMEM, LATE, HBM, HBM, FREE] + [LOAD] * 3,
        [pltpu.VMEM(wide, f32)] + work_scratch(order)
        + [pltpu.VMEM(window, f32)] + [pltpu.VMEM((capacity,) + window, f32)] * 2 + [pltpu.VMEM((capacity, order, order), bf16)] * 2
        + list_scratch(capacity) + [pltpu.SemaphoreType.DMA((capacity,))] * 4 + [pltpu.SemaphoreType.DMA],
        capacity * one_pattern // 2,
    )(pos, me, probe, power, weights_old, far, wins, incoming, turns, twiddles, sorting)

    from_above = passed_along(bottom, "row", 1)
    from_below = passed_along(top, "row", -1)
    sums, to_left, to_right = call(
        functools.partial(rows_sum_kernel, dims), (shape(wide), coded_col, coded_col), (HBM, VMEM, VMEM), [LOAD, VMEM, VMEM], [pltpu.SemaphoreType.DMA], 1 << 26,
    )(share, from_above, from_below)
    from_left = passed_along(to_right, "col", 1)
    from_right = passed_along(to_left, "col", -1)
    chunks = probe_update(me, probe, numer, LOAD, [(FREE, to_left)], [])

    current, top, bottom, numer, probe_now = call(
        functools.partial(whole_kernel, dims), (shape(tile), shape((2, tile_rows, 2 * tile_cols)), coded_row, shares, shape(window)), (HBM, HBM) + (VMEM,) * 3,
        [SMEM, SMEM, LOAD, LOAD, VMEM, VMEM, LOAD, VMEM, HBM, LOAD, LOAD],
        [pltpu.VMEM(wide, f32), pltpu.VMEM(wide, f32), pltpu.VMEM((2,) + window, f32)] + work_scratch(order)
        + [pltpu.VMEM((3, order, order), f32), pltpu.VMEM((2,) + window, f32), pltpu.VMEM((capacity, order, order), bf16)]
        + list_scratch(capacity) + [pltpu.SemaphoreType.DMA((capacity,)), pltpu.SemaphoreType.DMA, pltpu.SemaphoreType.DMA],
        capacity * one_pattern,
    )(pos, me, ext, sums, from_left, from_right, weights_old, chunks, sorted_amps, turns, twiddles)

    from_above = passed_along(bottom, "row", 1)
    weights_new = weights(probe_now, 1, VMEM)
    own, to_right = call(
        functools.partial(fold_kernel, dims), (shape(tile), coded_tile), (HBM, VMEM), [LOAD, VMEM, HBM], [pltpu.VMEM(tile, f32), pltpu.SemaphoreType.DMA], 1 << 26,
    )(top, from_above, weights_new)
    from_left = passed_along(to_right, "col", 1)
    new_object = call(functools.partial(object_kernel, dims), shape(tile), VMEM, [LOAD, LOAD, VMEM, LOAD, LOAD], [], 1 << 26)(
        current, own, from_left, weights_old, weights_new
    )
    chunks = probe_update(me, probe_now, numer, VMEM, [(FREE, to_right)], [(FREE, from_left)])
    new_probe = call(probe_kernel, shape(window), VMEM, [VMEM], [], 1 << 26)(chunks)
    return new_object, new_probe


def solution(mesh):
    placed = (P(None, "row", "col"), P(), P(("row", "col"), None, None), P())
    return jax.shard_map(local, mesh=mesh, in_specs=placed, out_specs=(P(None, "row", "col"), P()), check_vma=False)
```

```python
import functools

import jax
import jax.numpy as jnp
import numpy as np
from jax import lax
from jax.experimental import pallas as pl
from jax.experimental.pallas import tpu as pltpu
from jax.sharding import PartitionSpec as P

ITERS = 2
SEND = 2

amplitude_floor = 0.1
object_regular = 0.5
probe_regular = 1.0

LANES = 128
SUBLANES = 8
LEVELS = 32767.0
CHUNK = 32
VMEM = pl.BlockSpec(memory_space=pltpu.VMEM)
SMEM = pl.BlockSpec(memory_space=pltpu.SMEM)
HBM = pl.BlockSpec(memory_space=pltpu.HBM)
LOAD = object()
LATE = object()
FREE = pl.BlockSpec(memory_space=pl.ANY)
PIN = pl.BlockSpec(memory_space=pltpu.VMEM)
f32 = jnp.float32
bf16 = jnp.bfloat16


def tables(order):
    half = order // 2
    counter = np.arange(half)
    angles = 2.0 * np.pi * ((counter[:, None] * counter[None, :]) % half) / half
    cos, sin = np.cos(angles), np.sin(angles)
    scale = 1.0 / np.sqrt(order)
    turns = []
    for block in ([[cos, -sin], [sin, cos]], [[cos, sin], [-sin, cos]]):
        matrix = np.block(block) * scale
        high = matrix.astype(jnp.bfloat16)
        turns.append(np.stack([high, (matrix - high.astype(np.float64)).astype(jnp.bfloat16)]))
    turn = 2.0 * np.pi * counter / order
    twiddle = np.stack([np.cos(turn), -np.sin(turn)]).astype(np.float32)
    twiddles = np.concatenate(
        [np.broadcast_to(twiddle[:, :, None], (2, half, half)), np.broadcast_to(twiddle[:, None, :], (2, SUBLANES, half))], axis=1
    )
    sorting = np.zeros((order, order), np.float32)
    sorting[np.arange(half), 2 * np.arange(half)] = 1.0
    sorting[half + np.arange(half), 2 * np.arange(half) + 1] = 1.0
    return (
        jnp.asarray(np.stack(turns)),
        jnp.asarray(np.ascontiguousarray(twiddles)),
        jnp.asarray(np.stack([sorting, sorting.T]).astype(jnp.bfloat16)),
    )


def list_patterns(dims, pos_ref, me_ref, ys_ref, xs_ref, slots_ref):
    tile_rows, tile_cols, pat_count, col_count, capacity = dims
    my_row, my_col = me_ref[0], me_ref[1]
    band_count = pat_count * col_count
    first = my_row * band_count
    total = pos_ref.shape[0] // 2

    def visit(index, carry):
        found, source, rank = carry
        y = pos_ref[first + index]
        x = pos_ref[total + first + index]
        here = lax.div(x, tile_cols) == my_col
        holder = lax.div(index, pat_count)
        rank = jnp.where(holder == source, rank, 0)

        @pl.when(here & (found < capacity))
        def _():
            ys_ref[found] = y - my_row * tile_rows
            xs_ref[found] = x - my_col * tile_cols
            slots_ref[found] = holder * SEND + jnp.minimum(rank, SEND - 1)

        step = here.astype(jnp.int32)
        return found + step, holder, rank + step

    found, _, _ = lax.fori_loop(0, band_count, visit, (jnp.int32(0), jnp.int32(-1), jnp.int32(0)))
    return jnp.minimum(found, capacity)


def lane_index(rows):
    return lax.broadcasted_iota(jnp.int32, (rows, LANES), 1)


def shifted_left(tiles, shift):
    lane = lane_index(tiles[0].shape[0])
    turn = lax.rem(LANES - shift, LANES)
    rolled = [pltpu.roll(tile, turn, axis=1) for tile in tiles]
    inside = lane < LANES - shift
    return [jnp.where(inside, a, b) for a, b in zip(rolled[:-1], rolled[1:])]


def shifted_right(tiles, shift):
    lane = lane_index(tiles[0].shape[0])
    rolled = [pltpu.roll(tile, shift, axis=1) for tile in tiles]
    outside = lane < shift
    zero = jnp.zeros_like(rolled[0])
    firsts = [zero] + rolled
    seconds = rolled + [zero]
    return [jnp.where(outside, a, b) for a, b in zip(firsts, seconds)]


def row_groups(tile):
    return [tile[k : k + SUBLANES] for k in range(0, tile.shape[0], SUBLANES)]


def shifted_up(tile, shift):
    row = lax.broadcasted_iota(jnp.int32, (SUBLANES, LANES), 0)
    turn = lax.rem(SUBLANES - shift, SUBLANES)
    rolled = [pltpu.roll(group, turn, axis=0) for group in row_groups(tile)]
    inside = row < SUBLANES - shift
    return jnp.concatenate([jnp.where(inside, a, b) for a, b in zip(rolled[:-1], rolled[1:])], axis=0)


def shifted_down(before, tile, shift):
    row = lax.broadcasted_iota(jnp.int32, (SUBLANES, LANES), 0)
    rolled = [before] + [pltpu.roll(group, shift, axis=0) for group in row_groups(tile)]
    outside = row < shift
    return rolled[-1], jnp.concatenate([jnp.where(outside, a, b) for a, b in zip(rolled[:-1], rolled[1:])], axis=0)


class Deposit:
    def __init__(self, add, top, left):
        self.add = add
        self.row = pl.multiple_of(lax.div(top, SUBLANES) * SUBLANES, SUBLANES)
        self.col = pl.multiple_of(lax.div(left, LANES) * LANES, LANES)
        self.down = lax.rem(top, SUBLANES)
        self.right = lax.rem(left, LANES)
        self.carried = None

    def place(self, first, tiles):
        moved = jnp.concatenate(shifted_right(tiles, self.right), axis=1)
        self.add(pl.ds(self.row + first, tiles[0].shape[0]), pl.ds(self.col, moved.shape[1]), moved)

    def put(self, first, tiles):
        if self.carried is None:
            self.carried = [jnp.zeros((SUBLANES, LANES), f32) for _ in tiles]
        pairs = [shifted_down(before, tile, self.down) for before, tile in zip(self.carried, tiles)]
        self.carried = [carried for carried, _ in pairs]
        self.place(first, [tile for _, tile in pairs])

    def finish(self, first):
        row = lax.broadcasted_iota(jnp.int32, (SUBLANES, LANES), 0)
        self.place(first, [jnp.where(row < self.down, tile, 0.0) for tile in self.carried])


def lane_tiles(value):
    return [value[:, k : k + LANES] for k in range(0, value.shape[1], LANES)]


def store_split(ref, rows, cols, value):
    high = value.astype(bf16)
    ref[0, rows, cols] = high
    ref[1, rows, cols] = (value - high.astype(f32)).astype(bf16)


def right_dot(x_ref, table_ref):
    left = jnp.concatenate([x_ref[0], x_ref[1], x_ref[0]], axis=1)
    right = jnp.concatenate([table_ref[0], table_ref[0], table_ref[1]], axis=0)
    return jnp.dot(left, right, preferred_element_type=f32)


def left_dot(table_ref, x_ref):
    left = jnp.concatenate([table_ref[0], table_ref[0], table_ref[1]], axis=1)
    right = jnp.concatenate([x_ref[0], x_ref[1], x_ref[0]], axis=0)
    return jnp.dot(left, right, preferred_element_type=f32)


def repeated(group, rows):
    return jnp.concatenate([group] * (rows // SUBLANES), axis=0)


def encode(read, out_ref, rows, first, last):
    for col in range(0, out_ref.shape[1], LANES):
        cols = pl.ds(col, LANES)
        largest = jnp.full((SUBLANES, LANES), 1e-30, f32)
        for start in range(0, rows, CHUNK):
            for comp in range(2):
                for group in row_groups(jnp.abs(read(comp, pl.ds(start, CHUNK), cols))):
                    largest = jnp.maximum(largest, group)
        exponent = jnp.ceil(jnp.log2(largest))
        out_ref[last : last + SUBLANES, cols] = exponent.astype(jnp.int32)
        scale = repeated(jnp.exp2(-exponent) * LEVELS, CHUNK)
        for start in range(0, rows, CHUNK):
            codes = []
            for comp in range(2):
                scaled = jnp.clip(read(comp, pl.ds(start, CHUNK), cols) * scale, -LEVELS, LEVELS)
                codes.append(jnp.round(scaled).astype(jnp.int32))
            out_ref[pl.ds(first + start, CHUNK), cols] = (codes[0] << 16) | (codes[1] & 0xFFFF)


def decode(ref, start, last, col):
    cols = pl.ds(col, LANES)
    words = ref[pl.ds(start, CHUNK), cols]
    scale = repeated(jnp.exp2(ref[last : last + SUBLANES, cols].astype(f32)) * (1.0 / LEVELS), CHUNK)
    return (words >> 16).astype(f32) * scale, ((words << 16) >> 16).astype(f32) * scale


def largest_exponent(values):
    largest = jnp.full((SUBLANES, LANES), 1e-30, f32)
    for value in values:
        for group in row_groups(jnp.abs(value)):
            largest = jnp.maximum(largest, group)
    return jnp.ceil(jnp.log2(largest))


def fixed(value, exponent):
    scaled = value * repeated(jnp.exp2(-exponent) * LEVELS, value.shape[0])
    return jnp.round(jnp.clip(scaled, -LEVELS, LEVELS)).astype(jnp.int32)


def paired(first, second):
    return (first << 16) | (second & 0xFFFF)


def unpaired(words):
    return words >> 16, (words << 16) >> 16


def scaled_back(codes, exponent):
    return codes.astype(f32) * repeated(jnp.exp2(exponent.astype(f32)) * (1.0 / LEVELS), codes.shape[0])


def sums_rows(rows):
    return rows + rows // 2 + SUBLANES


def encode_sums(out_ref, cols, u_re, u_im, v):
    rows = v.shape[0]
    half = rows // 2
    of_u, of_v = largest_exponent([u_re, u_im]), largest_exponent([v])
    out_ref[0:rows, cols] = paired(fixed(u_re, of_u), fixed(u_im, of_u))
    codes = fixed(v, of_v)
    out_ref[rows : rows + half, cols] = paired(codes[:half], codes[half:])
    out_ref[rows + half : rows + half + SUBLANES, cols] = paired(of_u.astype(jnp.int32), of_v.astype(jnp.int32))


def decode_sums(ref, cols, rows):
    half = rows // 2
    of_u, of_v = unpaired(ref[rows + half : rows + half + SUBLANES, cols])
    u_re, u_im = unpaired(ref[0:rows, cols])
    v = jnp.concatenate(unpaired(ref[rows : rows + half, cols]), axis=0)
    return scaled_back(u_re, of_u), scaled_back(u_im, of_u), scaled_back(v, of_v)


def decode_probe(out_ref, chunks_ref):
    chunks = chunks_ref.shape[0]
    rows = out_ref.shape[1] // chunks
    for chunk in range(chunks):
        for col in range(0, out_ref.shape[2], LANES):
            cols = pl.ds(col, LANES)
            exponent = chunks_ref[chunk, rows : rows + SUBLANES, cols]
            for comp, codes in enumerate(unpaired(chunks_ref[chunk, 0:rows, cols])):
                out_ref[comp, chunk * rows : (chunk + 1) * rows, cols] = scaled_back(codes, exponent)


def cut_chunk(ext_ref, comp, first, top, left, rows):
    row = pl.multiple_of(lax.div(top, SUBLANES) * SUBLANES, SUBLANES)
    col = pl.multiple_of(lax.div(left, LANES) * LANES, LANES)
    block = ext_ref[comp, pl.ds(row + first, rows + SUBLANES), pl.ds(col, 3 * LANES)]
    tiles = shifted_left(lane_tiles(block), lax.rem(left, LANES))
    return [shifted_up(tile, lax.rem(top, SUBLANES)) for tile in tiles]


def forward(order, ext_ref, probe_ref, consts, y, x, win_ref, power_ref, weight, xa_ref, xb_ref, ya_ref, yb_ref, far_ref):
    turns, twiddles = consts
    half = order // 2
    tw_re = repeated(twiddles[0, half : half + SUBLANES, :], CHUNK)
    tw_im = repeated(twiddles[1, half : half + SUBLANES, :], CHUNK)
    for first in range(0, order, CHUNK):
        rows = pl.ds(first, CHUNK)
        win_re = cut_chunk(ext_ref, 0, first, y, x, CHUNK)
        win_im = cut_chunk(ext_ref, 1, first, y, x, CHUNK)
        exits = []
        for k in range(2):
            cols = pl.ds(k * half, half)
            win_ref[0, rows, cols] = win_re[k]
            win_ref[1, rows, cols] = win_im[k]
            power_ref[rows, cols] += weight * (win_re[k] * win_re[k] + win_im[k] * win_im[k])
            p_re, p_im = probe_ref[0, rows, cols], probe_ref[1, rows, cols]
            exits.append((p_re * win_re[k] - p_im * win_im[k], p_re * win_im[k] + p_im * win_re[k]))
        (lo_re, lo_im), (hi_re, hi_im) = exits
        store_split(xa_ref, rows, pl.ds(0, half), lo_re + hi_re)
        store_split(xa_ref, rows, pl.ds(half, half), lo_im + hi_im)
        d_re, d_im = lo_re - hi_re, lo_im - hi_im
        store_split(xb_ref, rows, pl.ds(0, half), d_re * tw_re - d_im * tw_im)
        store_split(xb_ref, rows, pl.ds(half, half), d_re * tw_im + d_im * tw_re)
    yield
    ya_ref[...] = right_dot(xa_ref, turns.at[0])
    yb_ref[...] = right_dot(xb_ref, turns.at[0])
    yield
    for first in range(0, half, CHUNK):
        rows = pl.ds(first, CHUNK)
        below = pl.ds(half + first, CHUNK)
        t_re, t_im = twiddles[0, rows, :], twiddles[1, rows, :]
        for k, y_ref in enumerate((ya_ref, yb_ref)):
            cols = pl.ds(k * half, half)
            up_re, up_im = y_ref[rows, 0:half], y_ref[rows, half:order]
            dn_re, dn_im = y_ref[below, 0:half], y_ref[below, half:order]
            store_split(xa_ref, rows, cols, up_re + dn_re)
            store_split(xa_ref, below, cols, up_im + dn_im)
            d_re, d_im = up_re - dn_re, up_im - dn_im
            store_split(xb_ref, rows, cols, d_re * t_re - d_im * t_im)
            store_split(xb_ref, below, cols, d_re * t_im + d_im * t_re)
    yield
    far_ref[0] = left_dot(turns.at[1], xa_ref)
    far_ref[1] = left_dot(turns.at[1], xb_ref)
    yield


def backward(order, far_ref, amp_ref, consts, y, x, weight, probe_ref, win_ref, xa_ref, xb_ref, ya_ref, yb_ref, grad_ref, numer_ref):
    turns, twiddles = consts
    half = order // 2
    tw_re = repeated(twiddles[0, half : half + SUBLANES, :], CHUNK)
    tw_im = repeated(twiddles[1, half : half + SUBLANES, :], CHUNK)
    for k, x_ref in enumerate((xa_ref, xb_ref)):
        for first in range(0, half, CHUNK):
            rows = pl.ds(first, CHUNK)
            below = pl.ds(half + first, CHUNK)
            far_re, far_im = far_ref[k, rows, :], far_ref[k, below, :]
            amp = amp_ref[pl.ds(k * half + first, CHUNK), :].astype(f32) * weight
            factor = amp * lax.rsqrt(far_re * far_re + far_im * far_im + amplitude_floor)
            store_split(x_ref, rows, slice(None), far_re * factor)
            store_split(x_ref, below, slice(None), far_im * factor)
    yield
    ya_ref[...] = left_dot(turns.at[0], xa_ref)
    yb_ref[...] = left_dot(turns.at[0], xb_ref)
    yield
    for first in range(0, half, CHUNK):
        rows = pl.ds(first, CHUNK)
        below = pl.ds(half + first, CHUNK)
        t_re, t_im = twiddles[0, rows, :], twiddles[1, rows, :]
        for k, x_ref in enumerate((xa_ref, xb_ref)):
            cols = slice(k * half, (k + 1) * half)
            a_re, a_im = ya_ref[rows, cols], ya_ref[below, cols]
            b_re, b_im = yb_ref[rows, cols], yb_ref[below, cols]
            c_re, c_im = b_re * t_re + b_im * t_im, b_im * t_re - b_re * t_im
            store_split(x_ref, rows, pl.ds(0, half), a_re + c_re)
            store_split(x_ref, rows, pl.ds(half, half), a_im + c_im)
            store_split(x_ref, below, pl.ds(0, half), a_re - c_re)
            store_split(x_ref, below, pl.ds(half, half), a_im - c_im)
    yield
    ya_ref[...] = right_dot(xa_ref, turns.at[1])
    yb_ref[...] = right_dot(xb_ref, turns.at[1])
    yield

    def adder(comp):
        def add(rows, cols, moved):
            grad_ref[comp, rows, cols] += moved

        return add

    deposits = [Deposit(adder(comp), y, x) for comp in range(2)]
    for first in range(0, order, CHUNK):
        rows = pl.ds(first, CHUNK)
        a_re, a_im = ya_ref[rows, 0:half], ya_ref[rows, half:order]
        b_re, b_im = yb_ref[rows, 0:half], yb_ref[rows, half:order]
        c_re, c_im = b_re * tw_re + b_im * tw_im, b_im * tw_re - b_re * tw_im
        waves = [(a_re + c_re, a_im + c_im), (a_re - c_re, a_im - c_im)]
        terms = ([], [])
        for k, (wave_re, wave_im) in enumerate(waves):
            cols = pl.ds(k * half, half)
            p_re, p_im = probe_ref[0, rows, cols], probe_ref[1, rows, cols]
            w_re, w_im = win_ref[0, rows, cols], win_ref[1, rows, cols]
            terms[0].append(p_re * wave_re + p_im * wave_im)
            terms[1].append(p_re * wave_im - p_im * wave_re)
            numer_ref[0, rows, cols] += w_re * wave_re + w_im * wave_im
            numer_ref[1, rows, cols] += w_re * wave_im - w_im * wave_re
        for comp in range(2):
            deposits[comp].put(first, terms[comp])
    for deposit in deposits:
        deposit.finish(order)
    yield


def interleaved(*stages):
    live = list(stages)
    while live:
        still = []
        for stage in live:
            try:
                next(stage)
                still.append(stage)
            except StopIteration:
                pass
        live = still


def outgoing_kernel(dims, pos_ref, me_ref, amp_ref, after_ref, also_ref, out_ref, sems):
    tile_rows, tile_cols, pat_count, col_count, capacity = dims
    first = (me_ref[0] * col_count + me_ref[1]) * pat_count
    total = pos_ref.shape[0] // 2
    owners = [lax.div(pos_ref[total + first + k], tile_cols) for k in range(pat_count)]
    copies = []
    for k in range(pat_count):
        rank = sum(((owners[e] == owners[k]).astype(jnp.int32) for e in range(k)), jnp.int32(0))
        slot = owners[k] * SEND + jnp.minimum(rank, SEND - 1)
        copies.append(pltpu.make_async_copy(amp_ref.at[k], out_ref.at[slot], sems.at[k]))
        copies[-1].start()
    for copy in copies:
        copy.wait()


def weights_kernel(dims, span, pos_ref, me_ref, probe_ref, out_ref, sums_ref, power_ref):
    tile_rows, tile_cols, pat_count, col_count, capacity = dims
    order = probe_ref.shape[1]
    top = (me_ref[0] - 1) * tile_rows
    left = (me_ref[1] - 1) * tile_cols
    total = pos_ref.shape[0] // 2
    for first in range(0, sums_ref.shape[0], order):
        sums_ref[pl.ds(first, order), :] = jnp.zeros((order, sums_ref.shape[1]), f32)
    power_ref[...] = probe_ref[0] * probe_ref[0] + probe_ref[1] * probe_ref[1]

    def visit(index, carry):
        y = pos_ref[index] - top
        x = pos_ref[total + index] - left

        @pl.when((y > 0) & (y < (span + 1) * tile_rows) & (x > 0) & (x < (span + 1) * tile_cols))
        def _():
            def add(rows, cols, moved):
                sums_ref[rows, cols] += moved

            deposit = Deposit(add, y, x)
            for first in range(0, order, CHUNK):
                deposit.put(first, lane_tiles(power_ref[pl.ds(first, CHUNK), :]))
            deposit.finish(order)

        return carry

    lax.fori_loop(0, total, visit, 0)
    pltpu.sync_copy(sums_ref.at[pl.ds(tile_rows, span * tile_rows), pl.ds(tile_cols, span * tile_cols)], out_ref)


def encode_kernel(obj_ref, out_ref):
    rows = obj_ref.shape[1]
    encode(lambda comp, at, cols: obj_ref[comp, at, cols], out_ref, rows, 0, rows)


def unfold(dims, ext_ref, own_ref, coded_refs):
    tile_rows, tile_cols = dims[:2]
    ext_ref[:, 0:tile_rows, 0:tile_cols] = own_ref[...]
    for (i, j), ref in zip(((0, 1), (1, 0), (1, 1)), coded_refs):
        for col in range(0, tile_cols, LANES):
            for start in range(0, tile_rows, CHUNK):
                parts = decode(ref, start, tile_rows, col)
                for comp in range(2):
                    ext_ref[comp, pl.ds(i * tile_rows + start, CHUNK), pl.ds(j * tile_cols + col, LANES)] = parts[comp]


def spread_sums(out_ref, u_ref, v_ref):
    chunks = out_ref.shape[0]
    rows = v_ref.shape[0] // chunks
    for chunk in range(chunks):
        at = pl.ds(chunk * rows, rows)
        for col in range(0, v_ref.shape[1], LANES):
            cols = pl.ds(col, LANES)
            encode_sums(out_ref.at[chunk], cols, u_ref[0, at, cols], u_ref[1, at, cols], v_ref[at, cols])


def added(parts):
    while len(parts) > 1:
        parts = [tuple(x + y for x, y in zip(a, b)) for a, b in zip(parts[::2], parts[1::2])]
    return parts[0]


def sums_kernel(rows, parts_ref, *refs):
    out_ref = refs[-1]
    for col in range(0, out_ref.shape[2], LANES):
        cols = pl.ds(col, LANES)
        total = added([decode_sums(parts_ref.at[k], cols, rows) for k in range(parts_ref.shape[0])])
        encode_sums(out_ref.at[0], cols, *total)
        for k in range(1, out_ref.shape[0]):
            out_ref[k, :, cols] = out_ref[0, :, cols]


def update_kernel(rows, count, me_ref, probe_ref, *refs):
    out_ref = refs[-1]
    first = pl.multiple_of(me_ref[1] * rows, SUBLANES)
    for col in range(0, out_ref.shape[2], LANES):
        cols = pl.ds(col, LANES)
        u_re, u_im, v = added([decode_sums(ref.at[k], cols, rows) for ref in refs[:count] for k in range(ref.shape[0])])
        scale = 1.0 / (v + probe_regular)
        re = (probe_ref[0, pl.ds(first, rows), cols] + u_re) * scale
        im = (probe_ref[1, pl.ds(first, rows), cols] + u_im) * scale
        exponent = largest_exponent([re, im])
        words = paired(fixed(re, exponent), fixed(im, exponent))
        for chunk in range(out_ref.shape[0]):
            out_ref[chunk, 0:rows, cols] = words
            out_ref[chunk, rows : rows + SUBLANES, cols] = exponent.astype(jnp.int32)


def probe_kernel(chunks_ref, out_ref):
    decode_probe(out_ref, chunks_ref)


def first_half_kernel(dims, pos_ref, me_ref, own_ref, right_ref, below_ref, diag_ref, probe_ref, turns, twiddles,
                      far_out, win_out, power_out, ext_out, ext_ref, xa_ref, xb_ref, ya_ref, yb_ref, far_ref, win_ref, ys_ref, xs_ref, slots_ref, sems, win_sems, ext_sem):
    tile_rows, tile_cols, pat_count, col_count, capacity = dims
    order = probe_ref.shape[1]
    count = list_patterns(dims, pos_ref, me_ref, ys_ref, xs_ref, slots_ref)
    unfold(dims, ext_ref, own_ref, (right_ref, below_ref, diag_ref))
    keep = pltpu.make_async_copy(ext_ref, ext_out, ext_sem)
    keep.start()
    power_out[...] = jnp.zeros_like(power_out)
    consts = (turns, twiddles)

    def pair(step, carry):
        stages = []
        for k in range(2):
            listed = 2 * step + k
            weight = (listed < count).astype(f32)
            index = jnp.minimum(listed, count - 1)
            stages.append(forward(order, ext_ref, probe_ref, consts, ys_ref[index], xs_ref[index], win_ref.at[listed], power_out, weight,
                                  xa_ref.at[k], xb_ref.at[k], ya_ref.at[k], yb_ref.at[k], far_ref.at[listed]))
        interleaved(*stages)
        for k in range(2):
            listed = 2 * step + k
            pltpu.make_async_copy(far_ref.at[listed], far_out.at[listed], sems.at[listed]).start()
            pltpu.make_async_copy(win_ref.at[listed], win_out.at[listed], win_sems.at[listed]).start()
        return carry

    pairs = lax.div(count + 1, 2)
    lax.fori_loop(0, pairs, pair, 0)

    def settle(listed, carry):
        pltpu.make_async_copy(far_ref.at[listed], far_out.at[listed], sems.at[listed]).wait()
        pltpu.make_async_copy(win_ref.at[listed], win_out.at[listed], win_sems.at[listed]).wait()
        return carry

    lax.fori_loop(0, 2 * pairs, settle, 0)
    keep.wait()


def second_half_kernel(dims, pos_ref, me_ref, probe_ref, power_ref, late_weights, far_in, win_in, amp_in, turns, twiddles, sorting,
                       share_out, top_out, bottom_out, numer_out, amp_out,
                       sum_ref, xa_ref, xb_ref, ya_ref, yb_ref, numer_ref, far_ref, win_ref, amp_ref, sorted_ref, ys_ref, xs_ref, slots_ref, far_sems, win_sems, amp_sems, out_sems, sum_sem):
    tile_rows, tile_cols, pat_count, col_count, capacity = dims
    order = probe_ref.shape[1]
    count = list_patterns(dims, pos_ref, me_ref, ys_ref, xs_ref, slots_ref)
    pairs = lax.div(count + 1, 2)

    def copies(listed):
        return (
            pltpu.make_async_copy(far_in.at[listed], far_ref.at[listed], far_sems.at[listed]),
            pltpu.make_async_copy(win_in.at[listed], win_ref.at[listed], win_sems.at[listed]),
            pltpu.make_async_copy(amp_in.at[slots_ref[jnp.minimum(listed, count - 1)]], amp_ref.at[listed], amp_sems.at[listed]),
        )

    def begin(listed, carry):
        for copy in copies(listed):
            copy.start()
        return carry

    lax.fori_loop(0, 2 * pairs, begin, 0)
    sum_ref[...] = jnp.zeros_like(sum_ref)
    numer_ref[...] = jnp.zeros_like(numer_ref)
    consts = (turns, twiddles)

    def pair(step, carry):
        stages = []
        for k in range(2):
            listed = 2 * step + k
            for copy in copies(listed):
                copy.wait()
        for k in range(2):
            listed = 2 * step + k
            weight = (listed < count).astype(f32)
            index = jnp.minimum(listed, count - 1)
            y, x = ys_ref[index], xs_ref[index]
            rows_sorted = jnp.dot(sorting[0], amp_ref[listed], preferred_element_type=f32).astype(bf16)
            sorted_ref[listed] = jnp.dot(rows_sorted, sorting[1], preferred_element_type=f32).astype(bf16)
            stages.append(backward(order, far_ref.at[listed], sorted_ref.at[listed], consts, y, x, weight, probe_ref, win_ref.at[listed],
                                   xa_ref.at[k], xb_ref.at[k], ya_ref.at[k], yb_ref.at[k], sum_ref, numer_ref))
        interleaved(*stages)
        for k in range(2):
            listed = 2 * step + k
            pltpu.make_async_copy(sorted_ref.at[listed], amp_out.at[listed], out_sems.at[listed]).start()
        return carry

    lax.fori_loop(0, pairs, pair, 0)
    weights_ref, weights_come = late_weights
    weights_come()
    for first in range(0, 2 * tile_rows, CHUNK):
        rows = pl.ds(first, CHUNK)
        scale = 1.0 / (weights_ref[rows, :] + object_regular)
        for comp in range(2):
            sum_ref[comp, rows, :] = sum_ref[comp, rows, :] * scale
    keep = pltpu.make_async_copy(sum_ref, share_out, sum_sem)
    keep.start()
    encode(lambda comp, at, cols: sum_ref[comp, at, cols], top_out, tile_rows, 0, tile_rows)
    encode(lambda comp, at, cols: sum_ref[comp, pl.ds(tile_rows + at.start, at.size), cols], bottom_out, tile_rows, 0, tile_rows)
    spread_sums(numer_out, numer_ref, power_ref)

    def settle(listed, carry):
        pltpu.make_async_copy(sorted_ref.at[listed], amp_out.at[listed], out_sems.at[listed]).wait()
        return carry

    lax.fori_loop(0, 2 * pairs, settle, 0)
    keep.wait()


def rows_sum_kernel(dims, share_ref, above_ref, below_ref, after_ref, sum_out, left_out, right_out, sem):
    tile_rows, tile_cols = dims[:2]
    for i, ref in enumerate((above_ref, below_ref)):
        for col in range(0, 2 * tile_cols, LANES):
            for start in range(0, tile_rows, CHUNK):
                rows, cols = pl.ds(i * tile_rows + start, CHUNK), pl.ds(col, LANES)
                parts = decode(ref, start, tile_rows, col)
                for comp in range(2):
                    share_ref[comp, rows, cols] += parts[comp]
    keep = pltpu.make_async_copy(share_ref, sum_out, sem)
    keep.start()
    for j, ref in enumerate((left_out, right_out)):
        for i in range(2):

            def read(comp, at, cols, i=i, j=j):
                return share_ref[comp, pl.ds(i * tile_rows + at.start, at.size), pl.ds(j * tile_cols + cols.start, cols.size)]

            encode(read, ref, tile_rows, i * tile_rows, 2 * tile_rows + i * SUBLANES)
    keep.wait()


def whole_kernel(dims, pos_ref, me_ref, old_ref, sum_ref, from_left_ref, from_right_ref, weights_ref,
                 chunks_ref, amp_in, turns, twiddles,
                 current_out, top_out, bottom_out, numer_out, probe_ref,
                 ext_ref, grad_ref, win_ref, xa_ref, xb_ref, ya_ref, yb_ref, numer_ref, far_ref, amp_ref, ys_ref, xs_ref, slots_ref, amp_sems, own_sem, top_sem):
    tile_rows, tile_cols, pat_count, col_count, capacity = dims
    order = probe_ref.shape[1]
    count = list_patterns(dims, pos_ref, me_ref, ys_ref, xs_ref, slots_ref)
    pairs = lax.div(count + 1, 2)
    decode_probe(probe_ref, chunks_ref)

    def fetch(listed):
        return pltpu.make_async_copy(amp_in.at[jnp.minimum(listed, count - 1)], amp_ref.at[listed], amp_sems.at[listed])

    def begin(listed, carry):
        fetch(listed).start()
        return carry

    lax.fori_loop(0, 2 * pairs, begin, 0)
    for j, ref in enumerate((from_left_ref, from_right_ref)):
        for i in range(2):
            for col in range(0, tile_cols, LANES):
                for start in range(0, tile_rows, CHUNK):
                    rows, cols = pl.ds(i * tile_rows + start, CHUNK), pl.ds(j * tile_cols + col, LANES)
                    parts = decode(ref, i * tile_rows + start, 2 * tile_rows + i * SUBLANES, col)
                    scale = object_regular / (weights_ref[rows, cols] + object_regular)
                    for comp in range(2):
                        ext_ref[comp, rows, cols] = old_ref[comp, rows, cols] * scale + (sum_ref[comp, rows, cols] + parts[comp])
    keep = pltpu.make_async_copy(ext_ref.at[:, pl.ds(0, tile_rows), pl.ds(0, tile_cols)], current_out, own_sem)
    keep.start()
    grad_ref[...] = jnp.zeros_like(grad_ref)
    numer_ref[...] = jnp.zeros_like(numer_ref)
    consts = (turns, twiddles)

    def pair(step, carry):
        stages = []
        for k in range(2):
            fetch(2 * step + k).wait()
        for k in range(2):
            listed = 2 * step + k
            weight = (listed < count).astype(f32)
            index = jnp.minimum(listed, count - 1)
            y, x = ys_ref[index], xs_ref[index]

            def both(k=k, listed=listed, weight=weight, y=y, x=x):
                yield from forward(order, ext_ref, probe_ref, consts, y, x, win_ref.at[k], numer_ref.at[2], weight,
                                   xa_ref.at[k], xb_ref.at[k], ya_ref.at[k], yb_ref.at[k], far_ref.at[k])
                yield from backward(order, far_ref.at[k], amp_ref.at[listed], consts, y, x, weight, probe_ref, win_ref.at[k],
                                    xa_ref.at[k], xb_ref.at[k], ya_ref.at[k], yb_ref.at[k], grad_ref, numer_ref)

            stages.append(both())
        interleaved(*stages)
        return carry

    lax.fori_loop(0, pairs, pair, 0)
    for first in range(0, tile_rows, CHUNK):
        rows = pl.ds(first, CHUNK)
        scale = 1.0 / (weights_ref[rows, :] + object_regular)
        for comp in range(2):
            grad_ref[comp, rows, :] = grad_ref[comp, rows, :] * scale
    give = pltpu.make_async_copy(grad_ref.at[:, pl.ds(0, tile_rows), :], top_out, top_sem)
    give.start()

    def read(comp, at, cols):
        rows = pl.ds(tile_rows + at.start, at.size)
        return grad_ref[comp, rows, cols] / (weights_ref[rows, cols] + object_regular)

    encode(read, bottom_out, tile_rows, 0, tile_rows)
    spread_sums(numer_out, numer_ref, numer_ref.at[2])
    keep.wait()
    give.wait()


def fold_kernel(dims, top_ref, above_ref, own_out, right_out, own_ref, sem):
    tile_rows, tile_cols = dims[:2]
    for col in range(0, 2 * tile_cols, LANES):
        for start in range(0, tile_rows, CHUNK):
            rows, cols = pl.ds(start, CHUNK), pl.ds(col, LANES)
            parts = decode(above_ref, start, tile_rows, col)
            for comp in range(2):
                if col < tile_cols:
                    own_ref[comp, rows, cols] = top_ref[comp, rows, cols] + parts[comp]
                else:
                    top_ref[comp, rows, cols] += parts[comp]
    keep = pltpu.make_async_copy(own_ref, own_out, sem)
    keep.start()
    encode(lambda comp, at, cols: top_ref[comp, at, pl.ds(tile_cols + cols.start, cols.size)], right_out, tile_rows, 0, tile_rows)
    keep.wait()


def object_kernel(dims, current_ref, own_ref, left_ref, before_ref, weights_ref, out_ref):
    tile_rows, tile_cols = dims[:2]
    for col in range(0, tile_cols, LANES):
        for start in range(0, tile_rows, CHUNK):
            rows, cols = pl.ds(start, CHUNK), pl.ds(col, LANES)
            scale = 1.0 / (weights_ref[rows, cols] + object_regular)
            back = (before_ref[rows, cols] + object_regular) * scale
            parts = decode(left_ref, start, tile_rows, col)
            for comp in range(2):
                old = object_regular * scale * current_ref[comp, rows, cols]
                out_ref[comp, rows, cols] = old + (own_ref[comp, rows, cols] + parts[comp]) * back


def shape(dims, dtype=f32):
    return jax.ShapeDtypeStruct(dims, dtype)


def work_scratch(order):
    return [
        pltpu.VMEM((2, 2, order, order), bf16),
        pltpu.VMEM((2, 2, order, order), bf16),
        pltpu.VMEM((2, order, order), f32),
        pltpu.VMEM((2, order, order), f32),
    ]


def list_scratch(capacity):
    return [pltpu.SMEM((capacity,), jnp.int32)] * 3


def call(kernel, outs, out_specs, in_specs, scratch, flops, limit=26 << 20):
    several = isinstance(outs, tuple)
    out_count = len(outs) if several else 1
    in_count = len(in_specs)
    loaded = [k for k, spec in enumerate(in_specs) if spec is LOAD or spec is LATE]

    def body(*refs):
        ins, rest = list(refs[:in_count]), refs[in_count:]
        given, kept = rest[: out_count + len(scratch)], rest[out_count + len(scratch) :]
        copies = [pltpu.make_async_copy(ins[k], kept[n], kept[-1].at[n]) for n, k in enumerate(loaded)]
        for copy in copies:
            copy.start()
        for n, k in enumerate(loaded):
            if in_specs[k] is LOAD:
                copies[n].wait()
                ins[k] = kept[n]
            else:
                ins[k] = (kept[n], copies[n].wait)
        kernel(*ins, *given)

    fixed_outs = [
        pltpu.HBM(out.shape, out.dtype) if spec is HBM else pltpu.VMEM(out.shape, out.dtype) if spec is PIN else out
        for out, spec in zip(outs if several else (outs,), out_specs if several else (out_specs,))
    ]
    places = [pltpu.HBM if spec in (LOAD, LATE, HBM) else pltpu.VMEM if spec is PIN else None for spec in in_specs]

    def called(*args):
        args = [arg if place is None else pltpu.with_memory_space_constraint(arg, place) for arg, place in zip(args, places)]
        own = [pltpu.VMEM(args[k].shape, args[k].dtype) for k in loaded]
        if loaded:
            own.append(pltpu.SemaphoreType.DMA((len(loaded),)))
        return pl.pallas_call(
            body,
            out_shape=tuple(fixed_outs) if several else fixed_outs[0],
            out_specs=out_specs,
            in_specs=[HBM if spec in (LOAD, LATE) else spec for spec in in_specs],
            scratch_shapes=list(scratch) + own,
            compiler_params=pltpu.CompilerParams(vmem_limit_bytes=limit),
            cost_estimate=pl.CostEstimate(flops=flops, bytes_accessed=8 << 20, transcendentals=0),
        )(*args)

    return called


def passed_along(value, axis, steps):
    count = lax.axis_size(axis)
    leading, last = (max(0, -steps), min(count, count - steps))
    return lax.ppermute(value, axis, [(source, source + steps) for source in range(leading, last)])


def swapped(value, axis, mask):
    return lax.ppermute(value, axis, [(k, k ^ mask) for k in range(lax.axis_size(axis))])


def probe_update(me, probe, numer, kind, at_once, before_sum, before_update):
    cols, order = lax.axis_size("col"), probe.shape[1]
    rows = order // cols
    parts = lax.all_to_all(numer, "col", split_axis=0, concat_axis=0, tiled=True)
    blocks = lax.axis_size("row") if at_once else 1
    total = call(
        functools.partial(sums_kernel, rows), shape((blocks, sums_rows(rows), order), jnp.int32), VMEM,
        [VMEM] + [spec for spec, _ in before_sum], [], 1 << 26,
    )(parts, *[value for _, value in before_sum])
    if at_once:
        totals = [lax.all_to_all(total, "row", split_axis=0, concat_axis=0, tiled=True)]
    else:
        totals = [total] + [swapped(total, "row", mask) for mask in range(1, lax.axis_size("row"))]
    fresh = call(
        functools.partial(update_kernel, rows, len(totals)), shape((cols, rows + SUBLANES, order), jnp.int32), VMEM,
        [SMEM, kind] + [VMEM] * len(totals) + [spec for spec, _ in before_update], [], 1 << 26,
    )(me, probe, *totals, *[value for _, value in before_update])
    return total, lax.all_to_all(fresh, "col", split_axis=0, concat_axis=0, tiled=True)


def local(obj, probe, amplitudes, positions):
    col_count = lax.axis_size("col")
    tile_rows, tile_cols = obj.shape[1], obj.shape[2]
    order = probe.shape[1]
    pat_count = amplitudes.shape[0]
    capacity = 2 * pat_count
    dims = (tile_rows, tile_cols, pat_count, col_count, capacity)
    me = jnp.stack([lax.axis_index("row"), lax.axis_index("col")]).astype(jnp.int32)
    pos = positions.T.reshape(-1)
    turns, twiddles, sorting = tables(order)
    tile = (2, tile_rows, tile_cols)
    window = (2, order, order)
    wide = (2, 2 * tile_rows, 2 * tile_cols)
    shares = shape((col_count, sums_rows(order // col_count), order), jnp.int32)
    coded_tile = shape((tile_rows + SUBLANES, tile_cols), jnp.int32)
    coded_row = shape((tile_rows + SUBLANES, 2 * tile_cols), jnp.int32)
    coded_col = shape((2 * (tile_rows + SUBLANES), tile_cols), jnp.int32)
    one_pattern = 24 * 2 * order**3

    coded = call(encode_kernel, coded_tile, VMEM, [LOAD], [], 1 << 26)(obj)
    right = passed_along(coded, "col", -1)
    below = passed_along(coded, "row", -1)
    diag = passed_along(right, "row", -1)

    outgoing = call(
        functools.partial(outgoing_kernel, dims), shape((col_count * SEND, order, order), bf16), HBM, [SMEM, SMEM, LOAD, FREE, FREE],
        [pltpu.SemaphoreType.DMA((pat_count,))], 1 << 20,
    )(pos, me, amplitudes, right, below)
    incoming = lax.all_to_all(outgoing, "col", split_axis=0, concat_axis=0, tiled=True)

    def weights(probe_now, span, kind):
        return call(
            functools.partial(weights_kernel, dims, span), shape((span * tile_rows, span * tile_cols)), HBM, [SMEM, SMEM, kind],
            [pltpu.VMEM(((span + 2) * tile_rows, (span + 2) * tile_cols), f32), pltpu.VMEM((order, order), f32)], 8 << 30,
        )(pos, me, probe_now)

    weights_old = weights(probe, 2, LOAD)

    far, wins, power, ext = call(
        functools.partial(first_half_kernel, dims), (shape((capacity,) + window), shape((capacity,) + window), shape((order, order)), shape(wide)), (HBM, HBM, VMEM, HBM),
        [SMEM, SMEM, LOAD] + [VMEM] * 3 + [LOAD] * 3,
        [pltpu.VMEM(wide, f32)] + work_scratch(order) + [pltpu.VMEM((capacity,) + window, f32)] * 2 + list_scratch(capacity)
        + [pltpu.SemaphoreType.DMA((capacity,))] * 2 + [pltpu.SemaphoreType.DMA],
        capacity * one_pattern // 2,
    )(pos, me, obj, right, below, diag, probe, turns, twiddles)

    share, top, bottom, numer, sorted_amps = call(
        functools.partial(second_half_kernel, dims),
        (shape(wide), coded_row, coded_row, shares, shape((capacity, order, order), bf16)),
        (HBM, VMEM, VMEM, VMEM, HBM),
        [SMEM, SMEM, LOAD, VMEM, LATE, HBM, HBM, FREE] + [LOAD] * 3,
        [pltpu.VMEM(wide, f32)] + work_scratch(order)
        + [pltpu.VMEM(window, f32)] + [pltpu.VMEM((capacity,) + window, f32)] * 2 + [pltpu.VMEM((capacity, order, order), bf16)] * 2
        + list_scratch(capacity) + [pltpu.SemaphoreType.DMA((capacity,))] * 4 + [pltpu.SemaphoreType.DMA],
        capacity * one_pattern // 2,
    )(pos, me, probe, power, weights_old, far, wins, incoming, turns, twiddles, sorting)

    from_above = passed_along(bottom, "row", 1)
    from_below = passed_along(top, "row", -1)
    total, chunks = probe_update(me, probe, numer, LOAD, True, [], [])
    sums, to_left, to_right = call(
        functools.partial(rows_sum_kernel, dims), (shape(wide), coded_col, coded_col), (HBM, VMEM, VMEM), [LOAD, VMEM, VMEM, FREE], [pltpu.SemaphoreType.DMA], 1 << 26,
    )(share, from_above, from_below, total)
    from_left = passed_along(to_right, "col", 1)
    from_right = passed_along(to_left, "col", -1)

    current, top, bottom, numer, probe_now = call(
        functools.partial(whole_kernel, dims), (shape(tile), shape((2, tile_rows, 2 * tile_cols)), coded_row, shares, shape(window)), (HBM, HBM) + (VMEM,) * 3,
        [SMEM, SMEM, LOAD, LOAD, VMEM, VMEM, LOAD, VMEM, HBM, LOAD, LOAD],
        [pltpu.VMEM(wide, f32), pltpu.VMEM(wide, f32), pltpu.VMEM((2,) + window, f32)] + work_scratch(order)
        + [pltpu.VMEM((3, order, order), f32), pltpu.VMEM((2,) + window, f32), pltpu.VMEM((capacity, order, order), bf16)]
        + list_scratch(capacity) + [pltpu.SemaphoreType.DMA((capacity,)), pltpu.SemaphoreType.DMA, pltpu.SemaphoreType.DMA],
        capacity * one_pattern,
    )(pos, me, ext, sums, from_left, from_right, weights_old, chunks, sorted_amps, turns, twiddles)

    from_above = passed_along(bottom, "row", 1)
    weights_new = weights(probe_now, 1, VMEM)
    own, to_right = call(
        functools.partial(fold_kernel, dims), (shape(tile), coded_tile), (HBM, VMEM), [LOAD, VMEM], [pltpu.VMEM(tile, f32), pltpu.SemaphoreType.DMA], 1 << 26,
    )(top, from_above)
    from_left = passed_along(to_right, "col", 1)
    new_object = call(functools.partial(object_kernel, dims), shape(tile), VMEM, [LOAD, LOAD, VMEM, LOAD, LOAD], [], 1 << 26)(
        current, own, from_left, weights_old, weights_new
    )
    _, chunks = probe_update(me, probe_now, numer, VMEM, False, [(FREE, to_right)], [(FREE, from_left)])
    new_probe = call(probe_kernel, shape(window), VMEM, [VMEM], [], 1 << 26)(chunks)
    return new_object, new_probe


def solution(mesh):
    placed = (P(None, "row", "col"), P(), P(("row", "col"), None, None), P())
    return jax.shard_map(local, mesh=mesh, in_specs=placed, out_specs=(P(None, "row", "col"), P()), check_vma=False)
```
